32 devices in a mesh: dp: 8 (over y, x, core), mp: 4 (over z).
Axes of the slice: x: 2, y: 2, z: 4, core: 2. Of those that a mesh axis runs over, the one named last changes fastest.
Arguments:
- hidden_in: float32 [16384, 768], P(('dp', 'mp')), may hold values from -6 to 6
- out_grad: float32 [16384, 768], P(('dp', 'mp')), may hold values from -6 to 6
- attn_weight: float32 [3, 768, 768], P(None, 'dp', 'mp'), may hold values from -0.109375 to 0.109375
- out_weight: float32 [768, 768], P('mp', 'dp'), may hold values from -2.5 to 2.5
- inner_weight: float32 [768, 3072], P('dp', 'mp'), may hold values from -0.21875 to 0.21875
- outer_weight: float32 [3072, 768], P('mp', 'dp'), may hold values from -0.109375 to 0.109375
- rel_bias: float32 [32, 12], replicated, may hold values from -4 to 4
- gains: float32 [2, 768], replicated, may hold values from 0.4 to 2.9
- lengths: int32 [16], P('dp'), may hold values from 256 to 1024, as said below
- table: int32 [2047], replicated, may hold values from 0 to 31, as said below
- attn_first: float32 [3, 768, 768], P(None, 'dp', 'mp'), may hold values from -0.0009765625 to 0.0009765625
- attn_second: float32 [3, 768, 768], P(None, 'dp', 'mp'), may hold values from 4.2385526e-10 to 1.695421e-09
- out_first: float32 [768, 768], P('mp', 'dp'), may hold values from -3.8146973e-05 to 3.8146973e-05
- out_second: float32 [768, 768], P('mp', 'dp'), may hold values from 5.298191e-13 to 2.1192763e-12
- inner_first: float32 [768, 3072], P('dp', 'mp'), may hold values from -6.1035156e-05 to 6.1035156e-05
- inner_second: float32 [768, 3072], P('dp', 'mp'), may hold values from 1.695421e-12 to 6.781684e-12
- outer_first: float32 [3072, 768], P('mp', 'dp'), may hold values from -9.1552734e-05 to 9.1552734e-05
- outer_second: float32 [3072, 768], P('mp', 'dp'), may hold values from 3.390842e-12 to 1.3563368e-11
- rel_first: float32 [32, 12], replicated, may hold values from -3.8146973e-05 to 3.8146973e-05
- rel_second: float32 [32, 12], replicated, may hold values from 5.298191e-13 to 2.1192763e-12
- gain_first: float32 [2, 768], replicated, may hold values from -0.0007324219 to 0.0007324219
- gain_second: float32 [2, 768], replicated, may hold values from 2.1192763e-10 to 8.477105e-10
Outputs:
- block_out: float32 [16384, 768], P(('dp', 'mp'))
- input_grad: float32 [16384, 768], P(('dp', 'mp'))
- grad_norm: float32 [], replicated
- attn_master: float32 [3, 768, 768], P(None, 'dp', 'mp')
- attn_moment: float32 [3, 768, 768], P(None, 'dp', 'mp')
- attn_square: float32 [3, 768, 768], P(None, 'dp', 'mp')
- out_master: float32 [768, 768], P('mp', 'dp')
- out_moment: float32 [768, 768], P('mp', 'dp')
- out_square: float32 [768, 768], P('mp', 'dp')
- inner_master: float32 [768, 3072], P('dp', 'mp')
- inner_moment: float32 [768, 3072], P('dp', 'mp')
- inner_square: float32 [768, 3072], P('dp', 'mp')
- outer_master: float32 [3072, 768], P('mp', 'dp')
- outer_moment: float32 [3072, 768], P('mp', 'dp')
- outer_square: float32 [3072, 768], P('mp', 'dp')
- rel_master: float32 [32, 12], replicated
- rel_moment: float32 [32, 12], replicated
- rel_square: float32 [32, 12], replicated
- gain_master: float32 [2, 768], replicated
- gain_moment: float32 [2, 768], replicated
- gain_square: float32 [2, 768], replicated
The draws below stay inside these ranges and needn't reach their ends.
Inputs may be any that keep to these rules, and one draw needn't show every extreme that they name: `lengths`: in each aligned group of 2 sequences at least one has length 1024. `table`: entry r + 1023 depends only on |r| and the sign of r: it is |r| for |r| < 8, does not fall as |r| grows, is 15 for |r| >= 128, and 16 is added where r > 0.
All inputs are finite; a program needn't handle non-finite values.
Results may differ from the reference program's by a relative error of at most 0.022.
The reference program's roundings to bfloat16 on the way count: a program that leaves them out, or rounds other values in their place, can miss the bound.
Values may be sent and summed in bfloat16 or wider, within the bound.
A program may use at most 192 MiB of HBM per device.

```python
import math
import jax
import jax.numpy as jnp
from jax import lax

D = 768
FF = 3072
HEADS = 12
HDIM = 64
BUCKETS = 32
SEQLEN = 1024
STEP = 10
SEQ_DEV = 2
NSEQ = 16
TOKENS = 16384


def draw_gains(key, part):
    key = jax.random.fold_in(key, 11)
    position = jnp.arange(D, dtype=jnp.float32) / (D - 1)
    incline = 0.6 + 1.2 * position
    jitter = jax.random.uniform(key, (2, D), jnp.float32, 0.8, 1.2)
    return incline[None, :] * jitter


def draw_lengths(key, part):
    key = jax.random.fold_in(key, 12)
    first_key, second_key = jax.random.split(key)
    drawn = jax.random.randint(first_key, (NSEQ,), SEQLEN // 4, SEQLEN + 1)
    chosen = jax.random.randint(second_key, (NSEQ // SEQ_DEV,), 0, SEQ_DEV)
    member = jnp.arange(NSEQ) % SEQ_DEV
    return jnp.where(member == jnp.repeat(chosen, SEQ_DEV), SEQLEN, drawn).astype(jnp.int32)


def draw_table(key, part):
    key = jax.random.fold_in(key, 13)
    exact = BUCKETS // 4
    cutoffs = jnp.sort(jax.random.permutation(key, 128 - exact - 1)[:exact - 1] + exact + 1)
    offset = jnp.arange(2 * SEQLEN - 1) - (SEQLEN - 1)
    distance = jnp.abs(offset)
    far_bucket = exact + jnp.sum((distance[:, None] >= cutoffs[None, :]).astype(jnp.int32), axis=1)
    bucket = jnp.where(distance < exact, distance, far_bucket) + BUCKETS // 2 * (offset > 0).astype(jnp.int32)
    return bucket.astype(jnp.int32)


def block_scale(rng, dims, pieces, low, top_value):
    level, own = 1.0, jax.random.fold_in(rng, 6)
    for dim, parts in pieces:
        heights = jnp.exp(jax.random.uniform(jax.random.fold_in(own, dim), (parts,), jnp.float32, low / len(pieces), top_value / len(pieces)))
        level = level * jnp.repeat(heights, dims[dim] // parts).reshape([-1 if axis == dim else 1 for axis in range(len(dims))])
    return level


def normal_values(rng, shape, spread, bound, pieces=(), kind=jnp.bfloat16):
    result = jax.random.normal(rng, shape, jnp.float32) * spread
    if len(pieces) > 0:
        result = block_scale(rng, shape, pieces, -0.22, 0.18) * result
    return jnp.clip(result, min=-bound, max=bound).astype(kind)


def setup_inputs(seed: int = 0) -> dict:
    splits = jax.random.split(jax.random.key(seed), 23)
    hidden_in = normal_values(splits[0], (TOKENS, D), 1.0, 6.0, ((0, 32),), jnp.float32)
    out_grad = normal_values(splits[1], (TOKENS, D), 1.0, 6.0, ((0, 32),), jnp.float32)
    attn_weight = normal_values(splits[2], (3, D, D), (4 * D) ** -0.5, 0.109375, ((1, 8), (2, 4)), jnp.float32)
    out_weight = normal_values(splits[3], (D, D), (max(1, D // 128)) ** -0.5, 2.5, ((0, 4), (1, 8)), jnp.float32)
    inner_weight = normal_values(splits[4], (D, FF), D ** -0.5, 0.21875, ((0, 8), (1, 4)), jnp.float32)
    outer_weight = normal_values(splits[5], (FF, D), FF ** -0.5, 0.109375, ((0, 4), (1, 8)), jnp.float32)
    rel_bias = normal_values(splits[6], (BUCKETS, HEADS), 1.0, 4.0, (), jnp.float32)
    gains = draw_gains(jax.random.fold_in(splits[22], 71), 0)
    lengths = draw_lengths(jax.random.fold_in(splits[22], 71), 0)
    table = draw_table(jax.random.fold_in(splits[22], 71), 0)
    attn_first = normal_values(splits[10], (3, D, D), (0.16 * (2 * D * FF) ** -0.5), 0.0009765625, ((1, 8), (2, 4)), jnp.float32)
    attn_second = jnp.clip(jnp.exp(math.log(1.6954210257935642e-09) - 1.3862944 * jax.random.uniform(splits[11], (3, D, D), jnp.float32) ** block_scale(splits[11], (3, D, D), ((1, 8), (2, 4)), -0.2, 0.2)), 4.2385525644839106e-10, 1.6954210257935642e-09)
    out_first = normal_values(splits[12], (D, D), (0.0056 * (2 * D * FF) ** -0.5), 3.814697265625e-05, ((0, 4), (1, 8)), jnp.float32)
    out_second = jnp.clip(jnp.exp(math.log(2.119276325610042e-12) - 1.3862944 * jax.random.uniform(splits[13], (D, D), jnp.float32) ** block_scale(splits[13], (D, D), ((0, 4), (1, 8)), -0.2, 0.2)), 5.298190814025105e-13, 2.119276325610042e-12)
    inner_first = normal_values(splits[14], (D, FF), (0.0099 * (2 * D * FF) ** -0.5), 6.103515625e-05, ((0, 8), (1, 4)), jnp.float32)
    inner_second = jnp.clip(jnp.exp(math.log(6.781684155215961e-12) - 1.3862944 * jax.random.uniform(splits[15], (D, FF), jnp.float32) ** block_scale(splits[15], (D, FF), ((0, 8), (1, 4)), -0.2, 0.2)), 1.6954210388039903e-12, 6.781684155215961e-12)
    outer_first = normal_values(splits[16], (FF, D), (0.014 * (2 * D * FF) ** -0.5), 9.1552734375e-05, ((0, 4), (1, 8)), jnp.float32)
    outer_second = jnp.clip(jnp.exp(math.log(1.3563368310431922e-11) - 1.3862944 * jax.random.uniform(splits[17], (FF, D), jnp.float32) ** block_scale(splits[17], (FF, D), ((0, 4), (1, 8)), -0.2, 0.2)), 3.3908420776079806e-12, 1.3563368310431922e-11)
    rel_first = normal_values(splits[18], (BUCKETS, HEADS), (0.0055 * (2 * D * FF) ** -0.5), 3.814697265625e-05, (), jnp.float32)
    rel_second = jnp.clip(jnp.exp(jax.random.uniform(splits[19], (BUCKETS, HEADS), jnp.float32, math.log(5.298190814025105e-13), math.log(2.119276325610042e-12))), 5.298190814025105e-13, 2.119276325610042e-12)
    gain_first = normal_values(splits[20], (2, D), (0.111 * (2 * D * FF) ** -0.5), 0.0007324219, (), jnp.float32)
    gain_second = jnp.clip(jnp.exp(jax.random.uniform(splits[21], (2, D), jnp.float32, math.log(2.1192762822419553e-10), math.log(8.477105128967821e-10))), 2.1192762822419553e-10, 8.477105128967821e-10)
    return dict(hidden_in=hidden_in, out_grad=out_grad, attn_weight=attn_weight, out_weight=out_weight, inner_weight=inner_weight, outer_weight=outer_weight, rel_bias=rel_bias, gains=gains, lengths=lengths, table=table, attn_first=attn_first, attn_second=attn_second, out_first=out_first, out_second=out_second, inner_first=inner_first, inner_second=inner_second, outer_first=outer_first, outer_second=outer_second, rel_first=rel_first, rel_second=rel_second, gain_first=gain_first, gain_second=gain_second)


NORM_EPS = 1e-06
CLIP = 1.0
BETA_ONE = 0.9
BETA_TWO = 0.999
ADAM_EPS = 1e-08
DECAY = 0.01
RATE_MATRIX = 0.05
RATE_OUT = 0.6
RATE_SMALL = 1.0

@jax.custom_vjp
def low(v):
    return lax.optimization_barrier(v.astype(jnp.bfloat16)).astype(jnp.float32)

@jax.custom_vjp
def low_back(v):
    return v

def low_keep(v):
    return (low(v), None)

def low_pass(kept, grad):
    return (grad,)

def back_keep(v):
    return (v, None)

def back_low(kept, grad):
    return (low(grad),)
low.defvjp(low_keep, low_pass)
low_back.defvjp(back_keep, back_low)

def matmul(left, right):
    return jnp.dot(left, right, precision=lax.Precision.HIGHEST, preferred_element_type=jnp.float32)

def rms_scaled(value, gain):
    return value * lax.rsqrt(lax.optimization_barrier(jnp.mean(value * value, axis=-1, keepdims=True)) + NORM_EPS) * gain

def forward(hidden_in, attn_weight, out_weight, inner_weight, outer_weight, rel_bias, gains, lengths, table):
    w_attn = low(attn_weight)
    w_out = low(out_weight)
    w_inner = low(inner_weight)
    w_outer = low(outer_weight)
    normed_one = low(rms_scaled(hidden_in, gains[0]))
    query = low_back(low(matmul(normed_one, w_attn[0]))).reshape(NSEQ, SEQLEN, HEADS, HDIM)
    keys = low_back(low(matmul(normed_one, w_attn[1]))).reshape(NSEQ, SEQLEN, HEADS, HDIM)
    values = low_back(low(matmul(normed_one, w_attn[2]))).reshape(NSEQ, SEQLEN, HEADS, HDIM)
    offsets = jnp.arange(SEQLEN)[None, :] - jnp.arange(SEQLEN)[:, None] + (SEQLEN - 1)
    bias = jnp.transpose(rel_bias[table[offsets]], (2, 0, 1))
    key_index = jnp.arange(SEQLEN)

    def attend(items):
        q_seq, k_seq, v_seq, length = items
        scores = jnp.einsum('qhd,khd->hqk', q_seq, k_seq, precision=lax.Precision.HIGHEST) + bias
        scores = low_back(scores)
        scores = jnp.where((key_index < length)[None, None, :], scores, -1e+30)
        chances = low(jax.nn.softmax(scores, axis=-1))
        context = jnp.einsum('hqk,khd->qhd', chances, v_seq, precision=lax.Precision.HIGHEST)
        return low_back(low(context)).reshape(SEQLEN, HEADS * HDIM)
    context = lax.map(jax.checkpoint(attend), (query, keys, values, lengths)).reshape(TOKENS, D)
    middle = hidden_in + low_back(matmul(context, w_out))
    normed_two = low(rms_scaled(middle, gains[1]))
    inner = low_back(matmul(normed_two, w_inner))
    active = low(jax.nn.gelu(inner))
    return middle + low_back(matmul(active, w_outer))

def adam_step(master, grad, first, second, factor, rate):
    clipped = grad * factor
    first_new = BETA_ONE * first + (1.0 - BETA_ONE) * clipped
    second_new = BETA_TWO * second + (1.0 - BETA_TWO) * clipped * clipped
    first_hat = first_new / (1.0 - BETA_ONE ** STEP)
    second_hat = second_new / (1.0 - BETA_TWO ** STEP)
    master_new = master - rate * (first_hat / (jnp.sqrt(second_hat) + ADAM_EPS) + DECAY * master)
    return (master_new, first_new, second_new)

def reference(hidden_in, out_grad, attn_weight, out_weight, inner_weight, outer_weight, rel_bias, gains, lengths, table, attn_first, attn_second, out_first, out_second, inner_first, inner_second, outer_first, outer_second, rel_first, rel_second, gain_first, gain_second):

    def wrapped(h_in, w_attn, w_out, w_inner, w_outer, w_rel, w_gain):
        return forward(h_in, w_attn, w_out, w_inner, w_outer, w_rel, w_gain, lengths, table)
    block_out, pullback = jax.vjp(wrapped, hidden_in, attn_weight, out_weight, inner_weight, outer_weight, rel_bias, gains)
    grads = pullback(out_grad)
    grad_norm = jnp.sqrt(sum((jnp.sum(grad * grad) for grad in grads[1:])))
    factor = jnp.minimum(1.0, CLIP / (grad_norm + 1e-06))
    attn_new = adam_step(attn_weight, grads[1], attn_first, attn_second, factor, RATE_MATRIX)
    out_new = adam_step(out_weight, grads[2], out_first, out_second, factor, RATE_OUT)
    inner_new = adam_step(inner_weight, grads[3], inner_first, inner_second, factor, RATE_MATRIX)
    outer_new = adam_step(outer_weight, grads[4], outer_first, outer_second, factor, RATE_MATRIX)
    rel_new = adam_step(rel_bias, grads[5], rel_first, rel_second, factor, RATE_SMALL)
    gain_new = adam_step(gains, grads[6], gain_first, gain_second, factor, RATE_SMALL)
    return (block_out, grads[0], grad_norm, attn_new[0], attn_new[1], attn_new[2], out_new[0], out_new[1], out_new[2], inner_new[0], inner_new[1], inner_new[2], outer_new[0], outer_new[1], outer_new[2], rel_new[0], rel_new[1], rel_new[2], gain_new[0], gain_new[1], gain_new[2])
```

```python
import functools

import jax
import jax.numpy as jnp
from jax import lax
from jax.experimental import pallas as pl
from jax.experimental.pallas import tpu as pltpu
from jax.sharding import PartitionSpec as P

HDIM = 64
SEQLEN = 1024
STEP = 10
NORM_EPS = 1e-06
CLIP = 1.0
BETA_ONE = 0.9
BETA_TWO = 0.999
ADAM_EPS = 1e-08
DECAY = 0.01
RATE_MATRIX = 0.05
RATE_OUT = 0.6
RATE_SMALL = 1.0

F32 = jnp.float32
BF16 = jnp.bfloat16
LANES = 128
NEG = -1e30

HEAD_AT = ((0, 0, 1, 2, 0), (0, 1, 1, 2, 1), (4, 0, 5, 4, 1))


def mm(a, b):
    return lax.dot_general(a, b, (((1,), (0,)), ((), ())), preferred_element_type=F32)


def mt(a, b):
    return lax.dot_general(a, b, (((1,), (1,)), ((), ())), preferred_element_type=F32)


def rms_scaled(value, gain):
    return value * lax.rsqrt(jnp.mean(value * value, axis=-1, keepdims=True) + NORM_EPS) * gain


def rms_back(value, gain, grad):
    factor = lax.rsqrt(jnp.mean(value * value, axis=-1, keepdims=True) + NORM_EPS)
    unit = value * factor
    gain_part = jnp.sum(grad * unit, axis=0, keepdims=True)
    scaled = grad * gain
    result = factor * (scaled - unit * jnp.mean(scaled * unit, axis=-1, keepdims=True))
    return (result, gain_part)


def adam_step(master, grad, first, second, factor, rate):
    clipped = grad * factor
    first_new = BETA_ONE * first + (1.0 - BETA_ONE) * clipped
    second_new = BETA_TWO * second + (1.0 - BETA_TWO) * clipped * clipped
    first_hat = first_new / (1.0 - BETA_ONE**STEP)
    second_hat = second_new / (1.0 - BETA_TWO**STEP)
    master_new = master - rate * (first_hat / (jnp.sqrt(second_hat) + ADAM_EPS) + DECAY * master)
    return (master_new, first_new, second_new)


def half_rows(half):
    lane = lax.broadcasted_iota(jnp.int32, (1, LANES), 1)
    keep = (lane < HDIM) if half == 0 else (lane >= HDIM)
    return keep.astype(F32).astype(BF16)


def bias_tile(line):
    wide = jnp.broadcast_to(line, (LANES, 4 * LANES))
    return pltpu.roll(wide, 0, 1, stride=1, stride_axis=0)


def near_parts(tile):
    return tile[:, LANES : 2 * LANES], tile[:, :LANES], tile[:, 3 * LANES :]


def corner_parts(tile, line, flags):
    before, same, after = near_parts(tile)
    first = (after - line[:, 3 * LANES : 3 * LANES + 1]) * flags[0]
    last = (before - line[:, LANES : LANES + 1]) * flags[1]
    return first, last


def add_bias(scores, tile, line, flags, nq):
    parts = near_parts(tile)
    corner = corner_parts(tile, line, flags)
    rows = []
    for jb in range(2 * nq):
        row = []
        for ib in range(nq):
            block = scores[jb * LANES : (jb + 1) * LANES, ib * LANES : (ib + 1) * LANES]
            if jb < nq and abs(jb - ib) <= 1:
                block = block + parts[jb - ib + 1]
            elif jb == nq and ib == nq - 1:
                block = block + corner[0]
            elif jb == 2 * nq - 1 and ib == 0:
                block = block + corner[1]
            row.append(block)
        rows.append(jnp.concatenate(row, axis=1))
    return rows


def query_aug(qaug, i, nq):
    rows = qaug.shape[0]
    return jnp.concatenate(
        [jnp.broadcast_to(qaug[i * nq + ib : i * nq + ib + 1, :], (LANES, LANES)) for ib in range(nq)], axis=0
    )


def forward_kernel(
    x_ref, xo_ref, w_ref, line_ref, qaug_ref, kaug_ref, hidden_ref,
    own_ref, oth_ref, ctx_ref, lse_ref, middle_ref,
    acc, s_ref, e_ref,
):
    m = pl.program_id(0)
    tokens = x_ref.shape[0]
    nq = tokens // LANES
    x, xo = x_ref[...], xo_ref[...]
    p_a = mm(x, w_ref[:, : 3 * LANES]).astype(BF16)
    p_b = mm(x, w_ref[:, 4 * LANES :]).astype(BF16)
    o_a = mm(xo, w_ref[:, LANES : 3 * LANES]).astype(BF16)
    o_b = mm(xo, w_ref[:, 4 * LANES :]).astype(BF16)
    own_ref[0, :, : 3 * LANES] = p_a
    own_ref[0, :, 3 * LANES :] = p_b
    oth_ref[0, :, : 2 * LANES] = o_a
    oth_ref[0, :, 2 * LANES :] = o_b
    cols_own = {0: p_a[:, :LANES], 1: p_a[:, LANES : 2 * LANES], 2: p_a[:, 2 * LANES :], 4: p_b[:, :LANES], 5: p_b[:, LANES:]}
    cols_oth = {1: o_a[:, :LANES], 2: o_a[:, LANES:], 4: o_b[:, :LANES], 5: o_b[:, LANES:]}
    both = {c: jnp.concatenate([cols_own[c], cols_oth[c]], axis=0) for c in (1, 2, 4, 5)}
    masks = [half_rows(0), half_rows(1)]
    flags = (line_ref[0, 3:4, :LANES], line_ref[0, 4:5, :LANES])
    v_t = {2: both[2].T, 4: both[4].T}
    count = lax.broadcasted_iota(jnp.int32, (HDIM, 2 * tokens), 0)
    ones = (count == 0).astype(F32).astype(BF16)
    pieces = []
    stats = []
    for i, (qc, qh, kc, vc, vh) in enumerate(HEAD_AT):
        line = line_ref[0, i : i + 1, :]
        tile = bias_tile(line)
        qa = cols_own[qc] * masks[qh] + query_aug(qaug_ref[0], i, nq) * masks[1 - qh]
        ka = both[kc] * masks[qh] + kaug_ref[...] * masks[1 - qh]
        scores = mt(ka, qa)
        peak = None
        for jb, row in enumerate(add_bias(scores, tile, line, flags, nq)):
            s_ref[i, jb * LANES : (jb + 1) * LANES, :] = row
            top = jnp.max(row.reshape(LANES // 8, 8, tokens), axis=0)
            peak = top if peak is None else jnp.maximum(peak, top)
        peak = jnp.max(peak, axis=0, keepdims=True)
        for jb in range(2 * nq):
            rows = slice(jb * LANES, (jb + 1) * LANES)
            e_ref[i, rows, :] = jnp.exp(s_ref[i, rows, :] - peak).astype(BF16)
        if vh == 0:
            va = jnp.concatenate([v_t[vc][:HDIM], ones], axis=0)
        else:
            va = jnp.concatenate([ones, v_t[vc][HDIM:]], axis=0)
        ot = mm(va, e_ref[i])
        at = HDIM if vh == 0 else 0
        total = ot[at : at + 1, :]
        stats.append(peak + jnp.log(total))
        real = ot[:HDIM] if vh == 0 else ot[HDIM:]
        pieces.append(real / total)
    zero = jnp.zeros((HDIM, tokens), F32)
    ctx_a = jnp.concatenate([pieces[0], pieces[1]], axis=0).T.astype(BF16)
    ctx_b = jnp.concatenate([zero, pieces[2]], axis=0).T.astype(BF16)
    ctx_ref[0, :, :LANES] = ctx_a
    ctx_ref[0, :, LANES:] = ctx_b
    for i in range(3):
        lse_ref[0, i : i + 1, :] = stats[i]
    lse_ref[0, 3:8, :] = jnp.zeros((5, tokens), F32)
    part = mt(ctx_a, w_ref[:, 3 * LANES : 4 * LANES]) + mt(ctx_b, w_ref[:, 5 * LANES :])

    @pl.when(m == 0)
    def _():
        acc[...] = hidden_ref[...] + part

    @pl.when(m > 0)
    def _():
        acc[...] += part

    @pl.when(m == pl.num_programs(0) - 1)
    def _():
        middle_ref[...] = acc[...]


def feed_kernel(
    middle_ref, grad_ref, gain_ref, wi_ref, wo_ref,
    out_ref, back_ref, gain_grad_ref, gi_ref, go_ref,
    x2_ref, x2t_ref, ob_ref, obt_ref, acc_out, acc_two,
):
    f = pl.program_id(0)

    @pl.when(f == 0)
    def _():
        x2 = rms_scaled(middle_ref[...], gain_ref[1:2, :]).astype(BF16)
        x2_ref[...] = x2
        x2t_ref[...] = x2.T
        ob = grad_ref[...].astype(BF16)
        ob_ref[...] = ob
        obt_ref[...] = ob.T
        acc_out[...] = jnp.zeros_like(acc_out)
        acc_two[...] = jnp.zeros_like(acc_two)

    inner = mm(x2_ref[...], wi_ref[...])
    active_back = mm(ob_ref[...], wo_ref[...])
    c = 0.7978845608028654
    sq = inner * inner
    th = jnp.tanh(c * (inner + 0.044715 * (sq * inner)))
    half = 0.5 * (1.0 + th)
    active = (inner * half).astype(BF16)
    slope = half + (0.5 * c) * inner * (1.0 - th * th) * (1.0 + (3 * 0.044715) * sq)
    inner_back = (slope * active_back).astype(BF16)
    acc_out[...] += mt(active, wo_ref[...])
    acc_two[...] += mt(inner_back, wi_ref[...])
    go_ref[...] = mm(obt_ref[...], active).astype(go_ref.dtype)
    gi_ref[...] = mm(x2t_ref[...], inner_back).astype(gi_ref.dtype)

    @pl.when(f == pl.num_programs(0) - 1)
    def _():
        out_ref[...] = middle_ref[...] + acc_out[...]
        result, gain_part = rms_back(middle_ref[...], gain_ref[1:2, :], acc_two[...])
        back_ref[...] = grad_ref[...] + result
        gain_grad_ref[...] = jnp.broadcast_to(gain_part, gain_grad_ref.shape)


def backward_kernel(
    x_ref, xo_ref, back_ref, w_ref, line_ref, qaug_ref, kaug_ref, own_ref, oth_ref, ctx_ref, lse_ref,
    ga_ref, one_own_ref, one_oth_ref, near_ref, sums_ref,
    xt_ref, xot_ref, ab_ref, abt_ref, acc_own, acc_oth,
):
    m = pl.program_id(0)
    tokens = x_ref.shape[0]
    nq = tokens // LANES

    @pl.when(m == 0)
    def _():
        xt_ref[...] = x_ref[...].T
        xot_ref[...] = xo_ref[...].T
        ab = back_ref[...].astype(BF16)
        ab_ref[...] = ab
        abt_ref[...] = ab.T
        acc_own[...] = jnp.zeros_like(acc_own)
        acc_oth[...] = jnp.zeros_like(acc_oth)

    ab = ab_ref[...]
    cb = {2: mm(ab, w_ref[:, 3 * LANES : 4 * LANES]).astype(BF16), 4: mm(ab, w_ref[:, 5 * LANES :]).astype(BF16)}
    ctx = {2: ctx_ref[0, :, :LANES], 4: ctx_ref[0, :, LANES:]}
    own = {c: own_ref[0, :, at * LANES : (at + 1) * LANES] for at, c in enumerate((0, 1, 2, 4, 5))}
    oth = {c: oth_ref[0, :, at * LANES : (at + 1) * LANES] for at, c in enumerate((1, 2, 4, 5))}
    masks = [half_rows(0), half_rows(1)]
    flags = (line_ref[0, 3:4, :LANES], line_ref[0, 4:5, :LANES])
    prod = {c: cb[c].astype(F32) * ctx[c].astype(F32) for c in (2, 4)}
    prod_hi = {c: prod[c].astype(BF16) for c in prod}
    prod_lo = {c: (prod[c] - prod_hi[c].astype(F32)).astype(BF16) for c in prod}
    dq_t = []
    dk = {}
    dv = {}
    for i, (qc, qh, kc, vc, vh) in enumerate(HEAD_AT):
        line = line_ref[0, i : i + 1, :]
        tile = bias_tile(line)
        qm = own[qc] * masks[qh]
        qa = qm + query_aug(qaug_ref[0], i, nq) * masks[1 - qh]
        om = cb[vc] * masks[vh]
        pick = jnp.broadcast_to(masks[vh], (8, LANES))
        center = (mt(pick, prod_hi[vc]) + mt(pick, prod_lo[vc]))[0:1, :]
        lse = lse_ref[0, i : i + 1, :]
        kaug = kaug_ref[...] * masks[1 - qh]
        dqt = None
        parts = near_parts(tile)
        corner = corner_parts(tile, line, flags)
        near = [None, None, None, None, None]
        for side, cols in enumerate((own, oth)):
            ka = cols[kc] * masks[qh] + kaug[side * tokens : (side + 1) * tokens]
            scores = mt(ka, qa)
            chance_back = mt(cols[vc], om)
            ps, ds = [], []
            for jb in range(nq):
                row_s, row_p, row_d = [], [], []
                for ib in range(nq):
                    at = (slice(jb * LANES, (jb + 1) * LANES), slice(ib * LANES, (ib + 1) * LANES))
                    block = scores[at]
                    kind = None
                    if side == 0 and abs(jb - ib) <= 1:
                        block = block + parts[jb - ib + 1]
                        kind = jb - ib + 1
                    elif side == 1 and jb == 0 and ib == nq - 1:
                        block = block + corner[0]
                        kind = 3
                    elif side == 1 and jb == nq - 1 and ib == 0:
                        block = block + corner[1]
                        kind = 4
                    p = jnp.exp(block - lse[:, at[1]])
                    d = p * (chance_back[at] - center[:, at[1]])
                    if kind is not None:
                        near[kind] = d if near[kind] is None else near[kind] + d
                    row_p.append(p.astype(BF16))
                    row_d.append(d.astype(BF16))
                ps.append(jnp.concatenate(row_p, axis=1))
                ds.append(jnp.concatenate(row_d, axis=1))
            pb = jnp.concatenate(ps, axis=0)
            db = jnp.concatenate(ds, axis=0)
            part_v = mm(pb, om)
            part_k = mm(db, qm)
            dv[vc, side] = part_v if (vc, side) not in dv else dv[vc, side] + part_v
            dk[kc, side] = part_k if (kc, side) not in dk else dk[kc, side] + part_k
            part_q = mm(ka.T, db)
            dqt = part_q if dqt is None else dqt + part_q
        at = HDIM if qh == 0 else 0
        sums_ref[0, i * 8 : (i + 1) * 8, :] = dqt[at + 8 : at + 16, :]
        dq_t.append(dqt[:HDIM] if qh == 0 else dqt[HDIM:])
        for kind in range(5):
            near_ref[0, i, kind] = near[kind]
    dq_a = jnp.concatenate([dq_t[0], dq_t[1]], axis=0).T
    dq_b = jnp.concatenate([dq_t[2], jnp.zeros_like(dq_t[2])], axis=0).T
    d_own = jnp.concatenate([dq_a, dk[1, 0], dv[2, 0], dq_b + dv[4, 0], dk[5, 0]], axis=1).astype(BF16)
    d_oth = jnp.concatenate([dk[1, 1], dv[2, 1], dv[4, 1], dk[5, 1]], axis=1).astype(BF16)
    xt, xot, abt = xt_ref[...], xot_ref[...], abt_ref[...]
    g_own = mm(xt, d_own)
    g_oth = mm(xot, d_oth)
    g_ctx = mm(abt, ctx_ref[0])
    ga_ref[:, :LANES] = g_own[:, :LANES].astype(ga_ref.dtype)
    ga_ref[:, LANES : 3 * LANES] = (g_own[:, LANES : 3 * LANES] + g_oth[:, : 2 * LANES]).astype(ga_ref.dtype)
    ga_ref[:, 3 * LANES : 4 * LANES] = g_ctx[:, :LANES].astype(ga_ref.dtype)
    ga_ref[:, 4 * LANES : 5 * LANES] = (g_own[:, 3 * LANES : 4 * LANES] + g_oth[:, 2 * LANES : 3 * LANES]).astype(ga_ref.dtype)
    ga_ref[:, 5 * LANES :] = (g_own[:, 4 * LANES :] + g_oth[:, 3 * LANES :] + g_ctx[:, LANES:]).astype(ga_ref.dtype)
    acc_own[...] += mt(d_own[:, : 3 * LANES], w_ref[:, : 3 * LANES]) + mt(d_own[:, 3 * LANES :], w_ref[:, 4 * LANES :])
    acc_oth[...] += mt(d_oth[:, : 2 * LANES], w_ref[:, LANES : 3 * LANES]) + mt(d_oth[:, 2 * LANES :], w_ref[:, 4 * LANES :])

    @pl.when(m == pl.num_programs(0) - 1)
    def _():
        one_own_ref[...] = acc_own[...]
        one_oth_ref[...] = acc_oth[...].astype(one_oth_ref.dtype)


def whole(shape):
    return pl.BlockSpec(shape, lambda m: (0,) * len(shape))


def params():
    return pltpu.CompilerParams(vmem_limit_bytes=60 * 2**20)


def run_forward(x, xo, wa, line, qaug, kaug, hidden, parts):
    t, d = x.shape
    return pl.pallas_call(
        forward_kernel,
        grid=(parts,),
        in_specs=[
            whole((t, d)), whole((t, d)),
            pl.BlockSpec((d, 6 * LANES), lambda m: (0, m)),
            pl.BlockSpec((1, 8, 4 * LANES), lambda m: (m, 0, 0)),
            pl.BlockSpec((1, 16, LANES), lambda m: (m, 0, 0)),
            whole((2 * t, LANES)), whole((t, d)),
        ],
        out_specs=[
            pl.BlockSpec((1, t, 5 * LANES), lambda m: (m, 0, 0)),
            pl.BlockSpec((1, t, 4 * LANES), lambda m: (m, 0, 0)),
            pl.BlockSpec((1, t, 2 * LANES), lambda m: (m, 0, 0)),
            pl.BlockSpec((1, 8, t), lambda m: (m, 0, 0)),
            whole((t, d)),
        ],
        out_shape=[
            jax.ShapeDtypeStruct((parts, t, 5 * LANES), BF16),
            jax.ShapeDtypeStruct((parts, t, 4 * LANES), BF16),
            jax.ShapeDtypeStruct((parts, t, 2 * LANES), BF16),
            jax.ShapeDtypeStruct((parts, 8, t), F32),
            jax.ShapeDtypeStruct((t, d), F32),
        ],
        scratch_shapes=[
            pltpu.VMEM((t, d), F32),
            pltpu.VMEM((3, 2 * t, t), F32),
            pltpu.VMEM((3, 2 * t, t), BF16),
        ],
        compiler_params=params(),
        name="attend_forward",
    )(x, xo, wa, line, qaug, kaug, hidden)


def run_feed(middle, grad, gains, wi, wo):
    t, d = middle.shape
    units = wi.shape[1]
    tile = min(512, units)
    return pl.pallas_call(
        feed_kernel,
        grid=(units // tile,),
        in_specs=[
            whole((t, d)), whole((t, d)), whole((2, d)),
            pl.BlockSpec((d, tile), lambda f: (0, f)),
            pl.BlockSpec((d, tile), lambda f: (0, f)),
        ],
        out_specs=[
            whole((t, d)), whole((t, d)), whole((8, d)),
            pl.BlockSpec((d, tile), lambda f: (0, f)),
            pl.BlockSpec((d, tile), lambda f: (0, f)),
        ],
        out_shape=[
            jax.ShapeDtypeStruct((t, d), F32),
            jax.ShapeDtypeStruct((t, d), F32),
            jax.ShapeDtypeStruct((8, d), F32),
            jax.ShapeDtypeStruct((d, units), BF16),
            jax.ShapeDtypeStruct((d, units), BF16),
        ],
        scratch_shapes=[
            pltpu.VMEM((t, d), BF16), pltpu.VMEM((d, t), BF16),
            pltpu.VMEM((t, d), BF16), pltpu.VMEM((d, t), BF16),
            pltpu.VMEM((t, d), F32), pltpu.VMEM((t, d), F32),
        ],
        compiler_params=params(),
        name="feed_both",
    )(middle, grad, gains, wi, wo)


def run_backward(x, xo, back, wa, line, qaug, kaug, own, oth, ctx, lse, parts):
    t, d = x.shape
    return pl.pallas_call(
        backward_kernel,
        grid=(parts,),
        in_specs=[
            whole((t, d)), whole((t, d)), whole((t, d)),
            pl.BlockSpec((d, 6 * LANES), lambda m: (0, m)),
            pl.BlockSpec((1, 8, 4 * LANES), lambda m: (m, 0, 0)),
            pl.BlockSpec((1, 16, LANES), lambda m: (m, 0, 0)),
            whole((2 * t, LANES)),
            pl.BlockSpec((1, t, 5 * LANES), lambda m: (m, 0, 0)),
            pl.BlockSpec((1, t, 4 * LANES), lambda m: (m, 0, 0)),
            pl.BlockSpec((1, t, 2 * LANES), lambda m: (m, 0, 0)),
            pl.BlockSpec((1, 8, t), lambda m: (m, 0, 0)),
        ],
        out_specs=[
            pl.BlockSpec((d, 6 * LANES), lambda m: (0, m)),
            whole((t, d)), whole((t, d)),
            pl.BlockSpec((1, 3, 5, LANES, LANES), lambda m: (m, 0, 0, 0, 0)),
            pl.BlockSpec((1, 24, t), lambda m: (m, 0, 0)),
        ],
        out_shape=[
            jax.ShapeDtypeStruct((d, parts * 6 * LANES), BF16),
            jax.ShapeDtypeStruct((t, d), F32),
            jax.ShapeDtypeStruct((t, d), BF16),
            jax.ShapeDtypeStruct((parts, 3, 5, LANES, LANES), F32),
            jax.ShapeDtypeStruct((parts, 24, t), F32),
        ],
        scratch_shapes=[
            pltpu.VMEM((d, t), BF16), pltpu.VMEM((d, t), BF16),
            pltpu.VMEM((t, d), BF16), pltpu.VMEM((d, t), BF16),
            pltpu.VMEM((t, d), F32), pltpu.VMEM((t, d), F32),
        ],
        compiler_params=params(),
        name="attend_backward",
    )(x, xo, back, wa, line, qaug, kaug, own, oth, ctx, lse)


def pack_attn(attn, out_t):
    cut = [[part[:, i * HDIM : (i + 1) * HDIM] for i in range(3)] for part in (attn[0], attn[1], attn[2], out_t)]
    q, k, v, o = cut
    return jnp.concatenate([q[0], q[1], k[0], k[1], v[0], v[1], o[0], o[1], q[2], v[2], k[2], o[2]], axis=1)


def unpack_attn(block):
    c = [block[:, i * HDIM : (i + 1) * HDIM] for i in range(12)]
    attn = jnp.stack(
        [
            jnp.concatenate([c[0], c[1], c[8]], axis=1),
            jnp.concatenate([c[2], c[3], c[10]], axis=1),
            jnp.concatenate([c[4], c[5], c[9]], axis=1),
        ]
    )
    return attn, jnp.concatenate([c[6], c[7], c[11]], axis=1)


def body(
    hidden_in, out_grad, attn_weight, out_weight, inner_weight, outer_weight, rel_bias, gains, lengths, table,
    attn_first, attn_second, out_first, out_second, inner_first, inner_second, outer_first, outer_second,
    rel_first, rel_second, gain_first, gain_second, *, parts,
):
    tokens = hidden_in.shape[0]
    nq = tokens // LANES
    heads = rel_bias.shape[1]
    per_seq = SEQLEN // tokens
    mp_index = lax.axis_index("mp")
    half = mp_index % per_seq
    length = lengths[mp_index // per_seq]

    shard = [
        pack_attn(attn_weight.astype(BF16), out_weight.astype(BF16).T),
        inner_weight.astype(BF16),
        outer_weight.astype(BF16).T,
    ]
    gathered = [lax.all_gather(lax.all_gather(s, "dp", axis=0, tiled=True), "mp", axis=1, tiled=True) for s in shard]
    wa, wi, wo = gathered

    x1 = rms_scaled(hidden_in, gains[0]).astype(BF16)
    swap = [(p, p ^ 1) for p in range(parts)]
    x1o = lax.ppermute(x1, "mp", swap)

    u = jnp.arange(4 * LANES)
    offset = jnp.where(u < 2 * LANES, -u, 4 * LANES - u)
    buckets = jnp.arange(rel_bias.shape[0], dtype=jnp.int32)
    line_hot = (jnp.take(table, offset + SEQLEN - 1)[:, None] == buckets[None, :]).astype(F32)
    line = jnp.dot(line_hot, rel_bias, precision=lax.Precision.HIGHEST).T.reshape(parts, heads // parts, 4 * LANES)
    first_flag = (half == 0).astype(F32)
    flags = jnp.stack([jnp.full((4 * LANES,), first_flag), jnp.full((4 * LANES,), 1.0 - first_flag)])
    line_in = jnp.concatenate(
        [line, jnp.broadcast_to(flags[None], (parts, 2, 4 * LANES)), jnp.zeros((parts, 3, 4 * LANES), F32)], axis=1
    )
    far_before, far_after = line[:, :, LANES], line[:, :, 3 * LANES]
    jb, ib = jnp.arange(nq)[None, :], jnp.arange(nq)[:, None]
    own_before, own_after = (jb < ib - 1).astype(F32), (jb > ib + 1).astype(F32)
    oth_before = jnp.full((nq, nq), 1.0 - first_flag)
    w_before = jnp.concatenate([own_before, oth_before], axis=1)
    w_after = jnp.concatenate([own_after, 1.0 - oth_before], axis=1)
    far = far_before[:, :, None, None] * w_before + far_after[:, :, None, None] * w_after
    far_hi = far.astype(BF16).astype(F32)
    far_lo = far - far_hi
    one = jnp.ones((parts, heads // parts, nq, 1), F32)
    blank = jnp.zeros((parts, heads // parts, nq, HDIM), F32)
    q64 = jnp.concatenate(
        [blank[..., :3], one, blank[..., :4], far_hi, far_lo, blank[..., : HDIM - 8 - 4 * nq]], axis=-1
    )
    qaug = jnp.concatenate([q64, q64], axis=-1).reshape(parts, 3 * nq, LANES)
    qaug = jnp.pad(qaug, ((0, 0), (0, 16 - 3 * nq), (0, 0))).astype(BF16)
    row = jnp.arange(2 * tokens)
    position = jnp.where(row < tokens, half * tokens + row, (1 - half) * tokens + row - tokens)
    masked = jnp.where(position < length, 0.0, NEG)
    col = jnp.arange(LANES) % HDIM
    block_of = row // LANES
    hot = ((col >= 8) & (col < 8 + 4 * nq))[None, :] & ((col[None, :] - 8) % (2 * nq) == block_of[:, None])
    kaug = jnp.where((col == 3)[None, :], masked[:, None], hot.astype(F32)).astype(BF16)

    own, oth, ctx, lse, middle = run_forward(x1, x1o, wa, line_in, qaug, kaug, hidden_in, parts)
    block_out, middle_back, gain_two, gi, go = run_feed(middle, out_grad, gains, wi, wo)
    ga, one_own, one_oth, near, sums = run_backward(
        x1, x1o, middle_back, wa, line_in, qaug, kaug, own, oth, ctx, lse, parts
    )
    one_back = one_own + lax.ppermute(one_oth, "mp", swap).astype(F32)
    input_grad, gain_one = rms_back(hidden_in, gains[0:1], one_back)
    input_grad = input_grad + middle_back

    nh = heads // parts
    near = near.reshape(heads, 5, LANES, LANES)
    first_w = first_flag
    blocks = jnp.stack(
        [near[:, 0] + near[:, 4] * (1.0 - first_w), near[:, 1], near[:, 2] + near[:, 3] * first_w], axis=1
    )
    r = jnp.arange(LANES)
    diff = r[None, :, None] - r[None, None, :] + (jnp.arange(3) - 1)[:, None, None] * LANES
    near_bucket = jnp.take(table, diff + SEQLEN - 1).reshape(1, -1)
    near_hot = (near_bucket == buckets[:, None]).astype(F32)
    near_grad = lax.dot_general(
        near_hot, blocks.reshape(heads, -1), (((1,), (1,)), ((), ())), precision=lax.Precision.HIGHEST
    )
    block_sums = jnp.sum(sums.reshape(heads, 2 * nq, nq, LANES), axis=-1)
    far_w = jnp.transpose(jnp.stack([w_before, w_after]), (0, 2, 1))
    corner = jnp.stack([jnp.sum(near[:, 4], (1, 2)) * (1.0 - first_w), jnp.sum(near[:, 3], (1, 2)) * first_w])
    far_grad = jnp.einsum("hji,sji->sh", block_sums, far_w, precision=lax.Precision.HIGHEST) - corner
    far_hot = (jnp.stack([table[0], table[2 * SEQLEN - 2]])[None, :] == buckets[:, None]).astype(F32)
    rel_part = near_grad + jnp.dot(far_hot, far_grad, precision=lax.Precision.HIGHEST)

    owned = [
        lax.psum_scatter(
            lax.psum_scatter(g, "mp", scatter_dimension=1, tiled=True), "dp", scatter_dimension=0, tiled=True
        ).astype(F32)
        for g in (ga, gi, go)
    ]
    g_attn, g_out_t = unpack_attn(owned[0])
    grads = (g_attn, g_out_t.T, owned[1], owned[2].T)
    square_part = sum(jnp.sum(g * g) for g in owned)
    gain_grad, rel_grad, square_total = lax.psum(
        (jnp.concatenate([gain_one, gain_two[:1]], axis=0), rel_part, square_part), ("dp", "mp")
    )
    grad_norm = jnp.sqrt(square_total + jnp.sum(gain_grad * gain_grad) + jnp.sum(rel_grad * rel_grad))
    factor = jnp.minimum(1.0, CLIP / (grad_norm + 1e-06))
    attn_new = adam_step(attn_weight, grads[0], attn_first, attn_second, factor, RATE_MATRIX)
    out_new = adam_step(out_weight, grads[1], out_first, out_second, factor, RATE_OUT)
    inner_new = adam_step(inner_weight, grads[2], inner_first, inner_second, factor, RATE_MATRIX)
    outer_new = adam_step(outer_weight, grads[3], outer_first, outer_second, factor, RATE_MATRIX)
    rel_new = adam_step(rel_bias, rel_grad, rel_first, rel_second, factor, RATE_SMALL)
    gain_new = adam_step(gains, gain_grad, gain_first, gain_second, factor, RATE_SMALL)
    return (block_out, input_grad, grad_norm, *attn_new, *out_new, *inner_new, *outer_new, *rel_new, *gain_new)


def solution(mesh):
    rows = P(("dp", "mp"), None)
    attn, up, down = P(None, "dp", "mp"), P("dp", "mp"), P("mp", "dp")
    in_specs = (
        rows, rows, attn, down, up, down, P(), P(), P("dp"), P(),
        attn, attn, down, down, up, up, down, down, P(), P(), P(), P(),
    )
    out_specs = (rows, rows, P()) + (attn,) * 3 + (down,) * 3 + (up,) * 3 + (down,) * 3 + (P(),) * 6
    return jax.shard_map(
        functools.partial(body, parts=mesh.shape["mp"]),
        mesh=mesh, in_specs=in_specs, out_specs=out_specs, check_vma=False,
    )
```

```python
import functools

import jax
import jax.numpy as jnp
from jax import lax
from jax.experimental import pallas as pl
from jax.experimental.pallas import tpu as pltpu
from jax.sharding import PartitionSpec as P

HDIM = 64
SEQLEN = 1024
STEP = 10
NORM_EPS = 1e-06
CLIP = 1.0
BETA_ONE = 0.9
BETA_TWO = 0.999
ADAM_EPS = 1e-08
DECAY = 0.01
RATE_MATRIX = 0.05
RATE_OUT = 0.6
RATE_SMALL = 1.0

F32 = jnp.float32
BF16 = jnp.bfloat16
LANES = 128
NEG = -1e30
MESH = pl.DeviceIdType.MESH

HEAD_AT = ((0, 0, 1, 2, 0), (0, 1, 1, 2, 1), (4, 0, 5, 4, 1))


def mm(a, b):
    return lax.dot_general(a, b, (((1,), (0,)), ((), ())), preferred_element_type=F32)


def mt(a, b):
    return lax.dot_general(a, b, (((1,), (1,)), ((), ())), preferred_element_type=F32)


def rms_scaled(value, gain):
    return value * lax.rsqrt(jnp.mean(value * value, axis=-1, keepdims=True) + NORM_EPS) * gain


def rms_back(value, gain, grad):
    factor = lax.rsqrt(jnp.mean(value * value, axis=-1, keepdims=True) + NORM_EPS)
    unit = value * factor
    gain_part = jnp.sum(grad * unit, axis=0, keepdims=True)
    scaled = grad * gain
    result = factor * (scaled - unit * jnp.mean(scaled * unit, axis=-1, keepdims=True))
    return (result, gain_part)


def adam_step(master, grad, first, second, factor, rate):
    clipped = grad * factor
    first_new = BETA_ONE * first + (1.0 - BETA_ONE) * clipped
    second_new = BETA_TWO * second + (1.0 - BETA_TWO) * clipped * clipped
    first_hat = first_new / (1.0 - BETA_ONE**STEP)
    second_hat = second_new / (1.0 - BETA_TWO**STEP)
    master_new = master - rate * (first_hat / (jnp.sqrt(second_hat) + ADAM_EPS) + DECAY * master)
    return (master_new, first_new, second_new)


def half_rows(half):
    lane = lax.broadcasted_iota(jnp.int32, (1, LANES), 1)
    keep = (lane < HDIM) if half == 0 else (lane >= HDIM)
    return keep.astype(F32).astype(BF16)


def bias_tile(line):
    wide = jnp.broadcast_to(line, (LANES, 4 * LANES))
    return pltpu.roll(wide, 0, 1, stride=1, stride_axis=0)


def near_parts(tile):
    return tile[:, LANES : 2 * LANES], tile[:, :LANES], tile[:, 3 * LANES :]


def corner_parts(tile, line, flags):
    before, same, after = near_parts(tile)
    first = (after - line[:, 3 * LANES : 3 * LANES + 1]) * flags[0]
    last = (before - line[:, LANES : LANES + 1]) * flags[1]
    return first, last


def add_bias(scores, tile, line, flags, nq):
    parts = near_parts(tile)
    corner = corner_parts(tile, line, flags)
    rows = []
    for jb in range(2 * nq):
        row = []
        for ib in range(nq):
            block = scores[jb * LANES : (jb + 1) * LANES, ib * LANES : (ib + 1) * LANES]
            if jb < nq and abs(jb - ib) <= 1:
                block = block + parts[jb - ib + 1]
            elif jb == nq and ib == nq - 1:
                block = block + corner[0]
            elif jb == 2 * nq - 1 and ib == 0:
                block = block + corner[1]
            row.append(block)
        rows.append(jnp.concatenate(row, axis=1))
    return rows


def query_aug(qaug, i, nq):
    rows = qaug.shape[0]
    return jnp.concatenate(
        [jnp.broadcast_to(qaug[i * nq + ib : i * nq + ib + 1, :], (LANES, LANES)) for ib in range(nq)], axis=0
    )


def peer(index, stride):
    return index + stride - 2 * stride * ((index // stride) % 2)


class Links:
    def __init__(self):
        self.dp = lax.axis_index("dp")
        self.mp = lax.axis_index("mp")
        self.core = self.dp % 2
        self.chip = self.dp // 2
        self.dp_x, self.dp_y, self.dp_s = peer(self.dp, 2), peer(self.dp, 4), peer(self.dp, 1)
        self.dp_d = peer(self.dp_x, 4)
        self.at_x, self.at_y, self.at_s = (self.dp_x, self.mp), (self.dp_y, self.mp), (self.dp_s, self.mp)
        z1, z2 = peer(self.mp, 1), peer(self.mp, 2)
        self.at_z = (None, (self.dp, z1), (self.dp, z2), (self.dp, peer(z1, 2)))

    def meet(self):
        barrier = pltpu.get_barrier_semaphore()
        others = (self.at_x, self.at_y, self.at_s) + self.at_z[1:]
        for other in others:
            pl.semaphore_signal(barrier, inc=1, device_id=other, device_id_type=MESH)
        pl.semaphore_wait(barrier, len(others))


def remote(src, dst, send, recv, to):
    return pltpu.make_async_remote_copy(
        src_ref=src, dst_ref=dst, send_sem=send, recv_sem=recv, device_id=to, device_id_type=MESH
    )


class Gather:
    def __init__(self, links, w, send, recv, zsend, zrecv):
        self.k, self.w, self.send, self.recv, self.zsend, self.zrecv = links, w, send, recv, zsend, zrecv
        self.rows = w.shape[2] // 8

    def block(self, unit, dp, lo=0, n=None):
        group, s = unit
        n = self.rows if n is None else n
        return self.w.at[group, s, pl.ds(pl.multiple_of(dp * self.rows + lo, 16), n), :]

    def copy(self, unit, kind, ref, to):
        at = unit[0] * 4 + unit[1]
        return remote(ref, ref, self.send.at[at, kind], self.recv.at[at, kind], to)

    def outgoing(self, unit, kind):
        k, half = self.k, self.rows // 2
        dp, lo, n, to = (
            (k.dp, 0, None, k.at_x),
            (k.dp, 0, None, k.at_y),
            (k.dp, 0, None, k.at_s),
            (k.dp_x, 0, half, k.at_y),
            (k.dp_x, 0, None, k.at_s),
            (k.dp_y, half, half, k.at_x),
            (k.dp_y, 0, None, k.at_s),
            (k.dp_d, 0, None, k.at_s),
        )[kind]
        return self.copy(unit, kind, self.block(unit, dp, lo, n), to)

    def arrived(self, unit, kind):
        k, half = self.k, self.rows // 2
        sib = k.dp_s
        dp, lo, n = {
            0: (k.dp_x, 0, None),
            1: (k.dp_y, 0, None),
            2: (sib, 0, None),
            3: (k.dp_d, 0, half),
            4: (peer(sib, 2), 0, None),
            5: (k.dp_d, half, half),
            6: (peer(sib, 4), 0, None),
            7: (peer(peer(sib, 2), 4), 0, None),
        }[kind]
        self.copy(unit, kind, self.block(unit, dp, lo, n), k.at_x).wait_recv()

    def z_copy(self, group, s):
        at = group * 3 + s - 1
        src = self.block((group, 0), self.k.dp)
        dst = self.block((group, s), self.k.dp)
        return remote(src, dst, self.zsend.at[at], self.zrecv.at[at], self.k.at_z[s])

    def z_arrived(self, unit):
        at = unit[0] * 3 + unit[1] - 1
        ref = self.block(unit, self.k.dp)
        remote(ref, ref, self.zsend.at[at], self.zrecv.at[at], self.k.at_x).wait_recv()

    def run(self, ops):
        for op in ops:
            (self.s1, self.s2, self.s3, self.s4)[op // 16 - 1](UNITS[op % 16])

    def at(self, loop, step, place):
        for number in range(4):
            ops = GATHER_PLAN.get((loop, number), {}).get(place)
            if ops:
                pl.when(step == number)(functools.partial(self.run, ops))

    def s1(self, unit):
        if unit[1] > 0:
            self.z_arrived(unit)
        for kind in (0, 1, 2):
            self.outgoing(unit, kind).start()

    def s2(self, unit):
        self.arrived(unit, 0)
        for kind in (3, 4):
            self.outgoing(unit, kind).start()
        self.arrived(unit, 1)
        for kind in (5, 6):
            self.outgoing(unit, kind).start()

    def s3(self, unit):
        self.arrived(unit, 3)
        self.arrived(unit, 5)
        self.outgoing(unit, 7).start()

    def s4(self, unit):
        for kind in (2, 4, 6, 7):
            self.arrived(unit, kind)

    def finish(self):
        def each(at, carry):
            for kind in range(8):
                self.outgoing((at // 4, at % 4), kind).wait_send()
            return carry

        lax.fori_loop(0, 12, each, 0)
        for group in range(3):
            for s in (1, 2, 3):
                self.z_copy(group, s).wait_send()


UNITS = ((0, 0), (0, 1), (0, 2), (1, 0), (2, 0), (0, 3), (1, 1), (2, 1), (1, 2), (2, 2), (1, 3), (2, 3))
GATHER_AHEAD = (0x10, 0x11, 0x20, 0x12, 0x30, 0x21, 0x13, 0x40, 0x31, 0x22, 0x14, 0x41, 0x32)
GATHER_PLAN = {
    ("attend", 0): {0: (0x23, 0x15, 0x42), 2: (0x33,)},
    ("attend", 1): {0: (0x24, 0x16), 1: (0x43,), 2: (0x34,)},
    ("attend", 2): {0: (0x25, 0x17), 1: (0x44,), 2: (0x35,), 3: (0x45,)},
    ("attend", 3): {0: (0x26, 0x18), 1: (0x36,), 2: (0x27, 0x19)},
    ("feed", 0): {0: (0x46,), 1: (0x37,), 2: (0x28, 0x1a, 0x47)},
    ("feed", 1): {1: (0x38,), 2: (0x29, 0x1b, 0x48)},
    ("feed", 2): {0: (0x39, 0x49), 1: (0x2a,), 2: (0x3a, 0x2b)},
    ("feed", 3): {0: (0x4a, 0x3b, 0x4b)},
}


def front_kernel(
    x_ref, shard_ref, line_ref, qaug_ref, kaug_ref, gain_ref, hidden_hbm, grad_hbm,
    own_hbm, oth_hbm, ctx_hbm, lse_ref, wa_hbm, xo_hbm, out_ref, back_ref, gain_grad_ref, gi_hbm, go_hbm,
    w, xo, own, oth, ctx, s_ref, e_ref, middle, grad, x2_ref, x2t_ref, ob_ref, obt_ref, acc_out, acc_two, gi, go,
    send, recv, zsend, zrecv, xsem, lsem, osem, gsem,
):
    tokens = x_ref.shape[0]
    nq = tokens // LANES
    links = Links()
    net = Gather(links, w, send, recv, zsend, zrecv)
    get_hidden = pltpu.make_async_copy(hidden_hbm, middle, lsem.at[0])
    get_grad = pltpu.make_async_copy(grad_hbm, grad, lsem.at[1])
    get_hidden.start()
    get_grad.start()
    place = [pltpu.make_async_copy(shard_ref.at[g], net.block((g, 0), links.dp), lsem.at[2 + g]) for g in range(3)]
    for copy in place:
        copy.start()
    links.meet()
    for copy in place:
        copy.wait()
    xcopy = remote(x_ref, xo, xsem.at[0], xsem.at[1], links.at_z[1])
    net.z_copy(0, 1).start()
    net.z_copy(0, 2).start()
    xcopy.start()
    net.z_copy(0, 3).start()
    for step in (1, 2, 3):
        net.z_copy(1, step).start()
        net.z_copy(2, step).start()
    net.run(GATHER_AHEAD)
    get_grad.wait()
    ob = grad[...].astype(BF16)
    ob_ref[...] = ob
    obt_ref[...] = ob.T
    get_hidden.wait()
    xcopy.wait_recv()

    masks = [half_rows(0), half_rows(1)]
    count = lax.broadcasted_iota(jnp.int32, (HDIM, 2 * tokens), 0)
    ones = (count == 0).astype(F32).astype(BF16)

    def attend(s, carry):
        x, other = x_ref[...], xo[...]
        p_a = mm(x, w[0, s, :, : 3 * LANES]).astype(BF16)
        p_b = mm(x, w[0, s, :, 4 * LANES :]).astype(BF16)
        o_a = mm(other, w[0, s, :, LANES : 3 * LANES]).astype(BF16)
        o_b = mm(other, w[0, s, :, 4 * LANES :]).astype(BF16)
        own[s, :, : 3 * LANES] = p_a
        own[s, :, 3 * LANES :] = p_b
        oth[s, :, : 2 * LANES] = o_a
        oth[s, :, 2 * LANES :] = o_b
        cols_own = {0: p_a[:, :LANES], 1: p_a[:, LANES : 2 * LANES], 2: p_a[:, 2 * LANES :], 4: p_b[:, :LANES], 5: p_b[:, LANES:]}
        cols_oth = {1: o_a[:, :LANES], 2: o_a[:, LANES:], 4: o_b[:, :LANES], 5: o_b[:, LANES:]}
        both = {c: jnp.concatenate([cols_own[c], cols_oth[c]], axis=0) for c in (1, 2, 4, 5)}
        flags = (line_ref[s, 3:4, :LANES], line_ref[s, 4:5, :LANES])
        v_t = {2: both[2].T, 4: both[4].T}
        pieces = []
        stats = []
        for i, (qc, qh, kc, vc, vh) in enumerate(HEAD_AT):
            net.at("attend", s, i)
            line = line_ref[s, i : i + 1, :]
            tile = bias_tile(line)
            qa = cols_own[qc] * masks[qh] + query_aug(qaug_ref[s], i, nq) * masks[1 - qh]
            ka = both[kc] * masks[qh] + kaug_ref[...] * masks[1 - qh]
            scores = mt(ka, qa)
            peak = None
            for jb, row in enumerate(add_bias(scores, tile, line, flags, nq)):
                s_ref[i % 2, jb * LANES : (jb + 1) * LANES, :] = row
                top = jnp.max(row.reshape(LANES // 8, 8, tokens), axis=0)
                peak = top if peak is None else jnp.maximum(peak, top)
            peak = jnp.max(peak, axis=0, keepdims=True)
            for jb in range(2 * nq):
                rows = slice(jb * LANES, (jb + 1) * LANES)
                e_ref[i % 2, rows, :] = jnp.exp(s_ref[i % 2, rows, :] - peak).astype(BF16)
            if vh == 0:
                va = jnp.concatenate([v_t[vc][:HDIM], ones], axis=0)
            else:
                va = jnp.concatenate([ones, v_t[vc][HDIM:]], axis=0)
            ot = mm(va, e_ref[i % 2])
            at = HDIM if vh == 0 else 0
            total = ot[at : at + 1, :]
            stats.append(peak + jnp.log(total))
            real = ot[:HDIM] if vh == 0 else ot[HDIM:]
            pieces.append(real / total)
        zero = jnp.zeros((HDIM, tokens), F32)
        ctx_a = jnp.concatenate([pieces[0], pieces[1]], axis=0).T.astype(BF16)
        ctx_b = jnp.concatenate([zero, pieces[2]], axis=0).T.astype(BF16)
        ctx[s, :, :LANES] = ctx_a
        ctx[s, :, LANES:] = ctx_b
        lse_ref[s] = jnp.concatenate(stats + [jnp.zeros((5, tokens), F32)], axis=0)
        middle[...] += mt(ctx_a, w[0, s, :, 3 * LANES : 4 * LANES]) + mt(ctx_b, w[0, s, :, 5 * LANES :])
        net.at("attend", s, 3)
        return carry

    lax.fori_loop(0, 4, attend, 0)
    saves = [
        pltpu.make_async_copy(a, b, osem.at[n])
        for n, (a, b) in enumerate(((own, own_hbm), (oth, oth_hbm), (ctx, ctx_hbm), (w.at[0], wa_hbm), (xo, xo_hbm)))
    ]
    for copy in saves:
        copy.start()

    x2 = rms_scaled(middle[...], gain_ref[1:2, :]).astype(BF16)
    x2_ref[...] = x2
    x2t_ref[...] = x2.T
    acc_out[...] = jnp.zeros_like(acc_out)
    acc_two[...] = jnp.zeros_like(acc_two)
    def g_copies(t):
        slot = t % 2
        return (
            pltpu.make_async_copy(gi.at[slot], gi_hbm.at[t], gsem.at[slot, 0]),
            pltpu.make_async_copy(go.at[slot], go_hbm.at[t], gsem.at[slot, 1]),
        )

    def feed(t, carry):
        slot = t % 2
        cols = w.shape[3]
        tile = 2 * LANES

        @pl.when(t >= 2)
        def _():
            for copy in g_copies(t - 2):
                copy.wait()

        for n in range(cols // tile):
            net.at("feed", t, n)
            at = slice(n * tile, (n + 1) * tile)
            wi = w[1, t, :, at]
            wo = w[2, t, :, at]
            inner = mm(x2_ref[...], wi)
            active_back = mm(ob_ref[...], wo)
            c = 0.7978845608028654
            sq = inner * inner
            th = jnp.tanh(c * (inner + 0.044715 * (sq * inner)))
            half = 0.5 * (1.0 + th)
            active = (inner * half).astype(BF16)
            slope = half + (0.5 * c) * inner * (1.0 - th * th) * (1.0 + (3 * 0.044715) * sq)
            inner_back = (slope * active_back).astype(BF16)
            acc_out[...] += mt(active, wo)
            acc_two[...] += mt(inner_back, wi)
            go[slot, :, at] = mm(obt_ref[...], active).astype(BF16)
            gi[slot, :, at] = mm(x2t_ref[...], inner_back).astype(BF16)
        for copy in g_copies(t):
            copy.start()

        return carry

    lax.fori_loop(0, 4, feed, 0)
    out_ref[...] = middle[...] + acc_out[...]
    result, gain_part = rms_back(middle[...], gain_ref[1:2, :], acc_two[...])
    back_ref[...] = grad[...] + result
    gain_grad_ref[...] = jnp.broadcast_to(gain_part, gain_grad_ref.shape)
    for t in (2, 3):
        for copy in g_copies(t):
            copy.wait()
    for copy in saves:
        copy.wait()
    xcopy.wait_send()
    net.finish()


class Scatter:
    def __init__(self, links, sources, sums, piece, diag, side, final, result, send, recv, psem):
        self.k, self.sources, self.sums, self.piece = links, sources, sums, piece
        self.diag, self.side, self.final, self.result = diag, side, final, result
        self.send, self.recv, self.psem = send, recv, psem
        self.rows = sums.shape[2]
        chip = links.chip
        self.chips = (chip, peer(chip, 1), peer(chip, 2), peer(peer(chip, 1), 2))

    def outgoing(self, u, kind):
        group, s = BACK_UNITS[u]
        k, half = self.k, self.rows // 2
        at, at_x, at_y, at_d = self.chips
        if kind == 0:
            src, dst, to = self.sources[group].at[s, :, 1 - k.core], self.sums.at[u], k.at_s
        elif kind == 1:
            src, dst, to = self.sums.at[u, at_d, pl.ds(0, half)], self.diag.at[u, 0], k.at_x
        elif kind == 2:
            src, dst, to = self.sums.at[u, at_d, pl.ds(half, half)], self.diag.at[u, 1], k.at_y
        elif kind == 3:
            src, dst, to = self.sums.at[u, at_x], self.side.at[u, 0], k.at_x
        elif kind == 4:
            src, dst, to = self.sums.at[u, at_y], self.side.at[u, 1], k.at_y
        else:
            src, dst, to = self.sums.at[u, at], self.final.at[group, s - 1], k.at_z[s]
        return remote(src, dst, self.send.at[u, kind], self.recv.at[u, kind], to)

    def local(self, u):
        group, s = BACK_UNITS[u]
        return pltpu.make_async_copy(self.sources[group].at[s, :, self.k.core], self.piece.at[u % 3], self.psem.at[u % 3])

    def s1(self, u):
        self.outgoing(u, 0).start()
        self.local(u).start()

    def s2(self, u):
        self.local(u).wait()
        self.outgoing(u, 0).wait_recv()
        for chip in range(4):
            self.sums[u, chip] = (self.sums[u, chip].astype(F32) + self.piece[u % 3, chip].astype(F32)).astype(BF16)
        self.outgoing(u, 1).start()
        self.outgoing(u, 2).start()

    def s3(self, u):
        half = self.rows // 2
        self.outgoing(u, 1).wait_recv()
        self.outgoing(u, 2).wait_recv()
        for chip, lo, n in ((self.chips[2], 0, 0), (self.chips[1], half, 1)):
            part = self.sums[u, chip, lo : lo + half].astype(F32) + self.diag[u, n].astype(F32)
            self.sums[u, chip, lo : lo + half] = part.astype(BF16)
        self.outgoing(u, 3).start()
        self.outgoing(u, 4).start()

    def s4(self, u):
        group, s = BACK_UNITS[u]
        self.outgoing(u, 3).wait_recv()
        self.outgoing(u, 4).wait_recv()
        at = self.chips[0]
        total = self.sums[u, at].astype(F32) + (self.side[u, 0].astype(F32) + self.side[u, 1].astype(F32))
        if s == 0:
            self.result[group] = total
        else:
            self.sums[u, at] = total.astype(BF16)
            self.outgoing(u, 5).start()

    def last(self, group):
        total = self.result[group]
        for u, (other, s) in enumerate(BACK_UNITS):
            if other == group and s > 0:
                self.outgoing(u, 5).wait_recv()
        for n in range(3):
            total = total + self.final[group, n].astype(F32)
        self.result[group] = total

    def run(self, ops):
        for op in ops:
            (self.s1, self.s2, self.s3, self.s4)[op // 16 - 1](op % 16)

    def at(self, loop, step, place):
        for number in range(4):
            ops = SCATTER_PLAN.get((loop, number), {}).get(place)
            if ops:
                pl.when(step == number)(functools.partial(self.run, ops))

    def finish(self):
        for u, (group, s) in enumerate(BACK_UNITS):
            for kind in range(5 if s == 0 else 6):
                self.outgoing(u, kind).wait_send()


BACK_UNITS = ((1, 3), (2, 3), (1, 2), (2, 2), (1, 1), (2, 1), (1, 0), (2, 0), (0, 3), (0, 2), (0, 1), (0, 0))
SCATTER_PLAN = {
    ("other", 0): {0: (0x30, 0x12), 2: (0x21,)},
    ("other", 1): {0: (0x31, 0x13), 1: (0x40,), 2: (0x22,)},
    ("other", 2): {0: (0x32, 0x14), 1: (0x41,), 2: (0x23,)},
    ("other", 3): {0: (0x33, 0x15), 1: (0x42,), 2: (0x24,)},
    ("own", 0): {0: (0x34, 0x16), 1: (0x43,), 2: (0x25,)},
    ("own", 1): {0: (0x35, 0x17), 1: (0x44,), 2: (0x26,)},
    ("own", 2): {0: (0x36, 0x18), 1: (0x45,), 2: (0x27,)},
    ("own", 3): {0: (0x37, 0x19), 1: (0x46,), 2: (0x28,)},
}
SCATTER_AFTER = ((0x1a, 0x1b, 0x38, 0x47, 0x29), (0x39, 0x48, 0x2a, 0x3a, 0x49, 0x2b, 0x3b, 0x4a, 0x4b))


def back_kernel(
    x_ref, line_ref, qaug_ref, kaug_ref, lse_ref, gain_ref,
    xo_hbm, back_hbm, hidden_hbm, wa_hbm, own_hbm, oth_hbm, ctx_hbm, gi_hbm, go_hbm,
    grad_ref, gain_grad_ref, line_grad_ref, sums_ref, result_ref,
    xo, back, hidden, wa, own, oth, ctx, xt, xot, ab_ref, abt, acc_own, acc_oth, oth_out, oth_in,
    dq_acc, d_oth, cb_ref, center_ref, near_ref, ga, sums, piece, diag, side, final,
    lsem, ssem, osem, send, recv, psem,
):
    tokens = x_ref.shape[0]
    nq = tokens // LANES
    links = Links()
    net = Scatter(links, (ga, gi_hbm, go_hbm), sums, piece, diag, side, final, result_ref, send, recv, psem)
    loads = [
        pltpu.make_async_copy(a, b, lsem.at[n])
        for n, (a, b) in enumerate(((back_hbm, back), (xo_hbm, xo), (hidden_hbm, hidden)))
    ]

    def step_loads(s):
        return [
            pltpu.make_async_copy(a.at[s], b.at[s], ssem.at[s, n])
            for n, (a, b) in enumerate(((wa_hbm, wa), (own_hbm, own), (oth_hbm, oth), (ctx_hbm, ctx)))
        ]

    loads[0].start()
    for copy in step_loads(3):
        copy.start()
    loads[1].start()
    for s in (2, 1, 0):
        for copy in step_loads(s):
            copy.start()
    loads[2].start()
    links.meet()
    net.run((0x10, 0x11))
    loads[0].wait()
    ab = back[...].astype(BF16)
    ab_ref[...] = ab
    abt[...] = ab.T
    net.run((0x20,))
    xt[...] = x_ref[...].T
    acc_own[...] = jnp.zeros_like(acc_own)
    acc_oth[...] = jnp.zeros_like(acc_oth)
    loads[1].wait()
    xot[...] = xo[...].T
    masks = [half_rows(0), half_rows(1)]
    own_at = {c: slice(at * LANES, (at + 1) * LANES) for at, c in enumerate((0, 1, 2, 4, 5))}
    oth_at = {c: slice(at * LANES, (at + 1) * LANES) for at, c in enumerate((1, 2, 4, 5))}
    cb_at = {2: slice(0, LANES), 4: slice(LANES, 2 * LANES)}
    at_row = lax.broadcasted_iota(jnp.int32, (LANES, LANES), 0) + lax.broadcasted_iota(jnp.int32, (LANES, LANES), 1)
    mirror = (at_row == LANES - 1).astype(F32).astype(BF16)

    def one_side(s, i, other):
        qc, qh, kc, vc, vh = HEAD_AT[i]
        line = line_ref[s, i : i + 1, :]
        tile = bias_tile(line)
        qm = own[s, :, own_at[qc]] * masks[qh]
        qa = qm + query_aug(qaug_ref[s], i, nq) * masks[1 - qh]
        om = cb_ref[s, :, cb_at[vc]] * masks[vh]
        center = center_ref[s, i : i + 1, :]
        lse = lse_ref[s, i : i + 1, :]
        flags = (line_ref[s, 3:4, :LANES], line_ref[s, 4:5, :LANES])
        parts = near_parts(tile)
        corner = corner_parts(tile, line, flags)
        side = 1 if other else 0
        k_cols = oth[s, :, oth_at[kc]] if other else own[s, :, own_at[kc]]
        v_cols = oth[s, :, oth_at[vc]] if other else own[s, :, own_at[vc]]
        ka = k_cols * masks[qh] + kaug_ref[side * tokens : (side + 1) * tokens] * masks[1 - qh]
        scores = mt(ka, qa)
        chance_back = mt(v_cols, om)
        near = [None] * 5
        ps, ds = [], []
        for jb in range(nq):
            row_p, row_d = [], []
            for ib in range(nq):
                at = (slice(jb * LANES, (jb + 1) * LANES), slice(ib * LANES, (ib + 1) * LANES))
                block = scores[at]
                kind = None
                if not other and abs(jb - ib) <= 1:
                    kind = jb - ib + 1
                    block = block + parts[kind]
                elif other and jb == 0 and ib == nq - 1:
                    kind = 3
                    block = block + corner[0]
                elif other and jb == nq - 1 and ib == 0:
                    kind = 4
                    block = block + corner[1]
                p = jnp.exp(block - lse[:, at[1]])
                d = p * (chance_back[at] - center[:, at[1]])
                if kind is not None:
                    near[kind] = d if near[kind] is None else near[kind] + d
                row_p.append(p.astype(BF16))
                row_d.append(d.astype(BF16))
            ps.append(jnp.concatenate(row_p, axis=1))
            ds.append(jnp.concatenate(row_d, axis=1))
        pb = jnp.concatenate(ps, axis=0)
        db = jnp.concatenate(ds, axis=0)
        return mm(ka.T, db), mm(db, qm), mm(pb, om), near

    def other_side(it, carry):
        s = 3 - it
        for copy in step_loads(s):
            copy.wait()
        cb = {
            2: mm(ab_ref[...], wa[s, :, 3 * LANES : 4 * LANES]).astype(BF16),
            4: mm(ab_ref[...], wa[s, :, 5 * LANES :]).astype(BF16),
        }
        centers = []
        for i in range(3):
            vc, vh = HEAD_AT[i][3:]
            prod = cb[vc].astype(F32) * ctx[s, :, cb_at[vc]].astype(F32)
            high = prod.astype(BF16)
            low = (prod - high.astype(F32)).astype(BF16)
            pick = jnp.broadcast_to(masks[vh], (8, LANES))
            centers.append((mt(pick, high) + mt(pick, low))[0:1, :])
        for c in cb:
            cb_ref[s, :, cb_at[c]] = cb[c]
        center_ref[s] = jnp.concatenate(centers + [jnp.zeros((5, tokens), F32)], axis=0)
        dk, dv = {}, {}
        for i, (qc, qh, kc, vc, vh) in enumerate(HEAD_AT):
            net.at("other", it, i)
            dq_acc[s, i], part_k, part_v, near = one_side(s, i, True)
            dk[kc] = dk[kc] + part_k if kc in dk else part_k
            dv[vc] = dv[vc] + part_v if vc in dv else part_v
            near_ref[s, i, 0] = near[3]
            near_ref[s, i, 1] = near[4]
        d = jnp.concatenate([dk[1], dv[2], dv[4], dk[5]], axis=1).astype(BF16)
        d_oth[s] = d
        acc_oth[...] += mt(d[:, : 2 * LANES], wa[s, :, LANES : 3 * LANES]) + mt(d[:, 2 * LANES :], wa[s, :, 4 * LANES :])
        return carry

    lax.fori_loop(0, 4, other_side, 0)
    oth_out[...] = acc_oth[...].astype(BF16)
    swap = remote(oth_out, oth_in, osem.at[0], osem.at[1], links.at_z[1])
    swap.start()

    def own_side(it, carry):
        s = 3 - it
        dk, dv, dq = {}, {}, []
        for i, (qc, qh, kc, vc, vh) in enumerate(HEAD_AT):
            net.at("own", it, i)
            part_q, part_k, part_v, near = one_side(s, i, False)
            part_q = part_q + dq_acc[s, i]
            dk[kc] = dk[kc] + part_k if kc in dk else part_k
            dv[vc] = dv[vc] + part_v if vc in dv else part_v
            at = HDIM if qh == 0 else 0
            sums_ref[s, i * 8 : (i + 1) * 8, :] = part_q[at + 8 : at + 16, :]
            dq.append(part_q[:HDIM] if qh == 0 else part_q[HDIM:])
            flags = (line_ref[s, 3:4, :LANES], line_ref[s, 4:5, :LANES])
            first, final_corner = near_ref[s, i, 0] * flags[0], near_ref[s, i, 1] * flags[1]
            blank = jnp.zeros((LANES, LANES), F32)
            tile = jnp.concatenate([near[1], near[0] + final_corner, blank, near[2] + first], axis=1)
            high = tile.astype(BF16)
            low = (tile - high.astype(F32)).astype(BF16)
            turned = pltpu.roll(mm(mirror, high) + mm(mirror, low), 0, 1, stride=1, stride_axis=0)
            line_grad_ref[s, i : i + 1, :] = jnp.sum(turned, axis=0, keepdims=True)
            line_grad_ref[s, 3 + i : 4 + i, :] = jnp.concatenate(
                [
                    jnp.sum(first, axis=0, keepdims=True),
                    jnp.sum(final_corner, axis=0, keepdims=True),
                    jnp.zeros((1, 2 * LANES), F32),
                ],
                axis=1,
            )
        line_grad_ref[s, 6:8, :] = jnp.zeros((2, 4 * LANES), F32)
        dq_a = jnp.concatenate([dq[0], dq[1]], axis=0).T
        dq_b = jnp.concatenate([dq[2], jnp.zeros_like(dq[2])], axis=0).T
        d_own = jnp.concatenate([dq_a, dk[1], dv[2], dq_b + dv[4], dk[5]], axis=1).astype(BF16)
        g_own = mm(xt[...], d_own)
        g_oth = mm(xot[...], d_oth[s])
        g_ctx = mm(abt[...], ctx[s])
        columns = [
            g_own[:, :LANES],
            g_own[:, LANES : 3 * LANES] + g_oth[:, : 2 * LANES],
            g_ctx[:, :LANES],
            g_own[:, 3 * LANES : 4 * LANES] + g_oth[:, 2 * LANES : 3 * LANES],
            g_own[:, 4 * LANES :] + g_oth[:, 3 * LANES :] + g_ctx[:, LANES:],
        ]
        g = jnp.concatenate(columns, axis=1).astype(BF16)
        rows = ga.shape[3]
        for n in range(8):
            ga[s, n // 2, n % 2] = g[n * rows : (n + 1) * rows, :]
        acc_own[...] += mt(d_own[:, : 3 * LANES], wa[s, :, : 3 * LANES]) + mt(d_own[:, 3 * LANES :], wa[s, :, 4 * LANES :])
        return carry

    lax.fori_loop(0, 4, own_side, 0)
    net.run(SCATTER_AFTER[0])
    loads[2].wait()
    swap.wait_recv()
    one_back = acc_own[...] + oth_in[...].astype(F32)
    grad, gain_part = rms_back(hidden[...], gain_ref[0:1, :], one_back)
    grad_ref[...] = grad + back[...]
    gain_grad_ref[...] = jnp.broadcast_to(gain_part, gain_grad_ref.shape)
    net.run(SCATTER_AFTER[1])
    for group in (1, 2, 0):
        net.last(group)
    swap.wait_send()
    net.finish()


def sum_kernel(x_ref, out_ref, held, other, send, recv):
    links = Links()
    near = []
    for k in range(1, 8):
        dp = links.dp
        for stride in (1, 2, 4):
            if k & stride:
                dp = peer(dp, stride)
        near.append((dp, links.mp))
    barrier = pltpu.get_barrier_semaphore()
    everyone = near + list(links.at_z[1:])
    for to in everyone:
        pl.semaphore_signal(barrier, inc=1, device_id=to, device_id_type=MESH)
    pl.semaphore_wait(barrier, len(everyone))
    first = [remote(x_ref, held.at[n], send.at[n], recv.at[n], to) for n, to in enumerate(near)]
    for copy in first:
        copy.start()
    total = x_ref[...]
    for copy in first:
        copy.wait_recv()
    for n in range(7):
        total = total + held[n]
    other[0] = total
    second = [
        remote(other.at[0], other.at[n], send.at[6 + n], recv.at[6 + n], links.at_z[n]) for n in (1, 2, 3)
    ]
    for copy in second:
        copy.start()
    for copy in second:
        copy.wait_recv()
    out_ref[...] = (other[0] + other[1]) + (other[2] + other[3])
    for copy in first + second:
        copy.wait_send()


def sum_all(x):
    dma = pltpu.SemaphoreType.DMA
    vmem = pl.BlockSpec(memory_space=pltpu.VMEM)
    return pl.pallas_call(
        sum_kernel,
        in_specs=[vmem],
        out_specs=vmem,
        out_shape=jax.ShapeDtypeStruct(x.shape, F32),
        scratch_shapes=[pltpu.VMEM((7, *x.shape), F32), pltpu.VMEM((4, *x.shape), F32), dma((10,)), dma((10,))],
        compiler_params=pltpu.CompilerParams(collective_id=2, has_side_effects=True),
        name="finish_sums",
    )(x)


def run_front(x, shard, line, qaug, kaug, gains, hidden, grad):
    t, d = x.shape
    parts, cols = line.shape[0], shard.shape[2]
    any_space = pl.BlockSpec(memory_space=pl.ANY)
    vmem = pl.BlockSpec(memory_space=pltpu.VMEM)
    dma = pltpu.SemaphoreType.DMA
    return pl.pallas_call(
        front_kernel,
        in_specs=[vmem] * 6 + [any_space] * 2,
        out_specs=[any_space] * 3 + [vmem] + [any_space] * 2 + [vmem] * 3 + [any_space] * 2,
        out_shape=[
            jax.ShapeDtypeStruct((parts, t, 5 * LANES), BF16),
            jax.ShapeDtypeStruct((parts, t, 4 * LANES), BF16),
            jax.ShapeDtypeStruct((parts, t, 2 * LANES), BF16),
            jax.ShapeDtypeStruct((parts, 8, t), F32),
            jax.ShapeDtypeStruct((parts, d, cols), BF16),
            jax.ShapeDtypeStruct((t, d), BF16),
            jax.ShapeDtypeStruct((t, d), F32),
            jax.ShapeDtypeStruct((t, d), F32),
            jax.ShapeDtypeStruct((8, d), F32),
            jax.ShapeDtypeStruct((parts, d, cols), BF16),
            jax.ShapeDtypeStruct((parts, d, cols), BF16),
        ],
        scratch_shapes=[
            pltpu.VMEM((3, parts, d, cols), BF16),
            pltpu.VMEM((t, d), BF16),
            pltpu.VMEM((parts, t, 5 * LANES), BF16),
            pltpu.VMEM((parts, t, 4 * LANES), BF16),
            pltpu.VMEM((parts, t, 2 * LANES), BF16),
            pltpu.VMEM((2, 2 * t, t), F32),
            pltpu.VMEM((2, 2 * t, t), BF16),
            pltpu.VMEM((t, d), F32),
            pltpu.VMEM((t, d), F32),
            pltpu.VMEM((t, d), BF16), pltpu.VMEM((d, t), BF16),
            pltpu.VMEM((t, d), BF16), pltpu.VMEM((d, t), BF16),
            pltpu.VMEM((t, d), F32), pltpu.VMEM((t, d), F32),
            pltpu.VMEM((2, d, cols), BF16), pltpu.VMEM((2, d, cols), BF16),
            dma((12, 8)), dma((12, 8)), dma((9,)), dma((9,)), dma((2,)), dma((5,)), dma((5,)), dma((2, 2)),
        ],
        compiler_params=pltpu.CompilerParams(
            vmem_limit_bytes=62 * 2**20, collective_id=0, has_side_effects=True
        ),
        name="front",
    )(x, shard, line, qaug, kaug, gains, hidden, grad)


def run_back(x, xo, back, hidden, wa, line, qaug, kaug, own, oth, ctx, lse, gi, go, gains):
    t, d = x.shape
    parts, cols = wa.shape[0], wa.shape[2]
    rows = d // 8
    any_space = pl.BlockSpec(memory_space=pl.ANY)
    vmem = pl.BlockSpec(memory_space=pltpu.VMEM)
    dma = pltpu.SemaphoreType.DMA
    split = (parts, 4, 2, rows, cols)
    return pl.pallas_call(
        back_kernel,
        in_specs=[vmem] * 6 + [any_space] * 9,
        out_specs=[vmem] * 5,
        out_shape=[
            jax.ShapeDtypeStruct((t, d), F32),
            jax.ShapeDtypeStruct((8, d), F32),
            jax.ShapeDtypeStruct((parts, 8, t), F32),
            jax.ShapeDtypeStruct((parts, 24, t), F32),
            jax.ShapeDtypeStruct((3, rows, cols), F32),
        ],
        scratch_shapes=[
            pltpu.VMEM((t, d), BF16), pltpu.VMEM((t, d), F32), pltpu.VMEM((t, d), F32),
            pltpu.VMEM(wa.shape, BF16), pltpu.VMEM(own.shape, BF16), pltpu.VMEM(oth.shape, BF16), pltpu.VMEM(ctx.shape, BF16),
            pltpu.VMEM((d, t), BF16), pltpu.VMEM((d, t), BF16), pltpu.VMEM((t, d), BF16), pltpu.VMEM((d, t), BF16),
            pltpu.VMEM((t, d), F32), pltpu.VMEM((t, d), F32), pltpu.VMEM((t, d), BF16), pltpu.VMEM((t, d), BF16),
            pltpu.VMEM((parts, 3, LANES, t), F32), pltpu.VMEM((parts, t, 4 * LANES), BF16),
            pltpu.VMEM((parts, t, 2 * LANES), BF16), pltpu.VMEM((parts, 8, t), F32), pltpu.VMEM((parts, 3, 2, LANES, LANES), F32),
            pltpu.VMEM(split, BF16), pltpu.VMEM((12, 4, rows, cols), BF16), pltpu.VMEM((3, 4, rows, cols), BF16),
            pltpu.VMEM((12, 2, rows // 2, cols), BF16), pltpu.VMEM((12, 2, rows, cols), BF16), pltpu.VMEM((3, 3, rows, cols), BF16),
            dma((3,)), dma((parts, 4)), dma((2,)), dma((12, 6)), dma((12, 6)), dma((3,)),
        ],
        compiler_params=pltpu.CompilerParams(
            vmem_limit_bytes=62 * 2**20, collective_id=1, has_side_effects=True
        ),
        name="back",
    )(x, line, qaug, kaug, lse, gains, xo, back, hidden, wa, own, oth, ctx, gi.reshape(split), go.reshape(split))


def pack_attn(attn, out_t):
    cut = [[part[:, i * HDIM : (i + 1) * HDIM] for i in range(3)] for part in (attn[0], attn[1], attn[2], out_t)]
    q, k, v, o = cut
    return jnp.concatenate([q[0], q[1], k[0], k[1], v[0], v[1], o[0], o[1], q[2], v[2], k[2], o[2]], axis=1)


def unpack_attn(block):
    c = [block[:, i * HDIM : (i + 1) * HDIM] for i in range(12)]
    attn = jnp.stack(
        [
            jnp.concatenate([c[0], c[1], c[8]], axis=1),
            jnp.concatenate([c[2], c[3], c[10]], axis=1),
            jnp.concatenate([c[4], c[5], c[9]], axis=1),
        ]
    )
    return attn, jnp.concatenate([c[6], c[7], c[11]], axis=1)


def body(
    hidden_in, out_grad, attn_weight, out_weight, inner_weight, outer_weight, rel_bias, gains, lengths, table,
    attn_first, attn_second, out_first, out_second, inner_first, inner_second, outer_first, outer_second,
    rel_first, rel_second, gain_first, gain_second, *, parts,
):
    tokens = hidden_in.shape[0]
    nq = tokens // LANES
    heads = rel_bias.shape[1]
    per_seq = SEQLEN // tokens
    mp_index = lax.axis_index("mp")
    half = mp_index % per_seq
    length = lengths[mp_index // per_seq]

    shard = [
        pack_attn(attn_weight.astype(BF16), out_weight.astype(BF16).T),
        inner_weight.astype(BF16),
        outer_weight.astype(BF16).T,
    ]
    order = jnp.bitwise_xor(mp_index, jnp.arange(parts))

    x1 = rms_scaled(hidden_in, gains[0]).astype(BF16)

    u = jnp.arange(4 * LANES)
    offset = jnp.where(u < 2 * LANES, -u, 4 * LANES - u)
    buckets = jnp.arange(rel_bias.shape[0], dtype=jnp.int32)
    line_hot = (jnp.take(table, offset + SEQLEN - 1)[:, None] == buckets[None, :]).astype(F32)
    line = jnp.dot(line_hot, rel_bias, precision=lax.Precision.HIGHEST).T.reshape(parts, heads // parts, 4 * LANES)
    first_flag = (half == 0).astype(F32)
    flags = jnp.stack([jnp.full((4 * LANES,), first_flag), jnp.full((4 * LANES,), 1.0 - first_flag)])
    line_in = jnp.concatenate(
        [line, jnp.broadcast_to(flags[None], (parts, 2, 4 * LANES)), jnp.zeros((parts, 3, 4 * LANES), F32)], axis=1
    )
    far_before, far_after = line[:, :, LANES], line[:, :, 3 * LANES]
    jb, ib = jnp.arange(nq)[None, :], jnp.arange(nq)[:, None]
    own_before, own_after = (jb < ib - 1).astype(F32), (jb > ib + 1).astype(F32)
    oth_before = jnp.full((nq, nq), 1.0 - first_flag)
    w_before = jnp.concatenate([own_before, oth_before], axis=1)
    w_after = jnp.concatenate([own_after, 1.0 - oth_before], axis=1)
    far = far_before[:, :, None, None] * w_before + far_after[:, :, None, None] * w_after
    far_hi = far.astype(BF16).astype(F32)
    far_lo = far - far_hi
    one = jnp.ones((parts, heads // parts, nq, 1), F32)
    blank = jnp.zeros((parts, heads // parts, nq, HDIM), F32)
    q64 = jnp.concatenate(
        [blank[..., :3], one, blank[..., :4], far_hi, far_lo, blank[..., : HDIM - 8 - 4 * nq]], axis=-1
    )
    qaug = jnp.concatenate([q64, q64], axis=-1).reshape(parts, 3 * nq, LANES)
    qaug = jnp.pad(qaug, ((0, 0), (0, 16 - 3 * nq), (0, 0))).astype(BF16)
    row = jnp.arange(2 * tokens)
    position = jnp.where(row < tokens, half * tokens + row, (1 - half) * tokens + row - tokens)
    masked = jnp.where(position < length, 0.0, NEG)
    col = jnp.arange(LANES) % HDIM
    block_of = row // LANES
    hot = ((col >= 8) & (col < 8 + 4 * nq))[None, :] & ((col[None, :] - 8) % (2 * nq) == block_of[:, None])
    kaug = jnp.where((col == 3)[None, :], masked[:, None], hot.astype(F32)).astype(BF16)

    line_in, qaug = jnp.take(line_in, order, axis=0), jnp.take(qaug, order, axis=0)
    own, oth, ctx, lse, wa, x1o, block_out, middle_back, gain_two, gi, go = run_front(
        x1, jnp.stack(shard), line_in, qaug, kaug, gains, hidden_in, out_grad
    )
    input_grad, gain_one, line_grad, sums, owned = run_back(
        x1, x1o, middle_back, hidden_in, wa, line_in, qaug, kaug, own, oth, ctx, lse, gi, go, gains
    )

    line_grad = jnp.take(line_grad, order, axis=0)
    near_line = jnp.roll(line_grad[:, :3], 1 - LANES, axis=2)
    sums = jnp.take(sums, order, axis=0)
    near_grad = jnp.einsum(
        "ub,hu->bh", line_hot, near_line.reshape(heads, 4 * LANES), precision=lax.Precision.HIGHEST
    )
    corner = jnp.sum(line_grad[:, 3:6].reshape(heads, 4, LANES), axis=-1)
    block_sums = jnp.sum(sums.reshape(heads, 2 * nq, nq, LANES), axis=-1)
    far_w = jnp.transpose(jnp.stack([w_before, w_after]), (0, 2, 1))
    far_grad = jnp.einsum("hji,sji->sh", block_sums, far_w, precision=lax.Precision.HIGHEST)
    far_grad = far_grad - jnp.stack([corner[:, 1], corner[:, 0]])
    far_hot = (jnp.stack([table[0], table[2 * SEQLEN - 2]])[None, :] == buckets[:, None]).astype(F32)
    rel_part = near_grad + jnp.dot(far_hot, far_grad, precision=lax.Precision.HIGHEST)

    g_attn, g_out_t = unpack_attn(owned[0])
    grads = (g_attn, g_out_t.T, owned[1], owned[2].T)
    square_part = jnp.sum(owned * owned)
    width = gains.shape[1]
    small = jnp.concatenate(
        [gain_one[0], gain_two[0], rel_part.reshape(-1), jnp.full((LANES,), square_part)]
    ).reshape(-1, LANES)
    small = sum_all(jnp.pad(small, ((0, -small.shape[0] % 8), (0, 0)))).reshape(-1)
    gain_grad = small[: 2 * width].reshape(2, width)
    rel_grad = small[2 * width : 2 * width + rel_bias.size].reshape(rel_bias.shape)
    square_total = small[2 * width + rel_bias.size]
    grad_norm = jnp.sqrt(square_total + jnp.sum(gain_grad * gain_grad) + jnp.sum(rel_grad * rel_grad))
    factor = jnp.minimum(1.0, CLIP / (grad_norm + 1e-06))
    attn_new = adam_step(attn_weight, grads[0], attn_first, attn_second, factor, RATE_MATRIX)
    out_new = adam_step(out_weight, grads[1], out_first, out_second, factor, RATE_OUT)
    inner_new = adam_step(inner_weight, grads[2], inner_first, inner_second, factor, RATE_MATRIX)
    outer_new = adam_step(outer_weight, grads[3], outer_first, outer_second, factor, RATE_MATRIX)
    rel_new = adam_step(rel_bias, rel_grad, rel_first, rel_second, factor, RATE_SMALL)
    gain_new = adam_step(gains, gain_grad, gain_first, gain_second, factor, RATE_SMALL)
    return (block_out, input_grad, grad_norm, *attn_new, *out_new, *inner_new, *outer_new, *rel_new, *gain_new)


def forward_kernel(
    x_ref, xo_ref, w_ref, line_ref, qaug_ref, kaug_ref, hidden_ref,
    own_ref, oth_ref, ctx_ref, lse_ref, middle_ref,
    acc, s_ref, e_ref,
):
    m = pl.program_id(0)
    tokens = x_ref.shape[0]
    nq = tokens // LANES
    x, xo = x_ref[...], xo_ref[...]
    p_a = mm(x, w_ref[:, : 3 * LANES]).astype(BF16)
    p_b = mm(x, w_ref[:, 4 * LANES :]).astype(BF16)
    o_a = mm(xo, w_ref[:, LANES : 3 * LANES]).astype(BF16)
    o_b = mm(xo, w_ref[:, 4 * LANES :]).astype(BF16)
    own_ref[0, :, : 3 * LANES] = p_a
    own_ref[0, :, 3 * LANES :] = p_b
    oth_ref[0, :, : 2 * LANES] = o_a
    oth_ref[0, :, 2 * LANES :] = o_b
    cols_own = {0: p_a[:, :LANES], 1: p_a[:, LANES : 2 * LANES], 2: p_a[:, 2 * LANES :], 4: p_b[:, :LANES], 5: p_b[:, LANES:]}
    cols_oth = {1: o_a[:, :LANES], 2: o_a[:, LANES:], 4: o_b[:, :LANES], 5: o_b[:, LANES:]}
    both = {c: jnp.concatenate([cols_own[c], cols_oth[c]], axis=0) for c in (1, 2, 4, 5)}
    masks = [half_rows(0), half_rows(1)]
    flags = (line_ref[0, 3:4, :LANES], line_ref[0, 4:5, :LANES])
    v_t = {2: both[2].T, 4: both[4].T}
    count = lax.broadcasted_iota(jnp.int32, (HDIM, 2 * tokens), 0)
    ones = (count == 0).astype(F32).astype(BF16)
    pieces = []
    stats = []
    for i, (qc, qh, kc, vc, vh) in enumerate(HEAD_AT):
        line = line_ref[0, i : i + 1, :]
        tile = bias_tile(line)
        qa = cols_own[qc] * masks[qh] + query_aug(qaug_ref[0], i, nq) * masks[1 - qh]
        ka = both[kc] * masks[qh] + kaug_ref[...] * masks[1 - qh]
        scores = mt(ka, qa)
        peak = None
        for jb, row in enumerate(add_bias(scores, tile, line, flags, nq)):
            s_ref[i, jb * LANES : (jb + 1) * LANES, :] = row
            top = jnp.max(row.reshape(LANES // 8, 8, tokens), axis=0)
            peak = top if peak is None else jnp.maximum(peak, top)
        peak = jnp.max(peak, axis=0, keepdims=True)
        for jb in range(2 * nq):
            rows = slice(jb * LANES, (jb + 1) * LANES)
            e_ref[i, rows, :] = jnp.exp(s_ref[i, rows, :] - peak).astype(BF16)
        if vh == 0:
            va = jnp.concatenate([v_t[vc][:HDIM], ones], axis=0)
        else:
            va = jnp.concatenate([ones, v_t[vc][HDIM:]], axis=0)
        ot = mm(va, e_ref[i])
        at = HDIM if vh == 0 else 0
        total = ot[at : at + 1, :]
        stats.append(peak + jnp.log(total))
        real = ot[:HDIM] if vh == 0 else ot[HDIM:]
        pieces.append(real / total)
    zero = jnp.zeros((HDIM, tokens), F32)
    ctx_a = jnp.concatenate([pieces[0], pieces[1]], axis=0).T.astype(BF16)
    ctx_b = jnp.concatenate([zero, pieces[2]], axis=0).T.astype(BF16)
    ctx_ref[0, :, :LANES] = ctx_a
    ctx_ref[0, :, LANES:] = ctx_b
    for i in range(3):
        lse_ref[0, i : i + 1, :] = stats[i]
    lse_ref[0, 3:8, :] = jnp.zeros((5, tokens), F32)
    part = mt(ctx_a, w_ref[:, 3 * LANES : 4 * LANES]) + mt(ctx_b, w_ref[:, 5 * LANES :])

    @pl.when(m == 0)
    def _():
        acc[...] = hidden_ref[...] + part

    @pl.when(m > 0)
    def _():
        acc[...] += part

    @pl.when(m == pl.num_programs(0) - 1)
    def _():
        middle_ref[...] = acc[...]


def feed_kernel(
    middle_ref, grad_ref, gain_ref, wi_ref, wo_ref,
    out_ref, back_ref, gain_grad_ref, gi_ref, go_ref,
    x2_ref, x2t_ref, ob_ref, obt_ref, acc_out, acc_two,
):
    f = pl.program_id(0)

    @pl.when(f == 0)
    def _():
        x2 = rms_scaled(middle_ref[...], gain_ref[1:2, :]).astype(BF16)
        x2_ref[...] = x2
        x2t_ref[...] = x2.T
        ob = grad_ref[...].astype(BF16)
        ob_ref[...] = ob
        obt_ref[...] = ob.T
        acc_out[...] = jnp.zeros_like(acc_out)
        acc_two[...] = jnp.zeros_like(acc_two)

    inner = mm(x2_ref[...], wi_ref[...])
    active_back = mm(ob_ref[...], wo_ref[...])
    c = 0.7978845608028654
    sq = inner * inner
    th = jnp.tanh(c * (inner + 0.044715 * (sq * inner)))
    half = 0.5 * (1.0 + th)
    active = (inner * half).astype(BF16)
    slope = half + (0.5 * c) * inner * (1.0 - th * th) * (1.0 + (3 * 0.044715) * sq)
    inner_back = (slope * active_back).astype(BF16)
    acc_out[...] += mt(active, wo_ref[...])
    acc_two[...] += mt(inner_back, wi_ref[...])
    go_ref[...] = mm(obt_ref[...], active).astype(go_ref.dtype)
    gi_ref[...] = mm(x2t_ref[...], inner_back).astype(gi_ref.dtype)

    @pl.when(f == pl.num_programs(0) - 1)
    def _():
        out_ref[...] = middle_ref[...] + acc_out[...]
        result, gain_part = rms_back(middle_ref[...], gain_ref[1:2, :], acc_two[...])
        back_ref[...] = grad_ref[...] + result
        gain_grad_ref[...] = jnp.broadcast_to(gain_part, gain_grad_ref.shape)


def backward_kernel(
    x_ref, xo_ref, back_ref, w_ref, line_ref, qaug_ref, kaug_ref, own_ref, oth_ref, ctx_ref, lse_ref,
    ga_ref, one_own_ref, one_oth_ref, near_ref, sums_ref,
    xt_ref, xot_ref, ab_ref, abt_ref, acc_own, acc_oth,
):
    m = pl.program_id(0)
    tokens = x_ref.shape[0]
    nq = tokens // LANES

    @pl.when(m == 0)
    def _():
        xt_ref[...] = x_ref[...].T
        xot_ref[...] = xo_ref[...].T
        ab = back_ref[...].astype(BF16)
        ab_ref[...] = ab
        abt_ref[...] = ab.T
        acc_own[...] = jnp.zeros_like(acc_own)
        acc_oth[...] = jnp.zeros_like(acc_oth)

    ab = ab_ref[...]
    cb = {2: mm(ab, w_ref[:, 3 * LANES : 4 * LANES]).astype(BF16), 4: mm(ab, w_ref[:, 5 * LANES :]).astype(BF16)}
    ctx = {2: ctx_ref[0, :, :LANES], 4: ctx_ref[0, :, LANES:]}
    own = {c: own_ref[0, :, at * LANES : (at + 1) * LANES] for at, c in enumerate((0, 1, 2, 4, 5))}
    oth = {c: oth_ref[0, :, at * LANES : (at + 1) * LANES] for at, c in enumerate((1, 2, 4, 5))}
    masks = [half_rows(0), half_rows(1)]
    flags = (line_ref[0, 3:4, :LANES], line_ref[0, 4:5, :LANES])
    prod = {c: cb[c].astype(F32) * ctx[c].astype(F32) for c in (2, 4)}
    prod_hi = {c: prod[c].astype(BF16) for c in prod}
    prod_lo = {c: (prod[c] - prod_hi[c].astype(F32)).astype(BF16) for c in prod}
    dq_t = []
    dk = {}
    dv = {}
    for i, (qc, qh, kc, vc, vh) in enumerate(HEAD_AT):
        line = line_ref[0, i : i + 1, :]
        tile = bias_tile(line)
        qm = own[qc] * masks[qh]
        qa = qm + query_aug(qaug_ref[0], i, nq) * masks[1 - qh]
        om = cb[vc] * masks[vh]
        pick = jnp.broadcast_to(masks[vh], (8, LANES))
        center = (mt(pick, prod_hi[vc]) + mt(pick, prod_lo[vc]))[0:1, :]
        lse = lse_ref[0, i : i + 1, :]
        kaug = kaug_ref[...] * masks[1 - qh]
        dqt = None
        parts = near_parts(tile)
        corner = corner_parts(tile, line, flags)
        near = [None, None, None, None, None]
        for side, cols in enumerate((own, oth)):
            ka = cols[kc] * masks[qh] + kaug[side * tokens : (side + 1) * tokens]
            scores = mt(ka, qa)
            chance_back = mt(cols[vc], om)
            ps, ds = [], []
            for jb in range(nq):
                row_s, row_p, row_d = [], [], []
                for ib in range(nq):
                    at = (slice(jb * LANES, (jb + 1) * LANES), slice(ib * LANES, (ib + 1) * LANES))
                    block = scores[at]
                    kind = None
                    if side == 0 and abs(jb - ib) <= 1:
                        block = block + parts[jb - ib + 1]
                        kind = jb - ib + 1
                    elif side == 1 and jb == 0 and ib == nq - 1:
                        block = block + corner[0]
                        kind = 3
                    elif side == 1 and jb == nq - 1 and ib == 0:
                        block = block + corner[1]
                        kind = 4
                    p = jnp.exp(block - lse[:, at[1]])
                    d = p * (chance_back[at] - center[:, at[1]])
                    if kind is not None:
                        near[kind] = d if near[kind] is None else near[kind] + d
                    row_p.append(p.astype(BF16))
                    row_d.append(d.astype(BF16))
                ps.append(jnp.concatenate(row_p, axis=1))
                ds.append(jnp.concatenate(row_d, axis=1))
            pb = jnp.concatenate(ps, axis=0)
            db = jnp.concatenate(ds, axis=0)
            part_v = mm(pb, om)
            part_k = mm(db, qm)
            dv[vc, side] = part_v if (vc, side) not in dv else dv[vc, side] + part_v
            dk[kc, side] = part_k if (kc, side) not in dk else dk[kc, side] + part_k
            part_q = mm(ka.T, db)
            dqt = part_q if dqt is None else dqt + part_q
        at = HDIM if qh == 0 else 0
        sums_ref[0, i * 8 : (i + 1) * 8, :] = dqt[at + 8 : at + 16, :]
        dq_t.append(dqt[:HDIM] if qh == 0 else dqt[HDIM:])
        for kind in range(5):
            near_ref[0, i, kind] = near[kind]
    dq_a = jnp.concatenate([dq_t[0], dq_t[1]], axis=0).T
    dq_b = jnp.concatenate([dq_t[2], jnp.zeros_like(dq_t[2])], axis=0).T
    d_own = jnp.concatenate([dq_a, dk[1, 0], dv[2, 0], dq_b + dv[4, 0], dk[5, 0]], axis=1).astype(BF16)
    d_oth = jnp.concatenate([dk[1, 1], dv[2, 1], dv[4, 1], dk[5, 1]], axis=1).astype(BF16)
    xt, xot, abt = xt_ref[...], xot_ref[...], abt_ref[...]
    g_own = mm(xt, d_own)
    g_oth = mm(xot, d_oth)
    g_ctx = mm(abt, ctx_ref[0])
    ga_ref[:, :LANES] = g_own[:, :LANES].astype(ga_ref.dtype)
    ga_ref[:, LANES : 3 * LANES] = (g_own[:, LANES : 3 * LANES] + g_oth[:, : 2 * LANES]).astype(ga_ref.dtype)
    ga_ref[:, 3 * LANES : 4 * LANES] = g_ctx[:, :LANES].astype(ga_ref.dtype)
    ga_ref[:, 4 * LANES : 5 * LANES] = (g_own[:, 3 * LANES : 4 * LANES] + g_oth[:, 2 * LANES : 3 * LANES]).astype(ga_ref.dtype)
    ga_ref[:, 5 * LANES :] = (g_own[:, 4 * LANES :] + g_oth[:, 3 * LANES :] + g_ctx[:, LANES:]).astype(ga_ref.dtype)
    acc_own[...] += mt(d_own[:, : 3 * LANES], w_ref[:, : 3 * LANES]) + mt(d_own[:, 3 * LANES :], w_ref[:, 4 * LANES :])
    acc_oth[...] += mt(d_oth[:, : 2 * LANES], w_ref[:, LANES : 3 * LANES]) + mt(d_oth[:, 2 * LANES :], w_ref[:, 4 * LANES :])

    @pl.when(m == pl.num_programs(0) - 1)
    def _():
        one_own_ref[...] = acc_own[...]
        one_oth_ref[...] = acc_oth[...].astype(one_oth_ref.dtype)


def whole(shape):
    return pl.BlockSpec(shape, lambda m: (0,) * len(shape))


def params():
    return pltpu.CompilerParams(vmem_limit_bytes=60 * 2**20)


def run_forward(x, xo, wa, line, qaug, kaug, hidden, parts):
    t, d = x.shape
    return pl.pallas_call(
        forward_kernel,
        grid=(parts,),
        in_specs=[
            whole((t, d)), whole((t, d)),
            pl.BlockSpec((d, 6 * LANES), lambda m: (0, m)),
            pl.BlockSpec((1, 8, 4 * LANES), lambda m: (m, 0, 0)),
            pl.BlockSpec((1, 16, LANES), lambda m: (m, 0, 0)),
            whole((2 * t, LANES)), whole((t, d)),
        ],
        out_specs=[
            pl.BlockSpec((1, t, 5 * LANES), lambda m: (m, 0, 0)),
            pl.BlockSpec((1, t, 4 * LANES), lambda m: (m, 0, 0)),
            pl.BlockSpec((1, t, 2 * LANES), lambda m: (m, 0, 0)),
            pl.BlockSpec((1, 8, t), lambda m: (m, 0, 0)),
            whole((t, d)),
        ],
        out_shape=[
            jax.ShapeDtypeStruct((parts, t, 5 * LANES), BF16),
            jax.ShapeDtypeStruct((parts, t, 4 * LANES), BF16),
            jax.ShapeDtypeStruct((parts, t, 2 * LANES), BF16),
            jax.ShapeDtypeStruct((parts, 8, t), F32),
            jax.ShapeDtypeStruct((t, d), F32),
        ],
        scratch_shapes=[
            pltpu.VMEM((t, d), F32),
            pltpu.VMEM((3, 2 * t, t), F32),
            pltpu.VMEM((3, 2 * t, t), BF16),
        ],
        compiler_params=params(),
        name="attend_forward",
    )(x, xo, wa, line, qaug, kaug, hidden)


def run_feed(middle, grad, gains, wi, wo):
    t, d = middle.shape
    units = wi.shape[1]
    tile = min(512, units)
    return pl.pallas_call(
        feed_kernel,
        grid=(units // tile,),
        in_specs=[
            whole((t, d)), whole((t, d)), whole((2, d)),
            pl.BlockSpec((d, tile), lambda f: (0, f)),
            pl.BlockSpec((d, tile), lambda f: (0, f)),
        ],
        out_specs=[
            whole((t, d)), whole((t, d)), whole((8, d)),
            pl.BlockSpec((d, tile), lambda f: (0, f)),
            pl.BlockSpec((d, tile), lambda f: (0, f)),
        ],
        out_shape=[
            jax.ShapeDtypeStruct((t, d), F32),
            jax.ShapeDtypeStruct((t, d), F32),
            jax.ShapeDtypeStruct((8, d), F32),
            jax.ShapeDtypeStruct((d, units), BF16),
            jax.ShapeDtypeStruct((d, units), BF16),
        ],
        scratch_shapes=[
            pltpu.VMEM((t, d), BF16), pltpu.VMEM((d, t), BF16),
            pltpu.VMEM((t, d), BF16), pltpu.VMEM((d, t), BF16),
            pltpu.VMEM((t, d), F32), pltpu.VMEM((t, d), F32),
        ],
        compiler_params=params(),
        name="feed_both",
    )(middle, grad, gains, wi, wo)


def run_backward(x, xo, back, wa, line, qaug, kaug, own, oth, ctx, lse, parts):
    t, d = x.shape
    return pl.pallas_call(
        backward_kernel,
        grid=(parts,),
        in_specs=[
            whole((t, d)), whole((t, d)), whole((t, d)),
            pl.BlockSpec((d, 6 * LANES), lambda m: (0, m)),
            pl.BlockSpec((1, 8, 4 * LANES), lambda m: (m, 0, 0)),
            pl.BlockSpec((1, 16, LANES), lambda m: (m, 0, 0)),
            whole((2 * t, LANES)),
            pl.BlockSpec((1, t, 5 * LANES), lambda m: (m, 0, 0)),
            pl.BlockSpec((1, t, 4 * LANES), lambda m: (m, 0, 0)),
            pl.BlockSpec((1, t, 2 * LANES), lambda m: (m, 0, 0)),
            pl.BlockSpec((1, 8, t), lambda m: (m, 0, 0)),
        ],
        out_specs=[
            pl.BlockSpec((d, 6 * LANES), lambda m: (0, m)),
            whole((t, d)), whole((t, d)),
            pl.BlockSpec((1, 3, 5, LANES, LANES), lambda m: (m, 0, 0, 0, 0)),
            pl.BlockSpec((1, 24, t), lambda m: (m, 0, 0)),
        ],
        out_shape=[
            jax.ShapeDtypeStruct((d, parts * 6 * LANES), BF16),
            jax.ShapeDtypeStruct((t, d), F32),
            jax.ShapeDtypeStruct((t, d), BF16),
            jax.ShapeDtypeStruct((parts, 3, 5, LANES, LANES), F32),
            jax.ShapeDtypeStruct((parts, 24, t), F32),
        ],
        scratch_shapes=[
            pltpu.VMEM((d, t), BF16), pltpu.VMEM((d, t), BF16),
            pltpu.VMEM((t, d), BF16), pltpu.VMEM((d, t), BF16),
            pltpu.VMEM((t, d), F32), pltpu.VMEM((t, d), F32),
        ],
        compiler_params=params(),
        name="attend_backward",
    )(x, xo, back, wa, line, qaug, kaug, own, oth, ctx, lse)


def general_body(
    hidden_in, out_grad, attn_weight, out_weight, inner_weight, outer_weight, rel_bias, gains, lengths, table,
    attn_first, attn_second, out_first, out_second, inner_first, inner_second, outer_first, outer_second,
    rel_first, rel_second, gain_first, gain_second, *, parts,
):
    tokens = hidden_in.shape[0]
    nq = tokens // LANES
    heads = rel_bias.shape[1]
    per_seq = SEQLEN // tokens
    mp_index = lax.axis_index("mp")
    half = mp_index % per_seq
    length = lengths[mp_index // per_seq]

    shard = [
        pack_attn(attn_weight.astype(BF16), out_weight.astype(BF16).T),
        inner_weight.astype(BF16),
        outer_weight.astype(BF16).T,
    ]
    gathered = [lax.all_gather(lax.all_gather(s, "dp", axis=0, tiled=True), "mp", axis=1, tiled=True) for s in shard]
    wa, wi, wo = gathered

    x1 = rms_scaled(hidden_in, gains[0]).astype(BF16)
    swap = [(p, p ^ 1) for p in range(parts)]
    x1o = lax.ppermute(x1, "mp", swap)

    u = jnp.arange(4 * LANES)
    offset = jnp.where(u < 2 * LANES, -u, 4 * LANES - u)
    buckets = jnp.arange(rel_bias.shape[0], dtype=jnp.int32)
    line_hot = (jnp.take(table, offset + SEQLEN - 1)[:, None] == buckets[None, :]).astype(F32)
    line = jnp.dot(line_hot, rel_bias, precision=lax.Precision.HIGHEST).T.reshape(parts, heads // parts, 4 * LANES)
    first_flag = (half == 0).astype(F32)
    flags = jnp.stack([jnp.full((4 * LANES,), first_flag), jnp.full((4 * LANES,), 1.0 - first_flag)])
    line_in = jnp.concatenate(
        [line, jnp.broadcast_to(flags[None], (parts, 2, 4 * LANES)), jnp.zeros((parts, 3, 4 * LANES), F32)], axis=1
    )
    far_before, far_after = line[:, :, LANES], line[:, :, 3 * LANES]
    jb, ib = jnp.arange(nq)[None, :], jnp.arange(nq)[:, None]
    own_before, own_after = (jb < ib - 1).astype(F32), (jb > ib + 1).astype(F32)
    oth_before = jnp.full((nq, nq), 1.0 - first_flag)
    w_before = jnp.concatenate([own_before, oth_before], axis=1)
    w_after = jnp.concatenate([own_after, 1.0 - oth_before], axis=1)
    far = far_before[:, :, None, None] * w_before + far_after[:, :, None, None] * w_after
    far_hi = far.astype(BF16).astype(F32)
    far_lo = far - far_hi
    one = jnp.ones((parts, heads // parts, nq, 1), F32)
    blank = jnp.zeros((parts, heads // parts, nq, HDIM), F32)
    q64 = jnp.concatenate(
        [blank[..., :3], one, blank[..., :4], far_hi, far_lo, blank[..., : HDIM - 8 - 4 * nq]], axis=-1
    )
    qaug = jnp.concatenate([q64, q64], axis=-1).reshape(parts, 3 * nq, LANES)
    qaug = jnp.pad(qaug, ((0, 0), (0, 16 - 3 * nq), (0, 0))).astype(BF16)
    row = jnp.arange(2 * tokens)
    position = jnp.where(row < tokens, half * tokens + row, (1 - half) * tokens + row - tokens)
    masked = jnp.where(position < length, 0.0, NEG)
    col = jnp.arange(LANES) % HDIM
    block_of = row // LANES
    hot = ((col >= 8) & (col < 8 + 4 * nq))[None, :] & ((col[None, :] - 8) % (2 * nq) == block_of[:, None])
    kaug = jnp.where((col == 3)[None, :], masked[:, None], hot.astype(F32)).astype(BF16)

    own, oth, ctx, lse, middle = run_forward(x1, x1o, wa, line_in, qaug, kaug, hidden_in, parts)
    block_out, middle_back, gain_two, gi, go = run_feed(middle, out_grad, gains, wi, wo)
    ga, one_own, one_oth, near, sums = run_backward(
        x1, x1o, middle_back, wa, line_in, qaug, kaug, own, oth, ctx, lse, parts
    )
    one_back = one_own + lax.ppermute(one_oth, "mp", swap).astype(F32)
    input_grad, gain_one = rms_back(hidden_in, gains[0:1], one_back)
    input_grad = input_grad + middle_back

    nh = heads // parts
    near = near.reshape(heads, 5, LANES, LANES)
    first_w = first_flag
    blocks = jnp.stack(
        [near[:, 0] + near[:, 4] * (1.0 - first_w), near[:, 1], near[:, 2] + near[:, 3] * first_w], axis=1
    )
    r = jnp.arange(LANES)
    diff = r[None, :, None] - r[None, None, :] + (jnp.arange(3) - 1)[:, None, None] * LANES
    near_bucket = jnp.take(table, diff + SEQLEN - 1).reshape(1, -1)
    near_hot = (near_bucket == buckets[:, None]).astype(F32)
    near_grad = lax.dot_general(
        near_hot, blocks.reshape(heads, -1), (((1,), (1,)), ((), ())), precision=lax.Precision.HIGHEST
    )
    block_sums = jnp.sum(sums.reshape(heads, 2 * nq, nq, LANES), axis=-1)
    far_w = jnp.transpose(jnp.stack([w_before, w_after]), (0, 2, 1))
    corner = jnp.stack([jnp.sum(near[:, 4], (1, 2)) * (1.0 - first_w), jnp.sum(near[:, 3], (1, 2)) * first_w])
    far_grad = jnp.einsum("hji,sji->sh", block_sums, far_w, precision=lax.Precision.HIGHEST) - corner
    far_hot = (jnp.stack([table[0], table[2 * SEQLEN - 2]])[None, :] == buckets[:, None]).astype(F32)
    rel_part = near_grad + jnp.dot(far_hot, far_grad, precision=lax.Precision.HIGHEST)

    owned = [
        lax.psum_scatter(
            lax.psum_scatter(g, "mp", scatter_dimension=1, tiled=True), "dp", scatter_dimension=0, tiled=True
        ).astype(F32)
        for g in (ga, gi, go)
    ]
    g_attn, g_out_t = unpack_attn(owned[0])
    grads = (g_attn, g_out_t.T, owned[1], owned[2].T)
    square_part = sum(jnp.sum(g * g) for g in owned)
    gain_grad, rel_grad, square_total = lax.psum(
        (jnp.concatenate([gain_one, gain_two[:1]], axis=0), rel_part, square_part), ("dp", "mp")
    )
    grad_norm = jnp.sqrt(square_total + jnp.sum(gain_grad * gain_grad) + jnp.sum(rel_grad * rel_grad))
    factor = jnp.minimum(1.0, CLIP / (grad_norm + 1e-06))
    attn_new = adam_step(attn_weight, grads[0], attn_first, attn_second, factor, RATE_MATRIX)
    out_new = adam_step(out_weight, grads[1], out_first, out_second, factor, RATE_OUT)
    inner_new = adam_step(inner_weight, grads[2], inner_first, inner_second, factor, RATE_MATRIX)
    outer_new = adam_step(outer_weight, grads[3], outer_first, outer_second, factor, RATE_MATRIX)
    rel_new = adam_step(rel_bias, rel_grad, rel_first, rel_second, factor, RATE_SMALL)
    gain_new = adam_step(gains, gain_grad, gain_first, gain_second, factor, RATE_SMALL)
    return (block_out, input_grad, grad_norm, *attn_new, *out_new, *inner_new, *outer_new, *rel_new, *gain_new)


def solution(mesh):
    rows = P(("dp", "mp"), None)
    attn, up, down = P(None, "dp", "mp"), P("dp", "mp"), P("mp", "dp")
    in_specs = (
        rows, rows, attn, down, up, down, P(), P(), P("dp"), P(),
        attn, attn, down, down, up, up, down, down, P(), P(), P(), P(),
    )
    out_specs = (rows, rows, P()) + (attn,) * 3 + (down,) * 3 + (up,) * 3 + (down,) * 3 + (P(),) * 6
    plan = body if (mesh.shape["dp"], mesh.shape["mp"]) == (8, 4) else general_body
    return jax.shard_map(
        functools.partial(plan, parts=mesh.shape["mp"]),
        mesh=mesh, in_specs=in_specs, out_specs=out_specs, check_vma=False,
    )
```

```python
import functools

import jax
import jax.numpy as jnp
from jax import lax
from jax.experimental import pallas as pl
from jax.experimental.pallas import tpu as pltpu
from jax.sharding import PartitionSpec as P

HDIM = 64
SEQLEN = 1024
STEP = 10
NORM_EPS = 1e-06
CLIP = 1.0
BETA_ONE = 0.9
BETA_TWO = 0.999
ADAM_EPS = 1e-08
DECAY = 0.01
RATE_MATRIX = 0.05
RATE_OUT = 0.6
RATE_SMALL = 1.0

F32 = jnp.float32
BF16 = jnp.bfloat16
LANES = 128
NEG = -1e30
MESH = pl.DeviceIdType.MESH

HEAD_AT = ((0, 0, 1, 2, 0), (0, 1, 1, 2, 1), (4, 0, 5, 4, 1))


def mm(a, b):
    return lax.dot_general(a, b, (((1,), (0,)), ((), ())), preferred_element_type=F32)


def mt(a, b):
    return lax.dot_general(a, b, (((1,), (1,)), ((), ())), preferred_element_type=F32)


def rms_scaled(value, gain):
    return value * lax.rsqrt(jnp.mean(value * value, axis=-1, keepdims=True) + NORM_EPS) * gain


def rms_back(value, gain, grad):
    factor = lax.rsqrt(jnp.mean(value * value, axis=-1, keepdims=True) + NORM_EPS)
    unit = value * factor
    gain_part = jnp.sum(grad * unit, axis=0, keepdims=True)
    scaled = grad * gain
    result = factor * (scaled - unit * jnp.mean(scaled * unit, axis=-1, keepdims=True))
    return (result, gain_part)


def adam_step(master, grad, first, second, factor, rate):
    clipped = grad * factor
    first_new = BETA_ONE * first + (1.0 - BETA_ONE) * clipped
    second_new = BETA_TWO * second + (1.0 - BETA_TWO) * clipped * clipped
    first_hat = first_new / (1.0 - BETA_ONE**STEP)
    second_hat = second_new / (1.0 - BETA_TWO**STEP)
    master_new = master - rate * (first_hat / (jnp.sqrt(second_hat) + ADAM_EPS) + DECAY * master)
    return (master_new, first_new, second_new)


def half_rows(half):
    lane = lax.broadcasted_iota(jnp.int32, (1, LANES), 1)
    keep = (lane < HDIM) if half == 0 else (lane >= HDIM)
    return keep.astype(F32).astype(BF16)


def bias_tile(line):
    wide = jnp.broadcast_to(line, (LANES, 4 * LANES))
    return pltpu.roll(wide, 0, 1, stride=1, stride_axis=0)


def near_parts(tile):
    return tile[:, LANES : 2 * LANES], tile[:, :LANES], tile[:, 3 * LANES :]


def corner_parts(tile, line, flags):
    before, same, after = near_parts(tile)
    first = (after - line[:, 3 * LANES : 3 * LANES + 1]) * flags
    last = (before - line[:, LANES : LANES + 1]) * (1.0 - flags)
    return first, last


def add_bias(scores, tile, line, flags, nq):
    parts = near_parts(tile)
    corner = corner_parts(tile, line, flags)
    rows = []
    for jb in range(2 * nq):
        row = []
        for ib in range(nq):
            block = scores[jb * LANES : (jb + 1) * LANES, ib * LANES : (ib + 1) * LANES]
            if jb < nq and abs(jb - ib) <= 1:
                block = block + parts[jb - ib + 1]
            elif jb == nq and ib == nq - 1:
                block = block + corner[0]
            elif jb == 2 * nq - 1 and ib == 0:
                block = block + corner[1]
            row.append(block)
        rows.append(jnp.concatenate(row, axis=1))
    return rows


def far_masks(first, nq):
    lane = lax.broadcasted_iota(jnp.int32, (8, LANES), 1) % HDIM
    ib = lax.broadcasted_iota(jnp.int32, (8, LANES), 0)
    jb = (lane - 8) % (2 * nq)
    coded = (lane >= 8) & (lane < 8 + 4 * nq)
    own_before = (coded & (jb < nq) & (jb < ib - 1)).astype(F32)
    own_after = (coded & (jb < nq) & (jb > ib + 1)).astype(F32)
    other = (coded & (jb >= nq)).astype(F32)
    high = (lane < 8 + 2 * nq).astype(F32)
    return own_before + other * (1.0 - first), own_after + other * first, high, (lane == 3).astype(F32)


def query_aug(line, masks, nq):
    before, after, high, one = masks
    far = line[:, LANES : LANES + 1] * before + line[:, 3 * LANES : 3 * LANES + 1] * after
    top = far.astype(BF16).astype(F32)
    rows = (high * top + (1.0 - high) * (far - top) + one).astype(BF16)
    return jnp.concatenate([jnp.broadcast_to(rows[ib : ib + 1, :], (LANES, LANES)) for ib in range(nq)], axis=0)


def turned_hot(table, origin):
    size = 4 * LANES
    hot = (lax.broadcasted_iota(jnp.int32, (LANES, size), 0) == table).astype(F32).astype(BF16)
    at = lax.broadcasted_iota(jnp.int32, (size, size), 0) + lax.broadcasted_iota(jnp.int32, (size, size), 1)
    turn = ((at == origin) | (at == origin + size)).astype(F32).astype(BF16)
    return mm(hot, turn).astype(BF16)


def key_aug(half, length, tokens):
    row = lax.broadcasted_iota(jnp.int32, (2 * tokens, LANES), 0)
    lane = lax.broadcasted_iota(jnp.int32, (2 * tokens, LANES), 1) % HDIM
    position = jnp.where(row < tokens, half * tokens + row, row - half * tokens)
    blocks = 2 * tokens // LANES
    hot = (lane >= 8) & (lane < 8 + 2 * blocks) & ((lane - 8) % blocks == row // LANES)
    masked = (lane == 3) & (position >= length)
    return jnp.where(masked, NEG, hot.astype(F32)).astype(BF16)


def peer(index, stride):
    return index + stride - 2 * stride * ((index // stride) % 2)


class Links:
    def __init__(self):
        self.dp = lax.axis_index("dp")
        self.mp = lax.axis_index("mp")
        self.core = self.dp % 2
        self.chip = self.dp // 2
        self.dp_x, self.dp_y, self.dp_s = peer(self.dp, 2), peer(self.dp, 4), peer(self.dp, 1)
        self.dp_d = peer(self.dp_x, 4)
        self.at_x, self.at_y, self.at_s = (self.dp_x, self.mp), (self.dp_y, self.mp), (self.dp_s, self.mp)
        z1, z2 = peer(self.mp, 1), peer(self.mp, 2)
        self.half = self.mp % 2
        self.first = (1 - self.half).astype(F32)
        self.at_z = (None, (self.dp, z1), (self.dp, z2), (self.dp, peer(z1, 2)))

    def column(self, s):
        return (self.mp + s) % 2 + 2 * ((self.mp // 2 + s // 2) % 2)

    def meet(self, more=()):
        barrier = pltpu.get_barrier_semaphore()
        others = (self.at_x, self.at_y, self.at_s) + self.at_z[1:] + tuple(more)
        for other in others:
            pl.semaphore_signal(barrier, inc=1, device_id=other, device_id_type=MESH)
        pl.semaphore_wait(barrier, len(others))


def remote(src, dst, send, recv, to):
    return pltpu.make_async_remote_copy(
        src_ref=src, dst_ref=dst, send_sem=send, recv_sem=recv, device_id=to, device_id_type=MESH
    )


class Gather:
    def __init__(self, links, w, send, recv, zsend, zrecv):
        self.k, self.w, self.send, self.recv, self.zsend, self.zrecv = links, w, send, recv, zsend, zrecv
        self.rows = w.shape[2] // 8

    def block(self, unit, dp, lo=0, n=None):
        group, s = unit
        n = self.rows if n is None else n
        return self.w.at[group, s, pl.ds(pl.multiple_of(dp * self.rows + lo, 16), n), :]

    def copy(self, unit, kind, ref, to):
        at = unit[0] * 4 + unit[1]
        return remote(ref, ref, self.send.at[at, kind], self.recv.at[at, kind], to)

    def outgoing(self, unit, kind):
        k, half = self.k, self.rows // 2
        dp, lo, n, to = (
            (k.dp, 0, None, k.at_x),
            (k.dp, 0, None, k.at_y),
            (k.dp, 0, None, k.at_s),
            (k.dp_x, 0, half, k.at_y),
            (k.dp_x, 0, None, k.at_s),
            (k.dp_y, half, half, k.at_x),
            (k.dp_y, 0, None, k.at_s),
            (k.dp_d, 0, None, k.at_s),
        )[kind]
        return self.copy(unit, kind, self.block(unit, dp, lo, n), to)

    def arrived(self, unit, kind):
        k, half = self.k, self.rows // 2
        sib = k.dp_s
        dp, lo, n = {
            0: (k.dp_x, 0, None),
            1: (k.dp_y, 0, None),
            2: (sib, 0, None),
            3: (k.dp_d, 0, half),
            4: (peer(sib, 2), 0, None),
            5: (k.dp_d, half, half),
            6: (peer(sib, 4), 0, None),
            7: (peer(peer(sib, 2), 4), 0, None),
        }[kind]
        self.copy(unit, kind, self.block(unit, dp, lo, n), k.at_x).wait_recv()

    def z_copy(self, group, s):
        at = group * 3 + s - 1
        src = self.block((group, 0), self.k.dp)
        dst = self.block((group, s), self.k.dp)
        return remote(src, dst, self.zsend.at[at], self.zrecv.at[at], self.k.at_z[s])

    def z_arrived(self, unit):
        at = unit[0] * 3 + unit[1] - 1
        ref = self.block(unit, self.k.dp)
        remote(ref, ref, self.zsend.at[at], self.zrecv.at[at], self.k.at_x).wait_recv()

    def run(self, ops):
        for op in ops:
            (self.s1, self.s2, self.s3, self.s4)[op // 16 - 1](UNITS[op % 16])

    def at(self, loop, step, place):
        for number in range(4):
            ops = GATHER_PLAN.get((loop, number), {}).get(place)
            if ops:
                pl.when(step == number)(functools.partial(self.run, ops))

    def s1(self, unit):
        if unit[1] > 0:
            self.z_arrived(unit)
        for kind in (0, 1, 2):
            self.outgoing(unit, kind).start()

    def s2(self, unit):
        self.arrived(unit, 0)
        for kind in (3, 4):
            self.outgoing(unit, kind).start()
        self.arrived(unit, 1)
        for kind in (5, 6):
            self.outgoing(unit, kind).start()

    def s3(self, unit):
        self.arrived(unit, 3)
        self.arrived(unit, 5)
        self.outgoing(unit, 7).start()

    def s4(self, unit):
        for kind in (2, 4, 6, 7):
            self.arrived(unit, kind)

    def finish(self):
        def each(at, carry):
            for kind in range(8):
                self.outgoing((at // 4, at % 4), kind).wait_send()
            return carry

        lax.fori_loop(0, 12, each, 0)
        for group in range(3):
            for s in (1, 2, 3):
                self.z_copy(group, s).wait_send()


UNITS = ((0, 0), (0, 1), (0, 2), (1, 0), (2, 0), (0, 3), (1, 1), (2, 1), (1, 2), (2, 2), (1, 3), (2, 3))
GATHER_AHEAD = (0x11, 0x20, 0x12, 0x30, 0x21, 0x13, 0x40, 0x31, 0x22, 0x14, 0x41, 0x32, 0x23, 0x42)
GATHER_PLAN = {
    ("attend", 0): {0: (0x33,), 1: (0x24,), 2: (0x15, 0x43)},
    ("attend", 1): {0: (0x34,), 1: (0x16, 0x25), 2: (0x44,)},
    ("attend", 2): {0: (0x17, 0x35), 1: (0x26,), 2: (0x18,), 3: (0x45,)},
    ("attend", 3): {0: (0x36,), 1: (0x19, 0x27), 2: (0x46,), 3: (0x1a, 0x37)},
    ("feed", 0): {0: (0x28,), 1: (0x47,), 2: (0x1b, 0x38)},
    ("feed", 1): {0: (0x29,), 1: (0x48,), 2: (0x39,)},
    ("feed", 2): {0: (0x49, 0x2a), 1: (0x3a,), 2: (0x2b, 0x4a)},
    ("feed", 3): {0: (0x3b, 0x4b)},
}


def front_kernel(
    lengths_ref, attn_ref, wout_ref, inner_ref, outer_ref, table_ref, rel_ref, gain_ref, hidden_hbm, grad_hbm,
    own_hbm, oth_hbm, ctx_hbm, lse_ref, wa_hbm, x_hbm, xo_hbm, line_ref, out_ref, back_ref, gain_grad_ref, gi_hbm, go_hbm,
    w, x_ref, xo, own, oth, ctx, s_ref, e_ref, middle, grad, x2_ref, x2t_ref, ob_ref, obt_ref, acc_out, acc_two, gi, go, kaug_ref,
    send, recv, zsend, zrecv, xsem, lsem, osem, gsem,
):
    tokens = x_ref.shape[0]
    nq = tokens // LANES
    links = Links()
    net = Gather(links, w, send, recv, zsend, zrecv)
    get_hidden = pltpu.make_async_copy(hidden_hbm, middle, lsem.at[0])
    get_grad = pltpu.make_async_copy(grad_hbm, grad, lsem.at[1])
    get_hidden.start()
    def own_block(group):
        return (group, 0, pl.ds(pl.multiple_of(links.dp * net.rows, 16), net.rows), slice(None))

    parts = [attn_ref[n].astype(BF16) for n in range(3)] + [wout_ref[...].T.astype(BF16)]
    q, k, v, o = [(part[:, :LANES], part[:, LANES:]) for part in parts]
    w[own_block(0)] = jnp.concatenate([q[0], k[0], v[0], o[0], q[1], v[1], k[1], o[1]], axis=1)
    w[own_block(1)] = inner_ref[...].astype(BF16)
    w[own_block(2)] = outer_ref[...].astype(BF16)
    get_grad.start()
    links.meet()
    net.z_copy(0, 1).start()
    net.s1(UNITS[0])
    get_hidden.wait()
    x_ref[...] = rms_scaled(middle[...], gain_ref[0:1, :]).astype(BF16)
    xcopy = remote(x_ref, xo, xsem.at[0], xsem.at[1], links.at_z[1])
    net.z_copy(0, 2).start()
    xcopy.start()
    net.z_copy(0, 3).start()
    for step in (1, 2, 3):
        net.z_copy(1, step).start()
        net.z_copy(2, step).start()
    hot = turned_hot(table_ref[...], 2 * LANES - 1)[: rel_ref.shape[1]]
    high = rel_ref[...].astype(BF16)
    rest = rel_ref[...] - high.astype(F32)
    mid = rest.astype(BF16)
    low = (rest - mid.astype(F32)).astype(BF16)
    line_ref[...] = mm(high, hot) + (mm(mid, hot) + mm(low, hot))
    kaug_ref[...] = key_aug(links.half, lengths_ref[links.mp // 2], tokens)
    far = far_masks(links.first, nq)
    net.run(GATHER_AHEAD[:8])
    get_grad.wait()
    ob = grad[...].astype(BF16)
    ob_ref[...] = ob
    obt_ref[...] = ob.T
    net.run(GATHER_AHEAD[8:])
    xcopy.wait_recv()

    masks = [half_rows(0), half_rows(1)]
    count = lax.broadcasted_iota(jnp.int32, (HDIM, 2 * tokens), 0)
    ones = (count == 0).astype(F32).astype(BF16)

    def attend(s, carry):
        x, other = x_ref[...], xo[...]
        p_a = mm(x, w[0, s, :, : 3 * LANES]).astype(BF16)
        p_b = mm(x, w[0, s, :, 4 * LANES :]).astype(BF16)
        o_a = mm(other, w[0, s, :, LANES : 3 * LANES]).astype(BF16)
        o_b = mm(other, w[0, s, :, 4 * LANES :]).astype(BF16)
        own[s, :, : 3 * LANES] = p_a
        own[s, :, 3 * LANES :] = p_b
        oth[s, :, : 2 * LANES] = o_a
        oth[s, :, 2 * LANES :] = o_b
        cols_own = {0: p_a[:, :LANES], 1: p_a[:, LANES : 2 * LANES], 2: p_a[:, 2 * LANES :], 4: p_b[:, :LANES], 5: p_b[:, LANES:]}
        cols_oth = {1: o_a[:, :LANES], 2: o_a[:, LANES:], 4: o_b[:, :LANES], 5: o_b[:, LANES:]}
        both = {c: jnp.concatenate([cols_own[c], cols_oth[c]], axis=0) for c in (1, 2, 4, 5)}
        m = links.column(s)
        v_t = {2: both[2].T, 4: both[4].T}
        pieces = []
        stats = []
        for i, (qc, qh, kc, vc, vh) in enumerate(HEAD_AT):
            net.at("attend", s, i)
            line = line_ref[pl.ds(3 * m + i, 1), :]
            tile = bias_tile(line)
            qa = cols_own[qc] * masks[qh] + query_aug(line, far, nq) * masks[1 - qh]
            ka = both[kc] * masks[qh] + kaug_ref[...] * masks[1 - qh]
            scores = mt(ka, qa)
            peak = None
            for jb, row in enumerate(add_bias(scores, tile, line, links.first, nq)):
                s_ref[i % 2, jb * LANES : (jb + 1) * LANES, :] = row
                top = jnp.max(row.reshape(LANES // 8, 8, tokens), axis=0)
                peak = top if peak is None else jnp.maximum(peak, top)
            peak = jnp.max(peak, axis=0, keepdims=True)
            for jb in range(2 * nq):
                rows = slice(jb * LANES, (jb + 1) * LANES)
                e_ref[i % 2, rows, :] = jnp.exp(s_ref[i % 2, rows, :] - peak).astype(BF16)
            if vh == 0:
                va = jnp.concatenate([v_t[vc][:HDIM], ones], axis=0)
            else:
                va = jnp.concatenate([ones, v_t[vc][HDIM:]], axis=0)
            ot = mm(va, e_ref[i % 2])
            at = HDIM if vh == 0 else 0
            total = ot[at : at + 1, :]
            stats.append(peak + jnp.log(total))
            real = ot[:HDIM] if vh == 0 else ot[HDIM:]
            pieces.append(real / total)
        zero = jnp.zeros((HDIM, tokens), F32)
        ctx_a = jnp.concatenate([pieces[0], pieces[1]], axis=0).T.astype(BF16)
        ctx_b = jnp.concatenate([zero, pieces[2]], axis=0).T.astype(BF16)
        ctx[s, :, :LANES] = ctx_a
        ctx[s, :, LANES:] = ctx_b
        lse_ref[s] = jnp.concatenate(stats + [jnp.zeros((5, tokens), F32)], axis=0)
        middle[...] += mt(ctx_a, w[0, s, :, 3 * LANES : 4 * LANES]) + mt(ctx_b, w[0, s, :, 5 * LANES :])
        net.at("attend", s, 3)
        return carry

    lax.fori_loop(0, 4, attend, 0)
    saves = [
        pltpu.make_async_copy(a, b, osem.at[n])
        for n, (a, b) in enumerate(((own, own_hbm), (oth, oth_hbm), (ctx, ctx_hbm), (w.at[0], wa_hbm), (xo, xo_hbm), (x_ref, x_hbm)))
    ]
    for copy in saves:
        copy.start()

    x2 = rms_scaled(middle[...], gain_ref[1:2, :]).astype(BF16)
    x2_ref[...] = x2
    x2t_ref[...] = x2.T
    acc_out[...] = jnp.zeros_like(acc_out)
    acc_two[...] = jnp.zeros_like(acc_two)
    def g_copies(t):
        slot = t % 2
        return (
            pltpu.make_async_copy(gi.at[slot], gi_hbm.at[t], gsem.at[slot, 0]),
            pltpu.make_async_copy(go.at[slot], go_hbm.at[t], gsem.at[slot, 1]),
        )

    def feed(t, carry):
        slot = t % 2
        cols = w.shape[3]
        tile = 2 * LANES

        @pl.when(t >= 2)
        def _():
            for copy in g_copies(t - 2):
                copy.wait()

        for n in range(cols // tile):
            net.at("feed", t, n)
            at = slice(n * tile, (n + 1) * tile)
            wi = w[1, t, :, at]
            wo = w[2, t, :, at]
            inner = mm(x2_ref[...], wi)
            active_back = mm(ob_ref[...], wo)
            c = 0.7978845608028654
            sq = inner * inner
            th = jnp.tanh(c * (inner + 0.044715 * (sq * inner)))
            half = 0.5 * (1.0 + th)
            active = (inner * half).astype(BF16)
            slope = half + (0.5 * c) * inner * (1.0 - th * th) * (1.0 + (3 * 0.044715) * sq)
            inner_back = (slope * active_back).astype(BF16)
            acc_out[...] += mt(active, wo)
            acc_two[...] += mt(inner_back, wi)
            go[slot, :, at] = mm(obt_ref[...], active).astype(BF16)
            gi[slot, :, at] = mm(x2t_ref[...], inner_back).astype(BF16)
        for copy in g_copies(t):
            copy.start()

        return carry

    lax.fori_loop(0, 4, feed, 0)
    out_ref[...] = middle[...] + acc_out[...]
    result, gain_part = rms_back(middle[...], gain_ref[1:2, :], acc_two[...])
    back_ref[...] = grad[...] + result
    gain_grad_ref[...] = jnp.broadcast_to(gain_part, gain_grad_ref.shape)
    for t in (2, 3):
        for copy in g_copies(t):
            copy.wait()
    for copy in saves:
        copy.wait()
    xcopy.wait_send()
    net.finish()


class Scatter:
    def __init__(self, links, sources, sums, piece, diag, side, final, result, send, recv, psem):
        self.k, self.sources, self.sums, self.piece = links, sources, sums, piece
        self.diag, self.side, self.final, self.result = diag, side, final, result
        self.send, self.recv, self.psem = send, recv, psem
        self.rows = sums.shape[2]
        chip = links.chip
        self.chips = (chip, peer(chip, 1), peer(chip, 2), peer(peer(chip, 1), 2))

    def outgoing(self, u, kind):
        group, s = BACK_UNITS[u]
        k, half = self.k, self.rows // 2
        at, at_x, at_y, at_d = self.chips
        if kind == 0:
            src, dst, to = self.sources[group].at[s, :, 1 - k.core], self.sums.at[u], k.at_s
        elif kind == 1:
            src, dst, to = self.sums.at[u, at_d, pl.ds(0, half)], self.diag.at[u, 0], k.at_x
        elif kind == 2:
            src, dst, to = self.sums.at[u, at_d, pl.ds(half, half)], self.diag.at[u, 1], k.at_y
        elif kind == 3:
            src, dst, to = self.sums.at[u, at_x], self.side.at[u, 0], k.at_x
        elif kind == 4:
            src, dst, to = self.sums.at[u, at_y], self.side.at[u, 1], k.at_y
        else:
            src, dst, to = self.sums.at[u, at], self.final.at[group, s - 1], k.at_z[s]
        return remote(src, dst, self.send.at[u, kind], self.recv.at[u, kind], to)

    def local(self, u):
        group, s = BACK_UNITS[u]
        return pltpu.make_async_copy(self.sources[group].at[s, :, self.k.core], self.piece.at[u % 3], self.psem.at[u % 3])

    def s1(self, u):
        self.outgoing(u, 0).start()
        self.local(u).start()

    def s2(self, u):
        self.local(u).wait()
        self.outgoing(u, 0).wait_recv()
        far = self.chips[3]
        self.sums[u, far] = self.sums[u, far] + self.piece[u % 3, far]
        self.outgoing(u, 1).start()
        self.outgoing(u, 2).start()
        for chip in self.chips[:3]:
            self.sums[u, chip] = self.sums[u, chip] + self.piece[u % 3, chip]

    def s3(self, u):
        half = self.rows // 2
        self.outgoing(u, 1).wait_recv()
        self.outgoing(u, 2).wait_recv()
        for chip, lo, n in ((self.chips[2], 0, 0), (self.chips[1], half, 1)):
            self.sums[u, chip, lo : lo + half] = self.sums[u, chip, lo : lo + half] + self.diag[u, n]
        self.outgoing(u, 3).start()
        self.outgoing(u, 4).start()

    def s4(self, u):
        group, s = BACK_UNITS[u]
        self.outgoing(u, 3).wait_recv()
        self.outgoing(u, 4).wait_recv()
        at = self.chips[0]
        total = self.sums[u, at].astype(F32) + (self.side[u, 0].astype(F32) + self.side[u, 1].astype(F32))
        if s == 0:
            self.result[group] = total
        else:
            self.sums[u, at] = total.astype(BF16)
            self.outgoing(u, 5).start()

    def last(self, group):
        total = self.result[group]
        for u, (other, s) in enumerate(BACK_UNITS):
            if other == group and s > 0:
                self.outgoing(u, 5).wait_recv()
        for n in range(3):
            total = total + self.final[group, n].astype(F32)
        self.result[group] = total

    def run(self, ops):
        for op in ops:
            (self.s1, self.s2, self.s3, self.s4)[op // 16 - 1](op % 16)

    def at(self, loop, step, place):
        for number in range(4):
            ops = SCATTER_PLAN.get((loop, number), {}).get(place)
            if ops:
                pl.when(step == number)(functools.partial(self.run, ops))

    def finish(self):
        for u, (group, s) in enumerate(BACK_UNITS):
            for kind in range(5 if s == 0 else 6):
                self.outgoing(u, kind).wait_send()


BACK_UNITS = ((1, 3), (2, 3), (1, 2), (2, 2), (1, 1), (2, 1), (1, 0), (2, 0), (0, 3), (0, 2), (0, 1), (0, 0))
SCATTER_AHEAD = ((0x10, 0x11, 0x12), (0x20,), (0x21,))
SCATTER_PLAN = {
    ("other", 0): {0: (0x30, 0x22, 0x13), 2: (0x31, 0x23, 0x14, 0x40)},
    ("other", 1): {1: (0x32, 0x24, 0x15, 0x41)},
    ("other", 2): {1: (0x33, 0x25, 0x16, 0x42)},
    ("other", 3): {0: (0x34, 0x26, 0x17, 0x43)},
    ("own", 0): {0: (0x35, 0x27, 0x44), 2: (0x36, 0x45), 3: (0x18,)},
    ("own", 1): {0: (0x37, 0x46), 1: (0x28,), 2: (0x47,), 3: (0x38, 0x19)},
    ("own", 2): {1: (0x29,), 2: (0x48,), 3: (0x39, 0x1a)},
    ("own", 3): {1: (0x2a,), 2: (0x49,), 3: (0x3a, 0x1b)},
}
SCATTER_AFTER = ((0x2b,), (0x4a, 0x3b), (0x4b,))


def back_kernel(
    lengths_ref, x_ref, line_ref, table_ref, lse_ref, gain_ref, gain_two_ref,
    xo_hbm, back_hbm, hidden_hbm, wa_hbm, own_hbm, oth_hbm, ctx_hbm, gi_hbm, go_hbm,
    grad_ref, small_ref, result_ref,
    xo, back, hidden, wa, own, oth, ctx, xt, xot, ab_ref, abt, acc_own, acc_oth, oth_out, oth_in,
    dq_acc, d_oth, cb_ref, center_ref, near_ref, ga, sums, piece, diag, side, final,
    kaug_ref, line_grad, far_grad, small, small_near, small_z,
    lsem, ssem, osem, send, recv, psem, tsend, trecv,
):
    tokens = x_ref.shape[0]
    nq = tokens // LANES
    links = Links()
    group = []
    for n in range(1, 8):
        dp = links.dp
        for stride in (1, 2, 4):
            if n & stride:
                dp = peer(dp, stride)
        group.append((dp, links.mp))
    net = Scatter(links, (ga, gi_hbm, go_hbm), sums, piece, diag, side, final, result_ref, send, recv, psem)
    loads = [
        pltpu.make_async_copy(a, b, lsem.at[n])
        for n, (a, b) in enumerate(((back_hbm, back), (xo_hbm, xo), (hidden_hbm, hidden)))
    ]

    def step_loads(s):
        return [
            pltpu.make_async_copy(a.at[s], b.at[s], ssem.at[s, n])
            for n, (a, b) in enumerate(((wa_hbm, wa), (own_hbm, own), (oth_hbm, oth), (ctx_hbm, ctx)))
        ]

    loads[0].start()
    for copy in step_loads(3):
        copy.start()
    loads[1].start()
    for s in (2, 1, 0):
        for copy in step_loads(s):
            copy.start()
    loads[2].start()
    links.meet([group[n] for n in (2, 4, 5, 6)])
    net.run(SCATTER_AHEAD[0])
    loads[0].wait()
    ab = back[...].astype(BF16)
    ab_ref[...] = ab
    abt[...] = ab.T
    net.run(SCATTER_AHEAD[1])
    xt[...] = x_ref[...].T
    acc_own[...] = jnp.zeros_like(acc_own)
    acc_oth[...] = jnp.zeros_like(acc_oth)
    loads[1].wait()
    xot[...] = xo[...].T
    net.run(SCATTER_AHEAD[2])
    kaug_ref[...] = key_aug(links.half, lengths_ref[links.mp // 2], tokens)
    far = far_masks(links.first, nq)
    line_grad[...] = jnp.zeros_like(line_grad)
    far_grad[...] = jnp.zeros_like(far_grad)
    jb = lax.broadcasted_iota(jnp.int32, (2 * nq, tokens), 0)
    ib = lax.broadcasted_iota(jnp.int32, (2 * nq, tokens), 1) // LANES
    edge_first = ((jb == nq) & (ib == nq - 1)).astype(F32)
    edge_last = ((jb == 2 * nq - 1) & (ib == 0)).astype(F32)
    other_key = (jb >= nq).astype(F32)
    sum_before = ((jb < nq) & (jb < ib - 1)).astype(F32) + (other_key - edge_last) * (1.0 - links.first)
    sum_after = ((jb < nq) & (jb > ib + 1)).astype(F32) + (other_key - edge_first) * links.first
    masks = [half_rows(0), half_rows(1)]
    own_at = {c: slice(at * LANES, (at + 1) * LANES) for at, c in enumerate((0, 1, 2, 4, 5))}
    oth_at = {c: slice(at * LANES, (at + 1) * LANES) for at, c in enumerate((1, 2, 4, 5))}
    cb_at = {2: slice(0, LANES), 4: slice(LANES, 2 * LANES)}
    at_row = lax.broadcasted_iota(jnp.int32, (LANES, LANES), 0) + lax.broadcasted_iota(jnp.int32, (LANES, LANES), 1)
    mirror = (at_row == LANES - 1).astype(F32).astype(BF16)

    def one_side(s, i, other):
        qc, qh, kc, vc, vh = HEAD_AT[i]
        line = line_ref[pl.ds(3 * links.column(s) + i, 1), :]
        tile = bias_tile(line)
        qm = own[s, :, own_at[qc]] * masks[qh]
        qa = qm + query_aug(line, far, nq) * masks[1 - qh]
        om = cb_ref[s, :, cb_at[vc]] * masks[vh]
        center = center_ref[s, i : i + 1, :]
        lse = lse_ref[s, i : i + 1, :]
        parts = near_parts(tile)
        corner = corner_parts(tile, line, links.first)
        side = 1 if other else 0
        k_cols = oth[s, :, oth_at[kc]] if other else own[s, :, own_at[kc]]
        v_cols = oth[s, :, oth_at[vc]] if other else own[s, :, own_at[vc]]
        ka = k_cols * masks[qh] + kaug_ref[side * tokens : (side + 1) * tokens] * masks[1 - qh]
        scores = mt(ka, qa)
        chance_back = mt(v_cols, om)
        near = [None] * 5
        ps, ds = [], []
        for jb in range(nq):
            row_p, row_d = [], []
            for ib in range(nq):
                at = (slice(jb * LANES, (jb + 1) * LANES), slice(ib * LANES, (ib + 1) * LANES))
                block = scores[at]
                kind = None
                if not other and abs(jb - ib) <= 1:
                    kind = jb - ib + 1
                    block = block + parts[kind]
                elif other and jb == 0 and ib == nq - 1:
                    kind = 3
                    block = block + corner[0]
                elif other and jb == nq - 1 and ib == 0:
                    kind = 4
                    block = block + corner[1]
                p = jnp.exp(block - lse[:, at[1]])
                d = p * (chance_back[at] - center[:, at[1]])
                if kind is not None:
                    near[kind] = d if near[kind] is None else near[kind] + d
                row_p.append(p.astype(BF16))
                row_d.append(d.astype(BF16))
            ps.append(jnp.concatenate(row_p, axis=1))
            ds.append(jnp.concatenate(row_d, axis=1))
        pb = jnp.concatenate(ps, axis=0)
        db = jnp.concatenate(ds, axis=0)
        return mm(ka.T, db), mm(db, qm), mm(pb, om), near

    def other_side(it, carry):
        s = 3 - it
        for copy in step_loads(s):
            copy.wait()
        cb = {
            2: mm(ab_ref[...], wa[s, :, 3 * LANES : 4 * LANES]).astype(BF16),
            4: mm(ab_ref[...], wa[s, :, 5 * LANES :]).astype(BF16),
        }
        centers = []
        for i in range(3):
            vc, vh = HEAD_AT[i][3:]
            prod = cb[vc].astype(F32) * ctx[s, :, cb_at[vc]].astype(F32)
            high = prod.astype(BF16)
            low = (prod - high.astype(F32)).astype(BF16)
            pick = jnp.broadcast_to(masks[vh], (8, LANES))
            centers.append((mt(pick, high) + mt(pick, low))[0:1, :])
        for c in cb:
            cb_ref[s, :, cb_at[c]] = cb[c]
        center_ref[s] = jnp.concatenate(centers + [jnp.zeros((5, tokens), F32)], axis=0)
        dk, dv = {}, {}
        for i, (qc, qh, kc, vc, vh) in enumerate(HEAD_AT):
            net.at("other", it, i)
            dq_acc[s, i], part_k, part_v, near = one_side(s, i, True)
            dk[kc] = dk[kc] + part_k if kc in dk else part_k
            dv[vc] = dv[vc] + part_v if vc in dv else part_v
            near_ref[s, i, 0] = near[3]
            near_ref[s, i, 1] = near[4]
        d = jnp.concatenate([dk[1], dv[2], dv[4], dk[5]], axis=1).astype(BF16)
        d_oth[s] = d
        acc_oth[...] += mt(d[:, : 2 * LANES], wa[s, :, LANES : 3 * LANES]) + mt(d[:, 2 * LANES :], wa[s, :, 4 * LANES :])
        return carry

    lax.fori_loop(0, 4, other_side, 0)
    oth_out[...] = acc_oth[...].astype(BF16)
    swap = remote(oth_out, oth_in, osem.at[0], osem.at[1], links.at_z[1])
    swap.start()

    def own_side(it, carry):
        s = 3 - it
        m = links.column(s)
        dk, dv, dq = {}, {}, []
        for i, (qc, qh, kc, vc, vh) in enumerate(HEAD_AT):
            net.at("own", it, i)
            part_q, part_k, part_v, near = one_side(s, i, False)
            part_q = part_q + dq_acc[s, i]
            dk[kc] = dk[kc] + part_k if kc in dk else part_k
            dv[vc] = dv[vc] + part_v if vc in dv else part_v
            at = HDIM if qh == 0 else 0
            block_sums = part_q[at + 8 : at + 8 + 2 * nq, :]
            head = pl.ds(3 * m + i, 1)
            far_grad[0, head, :] = jnp.sum(block_sums * sum_before, axis=0, keepdims=True)
            far_grad[1, head, :] = jnp.sum(block_sums * sum_after, axis=0, keepdims=True)
            dq.append(part_q[:HDIM] if qh == 0 else part_q[HDIM:])
            first, final_corner = near_ref[s, i, 0] * links.first, near_ref[s, i, 1] * (1.0 - links.first)
            blank = jnp.zeros((LANES, LANES), F32)
            tile = jnp.concatenate([near[1], near[0] + final_corner, blank, near[2] + first], axis=1)
            high = tile.astype(BF16)
            low = (tile - high.astype(F32)).astype(BF16)
            turned = pltpu.roll(mm(mirror, high) + mm(mirror, low), 0, 1, stride=1, stride_axis=0)
            line_grad[head, :] = jnp.sum(turned, axis=0, keepdims=True)
        dq_a = jnp.concatenate([dq[0], dq[1]], axis=0).T
        dq_b = jnp.concatenate([dq[2], jnp.zeros_like(dq[2])], axis=0).T
        d_own = jnp.concatenate([dq_a, dk[1], dv[2], dq_b + dv[4], dk[5]], axis=1).astype(BF16)
        g_own = mm(xt[...], d_own)
        g_oth = mm(xot[...], d_oth[s])
        g_ctx = mm(abt[...], ctx[s])
        columns = [
            g_own[:, :LANES],
            g_own[:, LANES : 3 * LANES] + g_oth[:, : 2 * LANES],
            g_ctx[:, :LANES],
            g_own[:, 3 * LANES : 4 * LANES] + g_oth[:, 2 * LANES : 3 * LANES],
            g_own[:, 4 * LANES :] + g_oth[:, 3 * LANES :] + g_ctx[:, LANES:],
        ]
        g = jnp.concatenate(columns, axis=1).astype(BF16)
        rows = ga.shape[3]
        for n in range(8):
            ga[s, n // 2, n % 2] = g[n * rows : (n + 1) * rows, :]
        net.at("own", it, 3)
        acc_own[...] += mt(d_own[:, : 3 * LANES], wa[s, :, : 3 * LANES]) + mt(d_own[:, 3 * LANES :], wa[s, :, 4 * LANES :])
        return carry

    lax.fori_loop(0, 4, own_side, 0)
    net.run(SCATTER_AFTER[0])
    loads[2].wait()
    swap.wait_recv()
    one_back = acc_own[...] + oth_in[...].astype(F32)
    grad, gain_part = rms_back(hidden[...], gain_ref[0:1, :], one_back)
    grad_ref[...] = grad + back[...]
    net.run(SCATTER_AFTER[1])
    lane = lax.broadcasted_iota(jnp.int32, (16, 4 * LANES), 1)
    by_line = (
        line_grad[...]
        + jnp.sum(far_grad[0], axis=1, keepdims=True) * (lane == 2 * LANES - 1).astype(F32)
        + jnp.sum(far_grad[1], axis=1, keepdims=True) * (lane == 4 * LANES - 1).astype(F32)
    )
    high = by_line.astype(BF16)
    low = (by_line - high.astype(F32)).astype(BF16)
    hot = turned_hot(table_ref[...], 3 * LANES - 2)
    small[0:16, :] = mt(high, hot) + mt(low, hot)
    for n in range(6):
        at = slice(n * LANES, (n + 1) * LANES)
        small[16 + n : 17 + n, :] = gain_part[:, at]
        small[22 + n : 23 + n, :] = gain_two_ref[0:1, at]
    net.run(SCATTER_AFTER[2])
    squares = jnp.zeros((8, LANES), F32)
    for weight in (1, 2, 0):
        net.last(weight)
        value = result_ref[weight]
        value = value * value
        for n in range(value.shape[1] // LANES):
            piece_sum = value[:, n * LANES : (n + 1) * LANES]
            squares = squares + jnp.sum(piece_sum.reshape(-1, 8, LANES), axis=0)
    small[28:32, :] = squares[0:4] + squares[4:8]
    near = [remote(small, small_near.at[n], tsend.at[n], trecv.at[n], to) for n, to in enumerate(group)]
    for copy in near:
        copy.start()
    for copy in near:
        copy.wait_recv()
    total = small[...]
    for n in range(7):
        total = total + small_near[n]
    small_z[0] = total
    along = [remote(small_z.at[0], small_z.at[n], tsend.at[6 + n], trecv.at[6 + n], links.at_z[n]) for n in (1, 2, 3)]
    for copy in along:
        copy.start()
    for copy in along:
        copy.wait_recv()
    small_ref[...] = (small_z[0] + small_z[1]) + (small_z[2] + small_z[3])
    for copy in near + along:
        copy.wait_send()
    swap.wait_send()
    net.finish()


def update_kernel(small_ref, grad_hbm, block_hbm, input_hbm, *refs):
    hbm, (block_out, input_out, norm_ref), new = refs[:18], refs[18:21], refs[21:39]
    held, grad_ref, pass_ref, sem = refs[39:57], refs[57], refs[58], refs[59]
    through = ((block_hbm, block_out), (input_hbm, input_out))
    fetch = [pltpu.make_async_copy(a, pass_ref.at[n], sem.at[n]) for n, (a, b) in enumerate(through)]
    store = [pltpu.make_async_copy(pass_ref.at[n], b, sem.at[21 + n]) for n, (a, b) in enumerate(through)]
    loads = [pltpu.make_async_copy(a, b, sem.at[2 + n]) for n, (a, b) in enumerate(zip(hbm, held))]
    loads.append(pltpu.make_async_copy(grad_hbm, grad_ref, sem.at[20]))
    for copy in loads[::-1] + fetch:
        copy.start()
    attn, out, inner, outer, rel, gain, attn_first, attn_second, out_first, out_second = held[:10]
    inner_first, inner_second, outer_first, outer_second, rel_first, rel_second, gain_first, gain_second = held[10:]
    small = small_ref[0:28, :]
    squares = jnp.sum(small * small, axis=0, keepdims=True) + jnp.sum(small_ref[28:32, :], axis=0, keepdims=True)
    norm = jnp.sqrt(jnp.sum(squares, axis=1, keepdims=True))
    norm_ref[...] = norm
    factor = jnp.minimum(1.0, CLIP / (norm + 1e-06))
    for copy in loads:
        copy.wait()
    for a, b in zip(fetch, store):
        a.wait()
        b.start()

    def step(at, grad, rate, master, first, second, outs):
        for ref, value in zip(outs, adam_step(master[at], grad, first[at], second[at], factor, rate)):
            ref[at] = value

    def turned(column):
        return pltpu.roll(column, HDIM, 1)[:, :HDIM]

    g = [grad_ref[0, :, n * LANES : (n + 1) * LANES] for n in range(6)]
    tails = (g[4][:, :HDIM], g[5][:, :HDIM], turned(g[4]))
    for n in range(3):
        step((n, slice(None), slice(0, LANES)), g[n], RATE_MATRIX, attn, attn_first, attn_second, new[0:3])
        step((n, slice(None), slice(LANES, LANES + HDIM)), tails[n], RATE_MATRIX, attn, attn_first, attn_second, new[0:3])
    rows = g[3].shape[0]
    blank = jnp.zeros((LANES - rows, LANES), F32)
    lower = pltpu.roll(g[5], HDIM, 1)
    whole = slice(None)
    step((slice(0, LANES), whole), jnp.concatenate([g[3], blank], axis=0).T[:, :rows], RATE_OUT, out, out_first, out_second, new[3:6])
    step(
        (slice(LANES, LANES + HDIM), whole),
        jnp.concatenate([lower, blank], axis=0).T[:HDIM, :rows],
        RATE_OUT, out, out_first, out_second, new[3:6],
    )
    step(whole, grad_ref[1], RATE_MATRIX, inner, inner_first, inner_second, new[6:9])
    step(whole, grad_ref[2], RATE_MATRIX, outer, outer_first, outer_second, new[9:12])
    heads, buckets = rel.shape
    step(whole, small_ref[0:heads, 0:buckets], RATE_SMALL, rel, rel_first, rel_second, new[12:15])
    gain_grad = jnp.concatenate(
        [
            jnp.concatenate([small_ref[at + n : at + n + 1, :] for n in range(6)], axis=1)
            for at in (16, 22)
        ],
        axis=0,
    )
    step(whole, gain_grad, RATE_SMALL, gain, gain_first, gain_second, new[15:18])
    for copy in store:
        copy.wait()


def run_front(lengths, attn, out, inner, outer, table, rel, gains, hidden, grad):
    t, d = hidden.shape
    parts, cols = rel.shape[0] // 3, inner.shape[1]
    any_space = pl.BlockSpec(memory_space=pl.ANY)
    vmem = pl.BlockSpec(memory_space=pltpu.VMEM)
    dma = pltpu.SemaphoreType.DMA
    return pl.pallas_call(
        front_kernel,
        in_specs=[pl.BlockSpec(memory_space=pltpu.SMEM)] + [vmem] * 7 + [any_space] * 2,
        out_specs=[any_space] * 3 + [vmem] + [any_space] * 3 + [vmem] * 4 + [any_space] * 2,
        out_shape=[
            jax.ShapeDtypeStruct((parts, t, 5 * LANES), BF16),
            jax.ShapeDtypeStruct((parts, t, 4 * LANES), BF16),
            jax.ShapeDtypeStruct((parts, t, 2 * LANES), BF16),
            jax.ShapeDtypeStruct((parts, 8, t), F32),
            jax.ShapeDtypeStruct((parts, d, cols), BF16),
            jax.ShapeDtypeStruct((t, d), BF16),
            jax.ShapeDtypeStruct((t, d), BF16),
            jax.ShapeDtypeStruct((rel.shape[0], 4 * LANES), F32),
            jax.ShapeDtypeStruct((t, d), F32),
            jax.ShapeDtypeStruct((t, d), F32),
            jax.ShapeDtypeStruct((8, d), F32),
            jax.ShapeDtypeStruct((parts, d, cols), BF16),
            jax.ShapeDtypeStruct((parts, d, cols), BF16),
        ],
        scratch_shapes=[
            pltpu.VMEM((3, parts, d, cols), BF16),
            pltpu.VMEM((t, d), BF16),
            pltpu.VMEM((t, d), BF16),
            pltpu.VMEM((parts, t, 5 * LANES), BF16),
            pltpu.VMEM((parts, t, 4 * LANES), BF16),
            pltpu.VMEM((parts, t, 2 * LANES), BF16),
            pltpu.VMEM((2, 2 * t, t), F32),
            pltpu.VMEM((2, 2 * t, t), BF16),
            pltpu.VMEM((t, d), F32),
            pltpu.VMEM((t, d), F32),
            pltpu.VMEM((t, d), BF16), pltpu.VMEM((d, t), BF16),
            pltpu.VMEM((t, d), BF16), pltpu.VMEM((d, t), BF16),
            pltpu.VMEM((t, d), F32), pltpu.VMEM((t, d), F32),
            pltpu.VMEM((2, d, cols), BF16), pltpu.VMEM((2, d, cols), BF16),
            pltpu.VMEM((2 * t, LANES), BF16),
            dma((12, 8)), dma((12, 8)), dma((9,)), dma((9,)), dma((2,)), dma((2,)), dma((6,)), dma((2, 2)),
        ],
        compiler_params=pltpu.CompilerParams(
            vmem_limit_bytes=62 * 2**20, collective_id=0, has_side_effects=True
        ),
        name="front",
    )(lengths, attn, out, inner, outer, table, rel, gains, hidden, grad)


def run_back(lengths, x, line, table, lse, gains, gain_two, xo, back, hidden, wa, own, oth, ctx, gi, go):
    t, d = x.shape
    parts, cols = wa.shape[0], wa.shape[2]
    rows = d // 8
    any_space = pl.BlockSpec(memory_space=pl.ANY)
    vmem = pl.BlockSpec(memory_space=pltpu.VMEM)
    dma = pltpu.SemaphoreType.DMA
    split = (parts, 4, 2, rows, cols)
    return pl.pallas_call(
        back_kernel,
        in_specs=[pl.BlockSpec(memory_space=pltpu.SMEM)] + [vmem] * 6 + [any_space] * 9,
        out_specs=[vmem] * 3,
        out_shape=[
            jax.ShapeDtypeStruct((t, d), F32),
            jax.ShapeDtypeStruct((32, LANES), F32),
            jax.ShapeDtypeStruct((3, rows, cols), F32),
        ],
        scratch_shapes=[
            pltpu.VMEM((t, d), BF16), pltpu.VMEM((t, d), F32), pltpu.VMEM((t, d), F32),
            pltpu.VMEM(wa.shape, BF16), pltpu.VMEM(own.shape, BF16), pltpu.VMEM(oth.shape, BF16), pltpu.VMEM(ctx.shape, BF16),
            pltpu.VMEM((d, t), BF16), pltpu.VMEM((d, t), BF16), pltpu.VMEM((t, d), BF16), pltpu.VMEM((d, t), BF16),
            pltpu.VMEM((t, d), F32), pltpu.VMEM((t, d), F32), pltpu.VMEM((t, d), BF16), pltpu.VMEM((t, d), BF16),
            pltpu.VMEM((parts, 3, LANES, t), F32), pltpu.VMEM((parts, t, 4 * LANES), BF16),
            pltpu.VMEM((parts, t, 2 * LANES), BF16), pltpu.VMEM((parts, 8, t), F32), pltpu.VMEM((parts, 3, 2, LANES, LANES), F32),
            pltpu.VMEM(split, BF16), pltpu.VMEM((12, 4, rows, cols), BF16), pltpu.VMEM((3, 4, rows, cols), BF16),
            pltpu.VMEM((12, 2, rows // 2, cols), BF16), pltpu.VMEM((12, 2, rows, cols), BF16), pltpu.VMEM((3, 3, rows, cols), BF16),
            pltpu.VMEM((2 * t, LANES), BF16), pltpu.VMEM((16, 4 * LANES), F32), pltpu.VMEM((2, 16, 4 * LANES), F32),
            pltpu.VMEM((32, LANES), F32), pltpu.VMEM((7, 32, LANES), F32), pltpu.VMEM((4, 32, LANES), F32),
            dma((3,)), dma((parts, 4)), dma((2,)), dma((12, 6)), dma((12, 6)), dma((3,)), dma((10,)), dma((10,)),
        ],
        compiler_params=pltpu.CompilerParams(
            vmem_limit_bytes=62 * 2**20, collective_id=1, has_side_effects=True
        ),
        name="back",
    )(lengths, x, line, table, lse, gains, gain_two, xo, back, hidden, wa, own, oth, ctx, gi.reshape(split), go.reshape(split))


def run_update(small, grads, block_out, input_grad, masters, moments):
    vmem = pl.BlockSpec(memory_space=pltpu.VMEM)
    hbm = pl.BlockSpec(memory_space=pltpu.HBM)
    like = lambda a: jax.ShapeDtypeStruct(a.shape, F32)
    return pl.pallas_call(
        update_kernel,
        in_specs=[vmem] + [hbm] * 21,
        out_specs=[hbm] * 2 + [vmem] * 19,
        out_shape=[like(block_out), like(input_grad), jax.ShapeDtypeStruct((1, 1), F32)]
        + [like(a) for a in masters for _ in range(3)],
        scratch_shapes=[pltpu.VMEM(a.shape, F32) for a in (*masters, *moments, grads)]
        + [pltpu.VMEM((2, *block_out.shape), F32), pltpu.SemaphoreType.DMA((23,))],
        compiler_params=pltpu.CompilerParams(vmem_limit_bytes=62 * 2**20),
        name="update",
    )(small, grads, block_out, input_grad, *masters, *moments)


def body(
    hidden_in, out_grad, attn_weight, out_weight, inner_weight, outer_weight, rel_bias, gains, lengths, table,
    attn_first, attn_second, out_first, out_second, inner_first, inner_second, outer_first, outer_second,
    rel_first, rel_second, gain_first, gain_second, *, parts,
):
    near_table = table[SEQLEN - 2 * LANES : SEQLEN + 2 * LANES].reshape(1, 4 * LANES)
    own, oth, ctx, lse, wa, x1, x1o, line, block_out, middle_back, gain_two, gi, go = run_front(
        lengths, attn_weight, out_weight, inner_weight, outer_weight.T, near_table, rel_bias.T, gains, hidden_in, out_grad
    )
    input_grad, small, owned = run_back(
        lengths, x1, line, near_table, lse, gains, gain_two, x1o, middle_back, hidden_in, wa, own, oth, ctx, gi, go
    )
    new = run_update(
        small, owned, block_out, input_grad,
        (attn_weight, out_weight, inner_weight, outer_weight.T, rel_bias.T, gains),
        (
            attn_first, attn_second, out_first, out_second, inner_first, inner_second,
            outer_first.T, outer_second.T, rel_first.T, rel_second.T, gain_first, gain_second,
        ),
    )
    masters = new[3:]
    return (
        new[0], new[1], new[2].reshape(()), *masters[:9], *(a.T for a in masters[9:12]), *(a.T for a in masters[12:15]), *masters[15:],
    )


def plain_corner_parts(tile, line, flags):
    before, same, after = near_parts(tile)
    first = (after - line[:, 3 * LANES : 3 * LANES + 1]) * flags[0]
    last = (before - line[:, LANES : LANES + 1]) * flags[1]
    return first, last


def plain_add_bias(scores, tile, line, flags, nq):
    parts = near_parts(tile)
    corner = plain_corner_parts(tile, line, flags)
    rows = []
    for jb in range(2 * nq):
        row = []
        for ib in range(nq):
            block = scores[jb * LANES : (jb + 1) * LANES, ib * LANES : (ib + 1) * LANES]
            if jb < nq and abs(jb - ib) <= 1:
                block = block + parts[jb - ib + 1]
            elif jb == nq and ib == nq - 1:
                block = block + corner[0]
            elif jb == 2 * nq - 1 and ib == 0:
                block = block + corner[1]
            row.append(block)
        rows.append(jnp.concatenate(row, axis=1))
    return rows


def plain_query_aug(qaug, i, nq):
    rows = qaug.shape[0]
    return jnp.concatenate(
        [jnp.broadcast_to(qaug[i * nq + ib : i * nq + ib + 1, :], (LANES, LANES)) for ib in range(nq)], axis=0
    )


def forward_kernel(
    x_ref, xo_ref, w_ref, line_ref, qaug_ref, kaug_ref, hidden_ref,
    own_ref, oth_ref, ctx_ref, lse_ref, middle_ref,
    acc, s_ref, e_ref,
):
    m = pl.program_id(0)
    tokens = x_ref.shape[0]
    nq = tokens // LANES
    x, xo = x_ref[...], xo_ref[...]
    p_a = mm(x, w_ref[:, : 3 * LANES]).astype(BF16)
    p_b = mm(x, w_ref[:, 4 * LANES :]).astype(BF16)
    o_a = mm(xo, w_ref[:, LANES : 3 * LANES]).astype(BF16)
    o_b = mm(xo, w_ref[:, 4 * LANES :]).astype(BF16)
    own_ref[0, :, : 3 * LANES] = p_a
    own_ref[0, :, 3 * LANES :] = p_b
    oth_ref[0, :, : 2 * LANES] = o_a
    oth_ref[0, :, 2 * LANES :] = o_b
    cols_own = {0: p_a[:, :LANES], 1: p_a[:, LANES : 2 * LANES], 2: p_a[:, 2 * LANES :], 4: p_b[:, :LANES], 5: p_b[:, LANES:]}
    cols_oth = {1: o_a[:, :LANES], 2: o_a[:, LANES:], 4: o_b[:, :LANES], 5: o_b[:, LANES:]}
    both = {c: jnp.concatenate([cols_own[c], cols_oth[c]], axis=0) for c in (1, 2, 4, 5)}
    masks = [half_rows(0), half_rows(1)]
    flags = (line_ref[0, 3:4, :LANES], line_ref[0, 4:5, :LANES])
    v_t = {2: both[2].T, 4: both[4].T}
    count = lax.broadcasted_iota(jnp.int32, (HDIM, 2 * tokens), 0)
    ones = (count == 0).astype(F32).astype(BF16)
    pieces = []
    stats = []
    for i, (qc, qh, kc, vc, vh) in enumerate(HEAD_AT):
        line = line_ref[0, i : i + 1, :]
        tile = bias_tile(line)
        qa = cols_own[qc] * masks[qh] + plain_query_aug(qaug_ref[0], i, nq) * masks[1 - qh]
        ka = both[kc] * masks[qh] + kaug_ref[...] * masks[1 - qh]
        scores = mt(ka, qa)
        peak = None
        for jb, row in enumerate(plain_add_bias(scores, tile, line, flags, nq)):
            s_ref[i, jb * LANES : (jb + 1) * LANES, :] = row
            top = jnp.max(row.reshape(LANES // 8, 8, tokens), axis=0)
            peak = top if peak is None else jnp.maximum(peak, top)
        peak = jnp.max(peak, axis=0, keepdims=True)
        for jb in range(2 * nq):
            rows = slice(jb * LANES, (jb + 1) * LANES)
            e_ref[i, rows, :] = jnp.exp(s_ref[i, rows, :] - peak).astype(BF16)
        if vh == 0:
            va = jnp.concatenate([v_t[vc][:HDIM], ones], axis=0)
        else:
            va = jnp.concatenate([ones, v_t[vc][HDIM:]], axis=0)
        ot = mm(va, e_ref[i])
        at = HDIM if vh == 0 else 0
        total = ot[at : at + 1, :]
        stats.append(peak + jnp.log(total))
        real = ot[:HDIM] if vh == 0 else ot[HDIM:]
        pieces.append(real / total)
    zero = jnp.zeros((HDIM, tokens), F32)
    ctx_a = jnp.concatenate([pieces[0], pieces[1]], axis=0).T.astype(BF16)
    ctx_b = jnp.concatenate([zero, pieces[2]], axis=0).T.astype(BF16)
    ctx_ref[0, :, :LANES] = ctx_a
    ctx_ref[0, :, LANES:] = ctx_b
    for i in range(3):
        lse_ref[0, i : i + 1, :] = stats[i]
    lse_ref[0, 3:8, :] = jnp.zeros((5, tokens), F32)
    part = mt(ctx_a, w_ref[:, 3 * LANES : 4 * LANES]) + mt(ctx_b, w_ref[:, 5 * LANES :])

    @pl.when(m == 0)
    def _():
        acc[...] = hidden_ref[...] + part

    @pl.when(m > 0)
    def _():
        acc[...] += part

    @pl.when(m == pl.num_programs(0) - 1)
    def _():
        middle_ref[...] = acc[...]


def feed_kernel(
    middle_ref, grad_ref, gain_ref, wi_ref, wo_ref,
    out_ref, back_ref, gain_grad_ref, gi_ref, go_ref,
    x2_ref, x2t_ref, ob_ref, obt_ref, acc_out, acc_two,
):
    f = pl.program_id(0)

    @pl.when(f == 0)
    def _():
        x2 = rms_scaled(middle_ref[...], gain_ref[1:2, :]).astype(BF16)
        x2_ref[...] = x2
        x2t_ref[...] = x2.T
        ob = grad_ref[...].astype(BF16)
        ob_ref[...] = ob
        obt_ref[...] = ob.T
        acc_out[...] = jnp.zeros_like(acc_out)
        acc_two[...] = jnp.zeros_like(acc_two)

    inner = mm(x2_ref[...], wi_ref[...])
    active_back = mm(ob_ref[...], wo_ref[...])
    c = 0.7978845608028654
    sq = inner * inner
    th = jnp.tanh(c * (inner + 0.044715 * (sq * inner)))
    half = 0.5 * (1.0 + th)
    active = (inner * half).astype(BF16)
    slope = half + (0.5 * c) * inner * (1.0 - th * th) * (1.0 + (3 * 0.044715) * sq)
    inner_back = (slope * active_back).astype(BF16)
    acc_out[...] += mt(active, wo_ref[...])
    acc_two[...] += mt(inner_back, wi_ref[...])
    go_ref[...] = mm(obt_ref[...], active).astype(go_ref.dtype)
    gi_ref[...] = mm(x2t_ref[...], inner_back).astype(gi_ref.dtype)

    @pl.when(f == pl.num_programs(0) - 1)
    def _():
        out_ref[...] = middle_ref[...] + acc_out[...]
        result, gain_part = rms_back(middle_ref[...], gain_ref[1:2, :], acc_two[...])
        back_ref[...] = grad_ref[...] + result
        gain_grad_ref[...] = jnp.broadcast_to(gain_part, gain_grad_ref.shape)


def backward_kernel(
    x_ref, xo_ref, back_ref, w_ref, line_ref, qaug_ref, kaug_ref, own_ref, oth_ref, ctx_ref, lse_ref,
    ga_ref, one_own_ref, one_oth_ref, near_ref, sums_ref,
    xt_ref, xot_ref, ab_ref, abt_ref, acc_own, acc_oth,
):
    m = pl.program_id(0)
    tokens = x_ref.shape[0]
    nq = tokens // LANES

    @pl.when(m == 0)
    def _():
        xt_ref[...] = x_ref[...].T
        xot_ref[...] = xo_ref[...].T
        ab = back_ref[...].astype(BF16)
        ab_ref[...] = ab
        abt_ref[...] = ab.T
        acc_own[...] = jnp.zeros_like(acc_own)
        acc_oth[...] = jnp.zeros_like(acc_oth)

    ab = ab_ref[...]
    cb = {2: mm(ab, w_ref[:, 3 * LANES : 4 * LANES]).astype(BF16), 4: mm(ab, w_ref[:, 5 * LANES :]).astype(BF16)}
    ctx = {2: ctx_ref[0, :, :LANES], 4: ctx_ref[0, :, LANES:]}
    own = {c: own_ref[0, :, at * LANES : (at + 1) * LANES] for at, c in enumerate((0, 1, 2, 4, 5))}
    oth = {c: oth_ref[0, :, at * LANES : (at + 1) * LANES] for at, c in enumerate((1, 2, 4, 5))}
    masks = [half_rows(0), half_rows(1)]
    flags = (line_ref[0, 3:4, :LANES], line_ref[0, 4:5, :LANES])
    prod = {c: cb[c].astype(F32) * ctx[c].astype(F32) for c in (2, 4)}
    prod_hi = {c: prod[c].astype(BF16) for c in prod}
    prod_lo = {c: (prod[c] - prod_hi[c].astype(F32)).astype(BF16) for c in prod}
    dq_t = []
    dk = {}
    dv = {}
    for i, (qc, qh, kc, vc, vh) in enumerate(HEAD_AT):
        line = line_ref[0, i : i + 1, :]
        tile = bias_tile(line)
        qm = own[qc] * masks[qh]
        qa = qm + plain_query_aug(qaug_ref[0], i, nq) * masks[1 - qh]
        om = cb[vc] * masks[vh]
        pick = jnp.broadcast_to(masks[vh], (8, LANES))
        center = (mt(pick, prod_hi[vc]) + mt(pick, prod_lo[vc]))[0:1, :]
        lse = lse_ref[0, i : i + 1, :]
        kaug = kaug_ref[...] * masks[1 - qh]
        dqt = None
        parts = near_parts(tile)
        corner = plain_corner_parts(tile, line, flags)
        near = [None, None, None, None, None]
        for side, cols in enumerate((own, oth)):
            ka = cols[kc] * masks[qh] + kaug[side * tokens : (side + 1) * tokens]
            scores = mt(ka, qa)
            chance_back = mt(cols[vc], om)
            ps, ds = [], []
            for jb in range(nq):
                row_s, row_p, row_d = [], [], []
                for ib in range(nq):
                    at = (slice(jb * LANES, (jb + 1) * LANES), slice(ib * LANES, (ib + 1) * LANES))
                    block = scores[at]
                    kind = None
                    if side == 0 and abs(jb - ib) <= 1:
                        block = block + parts[jb - ib + 1]
                        kind = jb - ib + 1
                    elif side == 1 and jb == 0 and ib == nq - 1:
                        block = block + corner[0]
                        kind = 3
                    elif side == 1 and jb == nq - 1 and ib == 0:
                        block = block + corner[1]
                        kind = 4
                    p = jnp.exp(block - lse[:, at[1]])
                    d = p * (chance_back[at] - center[:, at[1]])
                    if kind is not None:
                        near[kind] = d if near[kind] is None else near[kind] + d
                    row_p.append(p.astype(BF16))
                    row_d.append(d.astype(BF16))
                ps.append(jnp.concatenate(row_p, axis=1))
                ds.append(jnp.concatenate(row_d, axis=1))
            pb = jnp.concatenate(ps, axis=0)
            db = jnp.concatenate(ds, axis=0)
            part_v = mm(pb, om)
            part_k = mm(db, qm)
            dv[vc, side] = part_v if (vc, side) not in dv else dv[vc, side] + part_v
            dk[kc, side] = part_k if (kc, side) not in dk else dk[kc, side] + part_k
            part_q = mm(ka.T, db)
            dqt = part_q if dqt is None else dqt + part_q
        at = HDIM if qh == 0 else 0
        sums_ref[0, i * 8 : (i + 1) * 8, :] = dqt[at + 8 : at + 16, :]
        dq_t.append(dqt[:HDIM] if qh == 0 else dqt[HDIM:])
        for kind in range(5):
            near_ref[0, i, kind] = near[kind]
    dq_a = jnp.concatenate([dq_t[0], dq_t[1]], axis=0).T
    dq_b = jnp.concatenate([dq_t[2], jnp.zeros_like(dq_t[2])], axis=0).T
    d_own = jnp.concatenate([dq_a, dk[1, 0], dv[2, 0], dq_b + dv[4, 0], dk[5, 0]], axis=1).astype(BF16)
    d_oth = jnp.concatenate([dk[1, 1], dv[2, 1], dv[4, 1], dk[5, 1]], axis=1).astype(BF16)
    xt, xot, abt = xt_ref[...], xot_ref[...], abt_ref[...]
    g_own = mm(xt, d_own)
    g_oth = mm(xot, d_oth)
    g_ctx = mm(abt, ctx_ref[0])
    ga_ref[:, :LANES] = g_own[:, :LANES].astype(ga_ref.dtype)
    ga_ref[:, LANES : 3 * LANES] = (g_own[:, LANES : 3 * LANES] + g_oth[:, : 2 * LANES]).astype(ga_ref.dtype)
    ga_ref[:, 3 * LANES : 4 * LANES] = g_ctx[:, :LANES].astype(ga_ref.dtype)
    ga_ref[:, 4 * LANES : 5 * LANES] = (g_own[:, 3 * LANES : 4 * LANES] + g_oth[:, 2 * LANES : 3 * LANES]).astype(ga_ref.dtype)
    ga_ref[:, 5 * LANES :] = (g_own[:, 4 * LANES :] + g_oth[:, 3 * LANES :] + g_ctx[:, LANES:]).astype(ga_ref.dtype)
    acc_own[...] += mt(d_own[:, : 3 * LANES], w_ref[:, : 3 * LANES]) + mt(d_own[:, 3 * LANES :], w_ref[:, 4 * LANES :])
    acc_oth[...] += mt(d_oth[:, : 2 * LANES], w_ref[:, LANES : 3 * LANES]) + mt(d_oth[:, 2 * LANES :], w_ref[:, 4 * LANES :])

    @pl.when(m == pl.num_programs(0) - 1)
    def _():
        one_own_ref[...] = acc_own[...]
        one_oth_ref[...] = acc_oth[...].astype(one_oth_ref.dtype)


def whole(shape):
    return pl.BlockSpec(shape, lambda m: (0,) * len(shape))


def params():
    return pltpu.CompilerParams(vmem_limit_bytes=60 * 2**20)


def run_forward(x, xo, wa, line, qaug, kaug, hidden, parts):
    t, d = x.shape
    return pl.pallas_call(
        forward_kernel,
        grid=(parts,),
        in_specs=[
            whole((t, d)), whole((t, d)),
            pl.BlockSpec((d, 6 * LANES), lambda m: (0, m)),
            pl.BlockSpec((1, 8, 4 * LANES), lambda m: (m, 0, 0)),
            pl.BlockSpec((1, 16, LANES), lambda m: (m, 0, 0)),
            whole((2 * t, LANES)), whole((t, d)),
        ],
        out_specs=[
            pl.BlockSpec((1, t, 5 * LANES), lambda m: (m, 0, 0)),
            pl.BlockSpec((1, t, 4 * LANES), lambda m: (m, 0, 0)),
            pl.BlockSpec((1, t, 2 * LANES), lambda m: (m, 0, 0)),
            pl.BlockSpec((1, 8, t), lambda m: (m, 0, 0)),
            whole((t, d)),
        ],
        out_shape=[
            jax.ShapeDtypeStruct((parts, t, 5 * LANES), BF16),
            jax.ShapeDtypeStruct((parts, t, 4 * LANES), BF16),
            jax.ShapeDtypeStruct((parts, t, 2 * LANES), BF16),
            jax.ShapeDtypeStruct((parts, 8, t), F32),
            jax.ShapeDtypeStruct((t, d), F32),
        ],
        scratch_shapes=[
            pltpu.VMEM((t, d), F32),
            pltpu.VMEM((3, 2 * t, t), F32),
            pltpu.VMEM((3, 2 * t, t), BF16),
        ],
        compiler_params=params(),
        name="attend_forward",
    )(x, xo, wa, line, qaug, kaug, hidden)


def run_feed(middle, grad, gains, wi, wo):
    t, d = middle.shape
    units = wi.shape[1]
    tile = min(512, units)
    return pl.pallas_call(
        feed_kernel,
        grid=(units // tile,),
        in_specs=[
            whole((t, d)), whole((t, d)), whole((2, d)),
            pl.BlockSpec((d, tile), lambda f: (0, f)),
            pl.BlockSpec((d, tile), lambda f: (0, f)),
        ],
        out_specs=[
            whole((t, d)), whole((t, d)), whole((8, d)),
            pl.BlockSpec((d, tile), lambda f: (0, f)),
            pl.BlockSpec((d, tile), lambda f: (0, f)),
        ],
        out_shape=[
            jax.ShapeDtypeStruct((t, d), F32),
            jax.ShapeDtypeStruct((t, d), F32),
            jax.ShapeDtypeStruct((8, d), F32),
            jax.ShapeDtypeStruct((d, units), BF16),
            jax.ShapeDtypeStruct((d, units), BF16),
        ],
        scratch_shapes=[
            pltpu.VMEM((t, d), BF16), pltpu.VMEM((d, t), BF16),
            pltpu.VMEM((t, d), BF16), pltpu.VMEM((d, t), BF16),
            pltpu.VMEM((t, d), F32), pltpu.VMEM((t, d), F32),
        ],
        compiler_params=params(),
        name="feed_both",
    )(middle, grad, gains, wi, wo)


def run_backward(x, xo, back, wa, line, qaug, kaug, own, oth, ctx, lse, parts):
    t, d = x.shape
    return pl.pallas_call(
        backward_kernel,
        grid=(parts,),
        in_specs=[
            whole((t, d)), whole((t, d)), whole((t, d)),
            pl.BlockSpec((d, 6 * LANES), lambda m: (0, m)),
            pl.BlockSpec((1, 8, 4 * LANES), lambda m: (m, 0, 0)),
            pl.BlockSpec((1, 16, LANES), lambda m: (m, 0, 0)),
            whole((2 * t, LANES)),
            pl.BlockSpec((1, t, 5 * LANES), lambda m: (m, 0, 0)),
            pl.BlockSpec((1, t, 4 * LANES), lambda m: (m, 0, 0)),
            pl.BlockSpec((1, t, 2 * LANES), lambda m: (m, 0, 0)),
            pl.BlockSpec((1, 8, t), lambda m: (m, 0, 0)),
        ],
        out_specs=[
            pl.BlockSpec((d, 6 * LANES), lambda m: (0, m)),
            whole((t, d)), whole((t, d)),
            pl.BlockSpec((1, 3, 5, LANES, LANES), lambda m: (m, 0, 0, 0, 0)),
            pl.BlockSpec((1, 24, t), lambda m: (m, 0, 0)),
        ],
        out_shape=[
            jax.ShapeDtypeStruct((d, parts * 6 * LANES), BF16),
            jax.ShapeDtypeStruct((t, d), F32),
            jax.ShapeDtypeStruct((t, d), BF16),
            jax.ShapeDtypeStruct((parts, 3, 5, LANES, LANES), F32),
            jax.ShapeDtypeStruct((parts, 24, t), F32),
        ],
        scratch_shapes=[
            pltpu.VMEM((d, t), BF16), pltpu.VMEM((d, t), BF16),
            pltpu.VMEM((t, d), BF16), pltpu.VMEM((d, t), BF16),
            pltpu.VMEM((t, d), F32), pltpu.VMEM((t, d), F32),
        ],
        compiler_params=params(),
        name="attend_backward",
    )(x, xo, back, wa, line, qaug, kaug, own, oth, ctx, lse)


def pack_attn(attn, out_t):
    cut = [[part[:, i * HDIM : (i + 1) * HDIM] for i in range(3)] for part in (attn[0], attn[1], attn[2], out_t)]
    q, k, v, o = cut
    return jnp.concatenate([q[0], q[1], k[0], k[1], v[0], v[1], o[0], o[1], q[2], v[2], k[2], o[2]], axis=1)


def unpack_attn(block):
    c = [block[:, i * HDIM : (i + 1) * HDIM] for i in range(12)]
    attn = jnp.stack(
        [
            jnp.concatenate([c[0], c[1], c[8]], axis=1),
            jnp.concatenate([c[2], c[3], c[10]], axis=1),
            jnp.concatenate([c[4], c[5], c[9]], axis=1),
        ]
    )
    return attn, jnp.concatenate([c[6], c[7], c[11]], axis=1)


def general_body(
    hidden_in, out_grad, attn_weight, out_weight, inner_weight, outer_weight, rel_bias, gains, lengths, table,
    attn_first, attn_second, out_first, out_second, inner_first, inner_second, outer_first, outer_second,
    rel_first, rel_second, gain_first, gain_second, *, parts,
):
    tokens = hidden_in.shape[0]
    nq = tokens // LANES
    heads = rel_bias.shape[1]
    per_seq = SEQLEN // tokens
    mp_index = lax.axis_index("mp")
    half = mp_index % per_seq
    length = lengths[mp_index // per_seq]

    shard = [
        pack_attn(attn_weight.astype(BF16), out_weight.astype(BF16).T),
        inner_weight.astype(BF16),
        outer_weight.astype(BF16).T,
    ]
    gathered = [lax.all_gather(lax.all_gather(s, "dp", axis=0, tiled=True), "mp", axis=1, tiled=True) for s in shard]
    wa, wi, wo = gathered

    x1 = rms_scaled(hidden_in, gains[0]).astype(BF16)
    swap = [(p, p ^ 1) for p in range(parts)]
    x1o = lax.ppermute(x1, "mp", swap)

    u = jnp.arange(4 * LANES)
    offset = jnp.where(u < 2 * LANES, -u, 4 * LANES - u)
    buckets = jnp.arange(rel_bias.shape[0], dtype=jnp.int32)
    line_hot = (jnp.take(table, offset + SEQLEN - 1)[:, None] == buckets[None, :]).astype(F32)
    line = jnp.dot(line_hot, rel_bias, precision=lax.Precision.HIGHEST).T.reshape(parts, heads // parts, 4 * LANES)
    first_flag = (half == 0).astype(F32)
    flags = jnp.stack([jnp.full((4 * LANES,), first_flag), jnp.full((4 * LANES,), 1.0 - first_flag)])
    line_in = jnp.concatenate(
        [line, jnp.broadcast_to(flags[None], (parts, 2, 4 * LANES)), jnp.zeros((parts, 3, 4 * LANES), F32)], axis=1
    )
    far_before, far_after = line[:, :, LANES], line[:, :, 3 * LANES]
    jb, ib = jnp.arange(nq)[None, :], jnp.arange(nq)[:, None]
    own_before, own_after = (jb < ib - 1).astype(F32), (jb > ib + 1).astype(F32)
    oth_before = jnp.full((nq, nq), 1.0 - first_flag)
    w_before = jnp.concatenate([own_before, oth_before], axis=1)
    w_after = jnp.concatenate([own_after, 1.0 - oth_before], axis=1)
    far = far_before[:, :, None, None] * w_before + far_after[:, :, None, None] * w_after
    far_hi = far.astype(BF16).astype(F32)
    far_lo = far - far_hi
    one = jnp.ones((parts, heads // parts, nq, 1), F32)
    blank = jnp.zeros((parts, heads // parts, nq, HDIM), F32)
    q64 = jnp.concatenate(
        [blank[..., :3], one, blank[..., :4], far_hi, far_lo, blank[..., : HDIM - 8 - 4 * nq]], axis=-1
    )
    qaug = jnp.concatenate([q64, q64], axis=-1).reshape(parts, 3 * nq, LANES)
    qaug = jnp.pad(qaug, ((0, 0), (0, 16 - 3 * nq), (0, 0))).astype(BF16)
    row = jnp.arange(2 * tokens)
    position = jnp.where(row < tokens, half * tokens + row, (1 - half) * tokens + row - tokens)
    masked = jnp.where(position < length, 0.0, NEG)
    col = jnp.arange(LANES) % HDIM
    block_of = row // LANES
    hot = ((col >= 8) & (col < 8 + 4 * nq))[None, :] & ((col[None, :] - 8) % (2 * nq) == block_of[:, None])
    kaug = jnp.where((col == 3)[None, :], masked[:, None], hot.astype(F32)).astype(BF16)

    own, oth, ctx, lse, middle = run_forward(x1, x1o, wa, line_in, qaug, kaug, hidden_in, parts)
    block_out, middle_back, gain_two, gi, go = run_feed(middle, out_grad, gains, wi, wo)
    ga, one_own, one_oth, near, sums = run_backward(
        x1, x1o, middle_back, wa, line_in, qaug, kaug, own, oth, ctx, lse, parts
    )
    one_back = one_own + lax.ppermute(one_oth, "mp", swap).astype(F32)
    input_grad, gain_one = rms_back(hidden_in, gains[0:1], one_back)
    input_grad = input_grad + middle_back

    nh = heads // parts
    near = near.reshape(heads, 5, LANES, LANES)
    first_w = first_flag
    blocks = jnp.stack(
        [near[:, 0] + near[:, 4] * (1.0 - first_w), near[:, 1], near[:, 2] + near[:, 3] * first_w], axis=1
    )
    r = jnp.arange(LANES)
    diff = r[None, :, None] - r[None, None, :] + (jnp.arange(3) - 1)[:, None, None] * LANES
    near_bucket = jnp.take(table, diff + SEQLEN - 1).reshape(1, -1)
    near_hot = (near_bucket == buckets[:, None]).astype(F32)
    near_grad = lax.dot_general(
        near_hot, blocks.reshape(heads, -1), (((1,), (1,)), ((), ())), precision=lax.Precision.HIGHEST
    )
    block_sums = jnp.sum(sums.reshape(heads, 2 * nq, nq, LANES), axis=-1)
    far_w = jnp.transpose(jnp.stack([w_before, w_after]), (0, 2, 1))
    corner = jnp.stack([jnp.sum(near[:, 4], (1, 2)) * (1.0 - first_w), jnp.sum(near[:, 3], (1, 2)) * first_w])
    far_grad = jnp.einsum("hji,sji->sh", block_sums, far_w, precision=lax.Precision.HIGHEST) - corner
    far_hot = (jnp.stack([table[0], table[2 * SEQLEN - 2]])[None, :] == buckets[:, None]).astype(F32)
    rel_part = near_grad + jnp.dot(far_hot, far_grad, precision=lax.Precision.HIGHEST)

    owned = [
        lax.psum_scatter(
            lax.psum_scatter(g, "mp", scatter_dimension=1, tiled=True), "dp", scatter_dimension=0, tiled=True
        ).astype(F32)
        for g in (ga, gi, go)
    ]
    g_attn, g_out_t = unpack_attn(owned[0])
    grads = (g_attn, g_out_t.T, owned[1], owned[2].T)
    square_part = sum(jnp.sum(g * g) for g in owned)
    gain_grad, rel_grad, square_total = lax.psum(
        (jnp.concatenate([gain_one, gain_two[:1]], axis=0), rel_part, square_part), ("dp", "mp")
    )
    grad_norm = jnp.sqrt(square_total + jnp.sum(gain_grad * gain_grad) + jnp.sum(rel_grad * rel_grad))
    factor = jnp.minimum(1.0, CLIP / (grad_norm + 1e-06))
    attn_new = adam_step(attn_weight, grads[0], attn_first, attn_second, factor, RATE_MATRIX)
    out_new = adam_step(out_weight, grads[1], out_first, out_second, factor, RATE_OUT)
    inner_new = adam_step(inner_weight, grads[2], inner_first, inner_second, factor, RATE_MATRIX)
    outer_new = adam_step(outer_weight, grads[3], outer_first, outer_second, factor, RATE_MATRIX)
    rel_new = adam_step(rel_bias, rel_grad, rel_first, rel_second, factor, RATE_SMALL)
    gain_new = adam_step(gains, gain_grad, gain_first, gain_second, factor, RATE_SMALL)
    return (block_out, input_grad, grad_norm, *attn_new, *out_new, *inner_new, *outer_new, *rel_new, *gain_new)


def solution(mesh):
    rows = P(("dp", "mp"), None)
    attn, up, down = P(None, "dp", "mp"), P("dp", "mp"), P("mp", "dp")
    in_specs = (
        rows, rows, attn, down, up, down, P(), P(), P("dp"), P(),
        attn, attn, down, down, up, up, down, down, P(), P(), P(), P(),
    )
    out_specs = (rows, rows, P()) + (attn,) * 3 + (down,) * 3 + (up,) * 3 + (down,) * 3 + (P(),) * 6
    plan = body if (mesh.shape["dp"], mesh.shape["mp"]) == (8, 4) else general_body
    return jax.shard_map(
        functools.partial(plan, parts=mesh.shape["mp"]),
        mesh=mesh, in_specs=in_specs, out_specs=out_specs, check_vma=False,
    )
```

```python
import functools

import jax
import jax.numpy as jnp
from jax import lax
from jax.experimental import pallas as pl
from jax.experimental.pallas import tpu as pltpu
from jax.sharding import PartitionSpec as P

HDIM = 64
SEQLEN = 1024
STEP = 10
NORM_EPS = 1e-06
CLIP = 1.0
BETA_ONE = 0.9
BETA_TWO = 0.999
ADAM_EPS = 1e-08
DECAY = 0.01
RATE_MATRIX = 0.05
RATE_OUT = 0.6
RATE_SMALL = 1.0

F32 = jnp.float32
BF16 = jnp.bfloat16
LANES = 128
NEG = -1e30
MESH = pl.DeviceIdType.MESH

HEAD_AT = ((0, 0, 1, 2, 0), (0, 1, 1, 2, 1), (4, 0, 5, 4, 1))


def mm(a, b):
    return lax.dot_general(a, b, (((1,), (0,)), ((), ())), preferred_element_type=F32)


def mt(a, b):
    return lax.dot_general(a, b, (((1,), (1,)), ((), ())), preferred_element_type=F32)


def rms_scaled(value, gain):
    return value * lax.rsqrt(jnp.mean(value * value, axis=-1, keepdims=True) + NORM_EPS) * gain


def rms_back(value, gain, grad):
    factor = lax.rsqrt(jnp.mean(value * value, axis=-1, keepdims=True) + NORM_EPS)
    unit = value * factor
    gain_part = jnp.sum(grad * unit, axis=0, keepdims=True)
    scaled = grad * gain
    result = factor * (scaled - unit * jnp.mean(scaled * unit, axis=-1, keepdims=True))
    return (result, gain_part)


def adam_step(master, grad, first, second, factor, rate):
    clipped = grad * factor
    first_new = BETA_ONE * first + (1.0 - BETA_ONE) * clipped
    second_new = BETA_TWO * second + (1.0 - BETA_TWO) * clipped * clipped
    first_hat = first_new / (1.0 - BETA_ONE**STEP)
    second_hat = second_new / (1.0 - BETA_TWO**STEP)
    master_new = master - rate * (first_hat / (jnp.sqrt(second_hat) + ADAM_EPS) + DECAY * master)
    return (master_new, first_new, second_new)


def half_rows(half):
    lane = lax.broadcasted_iota(jnp.int32, (1, LANES), 1)
    keep = (lane < HDIM) if half == 0 else (lane >= HDIM)
    return keep.astype(F32).astype(BF16)


def bias_tile(line):
    wide = jnp.broadcast_to(line, (LANES, 4 * LANES))
    return pltpu.roll(wide, 0, 1, stride=1, stride_axis=0)


def near_parts(tile):
    return tile[:, LANES : 2 * LANES], tile[:, :LANES], tile[:, 3 * LANES :]


def corner_parts(tile, line, flags):
    before, same, after = near_parts(tile)
    first = (after - line[:, 3 * LANES : 3 * LANES + 1]) * flags
    last = (before - line[:, LANES : LANES + 1]) * (1.0 - flags)
    return first, last


def add_bias(scores, tile, line, flags, nq):
    parts = near_parts(tile)
    corner = corner_parts(tile, line, flags)
    rows = []
    for jb in range(2 * nq):
        row = []
        for ib in range(nq):
            block = scores[jb * LANES : (jb + 1) * LANES, ib * LANES : (ib + 1) * LANES]
            if jb < nq and abs(jb - ib) <= 1:
                block = block + parts[jb - ib + 1]
            elif jb == nq and ib == nq - 1:
                block = block + corner[0]
            elif jb == 2 * nq - 1 and ib == 0:
                block = block + corner[1]
            row.append(block)
        rows.append(jnp.concatenate(row, axis=1))
    return rows


def far_masks(first, nq):
    lane = lax.broadcasted_iota(jnp.int32, (8, LANES), 1) % HDIM
    ib = lax.broadcasted_iota(jnp.int32, (8, LANES), 0)
    jb = (lane - 8) % (2 * nq)
    coded = (lane >= 8) & (lane < 8 + 4 * nq)
    own_before = (coded & (jb < nq) & (jb < ib - 1)).astype(F32)
    own_after = (coded & (jb < nq) & (jb > ib + 1)).astype(F32)
    other = (coded & (jb >= nq)).astype(F32)
    high = (lane < 8 + 2 * nq).astype(F32)
    return own_before + other * (1.0 - first), own_after + other * first, high, (lane == 3).astype(F32)


def query_aug(line, masks, nq):
    before, after, high, one = masks
    far = line[:, LANES : LANES + 1] * before + line[:, 3 * LANES : 3 * LANES + 1] * after
    top = far.astype(BF16).astype(F32)
    rows = (high * top + (1.0 - high) * (far - top) + one).astype(BF16)
    return jnp.concatenate([jnp.broadcast_to(rows[ib : ib + 1, :], (LANES, LANES)) for ib in range(nq)], axis=0)


def turned_hot(table, origin):
    size = 4 * LANES
    hot = (lax.broadcasted_iota(jnp.int32, (LANES, size), 0) == table).astype(F32).astype(BF16)
    at = lax.broadcasted_iota(jnp.int32, (size, size), 0) + lax.broadcasted_iota(jnp.int32, (size, size), 1)
    turn = ((at == origin) | (at == origin + size)).astype(F32).astype(BF16)
    return mm(hot, turn).astype(BF16)


def key_aug(half, length, tokens):
    row = lax.broadcasted_iota(jnp.int32, (2 * tokens, LANES), 0)
    lane = lax.broadcasted_iota(jnp.int32, (2 * tokens, LANES), 1) % HDIM
    position = jnp.where(row < tokens, half * tokens + row, row - half * tokens)
    blocks = 2 * tokens // LANES
    hot = (lane >= 8) & (lane < 8 + 2 * blocks) & ((lane - 8) % blocks == row // LANES)
    masked = (lane == 3) & (position >= length)
    return jnp.where(masked, NEG, hot.astype(F32)).astype(BF16)


def peer(index, stride):
    return index + stride - 2 * stride * ((index // stride) % 2)


class Links:
    def __init__(self):
        self.dp = lax.axis_index("dp")
        self.mp = lax.axis_index("mp")
        self.core = self.dp % 2
        self.chip = self.dp // 2
        self.dp_x, self.dp_y, self.dp_s = peer(self.dp, 2), peer(self.dp, 4), peer(self.dp, 1)
        self.dp_d = peer(self.dp_x, 4)
        self.at_x, self.at_y, self.at_s = (self.dp_x, self.mp), (self.dp_y, self.mp), (self.dp_s, self.mp)
        z1, z2 = peer(self.mp, 1), peer(self.mp, 2)
        self.half = self.mp % 2
        self.first = (1 - self.half).astype(F32)
        self.at_z = (None, (self.dp, z1), (self.dp, z2), (self.dp, peer(z1, 2)))

    def column(self, s):
        return (self.mp + s) % 2 + 2 * ((self.mp // 2 + s // 2) % 2)

    def meet(self, more=()):
        barrier = pltpu.get_barrier_semaphore()
        others = (self.at_x, self.at_y, self.at_s) + self.at_z[1:] + tuple(more)
        for other in others:
            pl.semaphore_signal(barrier, inc=1, device_id=other, device_id_type=MESH)
        pl.semaphore_wait(barrier, len(others))


def remote(src, dst, send, recv, to):
    return pltpu.make_async_remote_copy(
        src_ref=src, dst_ref=dst, send_sem=send, recv_sem=recv, device_id=to, device_id_type=MESH
    )


class Gather:
    def __init__(self, links, w, send, recv, zsend, zrecv):
        self.k, self.w, self.send, self.recv, self.zsend, self.zrecv = links, w, send, recv, zsend, zrecv
        self.rows = w.shape[3]

    def block(self, unit, dp, lo=0, n=None):
        group, s = unit
        return self.w.at[group, s, dp] if n is None else self.w.at[group, s, dp, pl.ds(lo, n)]

    def copy(self, unit, kind, ref, to):
        at = unit[0] * 4 + unit[1]
        return remote(ref, ref, self.send.at[at, kind], self.recv.at[at, kind], to)

    def outgoing(self, unit, kind):
        k, half = self.k, self.rows // 2
        dp, lo, n, to = (
            (k.dp, 0, None, k.at_x),
            (k.dp, 0, None, k.at_y),
            (k.dp, 0, None, k.at_s),
            (k.dp_x, 0, half, k.at_y),
            (k.dp_x, 0, None, k.at_s),
            (k.dp_y, half, half, k.at_x),
            (k.dp_y, 0, None, k.at_s),
            (k.dp_d, 0, None, k.at_s),
        )[kind]
        return self.copy(unit, kind, self.block(unit, dp, lo, n), to)

    def arrived(self, unit, kind):
        k, half = self.k, self.rows // 2
        sib = k.dp_s
        dp, lo, n = {
            0: (k.dp_x, 0, None),
            1: (k.dp_y, 0, None),
            2: (sib, 0, None),
            3: (k.dp_d, 0, half),
            4: (peer(sib, 2), 0, None),
            5: (k.dp_d, half, half),
            6: (peer(sib, 4), 0, None),
            7: (peer(peer(sib, 2), 4), 0, None),
        }[kind]
        self.copy(unit, kind, self.block(unit, dp, lo, n), k.at_x).wait_recv()

    def z_copy(self, group, s):
        at = group * 3 + s - 1
        src = self.block((group, 0), self.k.dp)
        dst = self.block((group, s), self.k.dp)
        return remote(src, dst, self.zsend.at[at], self.zrecv.at[at], self.k.at_z[s])

    def z_arrived(self, unit):
        at = unit[0] * 3 + unit[1] - 1
        ref = self.block(unit, self.k.dp)
        remote(ref, ref, self.zsend.at[at], self.zrecv.at[at], self.k.at_x).wait_recv()

    def run(self, ops):
        for op in ops:
            (self.s1, self.s2, self.s3, self.s4)[op // 16 - 1](UNITS[op % 16])

    def at(self, loop, step, place):
        for number in range(4):
            ops = GATHER_PLAN.get((loop, number), {}).get(place)
            if ops:
                pl.when(step == number)(functools.partial(self.run, ops))

    def s1(self, unit):
        if unit[1] > 0:
            self.z_arrived(unit)
        for kind in (0, 1, 2):
            self.outgoing(unit, kind).start()

    def s2(self, unit):
        self.arrived(unit, 0)
        for kind in (3, 4):
            self.outgoing(unit, kind).start()
        self.arrived(unit, 1)
        for kind in (5, 6):
            self.outgoing(unit, kind).start()

    def s3(self, unit):
        self.arrived(unit, 3)
        self.arrived(unit, 5)
        self.outgoing(unit, 7).start()

    def s4(self, unit):
        for kind in (2, 4, 6, 7):
            self.arrived(unit, kind)

    def finish(self):
        def each(at, carry):
            for kind in range(8):
                self.outgoing((at // 4, at % 4), kind).wait_send()
            return carry

        lax.fori_loop(0, 12, each, 0)
        for group in (1, 2):
            for s in (1, 2, 3):
                self.z_copy(group, s).wait_send()


UNITS = ((0, 0), (1, 0), (2, 0), (0, 1), (0, 2), (0, 3), (1, 1), (2, 1), (1, 2), (2, 2), (1, 3), (2, 3))
GATHER_AHEAD = (
    (0x11, 0x12, 0x20, 0x13, 0x30),
    (0x21, 0x14, 0x40, 0x31, 0x22, 0x15, 0x41, 0x32, 0x23, 0x42, 0x33, 0x24, 0x43),
)
GATHER_PLAN = {
    ("attend", 0): {0: (0x34, 0x25), 2: (0x44,), 3: (0x16,)},
    ("attend", 1): {0: (0x35, 0x17), 3: (0x45, 0x26)},
    ("attend", 2): {0: (0x18,), 1: (0x36,), 3: (0x27, 0x46, 0x19)},
    ("attend", 3): {0: (0x37, 0x28, 0x1a), 3: (0x47,)},
    ("feed", 0): {0: (0x38,), 1: (0x29,), 2: (0x1b, 0x48)},
    ("feed", 1): {0: (0x39,), 1: (0x2a,), 2: (0x49,)},
    ("feed", 2): {0: (0x3a,), 1: (0x2b,), 2: (0x4a,)},
    ("feed", 3): {0: (0x3b, 0x4b)},
}


class Scatter:
    def __init__(self, links, sources, w, sums, piece, diag, side, final, result, send, recv, psem):
        self.k, self.sources, self.w, self.piece, self.final, self.result = links, sources, w, piece, final, result
        self.sums_room, self.diag_room, self.side_room = sums, diag, side
        self.send, self.recv, self.psem = send, recv, psem
        self.rows = w.shape[3]
        chip = links.chip
        self.chips = (chip, peer(chip, 1), peer(chip, 2), peer(peer(chip, 1), 2))

    def sums(self, u):
        return self.sums_room.at[u] if u < 8 else self.w.at[1, u - 8, pl.ds(0, 4)]

    def side(self, u, n):
        return self.side_room.at[u, n] if u < 8 else self.w.at[1, u - 8, 4 + n]

    def diag(self, u, n):
        half = self.rows // 2
        return self.diag_room.at[u, n] if u < 8 else self.w.at[1, u - 8, 6, pl.ds(n * half, half)]

    def outgoing(self, u, kind):
        group, s = BACK_UNITS[u]
        k, half = self.k, self.rows // 2
        at, at_x, at_y, at_d = self.chips
        sums = self.sums(u)
        if kind == 0:
            src, dst, to = self.sources[group].at[s, :, 1 - k.core], sums, k.at_s
        elif kind == 1:
            src, dst, to = sums.at[at_d, pl.ds(0, half)], self.diag(u, 0), k.at_x
        elif kind == 2:
            src, dst, to = sums.at[at_d, pl.ds(half, half)], self.diag(u, 1), k.at_y
        elif kind == 3:
            src, dst, to = sums.at[at_x], self.side(u, 0), k.at_x
        elif kind == 4:
            src, dst, to = sums.at[at_y], self.side(u, 1), k.at_y
        else:
            src, dst, to = sums.at[at], self.final.at[group, s - 1], k.at_z[s]
        return remote(src, dst, self.send.at[u, kind], self.recv.at[u, kind], to)

    def local(self, u):
        group, s = BACK_UNITS[u]
        return pltpu.make_async_copy(self.sources[group].at[s, :, self.k.core], self.piece.at[u % 3], self.psem.at[u % 3])

    def s1(self, u):
        self.outgoing(u, 0).start()
        self.local(u).start()

    def s2(self, u):
        self.local(u).wait()
        self.outgoing(u, 0).wait_recv()
        sums, far = self.sums(u), self.chips[3]
        sums[far] = sums[far] + self.piece[u % 3, far]
        self.outgoing(u, 1).start()
        self.outgoing(u, 2).start()
        for chip in self.chips[:3]:
            sums[chip] = sums[chip] + self.piece[u % 3, chip]

    def s3(self, u):
        half, sums = self.rows // 2, self.sums(u)
        self.outgoing(u, 1).wait_recv()
        self.outgoing(u, 2).wait_recv()
        for chip, lo, n in ((self.chips[2], 0, 0), (self.chips[1], half, 1)):
            sums[chip, lo : lo + half] = sums[chip, lo : lo + half] + self.diag(u, n)[...]
        self.outgoing(u, 3).start()
        self.outgoing(u, 4).start()

    def s4(self, u):
        group, s = BACK_UNITS[u]
        self.outgoing(u, 3).wait_recv()
        self.outgoing(u, 4).wait_recv()
        at, sums = self.chips[0], self.sums(u)
        total = sums[at].astype(F32) + (self.side(u, 0)[...].astype(F32) + self.side(u, 1)[...].astype(F32))
        if s == 0:
            self.result[group] = total
        else:
            sums[at] = total.astype(BF16)
            self.outgoing(u, 5).start()

    def last(self, group):
        total = self.result[group]
        for u, (other, s) in enumerate(BACK_UNITS):
            if other == group and s > 0:
                self.outgoing(u, 5).wait_recv()
        for n in range(3):
            total = total + self.final[group, n].astype(F32)
        self.result[group] = total

    def run(self, ops):
        for op in ops:
            (self.s1, self.s2, self.s3, self.s4)[op // 16 - 1](op % 16)

    def at(self, loop, step, place):
        for number in range(4):
            ops = SCATTER_PLAN.get((loop, number), {}).get(place)
            if ops:
                pl.when(step == number)(functools.partial(self.run, ops))

    def finish(self):
        for u, (group, s) in enumerate(BACK_UNITS):
            for kind in range(5 if s == 0 else 6):
                self.outgoing(u, kind).wait_send()


BACK_UNITS = ((1, 0), (2, 0), (1, 1), (2, 1), (1, 2), (2, 2), (1, 3), (2, 3), (0, 3), (0, 2), (0, 1), (0, 0))
SCATTER_PLAN = {
    ("feed", 2): {1: (0x10, 0x11)},
    ("feed", 3): {0: (0x20,), 1: (0x12, 0x13, 0x21), 2: (0x30, 0x22, 0x14)},
    ("other", 0): {0: (0x40,), 2: (0x32, 0x25, 0x17)},
    ("other", 1): {0: (0x41,), 2: (0x33, 0x26, 0x42)},
    ("other", 2): {1: (0x34, 0x27, 0x43)},
    ("other", 3): {0: (0x35, 0x44)},
    ("own", 0): {0: (0x36,), 1: (0x45,), 3: (0x37, 0x46, 0x18)},
    ("own", 1): {0: (0x28,), 1: (0x47,), 2: (0x38,), 3: (0x19,)},
    ("own", 2): {0: (0x29, 0x48), 2: (0x39,), 3: (0x1a,)},
    ("own", 3): {0: (0x2a, 0x49), 2: (0x3a,), 3: (0x1b,)},
}
SCATTER_BETWEEN = ((0x23, 0x15), (0x31, 0x24, 0x16))
SCATTER_AFTER = ((0x4a, 0x2b), (0x3b,), (0x4b,))


def layer_kernel(
    lengths_ref, attn_ref, wout_ref, inner_ref, outer_ref, table_ref, rel_ref, gain_ref, hidden_hbm, grad_hbm,
    out_hbm, input_hbm, small_ref, result_ref, gi_hbm, go_hbm,
    w, x_ref, xo, own, oth, ctx, s_ref, e_ref, middle, grad, x2_ref, x2t_ref, ob_ref, obt_ref, acc_out, acc_two, g_all, kaug_ref,
    lse_ref, line_ref, center_ref, near_ref, oth_in, sums, piece, diag, side, final,
    line_grad, far_grad, small, small_near, small_z,
    send, recv, zsend, zrecv, xsem, lsem, gsem, osem, bsend, brecv, psem, tsend, trecv,
):
    tokens = x_ref.shape[0]
    nq = tokens // LANES
    links = Links()
    net = Gather(links, w, send, recv, zsend, zrecv)
    group = []
    for n in range(1, 8):
        dp = links.dp
        for stride in (1, 2, 4):
            if n & stride:
                dp = peer(dp, stride)
        group.append((dp, links.mp))
    back = Scatter(links, (g_all, gi_hbm, go_hbm), w, sums, piece, diag, side, final, result_ref, bsend, brecv, psem)
    width = w.shape[2] * w.shape[3]

    def weights(kind, s, lo=0, hi=None):
        part = w[kind, s, :, :, lo:] if hi is None else w[kind, s, :, :, lo:hi]
        return part.reshape(width, part.shape[2])

    get_hidden = pltpu.make_async_copy(hidden_hbm, middle, lsem.at[0])
    get_grad = pltpu.make_async_copy(grad_hbm, grad, lsem.at[1])
    get_hidden.start()
    def own_block(group):
        return (group, 0, links.dp)

    parts = [attn_ref[n].astype(BF16) for n in range(3)] + [wout_ref[...].T.astype(BF16)]
    q, k, v, o = [(part[:, :LANES], part[:, LANES:]) for part in parts]
    w[own_block(0)] = jnp.concatenate([q[0], k[0], v[0], o[0], q[1], v[1], k[1], o[1]], axis=1)
    w[own_block(1)] = inner_ref[...].astype(BF16)
    w[own_block(2)] = outer_ref[...].astype(BF16)
    get_grad.start()
    links.meet([group[n] for n in (2, 4, 5, 6)])
    for step in (1, 2, 3):
        net.z_copy(0, step).start()
    net.s1(UNITS[0])
    get_hidden.wait()
    x_ref[...] = rms_scaled(middle[...], gain_ref[0:1, :]).astype(BF16)
    xcopy = remote(x_ref, xo, xsem.at[0], xsem.at[1], links.at_z[1])
    hot = turned_hot(table_ref[...], 2 * LANES - 1)[: rel_ref.shape[1]]
    high = rel_ref[...].astype(BF16)
    rest = rel_ref[...] - high.astype(F32)
    mid = rest.astype(BF16)
    low = (rest - mid.astype(F32)).astype(BF16)
    line_ref[...] = mm(high, hot) + (mm(mid, hot) + mm(low, hot))
    kaug_ref[...] = key_aug(links.half, lengths_ref[links.mp // 2], tokens)
    far = far_masks(links.first, nq)
    net.run(GATHER_AHEAD[0])
    for step in (1, 2, 3):
        net.z_copy(0, step).wait_send()
    xcopy.start()
    get_grad.wait()
    ob = grad[...].astype(BF16)
    ob_ref[...] = ob
    obt_ref[...] = ob.T
    net.run(GATHER_AHEAD[1])
    xcopy.wait_send()
    for step in (1, 2, 3):
        net.z_copy(1, step).start()
        net.z_copy(2, step).start()
    xcopy.wait_recv()

    masks = [half_rows(0), half_rows(1)]
    count = lax.broadcasted_iota(jnp.int32, (HDIM, 2 * tokens), 0)
    ones = (count == 0).astype(F32).astype(BF16)

    def attend(s, carry):
        x, other = x_ref[...], xo[...]
        p_a = mm(x, weights(0, s, 0, 3 * LANES)).astype(BF16)
        p_b = mm(x, weights(0, s, 4 * LANES)).astype(BF16)
        o_a = mm(other, weights(0, s, LANES, 3 * LANES)).astype(BF16)
        o_b = mm(other, weights(0, s, 4 * LANES)).astype(BF16)
        own[s, :, : 3 * LANES] = p_a
        own[s, :, 3 * LANES :] = p_b
        oth[s, :, : 2 * LANES] = o_a
        oth[s, :, 2 * LANES :] = o_b
        cols_own = {0: p_a[:, :LANES], 1: p_a[:, LANES : 2 * LANES], 2: p_a[:, 2 * LANES :], 4: p_b[:, :LANES], 5: p_b[:, LANES:]}
        cols_oth = {1: o_a[:, :LANES], 2: o_a[:, LANES:], 4: o_b[:, :LANES], 5: o_b[:, LANES:]}
        both = {c: jnp.concatenate([cols_own[c], cols_oth[c]], axis=0) for c in (1, 2, 4, 5)}
        m = links.column(s)
        v_t = {2: both[2].T, 4: both[4].T}
        pieces = []
        stats = []
        for i, (qc, qh, kc, vc, vh) in enumerate(HEAD_AT):
            net.at("attend", s, i)
            line = line_ref[pl.ds(3 * m + i, 1), :]
            tile = bias_tile(line)
            qa = cols_own[qc] * masks[qh] + query_aug(line, far, nq) * masks[1 - qh]
            ka = both[kc] * masks[qh] + kaug_ref[...] * masks[1 - qh]
            scores = mt(ka, qa)
            peak = None
            for jb, row in enumerate(add_bias(scores, tile, line, links.first, nq)):
                s_ref[i % 2 * 2 * nq + jb] = row
                top = jnp.max(row.reshape(LANES // 8, 8, tokens), axis=0)
                peak = top if peak is None else jnp.maximum(peak, top)
            peak = jnp.max(peak, axis=0, keepdims=True)
            for jb in range(2 * nq):
                rows = slice(jb % nq * LANES, (jb % nq + 1) * LANES)
                e_ref[i % 2 * 2 + jb // nq, rows, :] = jnp.exp(s_ref[i % 2 * 2 * nq + jb] - peak).astype(BF16)
            if vh == 0:
                va = jnp.concatenate([v_t[vc][:HDIM], ones], axis=0)
            else:
                va = jnp.concatenate([ones, v_t[vc][HDIM:]], axis=0)
            ot = mm(va, e_ref[i % 2 * 2 : i % 2 * 2 + 2].reshape(2 * tokens, tokens))
            at = HDIM if vh == 0 else 0
            total = ot[at : at + 1, :]
            stats.append(peak + jnp.log(total))
            real = ot[:HDIM] if vh == 0 else ot[HDIM:]
            pieces.append(real / total)
        zero = jnp.zeros((HDIM, tokens), F32)
        ctx_a = jnp.concatenate([pieces[0], pieces[1]], axis=0).T.astype(BF16)
        ctx_b = jnp.concatenate([zero, pieces[2]], axis=0).T.astype(BF16)
        ctx[s, :, :LANES] = ctx_a
        ctx[s, :, LANES:] = ctx_b
        lse_ref[s] = jnp.concatenate(stats + [jnp.zeros((5, tokens), F32)], axis=0)
        middle[...] += mt(ctx_a, weights(0, s, 3 * LANES, 4 * LANES)) + mt(ctx_b, weights(0, s, 5 * LANES))
        net.at("attend", s, 3)
        return carry

    lax.fori_loop(0, 4, attend, 0)

    x2 = rms_scaled(middle[...], gain_ref[1:2, :]).astype(BF16)
    x2_ref[...] = x2
    x2t_ref[...] = x2.T
    acc_out[...] = jnp.zeros_like(acc_out)
    acc_two[...] = jnp.zeros_like(acc_two)

    def g_copies(t):
        return (
            pltpu.make_async_copy(g_all.at[t % 2 * 2], gi_hbm.at[t], gsem.at[t % 2, 0]),
            pltpu.make_async_copy(g_all.at[t % 2 * 2 + 1], go_hbm.at[t], gsem.at[t % 2, 1]),
        )

    def feed(t, carry):
        tile = 2 * LANES
        for n in range(w.shape[4] // tile):
            net.at("feed", t, n)
            if n == 1:

                @pl.when(t >= 1)
                def _():
                    for copy in g_copies(t - 1):
                        copy.wait()

            back.at("feed", t, n)
            wi = weights(1, t, n * tile, (n + 1) * tile)
            wo = weights(2, t, n * tile, (n + 1) * tile)
            inner = mm(x2_ref[...], wi)
            active_back = mm(ob_ref[...], wo)
            c = 0.7978845608028654
            sq = inner * inner
            th = jnp.tanh(c * (inner + 0.044715 * (sq * inner)))
            half = 0.5 * (1.0 + th)
            active = (inner * half).astype(BF16)
            slope = half + (0.5 * c) * inner * (1.0 - th * th) * (1.0 + (3 * 0.044715) * sq)
            inner_back = (slope * active_back).astype(BF16)
            acc_out[...] += mt(active, wo)
            acc_two[...] += mt(inner_back, wi)
            at = slice(n * tile, (n + 1) * tile)
            shape = (*w.shape[2:4], tile)
            split = (shape[0] // 2, 2, *shape[1:])
            g_all[t % 2 * 2, :, :, :, at] = mm(x2t_ref[...], inner_back).astype(BF16).reshape(split)
            g_all[t % 2 * 2 + 1, :, :, :, at] = mm(obt_ref[...], active).astype(BF16).reshape(split)
        for copy in g_copies(t):
            copy.start()
        return carry

    lax.fori_loop(0, 4, feed, 0)
    back.run(SCATTER_BETWEEN[0])
    acc_out[...] += middle[...]
    put_out = pltpu.make_async_copy(acc_out, out_hbm, lsem.at[2])
    put_out.start()
    result, gain_two = rms_back(middle[...], gain_ref[1:2, :], acc_two[...])
    get_hidden = pltpu.make_async_copy(hidden_hbm, middle, lsem.at[0])
    get_hidden.start()
    grad[...] += result
    net.finish()
    for copy in g_copies(3):
        copy.wait()
    back.run(SCATTER_BETWEEN[1])
    ab_ref, abt, xt, acc_own, acc_oth, oth_out = x2_ref, x2t_ref, obt_ref, acc_out, acc_two, ob_ref
    ab = grad[...].astype(BF16)
    ab_ref[...] = ab
    abt[...] = ab.T
    xt[...] = x_ref[...].T
    w[2, 0, :, :, : tokens] = xo[...].T.reshape(*w.shape[2:4], tokens)
    acc_oth[...] = jnp.zeros_like(acc_oth)
    line_grad[...] = jnp.zeros_like(line_grad)
    far_grad[...] = jnp.zeros_like(far_grad)
    jb = lax.broadcasted_iota(jnp.int32, (2 * nq, tokens), 0)
    ib = lax.broadcasted_iota(jnp.int32, (2 * nq, tokens), 1) // LANES
    edge_first = ((jb == nq) & (ib == nq - 1)).astype(F32)
    edge_last = ((jb == 2 * nq - 1) & (ib == 0)).astype(F32)
    other_key = (jb >= nq).astype(F32)
    sum_before = ((jb < nq) & (jb < ib - 1)).astype(F32) + (other_key - edge_last) * (1.0 - links.first)
    sum_after = ((jb < nq) & (jb > ib + 1)).astype(F32) + (other_key - edge_first) * links.first
    own_at = {c: slice(at * LANES, (at + 1) * LANES) for at, c in enumerate((0, 1, 2, 4, 5))}
    oth_at = {c: slice(at * LANES, (at + 1) * LANES) for at, c in enumerate((1, 2, 4, 5))}
    cb_at = {2: slice(0, LANES), 4: slice(LANES, 2 * LANES)}
    at_row = lax.broadcasted_iota(jnp.int32, (LANES, LANES), 0) + lax.broadcasted_iota(jnp.int32, (LANES, LANES), 1)
    mirror = (at_row == LANES - 1).astype(F32).astype(BF16)

    def context_back(s):
        return {
            2: mm(ab_ref[...], weights(0, s, 3 * LANES, 4 * LANES)).astype(BF16),
            4: mm(ab_ref[...], weights(0, s, 5 * LANES)).astype(BF16),
        }

    def one_side(s, i, other, cb):
        qc, qh, kc, vc, vh = HEAD_AT[i]
        line = line_ref[pl.ds(3 * links.column(s) + i, 1), :]
        tile = bias_tile(line)
        qm = own[s, :, own_at[qc]] * masks[qh]
        qa = qm + query_aug(line, far, nq) * masks[1 - qh]
        om = cb[vc] * masks[vh]
        center = center_ref[s, i : i + 1, :]
        lse = lse_ref[s, i : i + 1, :]
        parts = near_parts(tile)
        corner = corner_parts(tile, line, links.first)
        side = 1 if other else 0
        k_cols = oth[s, :, oth_at[kc]] if other else own[s, :, own_at[kc]]
        v_cols = oth[s, :, oth_at[vc]] if other else own[s, :, own_at[vc]]
        ka = k_cols * masks[qh] + kaug_ref[side * tokens : (side + 1) * tokens] * masks[1 - qh]
        scores = mt(ka, qa)
        chance_back = mt(v_cols, om)
        near = [None] * 5
        ps, ds = [], []
        for jb in range(nq):
            row_p, row_d = [], []
            for ib in range(nq):
                at = (slice(jb * LANES, (jb + 1) * LANES), slice(ib * LANES, (ib + 1) * LANES))
                block = scores[at]
                kind = None
                if not other and abs(jb - ib) <= 1:
                    kind = jb - ib + 1
                    block = block + parts[kind]
                elif other and jb == 0 and ib == nq - 1:
                    kind = 3
                    block = block + corner[0]
                elif other and jb == nq - 1 and ib == 0:
                    kind = 4
                    block = block + corner[1]
                p = jnp.exp(block - lse[:, at[1]])
                d = p * (chance_back[at] - center[:, at[1]])
                if kind is not None:
                    near[kind] = d if near[kind] is None else near[kind] + d
                row_p.append(p.astype(BF16))
                row_d.append(d.astype(BF16))
            ps.append(jnp.concatenate(row_p, axis=1))
            ds.append(jnp.concatenate(row_d, axis=1))
        pb = jnp.concatenate(ps, axis=0)
        db = jnp.concatenate(ds, axis=0)
        return mm(ka.T, db), mm(db, qm), mm(pb, om), near

    def other_side(it, carry):
        s = 3 - it
        cb = context_back(s)
        centers = []
        for i in range(3):
            vc, vh = HEAD_AT[i][3:]
            prod = cb[vc].astype(F32) * ctx[s, :, cb_at[vc]].astype(F32)
            high = prod.astype(BF16)
            low = (prod - high.astype(F32)).astype(BF16)
            pick = jnp.broadcast_to(masks[vh], (8, LANES))
            centers.append((mt(pick, high) + mt(pick, low))[0:1, :])
        center_ref[s] = jnp.concatenate(centers + [jnp.zeros((5, tokens), F32)], axis=0)
        dk, dv = {}, {}
        for i, (qc, qh, kc, vc, vh) in enumerate(HEAD_AT):
            back.at("other", it, i)
            s_ref[3 * s + i], part_k, part_v, near = one_side(s, i, True, cb)
            dk[kc] = dk[kc] + part_k if kc in dk else part_k
            dv[vc] = dv[vc] + part_v if vc in dv else part_v
            near_ref[s, i] = near[3] * links.first + near[4] * (1.0 - links.first)
        d = jnp.concatenate([dk[1], dv[2], dv[4], dk[5]], axis=1).astype(BF16)
        e_ref[s] = d
        acc_oth[...] += mt(d[:, : 2 * LANES], weights(0, s, LANES, 3 * LANES)) + mt(d[:, 2 * LANES :], weights(0, s, 4 * LANES))
        return carry

    lax.fori_loop(0, 4, other_side, 0)
    oth_out[...] = acc_oth[...].astype(BF16)
    swap = remote(oth_out, oth_in, osem.at[0], osem.at[1], links.at_z[1])
    swap.start()

    def own_side(it, carry):
        s = 3 - it
        m = links.column(s)
        cb = context_back(s)
        dk, dv, dq = {}, {}, []
        for i, (qc, qh, kc, vc, vh) in enumerate(HEAD_AT):
            back.at("own", it, i)
            part_q, part_k, part_v, near = one_side(s, i, False, cb)
            part_q = part_q + s_ref[3 * s + i]
            dk[kc] = dk[kc] + part_k if kc in dk else part_k
            dv[vc] = dv[vc] + part_v if vc in dv else part_v
            at = HDIM if qh == 0 else 0
            block_sums = part_q[at + 8 : at + 8 + 2 * nq, :]
            head = pl.ds(3 * m + i, 1)
            far_grad[0, head, :] = jnp.sum(block_sums * sum_before, axis=0, keepdims=True)
            far_grad[1, head, :] = jnp.sum(block_sums * sum_after, axis=0, keepdims=True)
            dq.append(part_q[:HDIM] if qh == 0 else part_q[HDIM:])
            first, final_corner = near_ref[s, i] * links.first, near_ref[s, i] * (1.0 - links.first)
            blank = jnp.zeros((LANES, LANES), F32)
            tile = jnp.concatenate([near[1], near[0] + final_corner, blank, near[2] + first], axis=1)
            high = tile.astype(BF16)
            low = (tile - high.astype(F32)).astype(BF16)
            turned = pltpu.roll(mm(mirror, high) + mm(mirror, low), 0, 1, stride=1, stride_axis=0)
            line_grad[head, :] = jnp.sum(turned, axis=0, keepdims=True)
        dq_a = jnp.concatenate([dq[0], dq[1]], axis=0).T
        dq_b = jnp.concatenate([dq[2], jnp.zeros_like(dq[2])], axis=0).T
        d_own = jnp.concatenate([dq_a, dk[1], dv[2], dq_b + dv[4], dk[5]], axis=1).astype(BF16)
        g_own = mm(xt[...], d_own)
        g_oth = mm(w[2, 0, :, :, :tokens].reshape(width, tokens), e_ref[s])
        g_ctx = mm(abt[...], ctx[s])
        columns = [
            g_own[:, :LANES],
            g_own[:, LANES : 3 * LANES] + g_oth[:, : 2 * LANES],
            g_ctx[:, :LANES],
            g_own[:, 3 * LANES : 4 * LANES] + g_oth[:, 2 * LANES : 3 * LANES],
            g_own[:, 4 * LANES :] + g_oth[:, 3 * LANES :] + g_ctx[:, LANES:],
        ]
        g = jnp.concatenate(columns, axis=1).astype(BF16)
        rows = w.shape[3]
        for n in range(8):
            g_all[s, n // 2, n % 2] = g[n * rows : (n + 1) * rows, :]
        back.at("own", it, 3)
        acc_own[...] += mt(d_own[:, : 3 * LANES], weights(0, s, 0, 3 * LANES)) + mt(d_own[:, 3 * LANES :], weights(0, s, 4 * LANES))
        return carry

    put_out.wait()
    acc_own[...] = jnp.zeros_like(acc_own)
    lax.fori_loop(0, 4, own_side, 0)
    back.run(SCATTER_AFTER[0])
    get_hidden.wait()
    swap.wait_recv()
    one_back = acc_own[...] + oth_in[...].astype(F32)
    value, gain_part = rms_back(middle[...], gain_ref[0:1, :], one_back)
    acc_own[...] = value + grad[...]
    put_grad = pltpu.make_async_copy(acc_own, input_hbm, lsem.at[2])
    put_grad.start()
    back.run(SCATTER_AFTER[1])
    lane = lax.broadcasted_iota(jnp.int32, (16, 4 * LANES), 1)
    by_line = (
        line_grad[...]
        + jnp.sum(far_grad[0], axis=1, keepdims=True) * (lane == 2 * LANES - 1).astype(F32)
        + jnp.sum(far_grad[1], axis=1, keepdims=True) * (lane == 4 * LANES - 1).astype(F32)
    )
    high = by_line.astype(BF16)
    low = (by_line - high.astype(F32)).astype(BF16)
    hot = turned_hot(table_ref[...], 3 * LANES - 2)
    small[0:16, :] = mt(high, hot) + mt(low, hot)
    for n in range(6):
        at = slice(n * LANES, (n + 1) * LANES)
        small[16 + n : 17 + n, :] = gain_part[:, at]
        small[22 + n : 23 + n, :] = gain_two[:, at]
    back.run(SCATTER_AFTER[2])
    squares = jnp.zeros((8, LANES), F32)
    for weight in (1, 2, 0):
        back.last(weight)
        value = result_ref[weight]
        value = value * value
        for n in range(value.shape[1] // LANES):
            piece_sum = value[:, n * LANES : (n + 1) * LANES]
            squares = squares + jnp.sum(piece_sum.reshape(-1, 8, LANES), axis=0)
    small[28:32, :] = squares[0:4] + squares[4:8]
    near = [remote(small, small_near.at[n], tsend.at[n], trecv.at[n], to) for n, to in enumerate(group)]
    for copy in near:
        copy.start()
    for copy in near:
        copy.wait_recv()
    total = small[...]
    for n in range(7):
        total = total + small_near[n]
    small_z[0] = total
    along = [remote(small_z.at[0], small_z.at[n], tsend.at[6 + n], trecv.at[6 + n], links.at_z[n]) for n in (1, 2, 3)]
    for copy in along:
        copy.start()
    for copy in along:
        copy.wait_recv()
    small_ref[...] = (small_z[0] + small_z[1]) + (small_z[2] + small_z[3])
    for copy in near + along:
        copy.wait_send()
    put_grad.wait()
    swap.wait_send()
    back.finish()


def update_kernel(small_ref, grad_hbm, block_hbm, input_hbm, *refs):
    hbm, (block_out, input_out, norm_ref), new = refs[:18], refs[18:21], refs[21:39]
    held, grad_ref, pass_ref, sem = refs[39:57], refs[57], refs[58], refs[59]
    through = ((block_hbm, block_out), (input_hbm, input_out))
    fetch = [pltpu.make_async_copy(a, pass_ref.at[n], sem.at[n]) for n, (a, b) in enumerate(through)]
    store = [pltpu.make_async_copy(pass_ref.at[n], b, sem.at[21 + n]) for n, (a, b) in enumerate(through)]
    loads = [pltpu.make_async_copy(a, b, sem.at[2 + n]) for n, (a, b) in enumerate(zip(hbm, held))]
    loads.append(pltpu.make_async_copy(grad_hbm, grad_ref, sem.at[20]))
    for copy in loads[::-1] + fetch:
        copy.start()
    attn, out, inner, outer, rel, gain, attn_first, attn_second, out_first, out_second = held[:10]
    inner_first, inner_second, outer_first, outer_second, rel_first, rel_second, gain_first, gain_second = held[10:]
    small = small_ref[0:28, :]
    squares = jnp.sum(small * small, axis=0, keepdims=True) + jnp.sum(small_ref[28:32, :], axis=0, keepdims=True)
    norm = jnp.sqrt(jnp.sum(squares, axis=1, keepdims=True))
    norm_ref[...] = norm
    factor = jnp.minimum(1.0, CLIP / (norm + 1e-06))
    for copy in loads:
        copy.wait()
    for a, b in zip(fetch, store):
        a.wait()
        b.start()

    def step(at, grad, rate, master, first, second, outs):
        for ref, value in zip(outs, adam_step(master[at], grad, first[at], second[at], factor, rate)):
            ref[at] = value

    def turned(column):
        return pltpu.roll(column, HDIM, 1)[:, :HDIM]

    g = [grad_ref[0, :, n * LANES : (n + 1) * LANES] for n in range(6)]
    tails = (g[4][:, :HDIM], g[5][:, :HDIM], turned(g[4]))
    for n in range(3):
        step((n, slice(None), slice(0, LANES)), g[n], RATE_MATRIX, attn, attn_first, attn_second, new[0:3])
        step((n, slice(None), slice(LANES, LANES + HDIM)), tails[n], RATE_MATRIX, attn, attn_first, attn_second, new[0:3])
    rows = g[3].shape[0]
    blank = jnp.zeros((LANES - rows, LANES), F32)
    lower = pltpu.roll(g[5], HDIM, 1)
    whole = slice(None)
    step((slice(0, LANES), whole), jnp.concatenate([g[3], blank], axis=0).T[:, :rows], RATE_OUT, out, out_first, out_second, new[3:6])
    step(
        (slice(LANES, LANES + HDIM), whole),
        jnp.concatenate([lower, blank], axis=0).T[:HDIM, :rows],
        RATE_OUT, out, out_first, out_second, new[3:6],
    )
    step(whole, grad_ref[1], RATE_MATRIX, inner, inner_first, inner_second, new[6:9])
    step(whole, grad_ref[2], RATE_MATRIX, outer, outer_first, outer_second, new[9:12])
    heads, buckets = rel.shape
    step(whole, small_ref[0:heads, 0:buckets], RATE_SMALL, rel, rel_first, rel_second, new[12:15])
    gain_grad = jnp.concatenate(
        [
            jnp.concatenate([small_ref[at + n : at + n + 1, :] for n in range(6)], axis=1)
            for at in (16, 22)
        ],
        axis=0,
    )
    step(whole, gain_grad, RATE_SMALL, gain, gain_first, gain_second, new[15:18])
    for copy in store:
        copy.wait()


def run_layer(lengths, attn, out, inner, outer, table, rel, gains, hidden, grad):
    t, d = hidden.shape
    parts, (rows, cols) = rel.shape[0] // 3, inner.shape
    any_space = pl.BlockSpec(memory_space=pl.ANY)
    vmem = pl.BlockSpec(memory_space=pltpu.VMEM)
    dma = pltpu.SemaphoreType.DMA
    split = (parts, 4, 2, rows, cols)
    low = lambda *shape: pltpu.VMEM(shape, BF16)
    full = lambda *shape: pltpu.VMEM(shape, F32)
    return pl.pallas_call(
        layer_kernel,
        in_specs=[pl.BlockSpec(memory_space=pltpu.SMEM)] + [vmem] * 7 + [any_space] * 2,
        out_specs=[any_space] * 2 + [vmem] * 2 + [any_space] * 2,
        out_shape=[
            jax.ShapeDtypeStruct((t, d), F32),
            jax.ShapeDtypeStruct((t, d), F32),
            jax.ShapeDtypeStruct((32, LANES), F32),
            jax.ShapeDtypeStruct((3, rows, cols), F32),
            jax.ShapeDtypeStruct(split, BF16),
            jax.ShapeDtypeStruct(split, BF16),
        ],
        scratch_shapes=[
            low(3, parts, 8, rows, cols), low(t, d), low(t, d),
            low(parts, t, 5 * LANES), low(parts, t, 4 * LANES), low(parts, t, 2 * LANES),
            full(4 * t // LANES, LANES, t), low(4, t, t), full(t, d), full(t, d),
            low(t, d), low(d, t), low(t, d), low(d, t), full(t, d), full(t, d), low(*split), low(2 * t, LANES),
            full(parts, 8, t), full(rel.shape[0], 4 * LANES), full(parts, 8, t), full(parts, 3, LANES, LANES), low(t, d),
            low(8, 4, rows, cols), low(3, 4, rows, cols), low(8, 2, rows // 2, cols), low(8, 2, rows, cols), low(3, 3, rows, cols),
            full(16, 4 * LANES), full(2, 16, 4 * LANES), full(32, LANES), full(7, 32, LANES), full(4, 32, LANES),
            dma((12, 8)), dma((12, 8)), dma((9,)), dma((9,)), dma((2,)), dma((3,)), dma((2, 2)), dma((2,)),
            dma((12, 6)), dma((12, 6)), dma((3,)), dma((10,)), dma((10,)),
        ],
        compiler_params=pltpu.CompilerParams(
            vmem_limit_bytes=63 * 2**20, collective_id=0, has_side_effects=True
        ),
        name="layer",
    )(lengths, attn, out, inner, outer, table, rel, gains, hidden, grad)


def run_update(small, grads, block_out, input_grad, masters, moments):
    vmem = pl.BlockSpec(memory_space=pltpu.VMEM)
    hbm = pl.BlockSpec(memory_space=pltpu.HBM)
    like = lambda a: jax.ShapeDtypeStruct(a.shape, F32)
    return pl.pallas_call(
        update_kernel,
        in_specs=[vmem] + [hbm] * 21,
        out_specs=[hbm] * 2 + [vmem] * 19,
        out_shape=[like(block_out), like(input_grad), jax.ShapeDtypeStruct((1, 1), F32)]
        + [like(a) for a in masters for _ in range(3)],
        scratch_shapes=[pltpu.VMEM(a.shape, F32) for a in (*masters, *moments, grads)]
        + [pltpu.VMEM((2, *block_out.shape), F32), pltpu.SemaphoreType.DMA((23,))],
        compiler_params=pltpu.CompilerParams(vmem_limit_bytes=62 * 2**20),
        name="update",
    )(small, grads, block_out, input_grad, *masters, *moments)


def body(
    hidden_in, out_grad, attn_weight, out_weight, inner_weight, outer_weight, rel_bias, gains, lengths, table,
    attn_first, attn_second, out_first, out_second, inner_first, inner_second, outer_first, outer_second,
    rel_first, rel_second, gain_first, gain_second, *, parts,
):
    near_table = table[SEQLEN - 2 * LANES : SEQLEN + 2 * LANES].reshape(1, 4 * LANES)
    block_out, input_grad, small, owned, _, _ = run_layer(
        lengths, attn_weight, out_weight, inner_weight, outer_weight.T, near_table, rel_bias.T, gains, hidden_in, out_grad
    )
    new = run_update(
        small, owned, block_out, input_grad,
        (attn_weight, out_weight, inner_weight, outer_weight.T, rel_bias.T, gains),
        (
            attn_first, attn_second, out_first, out_second, inner_first, inner_second,
            outer_first.T, outer_second.T, rel_first.T, rel_second.T, gain_first, gain_second,
        ),
    )
    masters = new[3:]
    return (
        new[0], new[1], new[2].reshape(()), *masters[:9], *(a.T for a in masters[9:12]), *(a.T for a in masters[12:15]), *masters[15:],
    )


def plain_corner_parts(tile, line, flags):
    before, same, after = near_parts(tile)
    first = (after - line[:, 3 * LANES : 3 * LANES + 1]) * flags[0]
    last = (before - line[:, LANES : LANES + 1]) * flags[1]
    return first, last


def plain_add_bias(scores, tile, line, flags, nq):
    parts = near_parts(tile)
    corner = plain_corner_parts(tile, line, flags)
    rows = []
    for jb in range(2 * nq):
        row = []
        for ib in range(nq):
            block = scores[jb * LANES : (jb + 1) * LANES, ib * LANES : (ib + 1) * LANES]
            if jb < nq and abs(jb - ib) <= 1:
                block = block + parts[jb - ib + 1]
            elif jb == nq and ib == nq - 1:
                block = block + corner[0]
            elif jb == 2 * nq - 1 and ib == 0:
                block = block + corner[1]
            row.append(block)
        rows.append(jnp.concatenate(row, axis=1))
    return rows


def plain_query_aug(qaug, i, nq):
    rows = qaug.shape[0]
    return jnp.concatenate(
        [jnp.broadcast_to(qaug[i * nq + ib : i * nq + ib + 1, :], (LANES, LANES)) for ib in range(nq)], axis=0
    )


def forward_kernel(
    x_ref, xo_ref, w_ref, line_ref, qaug_ref, kaug_ref, hidden_ref,
    own_ref, oth_ref, ctx_ref, lse_ref, middle_ref,
    acc, s_ref, e_ref,
):
    m = pl.program_id(0)
    tokens = x_ref.shape[0]
    nq = tokens // LANES
    x, xo = x_ref[...], xo_ref[...]
    p_a = mm(x, w_ref[:, : 3 * LANES]).astype(BF16)
    p_b = mm(x, w_ref[:, 4 * LANES :]).astype(BF16)
    o_a = mm(xo, w_ref[:, LANES : 3 * LANES]).astype(BF16)
    o_b = mm(xo, w_ref[:, 4 * LANES :]).astype(BF16)
    own_ref[0, :, : 3 * LANES] = p_a
    own_ref[0, :, 3 * LANES :] = p_b
    oth_ref[0, :, : 2 * LANES] = o_a
    oth_ref[0, :, 2 * LANES :] = o_b
    cols_own = {0: p_a[:, :LANES], 1: p_a[:, LANES : 2 * LANES], 2: p_a[:, 2 * LANES :], 4: p_b[:, :LANES], 5: p_b[:, LANES:]}
    cols_oth = {1: o_a[:, :LANES], 2: o_a[:, LANES:], 4: o_b[:, :LANES], 5: o_b[:, LANES:]}
    both = {c: jnp.concatenate([cols_own[c], cols_oth[c]], axis=0) for c in (1, 2, 4, 5)}
    masks = [half_rows(0), half_rows(1)]
    flags = (line_ref[0, 3:4, :LANES], line_ref[0, 4:5, :LANES])
    v_t = {2: both[2].T, 4: both[4].T}
    count = lax.broadcasted_iota(jnp.int32, (HDIM, 2 * tokens), 0)
    ones = (count == 0).astype(F32).astype(BF16)
    pieces = []
    stats = []
    for i, (qc, qh, kc, vc, vh) in enumerate(HEAD_AT):
        line = line_ref[0, i : i + 1, :]
        tile = bias_tile(line)
        qa = cols_own[qc] * masks[qh] + plain_query_aug(qaug_ref[0], i, nq) * masks[1 - qh]
        ka = both[kc] * masks[qh] + kaug_ref[...] * masks[1 - qh]
        scores = mt(ka, qa)
        peak = None
        for jb, row in enumerate(plain_add_bias(scores, tile, line, flags, nq)):
            s_ref[i, jb * LANES : (jb + 1) * LANES, :] = row
            top = jnp.max(row.reshape(LANES // 8, 8, tokens), axis=0)
            peak = top if peak is None else jnp.maximum(peak, top)
        peak = jnp.max(peak, axis=0, keepdims=True)
        for jb in range(2 * nq):
            rows = slice(jb * LANES, (jb + 1) * LANES)
            e_ref[i, rows, :] = jnp.exp(s_ref[i, rows, :] - peak).astype(BF16)
        if vh == 0:
            va = jnp.concatenate([v_t[vc][:HDIM], ones], axis=0)
        else:
            va = jnp.concatenate([ones, v_t[vc][HDIM:]], axis=0)
        ot = mm(va, e_ref[i])
        at = HDIM if vh == 0 else 0
        total = ot[at : at + 1, :]
        stats.append(peak + jnp.log(total))
        real = ot[:HDIM] if vh == 0 else ot[HDIM:]
        pieces.append(real / total)
    zero = jnp.zeros((HDIM, tokens), F32)
    ctx_a = jnp.concatenate([pieces[0], pieces[1]], axis=0).T.astype(BF16)
    ctx_b = jnp.concatenate([zero, pieces[2]], axis=0).T.astype(BF16)
    ctx_ref[0, :, :LANES] = ctx_a
    ctx_ref[0, :, LANES:] = ctx_b
    for i in range(3):
        lse_ref[0, i : i + 1, :] = stats[i]
    lse_ref[0, 3:8, :] = jnp.zeros((5, tokens), F32)
    part = mt(ctx_a, w_ref[:, 3 * LANES : 4 * LANES]) + mt(ctx_b, w_ref[:, 5 * LANES :])

    @pl.when(m == 0)
    def _():
        acc[...] = hidden_ref[...] + part

    @pl.when(m > 0)
    def _():
        acc[...] += part

    @pl.when(m == pl.num_programs(0) - 1)
    def _():
        middle_ref[...] = acc[...]


def feed_kernel(
    middle_ref, grad_ref, gain_ref, wi_ref, wo_ref,
    out_ref, back_ref, gain_grad_ref, gi_ref, go_ref,
    x2_ref, x2t_ref, ob_ref, obt_ref, acc_out, acc_two,
):
    f = pl.program_id(0)

    @pl.when(f == 0)
    def _():
        x2 = rms_scaled(middle_ref[...], gain_ref[1:2, :]).astype(BF16)
        x2_ref[...] = x2
        x2t_ref[...] = x2.T
        ob = grad_ref[...].astype(BF16)
        ob_ref[...] = ob
        obt_ref[...] = ob.T
        acc_out[...] = jnp.zeros_like(acc_out)
        acc_two[...] = jnp.zeros_like(acc_two)

    inner = mm(x2_ref[...], wi_ref[...])
    active_back = mm(ob_ref[...], wo_ref[...])
    c = 0.7978845608028654
    sq = inner * inner
    th = jnp.tanh(c * (inner + 0.044715 * (sq * inner)))
    half = 0.5 * (1.0 + th)
    active = (inner * half).astype(BF16)
    slope = half + (0.5 * c) * inner * (1.0 - th * th) * (1.0 + (3 * 0.044715) * sq)
    inner_back = (slope * active_back).astype(BF16)
    acc_out[...] += mt(active, wo_ref[...])
    acc_two[...] += mt(inner_back, wi_ref[...])
    go_ref[...] = mm(obt_ref[...], active).astype(go_ref.dtype)
    gi_ref[...] = mm(x2t_ref[...], inner_back).astype(gi_ref.dtype)

    @pl.when(f == pl.num_programs(0) - 1)
    def _():
        out_ref[...] = middle_ref[...] + acc_out[...]
        result, gain_part = rms_back(middle_ref[...], gain_ref[1:2, :], acc_two[...])
        back_ref[...] = grad_ref[...] + result
        gain_grad_ref[...] = jnp.broadcast_to(gain_part, gain_grad_ref.shape)


def backward_kernel(
    x_ref, xo_ref, back_ref, w_ref, line_ref, qaug_ref, kaug_ref, own_ref, oth_ref, ctx_ref, lse_ref,
    ga_ref, one_own_ref, one_oth_ref, near_ref, sums_ref,
    xt_ref, xot_ref, ab_ref, abt_ref, acc_own, acc_oth,
):
    m = pl.program_id(0)
    tokens = x_ref.shape[0]
    nq = tokens // LANES

    @pl.when(m == 0)
    def _():
        xt_ref[...] = x_ref[...].T
        xot_ref[...] = xo_ref[...].T
        ab = back_ref[...].astype(BF16)
        ab_ref[...] = ab
        abt_ref[...] = ab.T
        acc_own[...] = jnp.zeros_like(acc_own)
        acc_oth[...] = jnp.zeros_like(acc_oth)

    ab = ab_ref[...]
    cb = {2: mm(ab, w_ref[:, 3 * LANES : 4 * LANES]).astype(BF16), 4: mm(ab, w_ref[:, 5 * LANES :]).astype(BF16)}
    ctx = {2: ctx_ref[0, :, :LANES], 4: ctx_ref[0, :, LANES:]}
    own = {c: own_ref[0, :, at * LANES : (at + 1) * LANES] for at, c in enumerate((0, 1, 2, 4, 5))}
    oth = {c: oth_ref[0, :, at * LANES : (at + 1) * LANES] for at, c in enumerate((1, 2, 4, 5))}
    masks = [half_rows(0), half_rows(1)]
    flags = (line_ref[0, 3:4, :LANES], line_ref[0, 4:5, :LANES])
    prod = {c: cb[c].astype(F32) * ctx[c].astype(F32) for c in (2, 4)}
    prod_hi = {c: prod[c].astype(BF16) for c in prod}
    prod_lo = {c: (prod[c] - prod_hi[c].astype(F32)).astype(BF16) for c in prod}
    dq_t = []
    dk = {}
    dv = {}
    for i, (qc, qh, kc, vc, vh) in enumerate(HEAD_AT):
        line = line_ref[0, i : i + 1, :]
        tile = bias_tile(line)
        qm = own[qc] * masks[qh]
        qa = qm + plain_query_aug(qaug_ref[0], i, nq) * masks[1 - qh]
        om = cb[vc] * masks[vh]
        pick = jnp.broadcast_to(masks[vh], (8, LANES))
        center = (mt(pick, prod_hi[vc]) + mt(pick, prod_lo[vc]))[0:1, :]
        lse = lse_ref[0, i : i + 1, :]
        kaug = kaug_ref[...] * masks[1 - qh]
        dqt = None
        parts = near_parts(tile)
        corner = plain_corner_parts(tile, line, flags)
        near = [None, None, None, None, None]
        for side, cols in enumerate((own, oth)):
            ka = cols[kc] * masks[qh] + kaug[side * tokens : (side + 1) * tokens]
            scores = mt(ka, qa)
            chance_back = mt(cols[vc], om)
            ps, ds = [], []
            for jb in range(nq):
                row_s, row_p, row_d = [], [], []
                for ib in range(nq):
                    at = (slice(jb * LANES, (jb + 1) * LANES), slice(ib * LANES, (ib + 1) * LANES))
                    block = scores[at]
                    kind = None
                    if side == 0 and abs(jb - ib) <= 1:
                        block = block + parts[jb - ib + 1]
                        kind = jb - ib + 1
                    elif side == 1 and jb == 0 and ib == nq - 1:
                        block = block + corner[0]
                        kind = 3
                    elif side == 1 and jb == nq - 1 and ib == 0:
                        block = block + corner[1]
                        kind = 4
                    p = jnp.exp(block - lse[:, at[1]])
                    d = p * (chance_back[at] - center[:, at[1]])
                    if kind is not None:
                        near[kind] = d if near[kind] is None else near[kind] + d
                    row_p.append(p.astype(BF16))
                    row_d.append(d.astype(BF16))
                ps.append(jnp.concatenate(row_p, axis=1))
                ds.append(jnp.concatenate(row_d, axis=1))
            pb = jnp.concatenate(ps, axis=0)
            db = jnp.concatenate(ds, axis=0)
            part_v = mm(pb, om)
            part_k = mm(db, qm)
            dv[vc, side] = part_v if (vc, side) not in dv else dv[vc, side] + part_v
            dk[kc, side] = part_k if (kc, side) not in dk else dk[kc, side] + part_k
            part_q = mm(ka.T, db)
            dqt = part_q if dqt is None else dqt + part_q
        at = HDIM if qh == 0 else 0
        sums_ref[0, i * 8 : (i + 1) * 8, :] = dqt[at + 8 : at + 16, :]
        dq_t.append(dqt[:HDIM] if qh == 0 else dqt[HDIM:])
        for kind in range(5):
            near_ref[0, i, kind] = near[kind]
    dq_a = jnp.concatenate([dq_t[0], dq_t[1]], axis=0).T
    dq_b = jnp.concatenate([dq_t[2], jnp.zeros_like(dq_t[2])], axis=0).T
    d_own = jnp.concatenate([dq_a, dk[1, 0], dv[2, 0], dq_b + dv[4, 0], dk[5, 0]], axis=1).astype(BF16)
    d_oth = jnp.concatenate([dk[1, 1], dv[2, 1], dv[4, 1], dk[5, 1]], axis=1).astype(BF16)
    xt, xot, abt = xt_ref[...], xot_ref[...], abt_ref[...]
    g_own = mm(xt, d_own)
    g_oth = mm(xot, d_oth)
    g_ctx = mm(abt, ctx_ref[0])
    ga_ref[:, :LANES] = g_own[:, :LANES].astype(ga_ref.dtype)
    ga_ref[:, LANES : 3 * LANES] = (g_own[:, LANES : 3 * LANES] + g_oth[:, : 2 * LANES]).astype(ga_ref.dtype)
    ga_ref[:, 3 * LANES : 4 * LANES] = g_ctx[:, :LANES].astype(ga_ref.dtype)
    ga_ref[:, 4 * LANES : 5 * LANES] = (g_own[:, 3 * LANES : 4 * LANES] + g_oth[:, 2 * LANES : 3 * LANES]).astype(ga_ref.dtype)
    ga_ref[:, 5 * LANES :] = (g_own[:, 4 * LANES :] + g_oth[:, 3 * LANES :] + g_ctx[:, LANES:]).astype(ga_ref.dtype)
    acc_own[...] += mt(d_own[:, : 3 * LANES], w_ref[:, : 3 * LANES]) + mt(d_own[:, 3 * LANES :], w_ref[:, 4 * LANES :])
    acc_oth[...] += mt(d_oth[:, : 2 * LANES], w_ref[:, LANES : 3 * LANES]) + mt(d_oth[:, 2 * LANES :], w_ref[:, 4 * LANES :])

    @pl.when(m == pl.num_programs(0) - 1)
    def _():
        one_own_ref[...] = acc_own[...]
        one_oth_ref[...] = acc_oth[...].astype(one_oth_ref.dtype)


def whole(shape):
    return pl.BlockSpec(shape, lambda m: (0,) * len(shape))


def params():
    return pltpu.CompilerParams(vmem_limit_bytes=60 * 2**20)


def run_forward(x, xo, wa, line, qaug, kaug, hidden, parts):
    t, d = x.shape
    return pl.pallas_call(
        forward_kernel,
        grid=(parts,),
        in_specs=[
            whole((t, d)), whole((t, d)),
            pl.BlockSpec((d, 6 * LANES), lambda m: (0, m)),
            pl.BlockSpec((1, 8, 4 * LANES), lambda m: (m, 0, 0)),
            pl.BlockSpec((1, 16, LANES), lambda m: (m, 0, 0)),
            whole((2 * t, LANES)), whole((t, d)),
        ],
        out_specs=[
            pl.BlockSpec((1, t, 5 * LANES), lambda m: (m, 0, 0)),
            pl.BlockSpec((1, t, 4 * LANES), lambda m: (m, 0, 0)),
            pl.BlockSpec((1, t, 2 * LANES), lambda m: (m, 0, 0)),
            pl.BlockSpec((1, 8, t), lambda m: (m, 0, 0)),
            whole((t, d)),
        ],
        out_shape=[
            jax.ShapeDtypeStruct((parts, t, 5 * LANES), BF16),
            jax.ShapeDtypeStruct((parts, t, 4 * LANES), BF16),
            jax.ShapeDtypeStruct((parts, t, 2 * LANES), BF16),
            jax.ShapeDtypeStruct((parts, 8, t), F32),
            jax.ShapeDtypeStruct((t, d), F32),
        ],
        scratch_shapes=[
            pltpu.VMEM((t, d), F32),
            pltpu.VMEM((3, 2 * t, t), F32),
            pltpu.VMEM((3, 2 * t, t), BF16),
        ],
        compiler_params=params(),
        name="attend_forward",
    )(x, xo, wa, line, qaug, kaug, hidden)


def run_feed(middle, grad, gains, wi, wo):
    t, d = middle.shape
    units = wi.shape[1]
    tile = min(512, units)
    return pl.pallas_call(
        feed_kernel,
        grid=(units // tile,),
        in_specs=[
            whole((t, d)), whole((t, d)), whole((2, d)),
            pl.BlockSpec((d, tile), lambda f: (0, f)),
            pl.BlockSpec((d, tile), lambda f: (0, f)),
        ],
        out_specs=[
            whole((t, d)), whole((t, d)), whole((8, d)),
            pl.BlockSpec((d, tile), lambda f: (0, f)),
            pl.BlockSpec((d, tile), lambda f: (0, f)),
        ],
        out_shape=[
            jax.ShapeDtypeStruct((t, d), F32),
            jax.ShapeDtypeStruct((t, d), F32),
            jax.ShapeDtypeStruct((8, d), F32),
            jax.ShapeDtypeStruct((d, units), BF16),
            jax.ShapeDtypeStruct((d, units), BF16),
        ],
        scratch_shapes=[
            pltpu.VMEM((t, d), BF16), pltpu.VMEM((d, t), BF16),
            pltpu.VMEM((t, d), BF16), pltpu.VMEM((d, t), BF16),
            pltpu.VMEM((t, d), F32), pltpu.VMEM((t, d), F32),
        ],
        compiler_params=params(),
        name="feed_both",
    )(middle, grad, gains, wi, wo)


def run_backward(x, xo, back, wa, line, qaug, kaug, own, oth, ctx, lse, parts):
    t, d = x.shape
    return pl.pallas_call(
        backward_kernel,
        grid=(parts,),
        in_specs=[
            whole((t, d)), whole((t, d)), whole((t, d)),
            pl.BlockSpec((d, 6 * LANES), lambda m: (0, m)),
            pl.BlockSpec((1, 8, 4 * LANES), lambda m: (m, 0, 0)),
            pl.BlockSpec((1, 16, LANES), lambda m: (m, 0, 0)),
            whole((2 * t, LANES)),
            pl.BlockSpec((1, t, 5 * LANES), lambda m: (m, 0, 0)),
            pl.BlockSpec((1, t, 4 * LANES), lambda m: (m, 0, 0)),
            pl.BlockSpec((1, t, 2 * LANES), lambda m: (m, 0, 0)),
            pl.BlockSpec((1, 8, t), lambda m: (m, 0, 0)),
        ],
        out_specs=[
            pl.BlockSpec((d, 6 * LANES), lambda m: (0, m)),
            whole((t, d)), whole((t, d)),
            pl.BlockSpec((1, 3, 5, LANES, LANES), lambda m: (m, 0, 0, 0, 0)),
            pl.BlockSpec((1, 24, t), lambda m: (m, 0, 0)),
        ],
        out_shape=[
            jax.ShapeDtypeStruct((d, parts * 6 * LANES), BF16),
            jax.ShapeDtypeStruct((t, d), F32),
            jax.ShapeDtypeStruct((t, d), BF16),
            jax.ShapeDtypeStruct((parts, 3, 5, LANES, LANES), F32),
            jax.ShapeDtypeStruct((parts, 24, t), F32),
        ],
        scratch_shapes=[
            pltpu.VMEM((d, t), BF16), pltpu.VMEM((d, t), BF16),
            pltpu.VMEM((t, d), BF16), pltpu.VMEM((d, t), BF16),
            pltpu.VMEM((t, d), F32), pltpu.VMEM((t, d), F32),
        ],
        compiler_params=params(),
        name="attend_backward",
    )(x, xo, back, wa, line, qaug, kaug, own, oth, ctx, lse)


def pack_attn(attn, out_t):
    cut = [[part[:, i * HDIM : (i + 1) * HDIM] for i in range(3)] for part in (attn[0], attn[1], attn[2], out_t)]
    q, k, v, o = cut
    return jnp.concatenate([q[0], q[1], k[0], k[1], v[0], v[1], o[0], o[1], q[2], v[2], k[2], o[2]], axis=1)


def unpack_attn(block):
    c = [block[:, i * HDIM : (i + 1) * HDIM] for i in range(12)]
    attn = jnp.stack(
        [
            jnp.concatenate([c[0], c[1], c[8]], axis=1),
            jnp.concatenate([c[2], c[3], c[10]], axis=1),
            jnp.concatenate([c[4], c[5], c[9]], axis=1),
        ]
    )
    return attn, jnp.concatenate([c[6], c[7], c[11]], axis=1)


def general_body(
    hidden_in, out_grad, attn_weight, out_weight, inner_weight, outer_weight, rel_bias, gains, lengths, table,
    attn_first, attn_second, out_first, out_second, inner_first, inner_second, outer_first, outer_second,
    rel_first, rel_second, gain_first, gain_second, *, parts,
):
    tokens = hidden_in.shape[0]
    nq = tokens // LANES
    heads = rel_bias.shape[1]
    per_seq = SEQLEN // tokens
    mp_index = lax.axis_index("mp")
    half = mp_index % per_seq
    length = lengths[mp_index // per_seq]

    shard = [
        pack_attn(attn_weight.astype(BF16), out_weight.astype(BF16).T),
        inner_weight.astype(BF16),
        outer_weight.astype(BF16).T,
    ]
    gathered = [lax.all_gather(lax.all_gather(s, "dp", axis=0, tiled=True), "mp", axis=1, tiled=True) for s in shard]
    wa, wi, wo = gathered

    x1 = rms_scaled(hidden_in, gains[0]).astype(BF16)
    swap = [(p, p ^ 1) for p in range(parts)]
    x1o = lax.ppermute(x1, "mp", swap)

    u = jnp.arange(4 * LANES)
    offset = jnp.where(u < 2 * LANES, -u, 4 * LANES - u)
    buckets = jnp.arange(rel_bias.shape[0], dtype=jnp.int32)
    line_hot = (jnp.take(table, offset + SEQLEN - 1)[:, None] == buckets[None, :]).astype(F32)
    line = jnp.dot(line_hot, rel_bias, precision=lax.Precision.HIGHEST).T.reshape(parts, heads // parts, 4 * LANES)
    first_flag = (half == 0).astype(F32)
    flags = jnp.stack([jnp.full((4 * LANES,), first_flag), jnp.full((4 * LANES,), 1.0 - first_flag)])
    line_in = jnp.concatenate(
        [line, jnp.broadcast_to(flags[None], (parts, 2, 4 * LANES)), jnp.zeros((parts, 3, 4 * LANES), F32)], axis=1
    )
    far_before, far_after = line[:, :, LANES], line[:, :, 3 * LANES]
    jb, ib = jnp.arange(nq)[None, :], jnp.arange(nq)[:, None]
    own_before, own_after = (jb < ib - 1).astype(F32), (jb > ib + 1).astype(F32)
    oth_before = jnp.full((nq, nq), 1.0 - first_flag)
    w_before = jnp.concatenate([own_before, oth_before], axis=1)
    w_after = jnp.concatenate([own_after, 1.0 - oth_before], axis=1)
    far = far_before[:, :, None, None] * w_before + far_after[:, :, None, None] * w_after
    far_hi = far.astype(BF16).astype(F32)
    far_lo = far - far_hi
    one = jnp.ones((parts, heads // parts, nq, 1), F32)
    blank = jnp.zeros((parts, heads // parts, nq, HDIM), F32)
    q64 = jnp.concatenate(
        [blank[..., :3], one, blank[..., :4], far_hi, far_lo, blank[..., : HDIM - 8 - 4 * nq]], axis=-1
    )
    qaug = jnp.concatenate([q64, q64], axis=-1).reshape(parts, 3 * nq, LANES)
    qaug = jnp.pad(qaug, ((0, 0), (0, 16 - 3 * nq), (0, 0))).astype(BF16)
    row = jnp.arange(2 * tokens)
    position = jnp.where(row < tokens, half * tokens + row, (1 - half) * tokens + row - tokens)
    masked = jnp.where(position < length, 0.0, NEG)
    col = jnp.arange(LANES) % HDIM
    block_of = row // LANES
    hot = ((col >= 8) & (col < 8 + 4 * nq))[None, :] & ((col[None, :] - 8) % (2 * nq) == block_of[:, None])
    kaug = jnp.where((col == 3)[None, :], masked[:, None], hot.astype(F32)).astype(BF16)

    own, oth, ctx, lse, middle = run_forward(x1, x1o, wa, line_in, qaug, kaug, hidden_in, parts)
    block_out, middle_back, gain_two, gi, go = run_feed(middle, out_grad, gains, wi, wo)
    ga, one_own, one_oth, near, sums = run_backward(
        x1, x1o, middle_back, wa, line_in, qaug, kaug, own, oth, ctx, lse, parts
    )
    one_back = one_own + lax.ppermute(one_oth, "mp", swap).astype(F32)
    input_grad, gain_one = rms_back(hidden_in, gains[0:1], one_back)
    input_grad = input_grad + middle_back

    nh = heads // parts
    near = near.reshape(heads, 5, LANES, LANES)
    first_w = first_flag
    blocks = jnp.stack(
        [near[:, 0] + near[:, 4] * (1.0 - first_w), near[:, 1], near[:, 2] + near[:, 3] * first_w], axis=1
    )
    r = jnp.arange(LANES)
    diff = r[None, :, None] - r[None, None, :] + (jnp.arange(3) - 1)[:, None, None] * LANES
    near_bucket = jnp.take(table, diff + SEQLEN - 1).reshape(1, -1)
    near_hot = (near_bucket == buckets[:, None]).astype(F32)
    near_grad = lax.dot_general(
        near_hot, blocks.reshape(heads, -1), (((1,), (1,)), ((), ())), precision=lax.Precision.HIGHEST
    )
    block_sums = jnp.sum(sums.reshape(heads, 2 * nq, nq, LANES), axis=-1)
    far_w = jnp.transpose(jnp.stack([w_before, w_after]), (0, 2, 1))
    corner = jnp.stack([jnp.sum(near[:, 4], (1, 2)) * (1.0 - first_w), jnp.sum(near[:, 3], (1, 2)) * first_w])
    far_grad = jnp.einsum("hji,sji->sh", block_sums, far_w, precision=lax.Precision.HIGHEST) - corner
    far_hot = (jnp.stack([table[0], table[2 * SEQLEN - 2]])[None, :] == buckets[:, None]).astype(F32)
    rel_part = near_grad + jnp.dot(far_hot, far_grad, precision=lax.Precision.HIGHEST)

    owned = [
        lax.psum_scatter(
            lax.psum_scatter(g, "mp", scatter_dimension=1, tiled=True), "dp", scatter_dimension=0, tiled=True
        ).astype(F32)
        for g in (ga, gi, go)
    ]
    g_attn, g_out_t = unpack_attn(owned[0])
    grads = (g_attn, g_out_t.T, owned[1], owned[2].T)
    square_part = sum(jnp.sum(g * g) for g in owned)
    gain_grad, rel_grad, square_total = lax.psum(
        (jnp.concatenate([gain_one, gain_two[:1]], axis=0), rel_part, square_part), ("dp", "mp")
    )
    grad_norm = jnp.sqrt(square_total + jnp.sum(gain_grad * gain_grad) + jnp.sum(rel_grad * rel_grad))
    factor = jnp.minimum(1.0, CLIP / (grad_norm + 1e-06))
    attn_new = adam_step(attn_weight, grads[0], attn_first, attn_second, factor, RATE_MATRIX)
    out_new = adam_step(out_weight, grads[1], out_first, out_second, factor, RATE_OUT)
    inner_new = adam_step(inner_weight, grads[2], inner_first, inner_second, factor, RATE_MATRIX)
    outer_new = adam_step(outer_weight, grads[3], outer_first, outer_second, factor, RATE_MATRIX)
    rel_new = adam_step(rel_bias, rel_grad, rel_first, rel_second, factor, RATE_SMALL)
    gain_new = adam_step(gains, gain_grad, gain_first, gain_second, factor, RATE_SMALL)
    return (block_out, input_grad, grad_norm, *attn_new, *out_new, *inner_new, *outer_new, *rel_new, *gain_new)


def solution(mesh):
    rows = P(("dp", "mp"), None)
    attn, up, down = P(None, "dp", "mp"), P("dp", "mp"), P("mp", "dp")
    in_specs = (
        rows, rows, attn, down, up, down, P(), P(), P("dp"), P(),
        attn, attn, down, down, up, up, down, down, P(), P(), P(), P(),
    )
    out_specs = (rows, rows, P()) + (attn,) * 3 + (down,) * 3 + (up,) * 3 + (down,) * 3 + (P(),) * 6
    plan = body if (mesh.shape["dp"], mesh.shape["mp"]) == (8, 4) else general_body
    return jax.shard_map(
        functools.partial(plan, parts=mesh.shape["mp"]),
        mesh=mesh, in_specs=in_specs, out_specs=out_specs, check_vma=False,
    )
```

```python
import functools

import jax
import jax.numpy as jnp
from jax import lax
from jax.experimental import pallas as pl
from jax.experimental.pallas import tpu as pltpu
from jax.sharding import PartitionSpec as P

HDIM = 64
SEQLEN = 1024
STEP = 10
NORM_EPS = 1e-06
CLIP = 1.0
BETA_ONE = 0.9
BETA_TWO = 0.999
ADAM_EPS = 1e-08
DECAY = 0.01
RATE_MATRIX = 0.05
RATE_OUT = 0.6
RATE_SMALL = 1.0

F32 = jnp.float32
BF16 = jnp.bfloat16
LANES = 128
NEG = -1e30
MESH = pl.DeviceIdType.MESH

HEAD_AT = ((0, 0, 1, 2, 0), (0, 1, 1, 2, 1), (4, 0, 5, 4, 1))


def mm(a, b):
    return lax.dot_general(a, b, (((1,), (0,)), ((), ())), preferred_element_type=F32)


def mt(a, b):
    return lax.dot_general(a, b, (((1,), (1,)), ((), ())), preferred_element_type=F32)


def rms_scaled(value, gain):
    return value * lax.rsqrt(jnp.mean(value * value, axis=-1, keepdims=True) + NORM_EPS) * gain


def rms_back(value, gain, grad):
    factor = lax.rsqrt(jnp.mean(value * value, axis=-1, keepdims=True) + NORM_EPS)
    unit = value * factor
    gain_part = jnp.sum(grad * unit, axis=0, keepdims=True)
    scaled = grad * gain
    result = factor * (scaled - unit * jnp.mean(scaled * unit, axis=-1, keepdims=True))
    return (result, gain_part)


def adam_step(master, grad, first, second, factor, rate):
    clipped = grad * factor
    first_new = BETA_ONE * first + (1.0 - BETA_ONE) * clipped
    second_new = BETA_TWO * second + (1.0 - BETA_TWO) * clipped * clipped
    first_hat = first_new / (1.0 - BETA_ONE**STEP)
    second_hat = second_new / (1.0 - BETA_TWO**STEP)
    master_new = master - rate * (first_hat / (jnp.sqrt(second_hat) + ADAM_EPS) + DECAY * master)
    return (master_new, first_new, second_new)


def half_rows(half):
    lane = lax.broadcasted_iota(jnp.int32, (1, LANES), 1)
    keep = (lane < HDIM) if half == 0 else (lane >= HDIM)
    return keep.astype(F32).astype(BF16)


def bias_tile(line):
    wide = jnp.broadcast_to(line, (LANES, 4 * LANES))
    return pltpu.roll(wide, 0, 1, stride=1, stride_axis=0)


def near_parts(tile):
    return tile[:, LANES : 2 * LANES], tile[:, :LANES], tile[:, 3 * LANES :]


def corner_parts(tile, line, flags):
    before, same, after = near_parts(tile)
    first = (after - line[:, 3 * LANES : 3 * LANES + 1]) * flags
    last = (before - line[:, LANES : LANES + 1]) * (1.0 - flags)
    return first, last


def add_bias(scores, tile, line, flags, nq):
    parts = near_parts(tile)
    corner = corner_parts(tile, line, flags)
    rows = []
    for jb in range(2 * nq):
        row = []
        for ib in range(nq):
            block = scores[jb * LANES : (jb + 1) * LANES, ib * LANES : (ib + 1) * LANES]
            if jb < nq and abs(jb - ib) <= 1:
                block = block + parts[jb - ib + 1]
            elif jb == nq and ib == nq - 1:
                block = block + corner[0]
            elif jb == 2 * nq - 1 and ib == 0:
                block = block + corner[1]
            row.append(block)
        rows.append(jnp.concatenate(row, axis=1))
    return rows


def far_masks(first, nq):
    lane = lax.broadcasted_iota(jnp.int32, (8, LANES), 1) % HDIM
    ib = lax.broadcasted_iota(jnp.int32, (8, LANES), 0)
    jb = (lane - 8) % (2 * nq)
    coded = (lane >= 8) & (lane < 8 + 4 * nq)
    own_before = (coded & (jb < nq) & (jb < ib - 1)).astype(F32)
    own_after = (coded & (jb < nq) & (jb > ib + 1)).astype(F32)
    other = (coded & (jb >= nq)).astype(F32)
    high = (lane < 8 + 2 * nq).astype(F32)
    return own_before + other * (1.0 - first), own_after + other * first, high, (lane == 3).astype(F32)


def query_aug(line, masks, nq):
    before, after, high, one = masks
    far = line[:, LANES : LANES + 1] * before + line[:, 3 * LANES : 3 * LANES + 1] * after
    top = far.astype(BF16).astype(F32)
    rows = (high * top + (1.0 - high) * (far - top) + one).astype(BF16)
    return jnp.concatenate([jnp.broadcast_to(rows[ib : ib + 1, :], (LANES, LANES)) for ib in range(nq)], axis=0)


def turned_hot(table, origin):
    size = 4 * LANES
    hot = (lax.broadcasted_iota(jnp.int32, (LANES, size), 0) == table).astype(F32).astype(BF16)
    at = lax.broadcasted_iota(jnp.int32, (size, size), 0) + lax.broadcasted_iota(jnp.int32, (size, size), 1)
    turn = ((at == origin) | (at == origin + size)).astype(F32).astype(BF16)
    return mm(hot, turn).astype(BF16)


def key_aug(half, length, tokens):
    row = lax.broadcasted_iota(jnp.int32, (2 * tokens, LANES), 0)
    lane = lax.broadcasted_iota(jnp.int32, (2 * tokens, LANES), 1) % HDIM
    position = jnp.where(row < tokens, half * tokens + row, row - half * tokens)
    blocks = 2 * tokens // LANES
    hot = (lane >= 8) & (lane < 8 + 2 * blocks) & ((lane - 8) % blocks == row // LANES)
    masked = (lane == 3) & (position >= length)
    return jnp.where(masked, NEG, hot.astype(F32)).astype(BF16)


def peer(index, stride):
    return index + stride - 2 * stride * ((index // stride) % 2)


class Links:
    def __init__(self):
        self.dp = lax.axis_index("dp")
        self.mp = lax.axis_index("mp")
        self.core = self.dp % 2
        self.chip = self.dp // 2
        self.dp_x, self.dp_y, self.dp_s = peer(self.dp, 2), peer(self.dp, 4), peer(self.dp, 1)
        self.dp_d = peer(self.dp_x, 4)
        self.at_x, self.at_y, self.at_s = (self.dp_x, self.mp), (self.dp_y, self.mp), (self.dp_s, self.mp)
        z1, z2 = peer(self.mp, 1), peer(self.mp, 2)
        self.half = self.mp % 2
        self.first = (1 - self.half).astype(F32)
        self.at_z = (None, (self.dp, z1), (self.dp, z2), (self.dp, peer(z1, 2)))

    def column(self, s):
        return (self.mp + s) % 2 + 2 * ((self.mp // 2 + s // 2) % 2)

    def meet(self, more=()):
        barrier = pltpu.get_barrier_semaphore()
        others = (self.at_x, self.at_y, self.at_s) + self.at_z[1:] + tuple(more)
        for other in others:
            pl.semaphore_signal(barrier, inc=1, device_id=other, device_id_type=MESH)
        pl.semaphore_wait(barrier, len(others))


def remote(src, dst, send, recv, to):
    return pltpu.make_async_remote_copy(
        src_ref=src, dst_ref=dst, send_sem=send, recv_sem=recv, device_id=to, device_id_type=MESH
    )


class Gather:
    def __init__(self, links, w, send, recv, zsend, zrecv):
        self.k, self.w, self.send, self.recv, self.zsend, self.zrecv = links, w, send, recv, zsend, zrecv
        self.rows = w.shape[3]

    def block(self, unit, dp, lo=0, n=None):
        group, s = unit
        return self.w.at[group, s, dp] if n is None else self.w.at[group, s, dp, pl.ds(lo, n)]

    def copy(self, unit, kind, ref, to):
        at = unit[0] * 4 + unit[1]
        return remote(ref, ref, self.send.at[at, kind], self.recv.at[at, kind], to)

    def outgoing(self, unit, kind):
        k, half = self.k, self.rows // 2
        dp, lo, n, to = (
            (k.dp, 0, None, k.at_x),
            (k.dp, 0, None, k.at_y),
            (k.dp, 0, None, k.at_s),
            (k.dp_x, 0, half, k.at_y),
            (k.dp_x, 0, None, k.at_s),
            (k.dp_y, half, half, k.at_x),
            (k.dp_y, 0, None, k.at_s),
            (k.dp_d, 0, None, k.at_s),
        )[kind]
        return self.copy(unit, kind, self.block(unit, dp, lo, n), to)

    def arrived(self, unit, kind):
        k, half = self.k, self.rows // 2
        sib = k.dp_s
        dp, lo, n = {
            0: (k.dp_x, 0, None),
            1: (k.dp_y, 0, None),
            2: (sib, 0, None),
            3: (k.dp_d, 0, half),
            4: (peer(sib, 2), 0, None),
            5: (k.dp_d, half, half),
            6: (peer(sib, 4), 0, None),
            7: (peer(peer(sib, 2), 4), 0, None),
        }[kind]
        self.copy(unit, kind, self.block(unit, dp, lo, n), k.at_x).wait_recv()

    def z_copy(self, group, s):
        at = group * 3 + s - 1
        src = self.block((group, 0), self.k.dp)
        dst = self.block((group, s), self.k.dp)
        return remote(src, dst, self.zsend.at[at], self.zrecv.at[at], self.k.at_z[s])

    def z_arrived(self, unit):
        at = unit[0] * 3 + unit[1] - 1
        ref = self.block(unit, self.k.dp)
        remote(ref, ref, self.zsend.at[at], self.zrecv.at[at], self.k.at_x).wait_recv()

    def run(self, ops):
        for op in ops:
            (self.s1, self.s2, self.s3, self.s4)[op // 16 - 1](UNITS[op % 16])

    def at(self, loop, step, place):
        for number in range(4):
            ops = GATHER_PLAN.get((loop, number), {}).get(place)
            if ops:
                pl.when(step == number)(functools.partial(self.run, ops))

    def s1(self, unit):
        if unit[1] > 0:
            self.z_arrived(unit)
        for kind in (0, 1, 2):
            self.outgoing(unit, kind).start()

    def s2(self, unit):
        self.arrived(unit, 0)
        for kind in (3, 4):
            self.outgoing(unit, kind).start()
        self.arrived(unit, 1)
        for kind in (5, 6):
            self.outgoing(unit, kind).start()

    def s3(self, unit):
        self.arrived(unit, 3)
        self.arrived(unit, 5)
        self.outgoing(unit, 7).start()

    def s4(self, unit):
        for kind in (2, 4, 6, 7):
            self.arrived(unit, kind)

    def finish(self):
        def each(at, carry):
            for kind in range(8):
                self.outgoing((at // 4, at % 4), kind).wait_send()
            return carry

        lax.fori_loop(0, 12, each, 0)
        for group in (1, 2):
            for s in (1, 2, 3):
                self.z_copy(group, s).wait_send()


UNITS = ((0, 0), (1, 0), (2, 0), (0, 1), (0, 2), (0, 3), (1, 1), (2, 1), (1, 2), (2, 2), (1, 3), (2, 3))
GATHER_AHEAD = (
    (0x11, 0x12, 0x20, 0x13, 0x30),
    (0x21, 0x14, 0x40, 0x31, 0x22, 0x15, 0x41, 0x32, 0x23, 0x42, 0x33, 0x24, 0x43),
)
GATHER_PLAN = {
    ("attend", 0): {0: (0x34, 0x25), 2: (0x44,), 3: (0x16,)},
    ("attend", 1): {0: (0x35, 0x17), 3: (0x45, 0x26)},
    ("attend", 2): {0: (0x18,), 1: (0x36,), 3: (0x27, 0x46, 0x19)},
    ("attend", 3): {0: (0x37, 0x28, 0x1a), 3: (0x47,)},
    ("feed", 0): {0: (0x38,), 1: (0x29,), 2: (0x1b, 0x48)},
    ("feed", 1): {0: (0x39,), 1: (0x2a,), 2: (0x49,)},
    ("feed", 2): {0: (0x3a,), 1: (0x2b,), 2: (0x4a,)},
    ("feed", 3): {0: (0x3b,), 3: (0x4b,)},
}


class Scatter:
    def __init__(self, links, sources, w, sums, piece, diag, side, final, result, send, recv, psem):
        self.k, self.sources, self.w, self.piece, self.final, self.result = links, sources, w, piece, final, result
        self.sums_room, self.diag_room, self.side_room = sums, diag, side
        self.send, self.recv, self.psem = send, recv, psem
        self.rows = w.shape[3]
        chip = links.chip
        self.chips = (chip, peer(chip, 1), peer(chip, 2), peer(peer(chip, 1), 2))

    def sums(self, u):
        return self.sums_room.at[u] if u < 8 else self.w.at[1, u - 8, pl.ds(0, 4)]

    def side(self, u, n):
        return self.side_room.at[u, n] if u < 8 else self.w.at[1, u - 8, 4 + n]

    def diag(self, u, n):
        half = self.rows // 2
        return self.diag_room.at[u, n] if u < 8 else self.w.at[1, u - 8, 6, pl.ds(n * half, half)]

    def outgoing(self, u, kind):
        group, s = BACK_UNITS[u]
        k, half = self.k, self.rows // 2
        at, at_x, at_y, at_d = self.chips
        sums = self.sums(u)
        if kind == 0:
            src, dst, to = self.sources[group].at[s, :, 1 - k.core], sums, k.at_s
        elif kind == 1:
            src, dst, to = sums.at[at_d, pl.ds(0, half)], self.diag(u, 0), k.at_x
        elif kind == 2:
            src, dst, to = sums.at[at_d, pl.ds(half, half)], self.diag(u, 1), k.at_y
        elif kind == 3:
            src, dst, to = sums.at[at_x], self.side(u, 0), k.at_x
        elif kind == 4:
            src, dst, to = sums.at[at_y], self.side(u, 1), k.at_y
        else:
            src, dst, to = sums.at[at], self.final.at[group, s - 1], k.at_z[s]
        return remote(src, dst, self.send.at[u, kind], self.recv.at[u, kind], to)

    def local(self, u):
        group, s = BACK_UNITS[u]
        return pltpu.make_async_copy(self.sources[group].at[s, :, self.k.core], self.piece.at[u % 3], self.psem.at[u % 3])

    def s1(self, u):
        self.outgoing(u, 0).start()
        self.local(u).start()

    def s2(self, u):
        self.local(u).wait()
        self.outgoing(u, 0).wait_recv()
        sums, far = self.sums(u), self.chips[3]
        sums[far] = sums[far] + self.piece[u % 3, far]
        self.outgoing(u, 1).start()
        self.outgoing(u, 2).start()
        for chip in self.chips[:3]:
            sums[chip] = sums[chip] + self.piece[u % 3, chip]

    def s3(self, u):
        half, sums = self.rows // 2, self.sums(u)
        self.outgoing(u, 1).wait_recv()
        self.outgoing(u, 2).wait_recv()
        for chip, lo, n in ((self.chips[2], 0, 0), (self.chips[1], half, 1)):
            sums[chip, lo : lo + half] = sums[chip, lo : lo + half] + self.diag(u, n)[...]
        self.outgoing(u, 3).start()
        self.outgoing(u, 4).start()

    def s4(self, u):
        group, s = BACK_UNITS[u]
        self.outgoing(u, 3).wait_recv()
        self.outgoing(u, 4).wait_recv()
        at, sums = self.chips[0], self.sums(u)
        total = sums[at].astype(F32) + (self.side(u, 0)[...].astype(F32) + self.side(u, 1)[...].astype(F32))
        if s == 0:
            self.result[group] = total
        else:
            sums[at] = total.astype(BF16)
            self.outgoing(u, 5).start()

    def last(self, group):
        total = self.result[group]
        for u, (other, s) in enumerate(BACK_UNITS):
            if other == group and s > 0:
                self.outgoing(u, 5).wait_recv()
        for n in range(3):
            total = total + self.final[group, n].astype(F32)
        self.result[group] = total

    def run(self, ops):
        for op in ops:
            (self.s1, self.s2, self.s3, self.s4)[op // 16 - 1](op % 16)

    def at(self, loop, step, place):
        for number in range(4):
            ops = SCATTER_PLAN.get((loop, number), {}).get(place)
            if ops:
                pl.when(step == number)(functools.partial(self.run, ops))

    def finish(self):
        for u, (group, s) in enumerate(BACK_UNITS):
            for kind in range(5 if s == 0 else 6):
                self.outgoing(u, kind).wait_send()


BACK_UNITS = ((1, 0), (2, 0), (1, 1), (2, 1), (1, 2), (2, 2), (1, 3), (2, 3), (0, 3), (0, 2), (0, 1), (0, 0))
SCATTER_PLAN = {
    ("feed", 1): {1: (0x10, 0x11)},
    ("feed", 2): {0: (0x20, 0x21), 1: (0x12, 0x13)},
    ("feed", 3): {0: (0x30, 0x31, 0x22, 0x23), 1: (0x14, 0x15)},
    ("other", 0): {0: (0x32, 0x33, 0x24, 0x25, 0x41, 0x17)},
    ("other", 1): {0: (0x42,)},
    ("other", 2): {0: (0x34, 0x35, 0x26, 0x27, 0x43)},
    ("other", 3): {0: (0x44,)},
    ("own", 0): {0: (0x36, 0x45), 1: (0x37,), 3: (0x18,)},
    ("own", 1): {0: (0x46,), 2: (0x28, 0x47), 3: (0x19,)},
    ("own", 2): {0: (0x38,), 2: (0x29,), 3: (0x1a,)},
    ("own", 3): {0: (0x48,), 1: (0x39,), 2: (0x2a,), 3: (0x1b,)},
}
SCATTER_BETWEEN = ((0x40,), (0x16,))
SCATTER_AFTER = ((0x49,), (0x3a, 0x2b), (0x4a, 0x3b, 0x4b))


def layer_kernel(
    lengths_ref, attn_ref, wout_ref, inner_ref, outer_ref, table_ref, rel_ref, gain_ref, hidden_hbm, grad_hbm,
    out_hbm, input_hbm, small_ref, result_ref, gi_hbm, go_hbm,
    w, x_ref, xo, own, oth, ctx, s_ref, e_ref, middle, grad, x2_ref, x2t_ref, ob_ref, obt_ref, acc_out, acc_two, g_all, kaug_ref,
    lse_ref, line_ref, center_ref, near_ref, oth_in, sums, piece, diag, side, final,
    line_grad, far_grad, small, small_near, small_z,
    send, recv, zsend, zrecv, xsem, lsem, gsem, osem, bsend, brecv, psem, tsend, trecv,
):
    tokens = x_ref.shape[0]
    nq = tokens // LANES
    links = Links()
    net = Gather(links, w, send, recv, zsend, zrecv)
    group = []
    for n in range(1, 8):
        dp = links.dp
        for stride in (1, 2, 4):
            if n & stride:
                dp = peer(dp, stride)
        group.append((dp, links.mp))
    back = Scatter(links, (g_all, gi_hbm, go_hbm), w, sums, piece, diag, side, final, result_ref, bsend, brecv, psem)
    width = w.shape[2] * w.shape[3]

    def weights(kind, s, lo=0, hi=None):
        part = w[kind, s, :, :, lo:] if hi is None else w[kind, s, :, :, lo:hi]
        return part.reshape(width, part.shape[2])

    get_hidden = pltpu.make_async_copy(hidden_hbm, middle, lsem.at[0])
    get_grad = pltpu.make_async_copy(grad_hbm, grad, lsem.at[1])
    get_hidden.start()
    def own_block(group):
        return (group, 0, links.dp)

    parts = [attn_ref[n].astype(BF16) for n in range(3)] + [wout_ref[...].T.astype(BF16)]
    q, k, v, o = [(part[:, :LANES], part[:, LANES:]) for part in parts]
    w[own_block(0)] = jnp.concatenate([q[0], k[0], v[0], o[0], q[1], v[1], k[1], o[1]], axis=1)
    w[own_block(1)] = inner_ref[...].astype(BF16)
    w[own_block(2)] = outer_ref[...].astype(BF16)
    get_grad.start()
    links.meet([group[n] for n in (2, 4, 5, 6)])
    for step in (1, 2, 3):
        net.z_copy(0, step).start()
    net.s1(UNITS[0])
    get_hidden.wait()
    x_ref[...] = rms_scaled(middle[...], gain_ref[0:1, :]).astype(BF16)
    xcopy = remote(x_ref, xo, xsem.at[0], xsem.at[1], links.at_z[1])
    near_table = table_ref[SEQLEN - 2 * LANES : SEQLEN + 2 * LANES].reshape(1, 4 * LANES)
    hot = turned_hot(near_table, 2 * LANES - 1)[: rel_ref.shape[1]]
    high = rel_ref[...].astype(BF16)
    rest = rel_ref[...] - high.astype(F32)
    mid = rest.astype(BF16)
    low = (rest - mid.astype(F32)).astype(BF16)
    line_ref[...] = mm(high, hot) + (mm(mid, hot) + mm(low, hot))
    kaug_ref[...] = key_aug(links.half, lengths_ref[links.mp // 2], tokens)
    far = far_masks(links.first, nq)
    net.run(GATHER_AHEAD[0])
    for step in (1, 2, 3):
        net.z_copy(0, step).wait_send()
    xcopy.start()
    get_grad.wait()
    ob = grad[...].astype(BF16)
    ob_ref[...] = ob
    obt_ref[...] = ob.T
    net.run(GATHER_AHEAD[1])
    xcopy.wait_send()
    for step in (1, 2, 3):
        net.z_copy(1, step).start()
        net.z_copy(2, step).start()
    xcopy.wait_recv()

    masks = [half_rows(0), half_rows(1)]
    count = lax.broadcasted_iota(jnp.int32, (HDIM, 2 * tokens), 0)
    ones = (count == 0).astype(F32).astype(BF16)

    def attend(s, carry):
        x, other = x_ref[...], xo[...]
        p_a = mm(x, weights(0, s, 0, 3 * LANES)).astype(BF16)
        p_b = mm(x, weights(0, s, 4 * LANES)).astype(BF16)
        o_a = mm(other, weights(0, s, LANES, 3 * LANES)).astype(BF16)
        o_b = mm(other, weights(0, s, 4 * LANES)).astype(BF16)
        own[s, :, : 3 * LANES] = p_a
        own[s, :, 3 * LANES :] = p_b
        oth[s, :, : 2 * LANES] = o_a
        oth[s, :, 2 * LANES :] = o_b
        cols_own = {0: p_a[:, :LANES], 1: p_a[:, LANES : 2 * LANES], 2: p_a[:, 2 * LANES :], 4: p_b[:, :LANES], 5: p_b[:, LANES:]}
        cols_oth = {1: o_a[:, :LANES], 2: o_a[:, LANES:], 4: o_b[:, :LANES], 5: o_b[:, LANES:]}
        both = {c: jnp.concatenate([cols_own[c], cols_oth[c]], axis=0) for c in (1, 2, 4, 5)}
        m = links.column(s)
        v_t = {2: both[2].T, 4: both[4].T}
        pieces = []
        stats = []
        for i, (qc, qh, kc, vc, vh) in enumerate(HEAD_AT):
            net.at("attend", s, i)
            line = line_ref[pl.ds(3 * m + i, 1), :]
            tile = bias_tile(line)
            qa = cols_own[qc] * masks[qh] + query_aug(line, far, nq) * masks[1 - qh]
            ka = both[kc] * masks[qh] + kaug_ref[...] * masks[1 - qh]
            scores = mt(ka, qa)
            peak = None
            for jb, row in enumerate(add_bias(scores, tile, line, links.first, nq)):
                s_ref[i % 2 * 2 * nq + jb] = row
                top = jnp.max(row.reshape(LANES // 8, 8, tokens), axis=0)
                peak = top if peak is None else jnp.maximum(peak, top)
            peak = jnp.max(peak, axis=0, keepdims=True)
            for jb in range(2 * nq):
                rows = slice(jb % nq * LANES, (jb % nq + 1) * LANES)
                e_ref[i % 2 * 2 + jb // nq, rows, :] = jnp.exp(s_ref[i % 2 * 2 * nq + jb] - peak).astype(BF16)
            if vh == 0:
                va = jnp.concatenate([v_t[vc][:HDIM], ones], axis=0)
            else:
                va = jnp.concatenate([ones, v_t[vc][HDIM:]], axis=0)
            ot = mm(va, e_ref[i % 2 * 2 : i % 2 * 2 + 2].reshape(2 * tokens, tokens))
            at = HDIM if vh == 0 else 0
            total = ot[at : at + 1, :]
            stats.append(peak + jnp.log(total))
            real = ot[:HDIM] if vh == 0 else ot[HDIM:]
            pieces.append(real / total)
        zero = jnp.zeros((HDIM, tokens), F32)
        ctx_a = jnp.concatenate([pieces[0], pieces[1]], axis=0).T.astype(BF16)
        ctx_b = jnp.concatenate([zero, pieces[2]], axis=0).T.astype(BF16)
        ctx[s, :, :LANES] = ctx_a
        ctx[s, :, LANES:] = ctx_b
        lse_ref[s] = jnp.concatenate(stats + [jnp.zeros((5, tokens), F32)], axis=0)
        middle[...] += mt(ctx_a, weights(0, s, 3 * LANES, 4 * LANES)) + mt(ctx_b, weights(0, s, 5 * LANES))
        net.at("attend", s, 3)
        return carry

    lax.fori_loop(0, 4, attend, 0)

    x2 = rms_scaled(middle[...], gain_ref[1:2, :]).astype(BF16)
    x2_ref[...] = x2
    x2t_ref[...] = x2.T
    acc_out[...] = jnp.zeros_like(acc_out)
    acc_two[...] = jnp.zeros_like(acc_two)

    def g_copies(t):
        return (
            pltpu.make_async_copy(g_all.at[t % 2 * 2], gi_hbm.at[t], gsem.at[t % 2, 0]),
            pltpu.make_async_copy(g_all.at[t % 2 * 2 + 1], go_hbm.at[t], gsem.at[t % 2, 1]),
        )

    def feed(t, carry):
        tile = 2 * LANES
        for n in range(w.shape[4] // tile):
            net.at("feed", t, n)
            if n == 1:

                @pl.when(t >= 1)
                def _():
                    for copy in g_copies(t - 1):
                        copy.wait()

            back.at("feed", t, n)
            if n == 0:
                net.at("feed", t, 3)
            wi = weights(1, t, n * tile, (n + 1) * tile)
            wo = weights(2, t, n * tile, (n + 1) * tile)
            inner = mm(x2_ref[...], wi)
            active_back = mm(ob_ref[...], wo)
            c = 0.7978845608028654
            sq = inner * inner
            th = jnp.tanh(c * (inner + 0.044715 * (sq * inner)))
            half = 0.5 * (1.0 + th)
            active = (inner * half).astype(BF16)
            slope = half + (0.5 * c) * inner * (1.0 - th * th) * (1.0 + (3 * 0.044715) * sq)
            inner_back = (slope * active_back).astype(BF16)
            acc_out[...] += mt(active, wo)
            acc_two[...] += mt(inner_back, wi)
            at = slice(n * tile, (n + 1) * tile)
            shape = (*w.shape[2:4], tile)
            split = (shape[0] // 2, 2, *shape[1:])
            g_all[t % 2 * 2, :, :, :, at] = mm(x2t_ref[...], inner_back).astype(BF16).reshape(split)
            g_all[t % 2 * 2 + 1, :, :, :, at] = mm(obt_ref[...], active).astype(BF16).reshape(split)
        for copy in g_copies(t):
            copy.start()
        return carry

    lax.fori_loop(0, 4, feed, 0)
    back.run(SCATTER_BETWEEN[0])
    acc_out[...] += middle[...]
    put_out = pltpu.make_async_copy(acc_out, out_hbm, lsem.at[2])
    put_out.start()
    result, gain_two = rms_back(middle[...], gain_ref[1:2, :], acc_two[...])
    get_hidden = pltpu.make_async_copy(hidden_hbm, middle, lsem.at[0])
    get_hidden.start()
    grad[...] += result
    net.finish()
    for copy in g_copies(3):
        copy.wait()
    back.run(SCATTER_BETWEEN[1])
    ab_ref, abt, xt, acc_own, acc_oth, oth_out = x2_ref, x2t_ref, obt_ref, acc_out, acc_two, ob_ref
    ab = grad[...].astype(BF16)
    ab_ref[...] = ab
    abt[...] = ab.T
    xt[...] = x_ref[...].T
    w[2, 0, :, :, : tokens] = xo[...].T.reshape(*w.shape[2:4], tokens)
    acc_oth[...] = jnp.zeros_like(acc_oth)
    line_grad[...] = jnp.zeros_like(line_grad)
    far_grad[...] = jnp.zeros_like(far_grad)
    jb = lax.broadcasted_iota(jnp.int32, (2 * nq, tokens), 0)
    ib = lax.broadcasted_iota(jnp.int32, (2 * nq, tokens), 1) // LANES
    edge_first = ((jb == nq) & (ib == nq - 1)).astype(F32)
    edge_last = ((jb == 2 * nq - 1) & (ib == 0)).astype(F32)
    other_key = (jb >= nq).astype(F32)
    sum_before = ((jb < nq) & (jb < ib - 1)).astype(F32) + (other_key - edge_last) * (1.0 - links.first)
    sum_after = ((jb < nq) & (jb > ib + 1)).astype(F32) + (other_key - edge_first) * links.first
    own_at = {c: slice(at * LANES, (at + 1) * LANES) for at, c in enumerate((0, 1, 2, 4, 5))}
    oth_at = {c: slice(at * LANES, (at + 1) * LANES) for at, c in enumerate((1, 2, 4, 5))}
    cb_at = {2: slice(0, LANES), 4: slice(LANES, 2 * LANES)}
    at_row = lax.broadcasted_iota(jnp.int32, (LANES, LANES), 0) + lax.broadcasted_iota(jnp.int32, (LANES, LANES), 1)
    mirror = (at_row == LANES - 1).astype(F32).astype(BF16)

    def context_back(s):
        return {
            2: mm(ab_ref[...], weights(0, s, 3 * LANES, 4 * LANES)).astype(BF16),
            4: mm(ab_ref[...], weights(0, s, 5 * LANES)).astype(BF16),
        }

    def one_side(s, i, other, cb):
        qc, qh, kc, vc, vh = HEAD_AT[i]
        line = line_ref[pl.ds(3 * links.column(s) + i, 1), :]
        tile = bias_tile(line)
        qm = own[s, :, own_at[qc]] * masks[qh]
        qa = qm + query_aug(line, far, nq) * masks[1 - qh]
        om = cb[vc] * masks[vh]
        center = center_ref[s, i : i + 1, :]
        lse = lse_ref[s, i : i + 1, :]
        parts = near_parts(tile)
        corner = corner_parts(tile, line, links.first)
        side = 1 if other else 0
        k_cols = oth[s, :, oth_at[kc]] if other else own[s, :, own_at[kc]]
        v_cols = oth[s, :, oth_at[vc]] if other else own[s, :, own_at[vc]]
        ka = k_cols * masks[qh] + kaug_ref[side * tokens : (side + 1) * tokens] * masks[1 - qh]
        scores = mt(ka, qa)
        chance_back = mt(v_cols, om)
        near = [None] * 5
        ps, ds = [], []
        for jb in range(nq):
            row_p, row_d = [], []
            for ib in range(nq):
                at = (slice(jb * LANES, (jb + 1) * LANES), slice(ib * LANES, (ib + 1) * LANES))
                block = scores[at]
                kind = None
                if not other and abs(jb - ib) <= 1:
                    kind = jb - ib + 1
                    block = block + parts[kind]
                elif other and jb == 0 and ib == nq - 1:
                    kind = 3
                    block = block + corner[0]
                elif other and jb == nq - 1 and ib == 0:
                    kind = 4
                    block = block + corner[1]
                p = jnp.exp(block - lse[:, at[1]])
                d = p * (chance_back[at] - center[:, at[1]])
                if kind is not None:
                    near[kind] = d if near[kind] is None else near[kind] + d
                row_p.append(p.astype(BF16))
                row_d.append(d.astype(BF16))
            ps.append(jnp.concatenate(row_p, axis=1))
            ds.append(jnp.concatenate(row_d, axis=1))
        pb = jnp.concatenate(ps, axis=0)
        db = jnp.concatenate(ds, axis=0)
        return mm(ka.T, db), mm(db, qm), mm(pb, om), near

    def other_side(it, carry):
        s = 3 - it
        cb = context_back(s)
        centers = []
        for i in range(3):
            vc, vh = HEAD_AT[i][3:]
            prod = cb[vc].astype(F32) * ctx[s, :, cb_at[vc]].astype(F32)
            high = prod.astype(BF16)
            low = (prod - high.astype(F32)).astype(BF16)
            pick = jnp.broadcast_to(masks[vh], (8, LANES))
            centers.append((mt(pick, high) + mt(pick, low))[0:1, :])
        center_ref[s] = jnp.concatenate(centers + [jnp.zeros((5, tokens), F32)], axis=0)
        dk, dv = {}, {}
        for i, (qc, qh, kc, vc, vh) in enumerate(HEAD_AT):
            back.at("other", it, i)
            s_ref[3 * s + i], part_k, part_v, near = one_side(s, i, True, cb)
            dk[kc] = dk[kc] + part_k if kc in dk else part_k
            dv[vc] = dv[vc] + part_v if vc in dv else part_v
            near_ref[s, i] = near[3] * links.first + near[4] * (1.0 - links.first)
        d = jnp.concatenate([dk[1], dv[2], dv[4], dk[5]], axis=1).astype(BF16)
        e_ref[s] = d
        acc_oth[...] += mt(d[:, : 2 * LANES], weights(0, s, LANES, 3 * LANES)) + mt(d[:, 2 * LANES :], weights(0, s, 4 * LANES))
        return carry

    lax.fori_loop(0, 4, other_side, 0)
    oth_out[...] = acc_oth[...].astype(BF16)
    swap = remote(oth_out, oth_in, osem.at[0], osem.at[1], links.at_z[1])
    swap.start()

    def own_side(it, carry):
        s = 3 - it
        m = links.column(s)
        cb = context_back(s)
        dk, dv, dq = {}, {}, []
        for i, (qc, qh, kc, vc, vh) in enumerate(HEAD_AT):
            back.at("own", it, i)
            part_q, part_k, part_v, near = one_side(s, i, False, cb)
            part_q = part_q + s_ref[3 * s + i]
            dk[kc] = dk[kc] + part_k if kc in dk else part_k
            dv[vc] = dv[vc] + part_v if vc in dv else part_v
            at = HDIM if qh == 0 else 0
            block_sums = part_q[at + 8 : at + 8 + 2 * nq, :]
            head = pl.ds(3 * m + i, 1)
            far_grad[0, head, :] = jnp.sum(block_sums * sum_before, axis=0, keepdims=True)
            far_grad[1, head, :] = jnp.sum(block_sums * sum_after, axis=0, keepdims=True)
            dq.append(part_q[:HDIM] if qh == 0 else part_q[HDIM:])
            first, final_corner = near_ref[s, i] * links.first, near_ref[s, i] * (1.0 - links.first)
            blank = jnp.zeros((LANES, LANES), F32)
            tile = jnp.concatenate([near[1], near[0] + final_corner, blank, near[2] + first], axis=1)
            high = tile.astype(BF16)
            low = (tile - high.astype(F32)).astype(BF16)
            turned = pltpu.roll(mm(mirror, high) + mm(mirror, low), 0, 1, stride=1, stride_axis=0)
            line_grad[head, :] = jnp.sum(turned, axis=0, keepdims=True)
        dq_a = jnp.concatenate([dq[0], dq[1]], axis=0).T
        dq_b = jnp.concatenate([dq[2], jnp.zeros_like(dq[2])], axis=0).T
        d_own = jnp.concatenate([dq_a, dk[1], dv[2], dq_b + dv[4], dk[5]], axis=1).astype(BF16)
        g_own = mm(xt[...], d_own)
        g_oth = mm(w[2, 0, :, :, :tokens].reshape(width, tokens), e_ref[s])
        g_ctx = mm(abt[...], ctx[s])
        columns = [
            g_own[:, :LANES],
            g_own[:, LANES : 3 * LANES] + g_oth[:, : 2 * LANES],
            g_ctx[:, :LANES],
            g_own[:, 3 * LANES : 4 * LANES] + g_oth[:, 2 * LANES : 3 * LANES],
            g_own[:, 4 * LANES :] + g_oth[:, 3 * LANES :] + g_ctx[:, LANES:],
        ]
        g = jnp.concatenate(columns, axis=1).astype(BF16)
        rows = w.shape[3]
        for n in range(8):
            g_all[s, n // 2, n % 2] = g[n * rows : (n + 1) * rows, :]
        back.at("own", it, 3)
        acc_own[...] += mt(d_own[:, : 3 * LANES], weights(0, s, 0, 3 * LANES)) + mt(d_own[:, 3 * LANES :], weights(0, s, 4 * LANES))
        return carry

    put_out.wait()
    acc_own[...] = jnp.zeros_like(acc_own)
    lax.fori_loop(0, 4, own_side, 0)
    back.run(SCATTER_AFTER[0])
    get_hidden.wait()
    swap.wait_recv()
    one_back = acc_own[...] + oth_in[...].astype(F32)
    value, gain_part = rms_back(middle[...], gain_ref[0:1, :], one_back)
    acc_own[...] = value + grad[...]
    put_grad = pltpu.make_async_copy(acc_own, input_hbm, lsem.at[2])
    put_grad.start()
    lane = lax.broadcasted_iota(jnp.int32, (16, 4 * LANES), 1)
    by_line = (
        line_grad[...]
        + jnp.sum(far_grad[0], axis=1, keepdims=True) * (lane == 2 * LANES - 1).astype(F32)
        + jnp.sum(far_grad[1], axis=1, keepdims=True) * (lane == 4 * LANES - 1).astype(F32)
    )
    high = by_line.astype(BF16)
    low = (by_line - high.astype(F32)).astype(BF16)
    hot = turned_hot(near_table, 3 * LANES - 2)
    small[0:16, :] = mt(high, hot) + mt(low, hot)
    for n in range(6):
        at = slice(n * LANES, (n + 1) * LANES)
        small[16 + n : 17 + n, :] = gain_part[:, at]
        small[22 + n : 23 + n, :] = gain_two[:, at]
    small[28:32, :] = jnp.zeros((4, LANES), F32)

    def to_group(lo, n, at):
        here = small.at[pl.ds(lo, n)]
        return [remote(here, small_near.at[k, pl.ds(lo, n)], tsend.at[at + k], trecv.at[at + k], to) for k, to in enumerate(group)]

    def along_z(lo, n, at):
        here = small_z.at[0, pl.ds(lo, n)]
        return [
            remote(here, small_z.at[k, pl.ds(lo, n)], tsend.at[at + k], trecv.at[at + k], links.at_z[k]) for k in (1, 2, 3)
        ]

    def total(lo, n):
        value = small[lo : lo + n, :]
        for k in range(7):
            value = value + small_near[k, lo : lo + n, :]
        return value

    early = to_group(0, 32, 0)
    for copy in early:
        copy.start()
    back.run(SCATTER_AFTER[1])
    back.run(SCATTER_AFTER[2])
    squares = jnp.zeros((8, LANES), F32)
    for weight in (1, 2, 0):
        back.last(weight)
        value = result_ref[weight]
        value = value * value
        for n in range(value.shape[1] // LANES):
            piece_sum = value[:, n * LANES : (n + 1) * LANES]
            squares = squares + jnp.sum(piece_sum.reshape(-1, 8, LANES), axis=0)
    small[32:40, :] = squares
    late = to_group(32, 8, 11)
    for copy in late:
        copy.start()
    for copy in early:
        copy.wait_recv()
    small_z[0, 0:32, :] = total(0, 32)
    for copy in late:
        copy.wait_recv()
    small_z[0, 32:40, :] = total(32, 8)
    late_z = along_z(0, 40, 18)
    for copy in late_z:
        copy.start()
    back.finish()
    for copy in late_z:
        copy.wait_recv()
    small_ref[...] = (small_z[0] + small_z[1]) + (small_z[2] + small_z[3])
    for copy in early + late + late_z:
        copy.wait_send()
    put_grad.wait()
    swap.wait_send()


def update_kernel(small_ref, grad_hbm, block_hbm, input_hbm, *refs):
    hbm, (block_out, input_out, norm_ref), new_hbm = refs[:18], refs[18:21], refs[21:39]
    held, new, grad_ref, pass_ref, sem = refs[39:57], refs[57:75], refs[75], refs[76], refs[77]
    results = [pltpu.make_async_copy(a, b, sem.at[23 + n]) for n, (a, b) in enumerate(zip(new, new_hbm))]
    through = ((block_hbm, block_out), (input_hbm, input_out))
    fetch = [pltpu.make_async_copy(a, pass_ref.at[n], sem.at[n]) for n, (a, b) in enumerate(through)]
    store = [pltpu.make_async_copy(pass_ref.at[n], b, sem.at[21 + n]) for n, (a, b) in enumerate(through)]
    loads = [pltpu.make_async_copy(a, b, sem.at[2 + n]) for n, (a, b) in enumerate(zip(hbm, held))]
    loads.append(pltpu.make_async_copy(grad_hbm, grad_ref, sem.at[20]))
    for copy in loads[::-1] + fetch:
        copy.start()
    attn, out, inner, outer, rel, gain, attn_first, attn_second, out_first, out_second = held[:10]
    inner_first, inner_second, outer_first, outer_second, rel_first, rel_second, gain_first, gain_second = held[10:]
    small = small_ref[0:28, :]
    squares = jnp.sum(small * small, axis=0, keepdims=True) + jnp.sum(small_ref[32:40, :], axis=0, keepdims=True)
    norm = jnp.sqrt(jnp.sum(squares, axis=1, keepdims=True))
    norm_ref[...] = norm
    factor = jnp.minimum(1.0, CLIP / (norm + 1e-06))
    loads[18].wait()

    def ready(*which):
        for n in which:
            loads[n].wait()

    def put(*which):
        for n in which:
            results[n].start()

    def step(at, grad, rate, master, first, second, outs):
        for ref, value in zip(outs, adam_step(master[at], grad, first[at], second[at], factor, rate)):
            ref[at] = value

    whole = slice(None)

    def turned(column):
        return pltpu.roll(column, HDIM, 1)[:, :HDIM]

    ready(2, 10, 11)
    step(whole, grad_ref[1], RATE_MATRIX, inner, inner_first, inner_second, new[6:9])
    put(6, 7, 8)
    ready(3, 12, 13)
    step(whole, grad_ref[2], RATE_MATRIX, outer, outer_first, outer_second, new[9:12])
    put(9, 10, 11)
    for a, b in zip(fetch, store):
        a.wait()
        b.start()
    ready(0, 6, 7)
    g = [grad_ref[0, :, n * LANES : (n + 1) * LANES] for n in range(6)]
    tails = (g[4][:, :HDIM], g[5][:, :HDIM], turned(g[4]))
    for n in range(3):
        step((n, slice(None), slice(0, LANES)), g[n], RATE_MATRIX, attn, attn_first, attn_second, new[0:3])
        step((n, slice(None), slice(LANES, LANES + HDIM)), tails[n], RATE_MATRIX, attn, attn_first, attn_second, new[0:3])
    put(0, 1, 2)
    ready(1, 8, 9)
    rows = g[3].shape[0]
    blank = jnp.zeros((LANES - rows, LANES), F32)
    lower = pltpu.roll(g[5], HDIM, 1)
    step((slice(0, LANES), whole), jnp.concatenate([g[3], blank], axis=0).T[:, :rows], RATE_OUT, out, out_first, out_second, new[3:6])
    step(
        (slice(LANES, LANES + HDIM), whole),
        jnp.concatenate([lower, blank], axis=0).T[:HDIM, :rows],
        RATE_OUT, out, out_first, out_second, new[3:6],
    )
    put(3, 4, 5)
    ready(4, 5, 14, 15, 16, 17)
    heads, buckets = rel.shape
    step(whole, small_ref[0:heads, 0:buckets], RATE_SMALL, rel, rel_first, rel_second, new[12:15])
    gain_grad = jnp.concatenate(
        [
            jnp.concatenate([small_ref[at + n : at + n + 1, :] for n in range(6)], axis=1)
            for at in (16, 22)
        ],
        axis=0,
    )
    step(whole, gain_grad, RATE_SMALL, gain, gain_first, gain_second, new[15:18])
    put(*range(12, 18))
    for copy in store + results:
        copy.wait()


def run_layer(lengths, attn, out, inner, outer, table, rel, gains, hidden, grad):
    t, d = hidden.shape
    parts, (rows, cols) = rel.shape[0] // 3, inner.shape
    any_space = pl.BlockSpec(memory_space=pl.ANY)
    vmem = pl.BlockSpec(memory_space=pltpu.VMEM)
    dma = pltpu.SemaphoreType.DMA
    split = (parts, 4, 2, rows, cols)
    low = lambda *shape: pltpu.VMEM(shape, BF16)
    full = lambda *shape: pltpu.VMEM(shape, F32)
    return pl.pallas_call(
        layer_kernel,
        in_specs=[pl.BlockSpec(memory_space=pltpu.SMEM)] + [vmem] * 7 + [any_space] * 2,
        out_specs=[any_space] * 2 + [vmem] * 2 + [any_space] * 2,
        out_shape=[
            jax.ShapeDtypeStruct((t, d), F32),
            jax.ShapeDtypeStruct((t, d), F32),
            jax.ShapeDtypeStruct((40, LANES), F32),
            jax.ShapeDtypeStruct((3, rows, cols), F32),
            jax.ShapeDtypeStruct(split, BF16),
            jax.ShapeDtypeStruct(split, BF16),
        ],
        scratch_shapes=[
            low(3, parts, 8, rows, cols), low(t, d), low(t, d),
            low(parts, t, 5 * LANES), low(parts, t, 4 * LANES), low(parts, t, 2 * LANES),
            full(4 * t // LANES, LANES, t), low(4, t, t), full(t, d), full(t, d),
            low(t, d), low(d, t), low(t, d), low(d, t), full(t, d), full(t, d), low(*split), low(2 * t, LANES),
            full(parts, 8, t), full(rel.shape[0], 4 * LANES), full(parts, 8, t), full(parts, 3, LANES, LANES), low(t, d),
            low(8, 4, rows, cols), low(3, 4, rows, cols), low(8, 2, rows // 2, cols), low(8, 2, rows, cols), low(3, 3, rows, cols),
            full(16, 4 * LANES), full(2, 16, 4 * LANES), full(40, LANES), full(7, 40, LANES), full(4, 40, LANES),
            dma((12, 8)), dma((12, 8)), dma((9,)), dma((9,)), dma((2,)), dma((3,)), dma((2, 2)), dma((2,)),
            dma((12, 6)), dma((12, 6)), dma((3,)), dma((22,)), dma((22,)),
        ],
        compiler_params=pltpu.CompilerParams(
            vmem_limit_bytes=63 * 2**20, collective_id=0, has_side_effects=True
        ),
        name="layer",
    )(lengths, attn, out, inner, outer, table, rel, gains, hidden, grad)


def run_update(small, grads, block_out, input_grad, masters, moments):
    vmem = pl.BlockSpec(memory_space=pltpu.VMEM)
    hbm = pl.BlockSpec(memory_space=pltpu.HBM)
    like = lambda a: jax.ShapeDtypeStruct(a.shape, F32)
    return pl.pallas_call(
        update_kernel,
        in_specs=[vmem] + [hbm] * 21,
        out_specs=[hbm] * 2 + [vmem] + [hbm] * 18,
        out_shape=[like(block_out), like(input_grad), jax.ShapeDtypeStruct((1, 1), F32)]
        + [like(a) for a in masters for _ in range(3)],
        scratch_shapes=[pltpu.VMEM(a.shape, F32) for a in (*masters, *moments)]
        + [pltpu.VMEM(a.shape, F32) for a in masters for _ in range(3)]
        + [pltpu.VMEM(grads.shape, F32)]
        + [pltpu.VMEM((2, *block_out.shape), F32), pltpu.SemaphoreType.DMA((41,))],
        compiler_params=pltpu.CompilerParams(vmem_limit_bytes=62 * 2**20),
        name="update",
    )(small, grads, block_out, input_grad, *masters, *moments)


def body(
    hidden_in, out_grad, attn_weight, out_weight, inner_weight, outer_weight, rel_bias, gains, lengths, table,
    attn_first, attn_second, out_first, out_second, inner_first, inner_second, outer_first, outer_second,
    rel_first, rel_second, gain_first, gain_second, *, parts,
):
    block_out, input_grad, small, owned, _, _ = run_layer(
        lengths, attn_weight, out_weight, inner_weight, outer_weight.T, table, rel_bias.T, gains, hidden_in, out_grad
    )
    new = run_update(
        small, owned, block_out, input_grad,
        (attn_weight, out_weight, inner_weight, outer_weight.T, rel_bias.T, gains),
        (
            attn_first, attn_second, out_first, out_second, inner_first, inner_second,
            outer_first.T, outer_second.T, rel_first.T, rel_second.T, gain_first, gain_second,
        ),
    )
    masters = new[3:]
    return (
        new[0], new[1], new[2].reshape(()), *masters[:9], *(a.T for a in masters[9:12]), *(a.T for a in masters[12:15]), *masters[15:],
    )


def plain_corner_parts(tile, line, flags):
    before, same, after = near_parts(tile)
    first = (after - line[:, 3 * LANES : 3 * LANES + 1]) * flags[0]
    last = (before - line[:, LANES : LANES + 1]) * flags[1]
    return first, last


def plain_add_bias(scores, tile, line, flags, nq):
    parts = near_parts(tile)
    corner = plain_corner_parts(tile, line, flags)
    rows = []
    for jb in range(2 * nq):
        row = []
        for ib in range(nq):
            block = scores[jb * LANES : (jb + 1) * LANES, ib * LANES : (ib + 1) * LANES]
            if jb < nq and abs(jb - ib) <= 1:
                block = block + parts[jb - ib + 1]
            elif jb == nq and ib == nq - 1:
                block = block + corner[0]
            elif jb == 2 * nq - 1 and ib == 0:
                block = block + corner[1]
            row.append(block)
        rows.append(jnp.concatenate(row, axis=1))
    return rows


def plain_query_aug(qaug, i, nq):
    rows = qaug.shape[0]
    return jnp.concatenate(
        [jnp.broadcast_to(qaug[i * nq + ib : i * nq + ib + 1, :], (LANES, LANES)) for ib in range(nq)], axis=0
    )


def forward_kernel(
    x_ref, xo_ref, w_ref, line_ref, qaug_ref, kaug_ref, hidden_ref,
    own_ref, oth_ref, ctx_ref, lse_ref, middle_ref,
    acc, s_ref, e_ref,
):
    m = pl.program_id(0)
    tokens = x_ref.shape[0]
    nq = tokens // LANES
    x, xo = x_ref[...], xo_ref[...]
    p_a = mm(x, w_ref[:, : 3 * LANES]).astype(BF16)
    p_b = mm(x, w_ref[:, 4 * LANES :]).astype(BF16)
    o_a = mm(xo, w_ref[:, LANES : 3 * LANES]).astype(BF16)
    o_b = mm(xo, w_ref[:, 4 * LANES :]).astype(BF16)
    own_ref[0, :, : 3 * LANES] = p_a
    own_ref[0, :, 3 * LANES :] = p_b
    oth_ref[0, :, : 2 * LANES] = o_a
    oth_ref[0, :, 2 * LANES :] = o_b
    cols_own = {0: p_a[:, :LANES], 1: p_a[:, LANES : 2 * LANES], 2: p_a[:, 2 * LANES :], 4: p_b[:, :LANES], 5: p_b[:, LANES:]}
    cols_oth = {1: o_a[:, :LANES], 2: o_a[:, LANES:], 4: o_b[:, :LANES], 5: o_b[:, LANES:]}
    both = {c: jnp.concatenate([cols_own[c], cols_oth[c]], axis=0) for c in (1, 2, 4, 5)}
    masks = [half_rows(0), half_rows(1)]
    flags = (line_ref[0, 3:4, :LANES], line_ref[0, 4:5, :LANES])
    v_t = {2: both[2].T, 4: both[4].T}
    count = lax.broadcasted_iota(jnp.int32, (HDIM, 2 * tokens), 0)
    ones = (count == 0).astype(F32).astype(BF16)
    pieces = []
    stats = []
    for i, (qc, qh, kc, vc, vh) in enumerate(HEAD_AT):
        line = line_ref[0, i : i + 1, :]
        tile = bias_tile(line)
        qa = cols_own[qc] * masks[qh] + plain_query_aug(qaug_ref[0], i, nq) * masks[1 - qh]
        ka = both[kc] * masks[qh] + kaug_ref[...] * masks[1 - qh]
        scores = mt(ka, qa)
        peak = None
        for jb, row in enumerate(plain_add_bias(scores, tile, line, flags, nq)):
            s_ref[i, jb * LANES : (jb + 1) * LANES, :] = row
            top = jnp.max(row.reshape(LANES // 8, 8, tokens), axis=0)
            peak = top if peak is None else jnp.maximum(peak, top)
        peak = jnp.max(peak, axis=0, keepdims=True)
        for jb in range(2 * nq):
            rows = slice(jb * LANES, (jb + 1) * LANES)
            e_ref[i, rows, :] = jnp.exp(s_ref[i, rows, :] - peak).astype(BF16)
        if vh == 0:
            va = jnp.concatenate([v_t[vc][:HDIM], ones], axis=0)
        else:
            va = jnp.concatenate([ones, v_t[vc][HDIM:]], axis=0)
        ot = mm(va, e_ref[i])
        at = HDIM if vh == 0 else 0
        total = ot[at : at + 1, :]
        stats.append(peak + jnp.log(total))
        real = ot[:HDIM] if vh == 0 else ot[HDIM:]
        pieces.append(real / total)
    zero = jnp.zeros((HDIM, tokens), F32)
    ctx_a = jnp.concatenate([pieces[0], pieces[1]], axis=0).T.astype(BF16)
    ctx_b = jnp.concatenate([zero, pieces[2]], axis=0).T.astype(BF16)
    ctx_ref[0, :, :LANES] = ctx_a
    ctx_ref[0, :, LANES:] = ctx_b
    for i in range(3):
        lse_ref[0, i : i + 1, :] = stats[i]
    lse_ref[0, 3:8, :] = jnp.zeros((5, tokens), F32)
    part = mt(ctx_a, w_ref[:, 3 * LANES : 4 * LANES]) + mt(ctx_b, w_ref[:, 5 * LANES :])

    @pl.when(m == 0)
    def _():
        acc[...] = hidden_ref[...] + part

    @pl.when(m > 0)
    def _():
        acc[...] += part

    @pl.when(m == pl.num_programs(0) - 1)
    def _():
        middle_ref[...] = acc[...]


def feed_kernel(
    middle_ref, grad_ref, gain_ref, wi_ref, wo_ref,
    out_ref, back_ref, gain_grad_ref, gi_ref, go_ref,
    x2_ref, x2t_ref, ob_ref, obt_ref, acc_out, acc_two,
):
    f = pl.program_id(0)

    @pl.when(f == 0)
    def _():
        x2 = rms_scaled(middle_ref[...], gain_ref[1:2, :]).astype(BF16)
        x2_ref[...] = x2
        x2t_ref[...] = x2.T
        ob = grad_ref[...].astype(BF16)
        ob_ref[...] = ob
        obt_ref[...] = ob.T
        acc_out[...] = jnp.zeros_like(acc_out)
        acc_two[...] = jnp.zeros_like(acc_two)

    inner = mm(x2_ref[...], wi_ref[...])
    active_back = mm(ob_ref[...], wo_ref[...])
    c = 0.7978845608028654
    sq = inner * inner
    th = jnp.tanh(c * (inner + 0.044715 * (sq * inner)))
    half = 0.5 * (1.0 + th)
    active = (inner * half).astype(BF16)
    slope = half + (0.5 * c) * inner * (1.0 - th * th) * (1.0 + (3 * 0.044715) * sq)
    inner_back = (slope * active_back).astype(BF16)
    acc_out[...] += mt(active, wo_ref[...])
    acc_two[...] += mt(inner_back, wi_ref[...])
    go_ref[...] = mm(obt_ref[...], active).astype(go_ref.dtype)
    gi_ref[...] = mm(x2t_ref[...], inner_back).astype(gi_ref.dtype)

    @pl.when(f == pl.num_programs(0) - 1)
    def _():
        out_ref[...] = middle_ref[...] + acc_out[...]
        result, gain_part = rms_back(middle_ref[...], gain_ref[1:2, :], acc_two[...])
        back_ref[...] = grad_ref[...] + result
        gain_grad_ref[...] = jnp.broadcast_to(gain_part, gain_grad_ref.shape)


def backward_kernel(
    x_ref, xo_ref, back_ref, w_ref, line_ref, qaug_ref, kaug_ref, own_ref, oth_ref, ctx_ref, lse_ref,
    ga_ref, one_own_ref, one_oth_ref, near_ref, sums_ref,
    xt_ref, xot_ref, ab_ref, abt_ref, acc_own, acc_oth,
):
    m = pl.program_id(0)
    tokens = x_ref.shape[0]
    nq = tokens // LANES

    @pl.when(m == 0)
    def _():
        xt_ref[...] = x_ref[...].T
        xot_ref[...] = xo_ref[...].T
        ab = back_ref[...].astype(BF16)
        ab_ref[...] = ab
        abt_ref[...] = ab.T
        acc_own[...] = jnp.zeros_like(acc_own)
        acc_oth[...] = jnp.zeros_like(acc_oth)

    ab = ab_ref[...]
    cb = {2: mm(ab, w_ref[:, 3 * LANES : 4 * LANES]).astype(BF16), 4: mm(ab, w_ref[:, 5 * LANES :]).astype(BF16)}
    ctx = {2: ctx_ref[0, :, :LANES], 4: ctx_ref[0, :, LANES:]}
    own = {c: own_ref[0, :, at * LANES : (at + 1) * LANES] for at, c in enumerate((0, 1, 2, 4, 5))}
    oth = {c: oth_ref[0, :, at * LANES : (at + 1) * LANES] for at, c in enumerate((1, 2, 4, 5))}
    masks = [half_rows(0), half_rows(1)]
    flags = (line_ref[0, 3:4, :LANES], line_ref[0, 4:5, :LANES])
    prod = {c: cb[c].astype(F32) * ctx[c].astype(F32) for c in (2, 4)}
    prod_hi = {c: prod[c].astype(BF16) for c in prod}
    prod_lo = {c: (prod[c] - prod_hi[c].astype(F32)).astype(BF16) for c in prod}
    dq_t = []
    dk = {}
    dv = {}
    for i, (qc, qh, kc, vc, vh) in enumerate(HEAD_AT):
        line = line_ref[0, i : i + 1, :]
        tile = bias_tile(line)
        qm = own[qc] * masks[qh]
        qa = qm + plain_query_aug(qaug_ref[0], i, nq) * masks[1 - qh]
        om = cb[vc] * masks[vh]
        pick = jnp.broadcast_to(masks[vh], (8, LANES))
        center = (mt(pick, prod_hi[vc]) + mt(pick, prod_lo[vc]))[0:1, :]
        lse = lse_ref[0, i : i + 1, :]
        kaug = kaug_ref[...] * masks[1 - qh]
        dqt = None
        parts = near_parts(tile)
        corner = plain_corner_parts(tile, line, flags)
        near = [None, None, None, None, None]
        for side, cols in enumerate((own, oth)):
            ka = cols[kc] * masks[qh] + kaug[side * tokens : (side + 1) * tokens]
            scores = mt(ka, qa)
            chance_back = mt(cols[vc], om)
            ps, ds = [], []
            for jb in range(nq):
                row_s, row_p, row_d = [], [], []
                for ib in range(nq):
                    at = (slice(jb * LANES, (jb + 1) * LANES), slice(ib * LANES, (ib + 1) * LANES))
                    block = scores[at]
                    kind = None
                    if side == 0 and abs(jb - ib) <= 1:
                        block = block + parts[jb - ib + 1]
                        kind = jb - ib + 1
                    elif side == 1 and jb == 0 and ib == nq - 1:
                        block = block + corner[0]
                        kind = 3
                    elif side == 1 and jb == nq - 1 and ib == 0:
                        block = block + corner[1]
                        kind = 4
                    p = jnp.exp(block - lse[:, at[1]])
                    d = p * (chance_back[at] - center[:, at[1]])
                    if kind is not None:
                        near[kind] = d if near[kind] is None else near[kind] + d
                    row_p.append(p.astype(BF16))
                    row_d.append(d.astype(BF16))
                ps.append(jnp.concatenate(row_p, axis=1))
                ds.append(jnp.concatenate(row_d, axis=1))
            pb = jnp.concatenate(ps, axis=0)
            db = jnp.concatenate(ds, axis=0)
            part_v = mm(pb, om)
            part_k = mm(db, qm)
            dv[vc, side] = part_v if (vc, side) not in dv else dv[vc, side] + part_v
            dk[kc, side] = part_k if (kc, side) not in dk else dk[kc, side] + part_k
            part_q = mm(ka.T, db)
            dqt = part_q if dqt is None else dqt + part_q
        at = HDIM if qh == 0 else 0
        sums_ref[0, i * 8 : (i + 1) * 8, :] = dqt[at + 8 : at + 16, :]
        dq_t.append(dqt[:HDIM] if qh == 0 else dqt[HDIM:])
        for kind in range(5):
            near_ref[0, i, kind] = near[kind]
    dq_a = jnp.concatenate([dq_t[0], dq_t[1]], axis=0).T
    dq_b = jnp.concatenate([dq_t[2], jnp.zeros_like(dq_t[2])], axis=0).T
    d_own = jnp.concatenate([dq_a, dk[1, 0], dv[2, 0], dq_b + dv[4, 0], dk[5, 0]], axis=1).astype(BF16)
    d_oth = jnp.concatenate([dk[1, 1], dv[2, 1], dv[4, 1], dk[5, 1]], axis=1).astype(BF16)
    xt, xot, abt = xt_ref[...], xot_ref[...], abt_ref[...]
    g_own = mm(xt, d_own)
    g_oth = mm(xot, d_oth)
    g_ctx = mm(abt, ctx_ref[0])
    ga_ref[:, :LANES] = g_own[:, :LANES].astype(ga_ref.dtype)
    ga_ref[:, LANES : 3 * LANES] = (g_own[:, LANES : 3 * LANES] + g_oth[:, : 2 * LANES]).astype(ga_ref.dtype)
    ga_ref[:, 3 * LANES : 4 * LANES] = g_ctx[:, :LANES].astype(ga_ref.dtype)
    ga_ref[:, 4 * LANES : 5 * LANES] = (g_own[:, 3 * LANES : 4 * LANES] + g_oth[:, 2 * LANES : 3 * LANES]).astype(ga_ref.dtype)
    ga_ref[:, 5 * LANES :] = (g_own[:, 4 * LANES :] + g_oth[:, 3 * LANES :] + g_ctx[:, LANES:]).astype(ga_ref.dtype)
    acc_own[...] += mt(d_own[:, : 3 * LANES], w_ref[:, : 3 * LANES]) + mt(d_own[:, 3 * LANES :], w_ref[:, 4 * LANES :])
    acc_oth[...] += mt(d_oth[:, : 2 * LANES], w_ref[:, LANES : 3 * LANES]) + mt(d_oth[:, 2 * LANES :], w_ref[:, 4 * LANES :])

    @pl.when(m == pl.num_programs(0) - 1)
    def _():
        one_own_ref[...] = acc_own[...]
        one_oth_ref[...] = acc_oth[...].astype(one_oth_ref.dtype)


def whole(shape):
    return pl.BlockSpec(shape, lambda m: (0,) * len(shape))


def params():
    return pltpu.CompilerParams(vmem_limit_bytes=60 * 2**20)


def run_forward(x, xo, wa, line, qaug, kaug, hidden, parts):
    t, d = x.shape
    return pl.pallas_call(
        forward_kernel,
        grid=(parts,),
        in_specs=[
            whole((t, d)), whole((t, d)),
            pl.BlockSpec((d, 6 * LANES), lambda m: (0, m)),
            pl.BlockSpec((1, 8, 4 * LANES), lambda m: (m, 0, 0)),
            pl.BlockSpec((1, 16, LANES), lambda m: (m, 0, 0)),
            whole((2 * t, LANES)), whole((t, d)),
        ],
        out_specs=[
            pl.BlockSpec((1, t, 5 * LANES), lambda m: (m, 0, 0)),
            pl.BlockSpec((1, t, 4 * LANES), lambda m: (m, 0, 0)),
            pl.BlockSpec((1, t, 2 * LANES), lambda m: (m, 0, 0)),
            pl.BlockSpec((1, 8, t), lambda m: (m, 0, 0)),
            whole((t, d)),
        ],
        out_shape=[
            jax.ShapeDtypeStruct((parts, t, 5 * LANES), BF16),
            jax.ShapeDtypeStruct((parts, t, 4 * LANES), BF16),
            jax.ShapeDtypeStruct((parts, t, 2 * LANES), BF16),
            jax.ShapeDtypeStruct((parts, 8, t), F32),
            jax.ShapeDtypeStruct((t, d), F32),
        ],
        scratch_shapes=[
            pltpu.VMEM((t, d), F32),
            pltpu.VMEM((3, 2 * t, t), F32),
            pltpu.VMEM((3, 2 * t, t), BF16),
        ],
        compiler_params=params(),
        name="attend_forward",
    )(x, xo, wa, line, qaug, kaug, hidden)


def run_feed(middle, grad, gains, wi, wo):
    t, d = middle.shape
    units = wi.shape[1]
    tile = min(512, units)
    return pl.pallas_call(
        feed_kernel,
        grid=(units // tile,),
        in_specs=[
            whole((t, d)), whole((t, d)), whole((2, d)),
            pl.BlockSpec((d, tile), lambda f: (0, f)),
            pl.BlockSpec((d, tile), lambda f: (0, f)),
        ],
        out_specs=[
            whole((t, d)), whole((t, d)), whole((8, d)),
            pl.BlockSpec((d, tile), lambda f: (0, f)),
            pl.BlockSpec((d, tile), lambda f: (0, f)),
        ],
        out_shape=[
            jax.ShapeDtypeStruct((t, d), F32),
            jax.ShapeDtypeStruct((t, d), F32),
            jax.ShapeDtypeStruct((8, d), F32),
            jax.ShapeDtypeStruct((d, units), BF16),
            jax.ShapeDtypeStruct((d, units), BF16),
        ],
        scratch_shapes=[
            pltpu.VMEM((t, d), BF16), pltpu.VMEM((d, t), BF16),
            pltpu.VMEM((t, d), BF16), pltpu.VMEM((d, t), BF16),
            pltpu.VMEM((t, d), F32), pltpu.VMEM((t, d), F32),
        ],
        compiler_params=params(),
        name="feed_both",
    )(middle, grad, gains, wi, wo)


def run_backward(x, xo, back, wa, line, qaug, kaug, own, oth, ctx, lse, parts):
    t, d = x.shape
    return pl.pallas_call(
        backward_kernel,
        grid=(parts,),
        in_specs=[
            whole((t, d)), whole((t, d)), whole((t, d)),
            pl.BlockSpec((d, 6 * LANES), lambda m: (0, m)),
            pl.BlockSpec((1, 8, 4 * LANES), lambda m: (m, 0, 0)),
            pl.BlockSpec((1, 16, LANES), lambda m: (m, 0, 0)),
            whole((2 * t, LANES)),
            pl.BlockSpec((1, t, 5 * LANES), lambda m: (m, 0, 0)),
            pl.BlockSpec((1, t, 4 * LANES), lambda m: (m, 0, 0)),
            pl.BlockSpec((1, t, 2 * LANES), lambda m: (m, 0, 0)),
            pl.BlockSpec((1, 8, t), lambda m: (m, 0, 0)),
        ],
        out_specs=[
            pl.BlockSpec((d, 6 * LANES), lambda m: (0, m)),
            whole((t, d)), whole((t, d)),
            pl.BlockSpec((1, 3, 5, LANES, LANES), lambda m: (m, 0, 0, 0, 0)),
            pl.BlockSpec((1, 24, t), lambda m: (m, 0, 0)),
        ],
        out_shape=[
            jax.ShapeDtypeStruct((d, parts * 6 * LANES), BF16),
            jax.ShapeDtypeStruct((t, d), F32),
            jax.ShapeDtypeStruct((t, d), BF16),
            jax.ShapeDtypeStruct((parts, 3, 5, LANES, LANES), F32),
            jax.ShapeDtypeStruct((parts, 24, t), F32),
        ],
        scratch_shapes=[
            pltpu.VMEM((d, t), BF16), pltpu.VMEM((d, t), BF16),
            pltpu.VMEM((t, d), BF16), pltpu.VMEM((d, t), BF16),
            pltpu.VMEM((t, d), F32), pltpu.VMEM((t, d), F32),
        ],
        compiler_params=params(),
        name="attend_backward",
    )(x, xo, back, wa, line, qaug, kaug, own, oth, ctx, lse)


def pack_attn(attn, out_t):
    cut = [[part[:, i * HDIM : (i + 1) * HDIM] for i in range(3)] for part in (attn[0], attn[1], attn[2], out_t)]
    q, k, v, o = cut
    return jnp.concatenate([q[0], q[1], k[0], k[1], v[0], v[1], o[0], o[1], q[2], v[2], k[2], o[2]], axis=1)


def unpack_attn(block):
    c = [block[:, i * HDIM : (i + 1) * HDIM] for i in range(12)]
    attn = jnp.stack(
        [
            jnp.concatenate([c[0], c[1], c[8]], axis=1),
            jnp.concatenate([c[2], c[3], c[10]], axis=1),
            jnp.concatenate([c[4], c[5], c[9]], axis=1),
        ]
    )
    return attn, jnp.concatenate([c[6], c[7], c[11]], axis=1)


def general_body(
    hidden_in, out_grad, attn_weight, out_weight, inner_weight, outer_weight, rel_bias, gains, lengths, table,
    attn_first, attn_second, out_first, out_second, inner_first, inner_second, outer_first, outer_second,
    rel_first, rel_second, gain_first, gain_second, *, parts,
):
    tokens = hidden_in.shape[0]
    nq = tokens // LANES
    heads = rel_bias.shape[1]
    per_seq = SEQLEN // tokens
    mp_index = lax.axis_index("mp")
    half = mp_index % per_seq
    length = lengths[mp_index // per_seq]

    shard = [
        pack_attn(attn_weight.astype(BF16), out_weight.astype(BF16).T),
        inner_weight.astype(BF16),
        outer_weight.astype(BF16).T,
    ]
    gathered = [lax.all_gather(lax.all_gather(s, "dp", axis=0, tiled=True), "mp", axis=1, tiled=True) for s in shard]
    wa, wi, wo = gathered

    x1 = rms_scaled(hidden_in, gains[0]).astype(BF16)
    swap = [(p, p ^ 1) for p in range(parts)]
    x1o = lax.ppermute(x1, "mp", swap)

    u = jnp.arange(4 * LANES)
    offset = jnp.where(u < 2 * LANES, -u, 4 * LANES - u)
    buckets = jnp.arange(rel_bias.shape[0], dtype=jnp.int32)
    line_hot = (jnp.take(table, offset + SEQLEN - 1)[:, None] == buckets[None, :]).astype(F32)
    line = jnp.dot(line_hot, rel_bias, precision=lax.Precision.HIGHEST).T.reshape(parts, heads // parts, 4 * LANES)
    first_flag = (half == 0).astype(F32)
    flags = jnp.stack([jnp.full((4 * LANES,), first_flag), jnp.full((4 * LANES,), 1.0 - first_flag)])
    line_in = jnp.concatenate(
        [line, jnp.broadcast_to(flags[None], (parts, 2, 4 * LANES)), jnp.zeros((parts, 3, 4 * LANES), F32)], axis=1
    )
    far_before, far_after = line[:, :, LANES], line[:, :, 3 * LANES]
    jb, ib = jnp.arange(nq)[None, :], jnp.arange(nq)[:, None]
    own_before, own_after = (jb < ib - 1).astype(F32), (jb > ib + 1).astype(F32)
    oth_before = jnp.full((nq, nq), 1.0 - first_flag)
    w_before = jnp.concatenate([own_before, oth_before], axis=1)
    w_after = jnp.concatenate([own_after, 1.0 - oth_before], axis=1)
    far = far_before[:, :, None, None] * w_before + far_after[:, :, None, None] * w_after
    far_hi = far.astype(BF16).astype(F32)
    far_lo = far - far_hi
    one = jnp.ones((parts, heads // parts, nq, 1), F32)
    blank = jnp.zeros((parts, heads // parts, nq, HDIM), F32)
    q64 = jnp.concatenate(
        [blank[..., :3], one, blank[..., :4], far_hi, far_lo, blank[..., : HDIM - 8 - 4 * nq]], axis=-1
    )
    qaug = jnp.concatenate([q64, q64], axis=-1).reshape(parts, 3 * nq, LANES)
    qaug = jnp.pad(qaug, ((0, 0), (0, 16 - 3 * nq), (0, 0))).astype(BF16)
    row = jnp.arange(2 * tokens)
    position = jnp.where(row < tokens, half * tokens + row, (1 - half) * tokens + row - tokens)
    masked = jnp.where(position < length, 0.0, NEG)
    col = jnp.arange(LANES) % HDIM
    block_of = row // LANES
    hot = ((col >= 8) & (col < 8 + 4 * nq))[None, :] & ((col[None, :] - 8) % (2 * nq) == block_of[:, None])
    kaug = jnp.where((col == 3)[None, :], masked[:, None], hot.astype(F32)).astype(BF16)

    own, oth, ctx, lse, middle = run_forward(x1, x1o, wa, line_in, qaug, kaug, hidden_in, parts)
    block_out, middle_back, gain_two, gi, go = run_feed(middle, out_grad, gains, wi, wo)
    ga, one_own, one_oth, near, sums = run_backward(
        x1, x1o, middle_back, wa, line_in, qaug, kaug, own, oth, ctx, lse, parts
    )
    one_back = one_own + lax.ppermute(one_oth, "mp", swap).astype(F32)
    input_grad, gain_one = rms_back(hidden_in, gains[0:1], one_back)
    input_grad = input_grad + middle_back

    nh = heads // parts
    near = near.reshape(heads, 5, LANES, LANES)
    first_w = first_flag
    blocks = jnp.stack(
        [near[:, 0] + near[:, 4] * (1.0 - first_w), near[:, 1], near[:, 2] + near[:, 3] * first_w], axis=1
    )
    r = jnp.arange(LANES)
    diff = r[None, :, None] - r[None, None, :] + (jnp.arange(3) - 1)[:, None, None] * LANES
    near_bucket = jnp.take(table, diff + SEQLEN - 1).reshape(1, -1)
    near_hot = (near_bucket == buckets[:, None]).astype(F32)
    near_grad = lax.dot_general(
        near_hot, blocks.reshape(heads, -1), (((1,), (1,)), ((), ())), precision=lax.Precision.HIGHEST
    )
    block_sums = jnp.sum(sums.reshape(heads, 2 * nq, nq, LANES), axis=-1)
    far_w = jnp.transpose(jnp.stack([w_before, w_after]), (0, 2, 1))
    corner = jnp.stack([jnp.sum(near[:, 4], (1, 2)) * (1.0 - first_w), jnp.sum(near[:, 3], (1, 2)) * first_w])
    far_grad = jnp.einsum("hji,sji->sh", block_sums, far_w, precision=lax.Precision.HIGHEST) - corner
    far_hot = (jnp.stack([table[0], table[2 * SEQLEN - 2]])[None, :] == buckets[:, None]).astype(F32)
    rel_part = near_grad + jnp.dot(far_hot, far_grad, precision=lax.Precision.HIGHEST)

    owned = [
        lax.psum_scatter(
            lax.psum_scatter(g, "mp", scatter_dimension=1, tiled=True), "dp", scatter_dimension=0, tiled=True
        ).astype(F32)
        for g in (ga, gi, go)
    ]
    g_attn, g_out_t = unpack_attn(owned[0])
    grads = (g_attn, g_out_t.T, owned[1], owned[2].T)
    square_part = sum(jnp.sum(g * g) for g in owned)
    gain_grad, rel_grad, square_total = lax.psum(
        (jnp.concatenate([gain_one, gain_two[:1]], axis=0), rel_part, square_part), ("dp", "mp")
    )
    grad_norm = jnp.sqrt(square_total + jnp.sum(gain_grad * gain_grad) + jnp.sum(rel_grad * rel_grad))
    factor = jnp.minimum(1.0, CLIP / (grad_norm + 1e-06))
    attn_new = adam_step(attn_weight, grads[0], attn_first, attn_second, factor, RATE_MATRIX)
    out_new = adam_step(out_weight, grads[1], out_first, out_second, factor, RATE_OUT)
    inner_new = adam_step(inner_weight, grads[2], inner_first, inner_second, factor, RATE_MATRIX)
    outer_new = adam_step(outer_weight, grads[3], outer_first, outer_second, factor, RATE_MATRIX)
    rel_new = adam_step(rel_bias, rel_grad, rel_first, rel_second, factor, RATE_SMALL)
    gain_new = adam_step(gains, gain_grad, gain_first, gain_second, factor, RATE_SMALL)
    return (block_out, input_grad, grad_norm, *attn_new, *out_new, *inner_new, *outer_new, *rel_new, *gain_new)


def solution(mesh):
    rows = P(("dp", "mp"), None)
    attn, up, down = P(None, "dp", "mp"), P("dp", "mp"), P("mp", "dp")
    in_specs = (
        rows, rows, attn, down, up, down, P(), P(), P("dp"), P(),
        attn, attn, down, down, up, up, down, down, P(), P(), P(), P(),
    )
    out_specs = (rows, rows, P()) + (attn,) * 3 + (down,) * 3 + (up,) * 3 + (down,) * 3 + (P(),) * 6
    plan = body if (mesh.shape["dp"], mesh.shape["mp"]) == (8, 4) else general_body
    return jax.shard_map(
        functools.partial(plan, parts=mesh.shape["mp"]),
        mesh=mesh, in_specs=in_specs, out_specs=out_specs, check_vma=False,
    )
```

```python
import functools

import jax
import jax.numpy as jnp
from jax import lax
from jax.experimental import pallas as pl
from jax.experimental.pallas import tpu as pltpu
from jax.sharding import PartitionSpec as P

HDIM = 64
SEQLEN = 1024
STEP = 10
NORM_EPS = 1e-06
CLIP = 1.0
BETA_ONE = 0.9
BETA_TWO = 0.999
ADAM_EPS = 1e-08
DECAY = 0.01
RATE_MATRIX = 0.05
RATE_OUT = 0.6
RATE_SMALL = 1.0

F32 = jnp.float32
BF16 = jnp.bfloat16
LANES = 128
NEG = -1e30
MESH = pl.DeviceIdType.MESH

HEAD_AT = ((0, 0, 1, 2, 0), (0, 1, 1, 2, 1), (4, 0, 5, 4, 1))


def mm(a, b):
    return lax.dot_general(a, b, (((1,), (0,)), ((), ())), preferred_element_type=F32)


def mt(a, b):
    return lax.dot_general(a, b, (((1,), (1,)), ((), ())), preferred_element_type=F32)


def rms_scaled(value, gain):
    return value * lax.rsqrt(jnp.mean(value * value, axis=-1, keepdims=True) + NORM_EPS) * gain


def rms_back(value, gain, grad):
    factor = lax.rsqrt(jnp.mean(value * value, axis=-1, keepdims=True) + NORM_EPS)
    unit = value * factor
    gain_part = jnp.sum(grad * unit, axis=0, keepdims=True)
    scaled = grad * gain
    result = factor * (scaled - unit * jnp.mean(scaled * unit, axis=-1, keepdims=True))
    return (result, gain_part)


def adam_step(master, grad, first, second, factor, rate):
    clipped = grad * factor
    first_new = BETA_ONE * first + (1.0 - BETA_ONE) * clipped
    second_new = BETA_TWO * second + (1.0 - BETA_TWO) * clipped * clipped
    first_hat = first_new / (1.0 - BETA_ONE**STEP)
    second_hat = second_new / (1.0 - BETA_TWO**STEP)
    master_new = master - rate * (first_hat / (jnp.sqrt(second_hat) + ADAM_EPS) + DECAY * master)
    return (master_new, first_new, second_new)


def half_rows(half):
    lane = lax.broadcasted_iota(jnp.int32, (1, LANES), 1)
    keep = (lane < HDIM) if half == 0 else (lane >= HDIM)
    return keep.astype(F32).astype(BF16)


def bias_tile(line):
    wide = jnp.broadcast_to(line, (LANES, 4 * LANES))
    return pltpu.roll(wide, 0, 1, stride=1, stride_axis=0)


def near_parts(tile):
    return tile[:, LANES : 2 * LANES], tile[:, :LANES], tile[:, 3 * LANES :]


def corner_parts(tile, line, flags):
    before, same, after = near_parts(tile)
    first = (after - line[:, 3 * LANES : 3 * LANES + 1]) * flags
    last = (before - line[:, LANES : LANES + 1]) * (1.0 - flags)
    return first, last


def add_bias(scores, tile, line, flags, nq):
    parts = near_parts(tile)
    corner = corner_parts(tile, line, flags)
    rows = []
    for jb in range(2 * nq):
        row = []
        for ib in range(nq):
            block = scores[jb * LANES : (jb + 1) * LANES, ib * LANES : (ib + 1) * LANES]
            if jb < nq and abs(jb - ib) <= 1:
                block = block + parts[jb - ib + 1]
            elif jb == nq and ib == nq - 1:
                block = block + corner[0]
            elif jb == 2 * nq - 1 and ib == 0:
                block = block + corner[1]
            row.append(block)
        rows.append(jnp.concatenate(row, axis=1))
    return rows


def far_masks(first, nq):
    lane = lax.broadcasted_iota(jnp.int32, (8, LANES), 1) % HDIM
    ib = lax.broadcasted_iota(jnp.int32, (8, LANES), 0)
    jb = (lane - 8) % (2 * nq)
    coded = (lane >= 8) & (lane < 8 + 4 * nq)
    own_before = (coded & (jb < nq) & (jb < ib - 1)).astype(F32)
    own_after = (coded & (jb < nq) & (jb > ib + 1)).astype(F32)
    other = (coded & (jb >= nq)).astype(F32)
    high = (lane < 8 + 2 * nq).astype(F32)
    return own_before + other * (1.0 - first), own_after + other * first, high, (lane == 3).astype(F32)


def query_aug(line, masks, nq):
    before, after, high, one = masks
    far = line[:, LANES : LANES + 1] * before + line[:, 3 * LANES : 3 * LANES + 1] * after
    top = far.astype(BF16).astype(F32)
    rows = (high * top + (1.0 - high) * (far - top) + one).astype(BF16)
    return jnp.concatenate([jnp.broadcast_to(rows[ib : ib + 1, :], (LANES, LANES)) for ib in range(nq)], axis=0)


def turned_hot(table, origin):
    size = 4 * LANES
    hot = (lax.broadcasted_iota(jnp.int32, (LANES, size), 0) == table).astype(F32).astype(BF16)
    at = lax.broadcasted_iota(jnp.int32, (size, size), 0) + lax.broadcasted_iota(jnp.int32, (size, size), 1)
    turn = ((at == origin) | (at == origin + size)).astype(F32).astype(BF16)
    return mm(hot, turn).astype(BF16)


def key_aug(half, length, tokens):
    row = lax.broadcasted_iota(jnp.int32, (2 * tokens, LANES), 0)
    lane = lax.broadcasted_iota(jnp.int32, (2 * tokens, LANES), 1) % HDIM
    position = jnp.where(row < tokens, half * tokens + row, row - half * tokens)
    blocks = 2 * tokens // LANES
    hot = (lane >= 8) & (lane < 8 + 2 * blocks) & ((lane - 8) % blocks == row // LANES)
    masked = (lane == 3) & (position >= length)
    return jnp.where(masked, NEG, hot.astype(F32)).astype(BF16)


def peer(index, stride):
    return index + stride - 2 * stride * ((index // stride) % 2)


class Links:
    def __init__(self):
        self.dp = lax.axis_index("dp")
        self.mp = lax.axis_index("mp")
        self.core = self.dp % 2
        self.chip = self.dp // 2
        self.dp_x, self.dp_y, self.dp_s = peer(self.dp, 2), peer(self.dp, 4), peer(self.dp, 1)
        self.dp_d = peer(self.dp_x, 4)
        self.at_x, self.at_y, self.at_s = (self.dp_x, self.mp), (self.dp_y, self.mp), (self.dp_s, self.mp)
        z1, z2 = peer(self.mp, 1), peer(self.mp, 2)
        self.half = self.mp % 2
        self.first = (1 - self.half).astype(F32)
        self.at_z = (None, (self.dp, z1), (self.dp, z2), (self.dp, peer(z1, 2)))

    def column(self, s):
        return (self.mp + s) % 2 + 2 * ((self.mp // 2 + s // 2) % 2)

    def meet(self, more=()):
        barrier = pltpu.get_barrier_semaphore()
        others = (self.at_x, self.at_y, self.at_s) + self.at_z[1:] + tuple(more)
        for other in others:
            pl.semaphore_signal(barrier, inc=1, device_id=other, device_id_type=MESH)
        pl.semaphore_wait(barrier, len(others))


def remote(src, dst, send, recv, to):
    return pltpu.make_async_remote_copy(
        src_ref=src, dst_ref=dst, send_sem=send, recv_sem=recv, device_id=to, device_id_type=MESH
    )


class Gather:
    def __init__(self, links, w, send, recv, zsend, zrecv):
        self.k, self.w, self.send, self.recv, self.zsend, self.zrecv = links, w, send, recv, zsend, zrecv
        self.rows = w.shape[3]

    def block(self, unit, dp, lo=0, n=None):
        group, s = unit
        return self.w.at[group, s, dp] if n is None else self.w.at[group, s, dp, pl.ds(lo, n)]

    def copy(self, unit, kind, ref, to):
        at = unit[0] * 4 + unit[1]
        return remote(ref, ref, self.send.at[at, kind], self.recv.at[at, kind], to)

    def outgoing(self, unit, kind):
        k, half = self.k, self.rows // 2
        dp, lo, n, to = (
            (k.dp, 0, None, k.at_x),
            (k.dp, 0, None, k.at_y),
            (k.dp, 0, None, k.at_s),
            (k.dp_x, 0, half, k.at_y),
            (k.dp_x, 0, None, k.at_s),
            (k.dp_y, half, half, k.at_x),
            (k.dp_y, 0, None, k.at_s),
            (k.dp_d, 0, None, k.at_s),
        )[kind]
        return self.copy(unit, kind, self.block(unit, dp, lo, n), to)

    def arrived(self, unit, kind):
        k, half = self.k, self.rows // 2
        sib = k.dp_s
        dp, lo, n = {
            0: (k.dp_x, 0, None),
            1: (k.dp_y, 0, None),
            2: (sib, 0, None),
            3: (k.dp_d, 0, half),
            4: (peer(sib, 2), 0, None),
            5: (k.dp_d, half, half),
            6: (peer(sib, 4), 0, None),
            7: (peer(peer(sib, 2), 4), 0, None),
        }[kind]
        self.copy(unit, kind, self.block(unit, dp, lo, n), k.at_x).wait_recv()

    def z_copy(self, group, s):
        at = group * 3 + s - 1
        src = self.block((group, 0), self.k.dp)
        dst = self.block((group, s), self.k.dp)
        return remote(src, dst, self.zsend.at[at], self.zrecv.at[at], self.k.at_z[s])

    def z_arrived(self, unit):
        at = unit[0] * 3 + unit[1] - 1
        ref = self.block(unit, self.k.dp)
        remote(ref, ref, self.zsend.at[at], self.zrecv.at[at], self.k.at_x).wait_recv()

    def run(self, ops):
        for op in ops:
            (self.s1, self.s2, self.s3, self.s4)[op // 16 - 1](UNITS[op % 16])

    def at(self, loop, step, place):
        for number in range(4):
            ops = GATHER_PLAN.get((loop, number), {}).get(place)
            if ops:
                pl.when(step == number)(functools.partial(self.run, ops))

    def s1(self, unit):
        if unit[1] > 0:
            self.z_arrived(unit)
        for kind in (0, 1, 2):
            self.outgoing(unit, kind).start()

    def s2(self, unit):
        self.arrived(unit, 0)
        for kind in (3, 4):
            self.outgoing(unit, kind).start()
        self.arrived(unit, 1)
        for kind in (5, 6):
            self.outgoing(unit, kind).start()

    def s3(self, unit):
        self.arrived(unit, 3)
        self.arrived(unit, 5)
        self.outgoing(unit, 7).start()

    def s4(self, unit):
        for kind in (2, 4, 6, 7):
            self.arrived(unit, kind)

    def finish(self):
        def each(at, carry):
            for kind in range(8):
                self.outgoing((at // 4, at % 4), kind).wait_send()
            return carry

        lax.fori_loop(0, 12, each, 0)
        for group in range(3):
            for s in (1, 2, 3):
                self.z_copy(group, s).wait_send()


UNITS = ((0, 0), (1, 0), (2, 0), (0, 1), (0, 2), (0, 3), (1, 1), (2, 1), (1, 2), (2, 2), (1, 3), (2, 3))
GATHER_AHEAD = (
    (),
    (0x11, 0x20, 0x12, 0x21, 0x13, 0x30, 0x40, 0x22, 0x31, 0x41, 0x23, 0x32, 0x42, 0x33),
)
GATHER_PLAN = {
    ("attend", 0): {0: (0x43,)},
    ("attend", 1): {0: (0x14,), 2: (0x15,), 3: (0x24, 0x16, 0x25, 0x17, 0x34, 0x44)},
    ("attend", 2): {0: (0x26, 0x18), 1: (0x35,), 3: (0x45,)},
    ("attend", 3): {0: (0x27, 0x36, 0x19), 2: (0x46,), 3: (0x28, 0x1a)},
    ("feed", 0): {1: (0x37,)},
    ("feed", 1): {0: (0x47,), 1: (0x29, 0x1b), 2: (0x38,)},
    ("feed", 2): {0: (0x2a, 0x48, 0x39, 0x49), 2: (0x2b,)},
    ("feed", 3): {0: (0x3a, 0x4a, 0x3b, 0x4b)},
}


class Scatter:
    def __init__(self, links, sources, w, sums, piece, diag, side, final, result, send, recv, psem):
        self.k, self.sources, self.w, self.piece, self.final, self.result = links, sources, w, piece, final, result
        self.sums_room, self.diag_room, self.side_room = sums, diag, side
        self.send, self.recv, self.psem = send, recv, psem
        self.rows = w.shape[3]
        chip = links.chip
        self.chips = (chip, peer(chip, 1), peer(chip, 2), peer(peer(chip, 1), 2))

    def sums(self, u):
        return self.sums_room.at[u] if u < 8 else self.w.at[1, u - 8, pl.ds(0, 4)]

    def side(self, u, n):
        return self.side_room.at[u, n] if u < 8 else self.w.at[1, u - 8, 4 + n]

    def diag(self, u, n):
        half = self.rows // 2
        return self.diag_room.at[u, n] if u < 8 else self.w.at[1, u - 8, 6, pl.ds(n * half, half)]

    def outgoing(self, u, kind):
        group, s = BACK_UNITS[u]
        k, half = self.k, self.rows // 2
        at, at_x, at_y, at_d = self.chips
        sums = self.sums(u)
        if kind == 0:
            src, dst, to = self.sources[group].at[s, :, 1 - k.core], sums, k.at_s
        elif kind == 1:
            src, dst, to = sums.at[at_d, pl.ds(0, half)], self.diag(u, 0), k.at_x
        elif kind == 2:
            src, dst, to = sums.at[at_d, pl.ds(half, half)], self.diag(u, 1), k.at_y
        elif kind == 3:
            src, dst, to = sums.at[at_x], self.side(u, 0), k.at_x
        elif kind == 4:
            src, dst, to = sums.at[at_y], self.side(u, 1), k.at_y
        else:
            src, dst, to = sums.at[at], self.final.at[group, s - 1], k.at_z[s]
        return remote(src, dst, self.send.at[u, kind], self.recv.at[u, kind], to)

    def local(self, u):
        group, s = BACK_UNITS[u]
        return pltpu.make_async_copy(self.sources[group].at[s, :, self.k.core], self.piece.at[u % 3], self.psem.at[u % 3])

    def s1(self, u):
        self.outgoing(u, 0).start()
        self.local(u).start()

    def s2(self, u):
        self.local(u).wait()
        self.outgoing(u, 0).wait_recv()
        sums, far = self.sums(u), self.chips[3]
        sums[far] = sums[far] + self.piece[u % 3, far]
        self.outgoing(u, 1).start()
        self.outgoing(u, 2).start()
        for chip in self.chips[:3]:
            sums[chip] = sums[chip] + self.piece[u % 3, chip]

    def s3(self, u):
        half, sums = self.rows // 2, self.sums(u)
        self.outgoing(u, 1).wait_recv()
        self.outgoing(u, 2).wait_recv()
        for chip, lo, n in ((self.chips[2], 0, 0), (self.chips[1], half, 1)):
            sums[chip, lo : lo + half] = sums[chip, lo : lo + half] + self.diag(u, n)[...]
        self.outgoing(u, 3).start()
        self.outgoing(u, 4).start()

    def s4(self, u):
        group, s = BACK_UNITS[u]
        self.outgoing(u, 3).wait_recv()
        self.outgoing(u, 4).wait_recv()
        at, sums = self.chips[0], self.sums(u)
        total = sums[at].astype(F32) + (self.side(u, 0)[...].astype(F32) + self.side(u, 1)[...].astype(F32))
        if s == 0:
            self.result[group] = total
        else:
            sums[at] = total.astype(BF16)
            self.outgoing(u, 5).start()

    def last(self, group):
        total = self.result[group]
        for u, (other, s) in enumerate(BACK_UNITS):
            if other == group and s > 0:
                self.outgoing(u, 5).wait_recv()
        for n in range(3):
            total = total + self.final[group, n].astype(F32)
        self.result[group] = total

    def run(self, ops):
        for op in ops:
            (self.s1, self.s2, self.s3, self.s4)[op // 16 - 1](op % 16)

    def at(self, loop, step, place):
        for number in range(4):
            ops = SCATTER_PLAN.get((loop, number), {}).get(place)
            if ops:
                pl.when(step == number)(functools.partial(self.run, ops))

    def finish(self):
        for u, (group, s) in enumerate(BACK_UNITS):
            for kind in range(5 if s == 0 else 6):
                self.outgoing(u, kind).wait_send()


BACK_UNITS = ((1, 0), (2, 0), (1, 1), (2, 1), (1, 2), (2, 2), (1, 3), (2, 3), (0, 3), (0, 2), (0, 1), (0, 0))
SCATTER_PLAN = {
    ("feed", 1): {1: (0x10, 0x11)},
    ("feed", 2): {0: (0x20, 0x21), 1: (0x12, 0x13)},
    ("feed", 3): {0: (0x30, 0x31, 0x22, 0x23), 1: (0x14, 0x15)},
    ("other", 0): {0: (0x32, 0x33, 0x24, 0x25, 0x41, 0x17)},
    ("other", 1): {0: (0x42,)},
    ("other", 2): {0: (0x34, 0x35, 0x26, 0x27, 0x43)},
    ("other", 3): {0: (0x44,)},
    ("own", 0): {0: (0x36, 0x45), 1: (0x37,), 3: (0x18,)},
    ("own", 1): {0: (0x46,), 2: (0x28, 0x47), 3: (0x19,)},
    ("own", 2): {0: (0x38,), 2: (0x29,), 3: (0x1a,)},
    ("own", 3): {0: (0x48,), 1: (0x39,), 2: (0x2a,), 3: (0x1b,)},
}
SCATTER_BETWEEN = ((0x40,), (0x16,))
SCATTER_AFTER = ((0x49,), (0x3a, 0x2b), (0x4a, 0x3b), (0x4b,))


def layer_kernel(
    lengths_ref, attn_ref, wout_ref, inner_ref, outer_ref, table_ref, rel_ref, gain_ref, hidden_hbm, grad_hbm,
    out_hbm, input_hbm, small_ref, result_ref, gi_hbm, go_hbm,
    w, x_ref, xo, own, oth, ctx, s_ref, e_ref, middle, grad, x2_ref, x2t_ref, ob_ref, obt_ref, acc_out, acc_two, g_all, kaug_ref,
    lse_ref, line_ref, center_ref, near_ref, oth_in, sums, piece, diag, side, final,
    line_grad, far_grad, small, small_near, small_z,
    send, recv, zsend, zrecv, xsem, lsem, gsem, osem, bsend, brecv, psem, tsend, trecv,
):
    tokens = x_ref.shape[0]
    nq = tokens // LANES
    links = Links()
    net = Gather(links, w, send, recv, zsend, zrecv)
    group = []
    for n in range(1, 8):
        dp = links.dp
        for stride in (1, 2, 4):
            if n & stride:
                dp = peer(dp, stride)
        group.append((dp, links.mp))
    back = Scatter(links, (g_all, gi_hbm, go_hbm), w, sums, piece, diag, side, final, result_ref, bsend, brecv, psem)
    width = w.shape[2] * w.shape[3]

    def weights(kind, s, lo=0, hi=None):
        part = w[kind, s, :, :, lo:] if hi is None else w[kind, s, :, :, lo:hi]
        return part.reshape(width, part.shape[2])

    get_hidden = pltpu.make_async_copy(hidden_hbm, middle, lsem.at[0])
    get_grad = pltpu.make_async_copy(grad_hbm, grad, lsem.at[1])
    get_hidden.start()
    def own_block(group):
        return (group, 0, links.dp)

    parts = [attn_ref[n].astype(BF16) for n in range(3)] + [wout_ref[...].T.astype(BF16)]
    q, k, v, o = [(part[:, :LANES], part[:, LANES:]) for part in parts]
    w[own_block(0)] = jnp.concatenate([q[0], k[0], v[0], o[0], q[1], v[1], k[1], o[1]], axis=1)
    w[own_block(1)] = inner_ref[...].astype(BF16)
    w[own_block(2)] = outer_ref[...].astype(BF16)
    get_grad.start()
    links.meet([group[n] for n in (2, 4, 5, 6)])
    net.z_copy(0, 1).start()
    inner_z = links.mp % 3 != 0

    @pl.when(inner_z)
    def _():
        for kind in range(3):
            net.z_copy(kind, 3).start()

    net.s1(UNITS[0])
    get_hidden.wait()
    x_ref[...] = rms_scaled(middle[...], gain_ref[0:1, :]).astype(BF16)
    xcopy = remote(x_ref, xo, xsem.at[0], xsem.at[1], links.at_z[1])
    xcopy.start()
    near_table = table_ref[SEQLEN - 2 * LANES : SEQLEN + 2 * LANES].reshape(1, 4 * LANES)
    hot = turned_hot(near_table, 2 * LANES - 1)[: rel_ref.shape[1]]
    high = rel_ref[...].astype(BF16)
    rest = rel_ref[...] - high.astype(F32)
    mid = rest.astype(BF16)
    low = (rest - mid.astype(F32)).astype(BF16)
    line_ref[...] = mm(high, hot) + (mm(mid, hot) + mm(low, hot))
    kaug_ref[...] = key_aug(links.half, lengths_ref[links.mp // 2], tokens)
    far = far_masks(links.first, nq)
    net.run(GATHER_AHEAD[0])
    get_grad.wait()
    ob = grad[...].astype(BF16)
    ob_ref[...] = ob
    obt_ref[...] = ob.T
    net.run(GATHER_AHEAD[1])
    xcopy.wait_send()
    net.z_copy(0, 2).start()

    @pl.when(jnp.logical_not(inner_z))
    def _():
        net.z_copy(0, 3).start()

    for step in (1, 2):
        net.z_copy(1, step).start()
        net.z_copy(2, step).start()

    @pl.when(jnp.logical_not(inner_z))
    def _():
        net.z_copy(1, 3).start()
        net.z_copy(2, 3).start()

    xcopy.wait_recv()

    masks = [half_rows(0), half_rows(1)]
    count = lax.broadcasted_iota(jnp.int32, (HDIM, 2 * tokens), 0)
    ones = (count == 0).astype(F32).astype(BF16)

    def attend(s, carry):
        x, other = x_ref[...], xo[...]
        p_a = mm(x, weights(0, s, 0, 3 * LANES)).astype(BF16)
        p_b = mm(x, weights(0, s, 4 * LANES)).astype(BF16)
        o_a = mm(other, weights(0, s, LANES, 3 * LANES)).astype(BF16)
        o_b = mm(other, weights(0, s, 4 * LANES)).astype(BF16)
        own[s, :, : 3 * LANES] = p_a
        own[s, :, 3 * LANES :] = p_b
        oth[s, :, : 2 * LANES] = o_a
        oth[s, :, 2 * LANES :] = o_b
        cols_own = {0: p_a[:, :LANES], 1: p_a[:, LANES : 2 * LANES], 2: p_a[:, 2 * LANES :], 4: p_b[:, :LANES], 5: p_b[:, LANES:]}
        cols_oth = {1: o_a[:, :LANES], 2: o_a[:, LANES:], 4: o_b[:, :LANES], 5: o_b[:, LANES:]}
        both = {c: jnp.concatenate([cols_own[c], cols_oth[c]], axis=0) for c in (1, 2, 4, 5)}
        m = links.column(s)
        v_t = {2: both[2].T, 4: both[4].T}
        pieces = []
        stats = []
        for i, (qc, qh, kc, vc, vh) in enumerate(HEAD_AT):
            net.at("attend", s, i)
            line = line_ref[pl.ds(3 * m + i, 1), :]
            tile = bias_tile(line)
            qa = cols_own[qc] * masks[qh] + query_aug(line, far, nq) * masks[1 - qh]
            ka = both[kc] * masks[qh] + kaug_ref[...] * masks[1 - qh]
            scores = mt(ka, qa)
            peak = None
            for jb, row in enumerate(add_bias(scores, tile, line, links.first, nq)):
                s_ref[i % 2 * 2 * nq + jb] = row
                top = jnp.max(row.reshape(LANES // 8, 8, tokens), axis=0)
                peak = top if peak is None else jnp.maximum(peak, top)
            peak = jnp.max(peak, axis=0, keepdims=True)
            for jb in range(2 * nq):
                rows = slice(jb % nq * LANES, (jb % nq + 1) * LANES)
                e_ref[i % 2 * 2 + jb // nq, rows, :] = jnp.exp(s_ref[i % 2 * 2 * nq + jb] - peak).astype(BF16)
            if vh == 0:
                va = jnp.concatenate([v_t[vc][:HDIM], ones], axis=0)
            else:
                va = jnp.concatenate([ones, v_t[vc][HDIM:]], axis=0)
            ot = mm(va, e_ref[i % 2 * 2 : i % 2 * 2 + 2].reshape(2 * tokens, tokens))
            at = HDIM if vh == 0 else 0
            total = ot[at : at + 1, :]
            stats.append(peak + jnp.log(total))
            real = ot[:HDIM] if vh == 0 else ot[HDIM:]
            pieces.append(real / total)
        zero = jnp.zeros((HDIM, tokens), F32)
        ctx_a = jnp.concatenate([pieces[0], pieces[1]], axis=0).T.astype(BF16)
        ctx_b = jnp.concatenate([zero, pieces[2]], axis=0).T.astype(BF16)
        ctx[s, :, :LANES] = ctx_a
        ctx[s, :, LANES:] = ctx_b
        lse_ref[s] = jnp.concatenate(stats + [jnp.zeros((5, tokens), F32)], axis=0)
        middle[...] += mt(ctx_a, weights(0, s, 3 * LANES, 4 * LANES)) + mt(ctx_b, weights(0, s, 5 * LANES))
        net.at("attend", s, 3)
        return carry

    lax.fori_loop(0, 4, attend, 0)

    x2 = rms_scaled(middle[...], gain_ref[1:2, :]).astype(BF16)
    x2_ref[...] = x2
    x2t_ref[...] = x2.T
    acc_out[...] = jnp.zeros_like(acc_out)
    acc_two[...] = jnp.zeros_like(acc_two)

    def g_copies(t):
        return (
            pltpu.make_async_copy(g_all.at[t % 2 * 2], gi_hbm.at[t], gsem.at[t % 2, 0]),
            pltpu.make_async_copy(g_all.at[t % 2 * 2 + 1], go_hbm.at[t], gsem.at[t % 2, 1]),
        )

    def feed(t, carry):
        tile = 2 * LANES
        for n in range(w.shape[4] // tile):
            net.at("feed", t, n)
            if n == 1:

                @pl.when(t >= 1)
                def _():
                    for copy in g_copies(t - 1):
                        copy.wait()

            back.at("feed", t, n)
            if n == 0:
                net.at("feed", t, 3)
            wi = weights(1, t, n * tile, (n + 1) * tile)
            wo = weights(2, t, n * tile, (n + 1) * tile)
            inner = mm(x2_ref[...], wi)
            active_back = mm(ob_ref[...], wo)
            c = 0.7978845608028654
            sq = inner * inner
            th = jnp.tanh(c * (inner + 0.044715 * (sq * inner)))
            half = 0.5 * (1.0 + th)
            active = (inner * half).astype(BF16)
            slope = half + (0.5 * c) * inner * (1.0 - th * th) * (1.0 + (3 * 0.044715) * sq)
            inner_back = (slope * active_back).astype(BF16)
            acc_out[...] += mt(active, wo)
            acc_two[...] += mt(inner_back, wi)
            at = slice(n * tile, (n + 1) * tile)
            shape = (*w.shape[2:4], tile)
            split = (shape[0] // 2, 2, *shape[1:])
            g_all[t % 2 * 2, :, :, :, at] = mm(x2t_ref[...], inner_back).astype(BF16).reshape(split)
            g_all[t % 2 * 2 + 1, :, :, :, at] = mm(obt_ref[...], active).astype(BF16).reshape(split)
        for copy in g_copies(t):
            copy.start()
        return carry

    lax.fori_loop(0, 4, feed, 0)
    back.run(SCATTER_BETWEEN[0])
    acc_out[...] += middle[...]
    put_out = pltpu.make_async_copy(acc_out, out_hbm, lsem.at[2])
    put_out.start()
    result, gain_two = rms_back(middle[...], gain_ref[1:2, :], acc_two[...])
    get_hidden = pltpu.make_async_copy(hidden_hbm, middle, lsem.at[0])
    get_hidden.start()
    grad[...] += result
    net.finish()
    for copy in g_copies(3):
        copy.wait()
    back.run(SCATTER_BETWEEN[1])
    ab_ref, abt, xt, acc_own, acc_oth, oth_out = x2_ref, x2t_ref, obt_ref, acc_out, acc_two, ob_ref
    ab = grad[...].astype(BF16)
    ab_ref[...] = ab
    abt[...] = ab.T
    xt[...] = x_ref[...].T
    w[2, 0, :, :, : tokens] = xo[...].T.reshape(*w.shape[2:4], tokens)
    acc_oth[...] = jnp.zeros_like(acc_oth)
    line_grad[...] = jnp.zeros_like(line_grad)
    far_grad[...] = jnp.zeros_like(far_grad)
    jb = lax.broadcasted_iota(jnp.int32, (2 * nq, tokens), 0)
    ib = lax.broadcasted_iota(jnp.int32, (2 * nq, tokens), 1) // LANES
    edge_first = ((jb == nq) & (ib == nq - 1)).astype(F32)
    edge_last = ((jb == 2 * nq - 1) & (ib == 0)).astype(F32)
    other_key = (jb >= nq).astype(F32)
    sum_before = ((jb < nq) & (jb < ib - 1)).astype(F32) + (other_key - edge_last) * (1.0 - links.first)
    sum_after = ((jb < nq) & (jb > ib + 1)).astype(F32) + (other_key - edge_first) * links.first
    own_at = {c: slice(at * LANES, (at + 1) * LANES) for at, c in enumerate((0, 1, 2, 4, 5))}
    oth_at = {c: slice(at * LANES, (at + 1) * LANES) for at, c in enumerate((1, 2, 4, 5))}
    cb_at = {2: slice(0, LANES), 4: slice(LANES, 2 * LANES)}
    at_row = lax.broadcasted_iota(jnp.int32, (LANES, LANES), 0) + lax.broadcasted_iota(jnp.int32, (LANES, LANES), 1)
    mirror = (at_row == LANES - 1).astype(F32).astype(BF16)

    def context_back(s):
        return {
            2: mm(ab_ref[...], weights(0, s, 3 * LANES, 4 * LANES)).astype(BF16),
            4: mm(ab_ref[...], weights(0, s, 5 * LANES)).astype(BF16),
        }

    def one_side(s, i, other, cb):
        qc, qh, kc, vc, vh = HEAD_AT[i]
        line = line_ref[pl.ds(3 * links.column(s) + i, 1), :]
        tile = bias_tile(line)
        qm = own[s, :, own_at[qc]] * masks[qh]
        qa = qm + query_aug(line, far, nq) * masks[1 - qh]
        om = cb[vc] * masks[vh]
        center = center_ref[s, i : i + 1, :]
        lse = lse_ref[s, i : i + 1, :]
        parts = near_parts(tile)
        corner = corner_parts(tile, line, links.first)
        side = 1 if other else 0
        k_cols = oth[s, :, oth_at[kc]] if other else own[s, :, own_at[kc]]
        v_cols = oth[s, :, oth_at[vc]] if other else own[s, :, own_at[vc]]
        ka = k_cols * masks[qh] + kaug_ref[side * tokens : (side + 1) * tokens] * masks[1 - qh]
        scores = mt(ka, qa)
        chance_back = mt(v_cols, om)
        near = [None] * 5
        ps, ds = [], []
        for jb in range(nq):
            row_p, row_d = [], []
            for ib in range(nq):
                at = (slice(jb * LANES, (jb + 1) * LANES), slice(ib * LANES, (ib + 1) * LANES))
                block = scores[at]
                kind = None
                if not other and abs(jb - ib) <= 1:
                    kind = jb - ib + 1
                    block = block + parts[kind]
                elif other and jb == 0 and ib == nq - 1:
                    kind = 3
                    block = block + corner[0]
                elif other and jb == nq - 1 and ib == 0:
                    kind = 4
                    block = block + corner[1]
                p = jnp.exp(block - lse[:, at[1]])
                d = p * (chance_back[at] - center[:, at[1]])
                if kind is not None:
                    near[kind] = d if near[kind] is None else near[kind] + d
                row_p.append(p.astype(BF16))
                row_d.append(d.astype(BF16))
            ps.append(jnp.concatenate(row_p, axis=1))
            ds.append(jnp.concatenate(row_d, axis=1))
        pb = jnp.concatenate(ps, axis=0)
        db = jnp.concatenate(ds, axis=0)
        return mm(ka.T, db), mm(db, qm), mm(pb, om), near

    def other_side(it, carry):
        s = 3 - it
        cb = context_back(s)
        centers = []
        for i in range(3):
            vc, vh = HEAD_AT[i][3:]
            prod = cb[vc].astype(F32) * ctx[s, :, cb_at[vc]].astype(F32)
            high = prod.astype(BF16)
            low = (prod - high.astype(F32)).astype(BF16)
            pick = jnp.broadcast_to(masks[vh], (8, LANES))
            centers.append((mt(pick, high) + mt(pick, low))[0:1, :])
        center_ref[s] = jnp.concatenate(centers + [jnp.zeros((5, tokens), F32)], axis=0)
        dk, dv = {}, {}
        for i, (qc, qh, kc, vc, vh) in enumerate(HEAD_AT):
            back.at("other", it, i)
            s_ref[3 * s + i], part_k, part_v, near = one_side(s, i, True, cb)
            dk[kc] = dk[kc] + part_k if kc in dk else part_k
            dv[vc] = dv[vc] + part_v if vc in dv else part_v
            near_ref[s, i] = near[3] * links.first + near[4] * (1.0 - links.first)
        d = jnp.concatenate([dk[1], dv[2], dv[4], dk[5]], axis=1).astype(BF16)
        e_ref[s] = d
        acc_oth[...] += mt(d[:, : 2 * LANES], weights(0, s, LANES, 3 * LANES)) + mt(d[:, 2 * LANES :], weights(0, s, 4 * LANES))
        return carry

    lax.fori_loop(0, 4, other_side, 0)
    oth_out[...] = acc_oth[...].astype(BF16)
    swap = remote(oth_out, oth_in, osem.at[0], osem.at[1], links.at_z[1])
    swap.start()

    def own_side(it, carry):
        s = 3 - it
        m = links.column(s)
        cb = context_back(s)
        dk, dv, dq = {}, {}, []
        for i, (qc, qh, kc, vc, vh) in enumerate(HEAD_AT):
            back.at("own", it, i)
            part_q, part_k, part_v, near = one_side(s, i, False, cb)
            part_q = part_q + s_ref[3 * s + i]
            dk[kc] = dk[kc] + part_k if kc in dk else part_k
            dv[vc] = dv[vc] + part_v if vc in dv else part_v
            at = HDIM if qh == 0 else 0
            block_sums = part_q[at + 8 : at + 8 + 2 * nq, :]
            head = pl.ds(3 * m + i, 1)
            far_grad[0, head, :] = jnp.sum(block_sums * sum_before, axis=0, keepdims=True)
            far_grad[1, head, :] = jnp.sum(block_sums * sum_after, axis=0, keepdims=True)
            dq.append(part_q[:HDIM] if qh == 0 else part_q[HDIM:])
            first, final_corner = near_ref[s, i] * links.first, near_ref[s, i] * (1.0 - links.first)
            blank = jnp.zeros((LANES, LANES), F32)
            tile = jnp.concatenate([near[1], near[0] + final_corner, blank, near[2] + first], axis=1)
            high = tile.astype(BF16)
            low = (tile - high.astype(F32)).astype(BF16)
            turned = pltpu.roll(mm(mirror, high) + mm(mirror, low), 0, 1, stride=1, stride_axis=0)
            line_grad[head, :] = jnp.sum(turned, axis=0, keepdims=True)
        dq_a = jnp.concatenate([dq[0], dq[1]], axis=0).T
        dq_b = jnp.concatenate([dq[2], jnp.zeros_like(dq[2])], axis=0).T
        d_own = jnp.concatenate([dq_a, dk[1], dv[2], dq_b + dv[4], dk[5]], axis=1).astype(BF16)
        g_own = mm(xt[...], d_own)
        g_oth = mm(w[2, 0, :, :, :tokens].reshape(width, tokens), e_ref[s])
        g_ctx = mm(abt[...], ctx[s])
        columns = [
            g_own[:, :LANES],
            g_own[:, LANES : 3 * LANES] + g_oth[:, : 2 * LANES],
            g_ctx[:, :LANES],
            g_own[:, 3 * LANES : 4 * LANES] + g_oth[:, 2 * LANES : 3 * LANES],
            g_own[:, 4 * LANES :] + g_oth[:, 3 * LANES :] + g_ctx[:, LANES:],
        ]
        g = jnp.concatenate(columns, axis=1).astype(BF16)
        rows = w.shape[3]
        for n in range(8):
            g_all[s, n // 2, n % 2] = g[n * rows : (n + 1) * rows, :]
        back.at("own", it, 3)
        acc_own[...] += mt(d_own[:, : 3 * LANES], weights(0, s, 0, 3 * LANES)) + mt(d_own[:, 3 * LANES :], weights(0, s, 4 * LANES))
        return carry

    put_out.wait()
    acc_own[...] = jnp.zeros_like(acc_own)
    lax.fori_loop(0, 4, own_side, 0)
    back.run(SCATTER_AFTER[0])
    back.run(SCATTER_AFTER[1])
    get_hidden.wait()
    swap.wait_recv()
    one_back = acc_own[...] + oth_in[...].astype(F32)
    value, gain_part = rms_back(middle[...], gain_ref[0:1, :], one_back)
    acc_own[...] = value + grad[...]
    put_grad = pltpu.make_async_copy(acc_own, input_hbm, lsem.at[2])
    put_grad.start()
    lane = lax.broadcasted_iota(jnp.int32, (16, 4 * LANES), 1)
    by_line = (
        line_grad[...]
        + jnp.sum(far_grad[0], axis=1, keepdims=True) * (lane == 2 * LANES - 1).astype(F32)
        + jnp.sum(far_grad[1], axis=1, keepdims=True) * (lane == 4 * LANES - 1).astype(F32)
    )
    high = by_line.astype(BF16)
    low = (by_line - high.astype(F32)).astype(BF16)
    hot = turned_hot(near_table, 3 * LANES - 2)
    small[0:16, :] = mt(high, hot) + mt(low, hot)
    for n in range(6):
        at = slice(n * LANES, (n + 1) * LANES)
        small[16 + n : 17 + n, :] = gain_part[:, at]
        small[22 + n : 23 + n, :] = gain_two[:, at]
    small[28:32, :] = jnp.zeros((4, LANES), F32)

    def to_group(lo, n, at):
        here = small.at[pl.ds(lo, n)]
        return [remote(here, small_near.at[k, pl.ds(lo, n)], tsend.at[at + k], trecv.at[at + k], to) for k, to in enumerate(group)]

    def along_z(lo, n, at):
        here = small_z.at[0, pl.ds(lo, n)]
        return [
            remote(here, small_z.at[k, pl.ds(lo, n)], tsend.at[at + k], trecv.at[at + k], links.at_z[k]) for k in (1, 2, 3)
        ]

    def total(lo, n):
        value = small[lo : lo + n, :]
        for k in range(7):
            value = value + small_near[k, lo : lo + n, :]
        return value

    def squares_of(weight):
        back.last(weight)
        value = result_ref[weight]
        value = value * value
        parts = [
            jnp.sum(value[:, n * LANES : (n + 1) * LANES].reshape(-1, 8, LANES), axis=0) for n in range(value.shape[1] // LANES)
        ]
        return functools.reduce(jnp.add, parts)

    squares = squares_of(1) + squares_of(2)
    back.run(SCATTER_AFTER[2])
    early = to_group(0, 32, 0)
    for copy in early:
        copy.start()
    back.run(SCATTER_AFTER[3])
    squares = squares + squares_of(0)
    small[32:40, :] = squares
    late = to_group(32, 8, 11)
    for copy in late:
        copy.start()
    for copy in early:
        copy.wait_recv()
    small_z[0, 0:32, :] = total(0, 32)
    for copy in late:
        copy.wait_recv()
    small_z[0, 32:40, :] = total(32, 8)
    late_z = along_z(0, 40, 18)
    for copy in late_z:
        copy.start()
    back.finish()
    for copy in late_z:
        copy.wait_recv()
    small_ref[...] = (small_z[0] + small_z[1]) + (small_z[2] + small_z[3])
    for copy in early + late + late_z:
        copy.wait_send()
    put_grad.wait()
    swap.wait_send()


def update_kernel(small_ref, grad_hbm, block_hbm, input_hbm, *refs):
    hbm, (block_out, input_out, norm_ref), new_hbm = refs[:18], refs[18:21], refs[21:39]
    held, new, grad_ref, pass_ref, sem = refs[39:57], refs[57:75], refs[75], refs[76], refs[77]
    results = [pltpu.make_async_copy(a, b, sem.at[23 + n]) for n, (a, b) in enumerate(zip(new, new_hbm))]
    through = ((block_hbm, block_out), (input_hbm, input_out))
    fetch = [pltpu.make_async_copy(a, pass_ref.at[n], sem.at[n]) for n, (a, b) in enumerate(through)]
    store = [pltpu.make_async_copy(pass_ref.at[n], b, sem.at[21 + n]) for n, (a, b) in enumerate(through)]
    loads = [pltpu.make_async_copy(a, b, sem.at[2 + n]) for n, (a, b) in enumerate(zip(hbm, held))]
    loads.append(pltpu.make_async_copy(grad_hbm, grad_ref, sem.at[20]))
    for copy in loads[::-1] + fetch:
        copy.start()
    attn, out, inner, outer, rel, gain, attn_first, attn_second, out_first, out_second = held[:10]
    inner_first, inner_second, outer_first, outer_second, rel_first, rel_second, gain_first, gain_second = held[10:]
    small = small_ref[0:28, :]
    squares = jnp.sum(small * small, axis=0, keepdims=True) + jnp.sum(small_ref[32:40, :], axis=0, keepdims=True)
    norm = jnp.sqrt(jnp.sum(squares, axis=1, keepdims=True))
    norm_ref[...] = norm
    factor = jnp.minimum(1.0, CLIP / (norm + 1e-06))
    loads[18].wait()

    def ready(*which):
        for n in which:
            loads[n].wait()

    def put(*which):
        for n in which:
            results[n].start()

    def step(at, grad, rate, master, first, second, outs):
        for ref, value in zip(outs, adam_step(master[at], grad, first[at], second[at], factor, rate)):
            ref[at] = value

    whole = slice(None)

    def turned(column):
        return pltpu.roll(column, HDIM, 1)[:, :HDIM]

    ready(2, 10, 11)
    step(whole, grad_ref[1], RATE_MATRIX, inner, inner_first, inner_second, new[6:9])
    put(6, 7, 8)
    ready(3, 12, 13)
    step(whole, grad_ref[2], RATE_MATRIX, outer, outer_first, outer_second, new[9:12])
    put(9, 10, 11)
    for a, b in zip(fetch, store):
        a.wait()
        b.start()
    ready(0, 6, 7)
    g = [grad_ref[0, :, n * LANES : (n + 1) * LANES] for n in range(6)]
    tails = (g[4][:, :HDIM], g[5][:, :HDIM], turned(g[4]))
    for n in range(3):
        step((n, slice(None), slice(0, LANES)), g[n], RATE_MATRIX, attn, attn_first, attn_second, new[0:3])
        step((n, slice(None), slice(LANES, LANES + HDIM)), tails[n], RATE_MATRIX, attn, attn_first, attn_second, new[0:3])
    put(0, 1, 2)
    ready(1, 8, 9)
    rows = g[3].shape[0]
    blank = jnp.zeros((LANES - rows, LANES), F32)
    lower = pltpu.roll(g[5], HDIM, 1)
    step((slice(0, LANES), whole), jnp.concatenate([g[3], blank], axis=0).T[:, :rows], RATE_OUT, out, out_first, out_second, new[3:6])
    step(
        (slice(LANES, LANES + HDIM), whole),
        jnp.concatenate([lower, blank], axis=0).T[:HDIM, :rows],
        RATE_OUT, out, out_first, out_second, new[3:6],
    )
    put(3, 4, 5)
    ready(4, 5, 14, 15, 16, 17)
    heads, buckets = rel.shape
    step(whole, small_ref[0:heads, 0:buckets], RATE_SMALL, rel, rel_first, rel_second, new[12:15])
    gain_grad = jnp.concatenate(
        [
            jnp.concatenate([small_ref[at + n : at + n + 1, :] for n in range(6)], axis=1)
            for at in (16, 22)
        ],
        axis=0,
    )
    step(whole, gain_grad, RATE_SMALL, gain, gain_first, gain_second, new[15:18])
    put(*range(12, 18))
    for copy in store + results:
        copy.wait()


def run_layer(lengths, attn, out, inner, outer, table, rel, gains, hidden, grad):
    t, d = hidden.shape
    parts, (rows, cols) = rel.shape[0] // 3, inner.shape
    any_space = pl.BlockSpec(memory_space=pl.ANY)
    vmem = pl.BlockSpec(memory_space=pltpu.VMEM)
    dma = pltpu.SemaphoreType.DMA
    split = (parts, 4, 2, rows, cols)
    low = lambda *shape: pltpu.VMEM(shape, BF16)
    full = lambda *shape: pltpu.VMEM(shape, F32)
    return pl.pallas_call(
        layer_kernel,
        in_specs=[pl.BlockSpec(memory_space=pltpu.SMEM)] + [vmem] * 7 + [any_space] * 2,
        out_specs=[any_space] * 2 + [vmem] * 2 + [any_space] * 2,
        out_shape=[
            jax.ShapeDtypeStruct((t, d), F32),
            jax.ShapeDtypeStruct((t, d), F32),
            jax.ShapeDtypeStruct((40, LANES), F32),
            jax.ShapeDtypeStruct((3, rows, cols), F32),
            jax.ShapeDtypeStruct(split, BF16),
            jax.ShapeDtypeStruct(split, BF16),
        ],
        scratch_shapes=[
            low(3, parts, 8, rows, cols), low(t, d), low(t, d),
            low(parts, t, 5 * LANES), low(parts, t, 4 * LANES), low(parts, t, 2 * LANES),
            full(4 * t // LANES, LANES, t), low(4, t, t), full(t, d), full(t, d),
            low(t, d), low(d, t), low(t, d), low(d, t), full(t, d), full(t, d), low(*split), low(2 * t, LANES),
            full(parts, 8, t), full(rel.shape[0], 4 * LANES), full(parts, 8, t), full(parts, 3, LANES, LANES), low(t, d),
            low(8, 4, rows, cols), low(3, 4, rows, cols), low(8, 2, rows // 2, cols), low(8, 2, rows, cols), low(3, 3, rows, cols),
            full(16, 4 * LANES), full(2, 16, 4 * LANES), full(40, LANES), full(7, 40, LANES), full(4, 40, LANES),
            dma((12, 8)), dma((12, 8)), dma((9,)), dma((9,)), dma((2,)), dma((3,)), dma((2, 2)), dma((2,)),
            dma((12, 6)), dma((12, 6)), dma((3,)), dma((22,)), dma((22,)),
        ],
        compiler_params=pltpu.CompilerParams(
            vmem_limit_bytes=63 * 2**20, collective_id=0, has_side_effects=True
        ),
        name="layer",
    )(lengths, attn, out, inner, outer, table, rel, gains, hidden, grad)


def run_update(small, grads, block_out, input_grad, masters, moments):
    vmem = pl.BlockSpec(memory_space=pltpu.VMEM)
    hbm = pl.BlockSpec(memory_space=pltpu.HBM)
    like = lambda a: jax.ShapeDtypeStruct(a.shape, F32)
    return pl.pallas_call(
        update_kernel,
        in_specs=[vmem] + [hbm] * 21,
        out_specs=[hbm] * 2 + [vmem] + [hbm] * 18,
        out_shape=[like(block_out), like(input_grad), jax.ShapeDtypeStruct((1, 1), F32)]
        + [like(a) for a in masters for _ in range(3)],
        scratch_shapes=[pltpu.VMEM(a.shape, F32) for a in (*masters, *moments)]
        + [pltpu.VMEM(a.shape, F32) for a in masters for _ in range(3)]
        + [pltpu.VMEM(grads.shape, F32)]
        + [pltpu.VMEM((2, *block_out.shape), F32), pltpu.SemaphoreType.DMA((41,))],
        compiler_params=pltpu.CompilerParams(vmem_limit_bytes=62 * 2**20),
        name="update",
    )(small, grads, block_out, input_grad, *masters, *moments)


def body(
    hidden_in, out_grad, attn_weight, out_weight, inner_weight, outer_weight, rel_bias, gains, lengths, table,
    attn_first, attn_second, out_first, out_second, inner_first, inner_second, outer_first, outer_second,
    rel_first, rel_second, gain_first, gain_second, *, parts,
):
    block_out, input_grad, small, owned, _, _ = run_layer(
        lengths, attn_weight, out_weight, inner_weight, outer_weight.T, table, rel_bias.T, gains, hidden_in, out_grad
    )
    new = run_update(
        small, owned, block_out, input_grad,
        (attn_weight, out_weight, inner_weight, outer_weight.T, rel_bias.T, gains),
        (
            attn_first, attn_second, out_first, out_second, inner_first, inner_second,
            outer_first.T, outer_second.T, rel_first.T, rel_second.T, gain_first, gain_second,
        ),
    )
    masters = new[3:]
    return (
        new[0], new[1], new[2].reshape(()), *masters[:9], *(a.T for a in masters[9:12]), *(a.T for a in masters[12:15]), *masters[15:],
    )


def plain_corner_parts(tile, line, flags):
    before, same, after = near_parts(tile)
    first = (after - line[:, 3 * LANES : 3 * LANES + 1]) * flags[0]
    last = (before - line[:, LANES : LANES + 1]) * flags[1]
    return first, last


def plain_add_bias(scores, tile, line, flags, nq):
    parts = near_parts(tile)
    corner = plain_corner_parts(tile, line, flags)
    rows = []
    for jb in range(2 * nq):
        row = []
        for ib in range(nq):
            block = scores[jb * LANES : (jb + 1) * LANES, ib * LANES : (ib + 1) * LANES]
            if jb < nq and abs(jb - ib) <= 1:
                block = block + parts[jb - ib + 1]
            elif jb == nq and ib == nq - 1:
                block = block + corner[0]
            elif jb == 2 * nq - 1 and ib == 0:
                block = block + corner[1]
            row.append(block)
        rows.append(jnp.concatenate(row, axis=1))
    return rows


def plain_query_aug(qaug, i, nq):
    rows = qaug.shape[0]
    return jnp.concatenate(
        [jnp.broadcast_to(qaug[i * nq + ib : i * nq + ib + 1, :], (LANES, LANES)) for ib in range(nq)], axis=0
    )


def forward_kernel(
    x_ref, xo_ref, w_ref, line_ref, qaug_ref, kaug_ref, hidden_ref,
    own_ref, oth_ref, ctx_ref, lse_ref, middle_ref,
    acc, s_ref, e_ref,
):
    m = pl.program_id(0)
    tokens = x_ref.shape[0]
    nq = tokens // LANES
    x, xo = x_ref[...], xo_ref[...]
    p_a = mm(x, w_ref[:, : 3 * LANES]).astype(BF16)
    p_b = mm(x, w_ref[:, 4 * LANES :]).astype(BF16)
    o_a = mm(xo, w_ref[:, LANES : 3 * LANES]).astype(BF16)
    o_b = mm(xo, w_ref[:, 4 * LANES :]).astype(BF16)
    own_ref[0, :, : 3 * LANES] = p_a
    own_ref[0, :, 3 * LANES :] = p_b
    oth_ref[0, :, : 2 * LANES] = o_a
    oth_ref[0, :, 2 * LANES :] = o_b
    cols_own = {0: p_a[:, :LANES], 1: p_a[:, LANES : 2 * LANES], 2: p_a[:, 2 * LANES :], 4: p_b[:, :LANES], 5: p_b[:, LANES:]}
    cols_oth = {1: o_a[:, :LANES], 2: o_a[:, LANES:], 4: o_b[:, :LANES], 5: o_b[:, LANES:]}
    both = {c: jnp.concatenate([cols_own[c], cols_oth[c]], axis=0) for c in (1, 2, 4, 5)}
    masks = [half_rows(0), half_rows(1)]
    flags = (line_ref[0, 3:4, :LANES], line_ref[0, 4:5, :LANES])
    v_t = {2: both[2].T, 4: both[4].T}
    count = lax.broadcasted_iota(jnp.int32, (HDIM, 2 * tokens), 0)
    ones = (count == 0).astype(F32).astype(BF16)
    pieces = []
    stats = []
    for i, (qc, qh, kc, vc, vh) in enumerate(HEAD_AT):
        line = line_ref[0, i : i + 1, :]
        tile = bias_tile(line)
        qa = cols_own[qc] * masks[qh] + plain_query_aug(qaug_ref[0], i, nq) * masks[1 - qh]
        ka = both[kc] * masks[qh] + kaug_ref[...] * masks[1 - qh]
        scores = mt(ka, qa)
        peak = None
        for jb, row in enumerate(plain_add_bias(scores, tile, line, flags, nq)):
            s_ref[i, jb * LANES : (jb + 1) * LANES, :] = row
            top = jnp.max(row.reshape(LANES // 8, 8, tokens), axis=0)
            peak = top if peak is None else jnp.maximum(peak, top)
        peak = jnp.max(peak, axis=0, keepdims=True)
        for jb in range(2 * nq):
            rows = slice(jb * LANES, (jb + 1) * LANES)
            e_ref[i, rows, :] = jnp.exp(s_ref[i, rows, :] - peak).astype(BF16)
        if vh == 0:
            va = jnp.concatenate([v_t[vc][:HDIM], ones], axis=0)
        else:
            va = jnp.concatenate([ones, v_t[vc][HDIM:]], axis=0)
        ot = mm(va, e_ref[i])
        at = HDIM if vh == 0 else 0
        total = ot[at : at + 1, :]
        stats.append(peak + jnp.log(total))
        real = ot[:HDIM] if vh == 0 else ot[HDIM:]
        pieces.append(real / total)
    zero = jnp.zeros((HDIM, tokens), F32)
    ctx_a = jnp.concatenate([pieces[0], pieces[1]], axis=0).T.astype(BF16)
    ctx_b = jnp.concatenate([zero, pieces[2]], axis=0).T.astype(BF16)
    ctx_ref[0, :, :LANES] = ctx_a
    ctx_ref[0, :, LANES:] = ctx_b
    for i in range(3):
        lse_ref[0, i : i + 1, :] = stats[i]
    lse_ref[0, 3:8, :] = jnp.zeros((5, tokens), F32)
    part = mt(ctx_a, w_ref[:, 3 * LANES : 4 * LANES]) + mt(ctx_b, w_ref[:, 5 * LANES :])

    @pl.when(m == 0)
    def _():
        acc[...] = hidden_ref[...] + part

    @pl.when(m > 0)
    def _():
        acc[...] += part

    @pl.when(m == pl.num_programs(0) - 1)
    def _():
        middle_ref[...] = acc[...]


def feed_kernel(
    middle_ref, grad_ref, gain_ref, wi_ref, wo_ref,
    out_ref, back_ref, gain_grad_ref, gi_ref, go_ref,
    x2_ref, x2t_ref, ob_ref, obt_ref, acc_out, acc_two,
):
    f = pl.program_id(0)

    @pl.when(f == 0)
    def _():
        x2 = rms_scaled(middle_ref[...], gain_ref[1:2, :]).astype(BF16)
        x2_ref[...] = x2
        x2t_ref[...] = x2.T
        ob = grad_ref[...].astype(BF16)
        ob_ref[...] = ob
        obt_ref[...] = ob.T
        acc_out[...] = jnp.zeros_like(acc_out)
        acc_two[...] = jnp.zeros_like(acc_two)

    inner = mm(x2_ref[...], wi_ref[...])
    active_back = mm(ob_ref[...], wo_ref[...])
    c = 0.7978845608028654
    sq = inner * inner
    th = jnp.tanh(c * (inner + 0.044715 * (sq * inner)))
    half = 0.5 * (1.0 + th)
    active = (inner * half).astype(BF16)
    slope = half + (0.5 * c) * inner * (1.0 - th * th) * (1.0 + (3 * 0.044715) * sq)
    inner_back = (slope * active_back).astype(BF16)
    acc_out[...] += mt(active, wo_ref[...])
    acc_two[...] += mt(inner_back, wi_ref[...])
    go_ref[...] = mm(obt_ref[...], active).astype(go_ref.dtype)
    gi_ref[...] = mm(x2t_ref[...], inner_back).astype(gi_ref.dtype)

    @pl.when(f == pl.num_programs(0) - 1)
    def _():
        out_ref[...] = middle_ref[...] + acc_out[...]
        result, gain_part = rms_back(middle_ref[...], gain_ref[1:2, :], acc_two[...])
        back_ref[...] = grad_ref[...] + result
        gain_grad_ref[...] = jnp.broadcast_to(gain_part, gain_grad_ref.shape)


def backward_kernel(
    x_ref, xo_ref, back_ref, w_ref, line_ref, qaug_ref, kaug_ref, own_ref, oth_ref, ctx_ref, lse_ref,
    ga_ref, one_own_ref, one_oth_ref, near_ref, sums_ref,
    xt_ref, xot_ref, ab_ref, abt_ref, acc_own, acc_oth,
):
    m = pl.program_id(0)
    tokens = x_ref.shape[0]
    nq = tokens // LANES

    @pl.when(m == 0)
    def _():
        xt_ref[...] = x_ref[...].T
        xot_ref[...] = xo_ref[...].T
        ab = back_ref[...].astype(BF16)
        ab_ref[...] = ab
        abt_ref[...] = ab.T
        acc_own[...] = jnp.zeros_like(acc_own)
        acc_oth[...] = jnp.zeros_like(acc_oth)

    ab = ab_ref[...]
    cb = {2: mm(ab, w_ref[:, 3 * LANES : 4 * LANES]).astype(BF16), 4: mm(ab, w_ref[:, 5 * LANES :]).astype(BF16)}
    ctx = {2: ctx_ref[0, :, :LANES], 4: ctx_ref[0, :, LANES:]}
    own = {c: own_ref[0, :, at * LANES : (at + 1) * LANES] for at, c in enumerate((0, 1, 2, 4, 5))}
    oth = {c: oth_ref[0, :, at * LANES : (at + 1) * LANES] for at, c in enumerate((1, 2, 4, 5))}
    masks = [half_rows(0), half_rows(1)]
    flags = (line_ref[0, 3:4, :LANES], line_ref[0, 4:5, :LANES])
    prod = {c: cb[c].astype(F32) * ctx[c].astype(F32) for c in (2, 4)}
    prod_hi = {c: prod[c].astype(BF16) for c in prod}
    prod_lo = {c: (prod[c] - prod_hi[c].astype(F32)).astype(BF16) for c in prod}
    dq_t = []
    dk = {}
    dv = {}
    for i, (qc, qh, kc, vc, vh) in enumerate(HEAD_AT):
        line = line_ref[0, i : i + 1, :]
        tile = bias_tile(line)
        qm = own[qc] * masks[qh]
        qa = qm + plain_query_aug(qaug_ref[0], i, nq) * masks[1 - qh]
        om = cb[vc] * masks[vh]
        pick = jnp.broadcast_to(masks[vh], (8, LANES))
        center = (mt(pick, prod_hi[vc]) + mt(pick, prod_lo[vc]))[0:1, :]
        lse = lse_ref[0, i : i + 1, :]
        kaug = kaug_ref[...] * masks[1 - qh]
        dqt = None
        parts = near_parts(tile)
        corner = plain_corner_parts(tile, line, flags)
        near = [None, None, None, None, None]
        for side, cols in enumerate((own, oth)):
            ka = cols[kc] * masks[qh] + kaug[side * tokens : (side + 1) * tokens]
            scores = mt(ka, qa)
            chance_back = mt(cols[vc], om)
            ps, ds = [], []
            for jb in range(nq):
                row_s, row_p, row_d = [], [], []
                for ib in range(nq):
                    at = (slice(jb * LANES, (jb + 1) * LANES), slice(ib * LANES, (ib + 1) * LANES))
                    block = scores[at]
                    kind = None
                    if side == 0 and abs(jb - ib) <= 1:
                        block = block + parts[jb - ib + 1]
                        kind = jb - ib + 1
                    elif side == 1 and jb == 0 and ib == nq - 1:
                        block = block + corner[0]
                        kind = 3
                    elif side == 1 and jb == nq - 1 and ib == 0:
                        block = block + corner[1]
                        kind = 4
                    p = jnp.exp(block - lse[:, at[1]])
                    d = p * (chance_back[at] - center[:, at[1]])
                    if kind is not None:
                        near[kind] = d if near[kind] is None else near[kind] + d
                    row_p.append(p.astype(BF16))
                    row_d.append(d.astype(BF16))
                ps.append(jnp.concatenate(row_p, axis=1))
                ds.append(jnp.concatenate(row_d, axis=1))
            pb = jnp.concatenate(ps, axis=0)
            db = jnp.concatenate(ds, axis=0)
            part_v = mm(pb, om)
            part_k = mm(db, qm)
            dv[vc, side] = part_v if (vc, side) not in dv else dv[vc, side] + part_v
            dk[kc, side] = part_k if (kc, side) not in dk else dk[kc, side] + part_k
            part_q = mm(ka.T, db)
            dqt = part_q if dqt is None else dqt + part_q
        at = HDIM if qh == 0 else 0
        sums_ref[0, i * 8 : (i + 1) * 8, :] = dqt[at + 8 : at + 16, :]
        dq_t.append(dqt[:HDIM] if qh == 0 else dqt[HDIM:])
        for kind in range(5):
            near_ref[0, i, kind] = near[kind]
    dq_a = jnp.concatenate([dq_t[0], dq_t[1]], axis=0).T
    dq_b = jnp.concatenate([dq_t[2], jnp.zeros_like(dq_t[2])], axis=0).T
    d_own = jnp.concatenate([dq_a, dk[1, 0], dv[2, 0], dq_b + dv[4, 0], dk[5, 0]], axis=1).astype(BF16)
    d_oth = jnp.concatenate([dk[1, 1], dv[2, 1], dv[4, 1], dk[5, 1]], axis=1).astype(BF16)
    xt, xot, abt = xt_ref[...], xot_ref[...], abt_ref[...]
    g_own = mm(xt, d_own)
    g_oth = mm(xot, d_oth)
    g_ctx = mm(abt, ctx_ref[0])
    ga_ref[:, :LANES] = g_own[:, :LANES].astype(ga_ref.dtype)
    ga_ref[:, LANES : 3 * LANES] = (g_own[:, LANES : 3 * LANES] + g_oth[:, : 2 * LANES]).astype(ga_ref.dtype)
    ga_ref[:, 3 * LANES : 4 * LANES] = g_ctx[:, :LANES].astype(ga_ref.dtype)
    ga_ref[:, 4 * LANES : 5 * LANES] = (g_own[:, 3 * LANES : 4 * LANES] + g_oth[:, 2 * LANES : 3 * LANES]).astype(ga_ref.dtype)
    ga_ref[:, 5 * LANES :] = (g_own[:, 4 * LANES :] + g_oth[:, 3 * LANES :] + g_ctx[:, LANES:]).astype(ga_ref.dtype)
    acc_own[...] += mt(d_own[:, : 3 * LANES], w_ref[:, : 3 * LANES]) + mt(d_own[:, 3 * LANES :], w_ref[:, 4 * LANES :])
    acc_oth[...] += mt(d_oth[:, : 2 * LANES], w_ref[:, LANES : 3 * LANES]) + mt(d_oth[:, 2 * LANES :], w_ref[:, 4 * LANES :])

    @pl.when(m == pl.num_programs(0) - 1)
    def _():
        one_own_ref[...] = acc_own[...]
        one_oth_ref[...] = acc_oth[...].astype(one_oth_ref.dtype)


def whole(shape):
    return pl.BlockSpec(shape, lambda m: (0,) * len(shape))


def params():
    return pltpu.CompilerParams(vmem_limit_bytes=60 * 2**20)


def run_forward(x, xo, wa, line, qaug, kaug, hidden, parts):
    t, d = x.shape
    return pl.pallas_call(
        forward_kernel,
        grid=(parts,),
        in_specs=[
            whole((t, d)), whole((t, d)),
            pl.BlockSpec((d, 6 * LANES), lambda m: (0, m)),
            pl.BlockSpec((1, 8, 4 * LANES), lambda m: (m, 0, 0)),
            pl.BlockSpec((1, 16, LANES), lambda m: (m, 0, 0)),
            whole((2 * t, LANES)), whole((t, d)),
        ],
        out_specs=[
            pl.BlockSpec((1, t, 5 * LANES), lambda m: (m, 0, 0)),
            pl.BlockSpec((1, t, 4 * LANES), lambda m: (m, 0, 0)),
            pl.BlockSpec((1, t, 2 * LANES), lambda m: (m, 0, 0)),
            pl.BlockSpec((1, 8, t), lambda m: (m, 0, 0)),
            whole((t, d)),
        ],
        out_shape=[
            jax.ShapeDtypeStruct((parts, t, 5 * LANES), BF16),
            jax.ShapeDtypeStruct((parts, t, 4 * LANES), BF16),
            jax.ShapeDtypeStruct((parts, t, 2 * LANES), BF16),
            jax.ShapeDtypeStruct((parts, 8, t), F32),
            jax.ShapeDtypeStruct((t, d), F32),
        ],
        scratch_shapes=[
            pltpu.VMEM((t, d), F32),
            pltpu.VMEM((3, 2 * t, t), F32),
            pltpu.VMEM((3, 2 * t, t), BF16),
        ],
        compiler_params=params(),
        name="attend_forward",
    )(x, xo, wa, line, qaug, kaug, hidden)


def run_feed(middle, grad, gains, wi, wo):
    t, d = middle.shape
    units = wi.shape[1]
    tile = min(512, units)
    return pl.pallas_call(
        feed_kernel,
        grid=(units // tile,),
        in_specs=[
            whole((t, d)), whole((t, d)), whole((2, d)),
            pl.BlockSpec((d, tile), lambda f: (0, f)),
            pl.BlockSpec((d, tile), lambda f: (0, f)),
        ],
        out_specs=[
            whole((t, d)), whole((t, d)), whole((8, d)),
            pl.BlockSpec((d, tile), lambda f: (0, f)),
            pl.BlockSpec((d, tile), lambda f: (0, f)),
        ],
        out_shape=[
            jax.ShapeDtypeStruct((t, d), F32),
            jax.ShapeDtypeStruct((t, d), F32),
            jax.ShapeDtypeStruct((8, d), F32),
            jax.ShapeDtypeStruct((d, units), BF16),
            jax.ShapeDtypeStruct((d, units), BF16),
        ],
        scratch_shapes=[
            pltpu.VMEM((t, d), BF16), pltpu.VMEM((d, t), BF16),
            pltpu.VMEM((t, d), BF16), pltpu.VMEM((d, t), BF16),
            pltpu.VMEM((t, d), F32), pltpu.VMEM((t, d), F32),
        ],
        compiler_params=params(),
        name="feed_both",
    )(middle, grad, gains, wi, wo)


def run_backward(x, xo, back, wa, line, qaug, kaug, own, oth, ctx, lse, parts):
    t, d = x.shape
    return pl.pallas_call(
        backward_kernel,
        grid=(parts,),
        in_specs=[
            whole((t, d)), whole((t, d)), whole((t, d)),
            pl.BlockSpec((d, 6 * LANES), lambda m: (0, m)),
            pl.BlockSpec((1, 8, 4 * LANES), lambda m: (m, 0, 0)),
            pl.BlockSpec((1, 16, LANES), lambda m: (m, 0, 0)),
            whole((2 * t, LANES)),
            pl.BlockSpec((1, t, 5 * LANES), lambda m: (m, 0, 0)),
            pl.BlockSpec((1, t, 4 * LANES), lambda m: (m, 0, 0)),
            pl.BlockSpec((1, t, 2 * LANES), lambda m: (m, 0, 0)),
            pl.BlockSpec((1, 8, t), lambda m: (m, 0, 0)),
        ],
        out_specs=[
            pl.BlockSpec((d, 6 * LANES), lambda m: (0, m)),
            whole((t, d)), whole((t, d)),
            pl.BlockSpec((1, 3, 5, LANES, LANES), lambda m: (m, 0, 0, 0, 0)),
            pl.BlockSpec((1, 24, t), lambda m: (m, 0, 0)),
        ],
        out_shape=[
            jax.ShapeDtypeStruct((d, parts * 6 * LANES), BF16),
            jax.ShapeDtypeStruct((t, d), F32),
            jax.ShapeDtypeStruct((t, d), BF16),
            jax.ShapeDtypeStruct((parts, 3, 5, LANES, LANES), F32),
            jax.ShapeDtypeStruct((parts, 24, t), F32),
        ],
        scratch_shapes=[
            pltpu.VMEM((d, t), BF16), pltpu.VMEM((d, t), BF16),
            pltpu.VMEM((t, d), BF16), pltpu.VMEM((d, t), BF16),
            pltpu.VMEM((t, d), F32), pltpu.VMEM((t, d), F32),
        ],
        compiler_params=params(),
        name="attend_backward",
    )(x, xo, back, wa, line, qaug, kaug, own, oth, ctx, lse)


def pack_attn(attn, out_t):
    cut = [[part[:, i * HDIM : (i + 1) * HDIM] for i in range(3)] for part in (attn[0], attn[1], attn[2], out_t)]
    q, k, v, o = cut
    return jnp.concatenate([q[0], q[1], k[0], k[1], v[0], v[1], o[0], o[1], q[2], v[2], k[2], o[2]], axis=1)


def unpack_attn(block):
    c = [block[:, i * HDIM : (i + 1) * HDIM] for i in range(12)]
    attn = jnp.stack(
        [
            jnp.concatenate([c[0], c[1], c[8]], axis=1),
            jnp.concatenate([c[2], c[3], c[10]], axis=1),
            jnp.concatenate([c[4], c[5], c[9]], axis=1),
        ]
    )
    return attn, jnp.concatenate([c[6], c[7], c[11]], axis=1)


def general_body(
    hidden_in, out_grad, attn_weight, out_weight, inner_weight, outer_weight, rel_bias, gains, lengths, table,
    attn_first, attn_second, out_first, out_second, inner_first, inner_second, outer_first, outer_second,
    rel_first, rel_second, gain_first, gain_second, *, parts,
):
    tokens = hidden_in.shape[0]
    nq = tokens // LANES
    heads = rel_bias.shape[1]
    per_seq = SEQLEN // tokens
    mp_index = lax.axis_index("mp")
    half = mp_index % per_seq
    length = lengths[mp_index // per_seq]

    shard = [
        pack_attn(attn_weight.astype(BF16), out_weight.astype(BF16).T),
        inner_weight.astype(BF16),
        outer_weight.astype(BF16).T,
    ]
    gathered = [lax.all_gather(lax.all_gather(s, "dp", axis=0, tiled=True), "mp", axis=1, tiled=True) for s in shard]
    wa, wi, wo = gathered

    x1 = rms_scaled(hidden_in, gains[0]).astype(BF16)
    swap = [(p, p ^ 1) for p in range(parts)]
    x1o = lax.ppermute(x1, "mp", swap)

    u = jnp.arange(4 * LANES)
    offset = jnp.where(u < 2 * LANES, -u, 4 * LANES - u)
    buckets = jnp.arange(rel_bias.shape[0], dtype=jnp.int32)
    line_hot = (jnp.take(table, offset + SEQLEN - 1)[:, None] == buckets[None, :]).astype(F32)
    line = jnp.dot(line_hot, rel_bias, precision=lax.Precision.HIGHEST).T.reshape(parts, heads // parts, 4 * LANES)
    first_flag = (half == 0).astype(F32)
    flags = jnp.stack([jnp.full((4 * LANES,), first_flag), jnp.full((4 * LANES,), 1.0 - first_flag)])
    line_in = jnp.concatenate(
        [line, jnp.broadcast_to(flags[None], (parts, 2, 4 * LANES)), jnp.zeros((parts, 3, 4 * LANES), F32)], axis=1
    )
    far_before, far_after = line[:, :, LANES], line[:, :, 3 * LANES]
    jb, ib = jnp.arange(nq)[None, :], jnp.arange(nq)[:, None]
    own_before, own_after = (jb < ib - 1).astype(F32), (jb > ib + 1).astype(F32)
    oth_before = jnp.full((nq, nq), 1.0 - first_flag)
    w_before = jnp.concatenate([own_before, oth_before], axis=1)
    w_after = jnp.concatenate([own_after, 1.0 - oth_before], axis=1)
    far = far_before[:, :, None, None] * w_before + far_after[:, :, None, None] * w_after
    far_hi = far.astype(BF16).astype(F32)
    far_lo = far - far_hi
    one = jnp.ones((parts, heads // parts, nq, 1), F32)
    blank = jnp.zeros((parts, heads // parts, nq, HDIM), F32)
    q64 = jnp.concatenate(
        [blank[..., :3], one, blank[..., :4], far_hi, far_lo, blank[..., : HDIM - 8 - 4 * nq]], axis=-1
    )
    qaug = jnp.concatenate([q64, q64], axis=-1).reshape(parts, 3 * nq, LANES)
    qaug = jnp.pad(qaug, ((0, 0), (0, 16 - 3 * nq), (0, 0))).astype(BF16)
    row = jnp.arange(2 * tokens)
    position = jnp.where(row < tokens, half * tokens + row, (1 - half) * tokens + row - tokens)
    masked = jnp.where(position < length, 0.0, NEG)
    col = jnp.arange(LANES) % HDIM
    block_of = row // LANES
    hot = ((col >= 8) & (col < 8 + 4 * nq))[None, :] & ((col[None, :] - 8) % (2 * nq) == block_of[:, None])
    kaug = jnp.where((col == 3)[None, :], masked[:, None], hot.astype(F32)).astype(BF16)

    own, oth, ctx, lse, middle = run_forward(x1, x1o, wa, line_in, qaug, kaug, hidden_in, parts)
    block_out, middle_back, gain_two, gi, go = run_feed(middle, out_grad, gains, wi, wo)
    ga, one_own, one_oth, near, sums = run_backward(
        x1, x1o, middle_back, wa, line_in, qaug, kaug, own, oth, ctx, lse, parts
    )
    one_back = one_own + lax.ppermute(one_oth, "mp", swap).astype(F32)
    input_grad, gain_one = rms_back(hidden_in, gains[0:1], one_back)
    input_grad = input_grad + middle_back

    nh = heads // parts
    near = near.reshape(heads, 5, LANES, LANES)
    first_w = first_flag
    blocks = jnp.stack(
        [near[:, 0] + near[:, 4] * (1.0 - first_w), near[:, 1], near[:, 2] + near[:, 3] * first_w], axis=1
    )
    r = jnp.arange(LANES)
    diff = r[None, :, None] - r[None, None, :] + (jnp.arange(3) - 1)[:, None, None] * LANES
    near_bucket = jnp.take(table, diff + SEQLEN - 1).reshape(1, -1)
    near_hot = (near_bucket == buckets[:, None]).astype(F32)
    near_grad = lax.dot_general(
        near_hot, blocks.reshape(heads, -1), (((1,), (1,)), ((), ())), precision=lax.Precision.HIGHEST
    )
    block_sums = jnp.sum(sums.reshape(heads, 2 * nq, nq, LANES), axis=-1)
    far_w = jnp.transpose(jnp.stack([w_before, w_after]), (0, 2, 1))
    corner = jnp.stack([jnp.sum(near[:, 4], (1, 2)) * (1.0 - first_w), jnp.sum(near[:, 3], (1, 2)) * first_w])
    far_grad = jnp.einsum("hji,sji->sh", block_sums, far_w, precision=lax.Precision.HIGHEST) - corner
    far_hot = (jnp.stack([table[0], table[2 * SEQLEN - 2]])[None, :] == buckets[:, None]).astype(F32)
    rel_part = near_grad + jnp.dot(far_hot, far_grad, precision=lax.Precision.HIGHEST)

    owned = [
        lax.psum_scatter(
            lax.psum_scatter(g, "mp", scatter_dimension=1, tiled=True), "dp", scatter_dimension=0, tiled=True
        ).astype(F32)
        for g in (ga, gi, go)
    ]
    g_attn, g_out_t = unpack_attn(owned[0])
    grads = (g_attn, g_out_t.T, owned[1], owned[2].T)
    square_part = sum(jnp.sum(g * g) for g in owned)
    gain_grad, rel_grad, square_total = lax.psum(
        (jnp.concatenate([gain_one, gain_two[:1]], axis=0), rel_part, square_part), ("dp", "mp")
    )
    grad_norm = jnp.sqrt(square_total + jnp.sum(gain_grad * gain_grad) + jnp.sum(rel_grad * rel_grad))
    factor = jnp.minimum(1.0, CLIP / (grad_norm + 1e-06))
    attn_new = adam_step(attn_weight, grads[0], attn_first, attn_second, factor, RATE_MATRIX)
    out_new = adam_step(out_weight, grads[1], out_first, out_second, factor, RATE_OUT)
    inner_new = adam_step(inner_weight, grads[2], inner_first, inner_second, factor, RATE_MATRIX)
    outer_new = adam_step(outer_weight, grads[3], outer_first, outer_second, factor, RATE_MATRIX)
    rel_new = adam_step(rel_bias, rel_grad, rel_first, rel_second, factor, RATE_SMALL)
    gain_new = adam_step(gains, gain_grad, gain_first, gain_second, factor, RATE_SMALL)
    return (block_out, input_grad, grad_norm, *attn_new, *out_new, *inner_new, *outer_new, *rel_new, *gain_new)


def solution(mesh):
    rows = P(("dp", "mp"), None)
    attn, up, down = P(None, "dp", "mp"), P("dp", "mp"), P("mp", "dp")
    in_specs = (
        rows, rows, attn, down, up, down, P(), P(), P("dp"), P(),
        attn, attn, down, down, up, up, down, down, P(), P(), P(), P(),
    )
    out_specs = (rows, rows, P()) + (attn,) * 3 + (down,) * 3 + (up,) * 3 + (down,) * 3 + (P(),) * 6
    plan = body if (mesh.shape["dp"], mesh.shape["mp"]) == (8, 4) else general_body
    return jax.shard_map(
        functools.partial(plan, parts=mesh.shape["mp"]),
        mesh=mesh, in_specs=in_specs, out_specs=out_specs, check_vma=False,
    )
```
